32 devices in a mesh: seq: 2 (over x), ctx: 4 (over z), mp: 4 (over y, core).
Axes of the slice: x: 2, y: 2, z: 4, core: 2. Of those that a mesh axis runs over, the one named last changes fastest.
Arguments:
- tokens: bfloat16 [5120, 1536], P(('seq', 'ctx')), may hold values from -6 to 6
- norm1_gain: float32 [1536], replicated, may hold values from 0.5 to 1.5
- w_query: bfloat16 [1536, 1536], P(None, 'mp'), may hold values from -0.15625 to 0.15625
- key_weight_matrix: bfloat16 [1536, 512], P(None, 'mp'), may hold values from -0.15625 to 0.15625
- value_weight_matrix: bfloat16 [1536, 512], P(None, 'mp'), may hold values from -0.15625 to 0.15625
- w_out: bfloat16 [1536, 1536], P('mp'), may hold values from -0.625 to 0.625
- norm2_gain: float32 [1536], replicated, may hold values from 0.5 to 1.5
- router: float32 [1536, 8], replicated, may hold values from -0.109375 to 0.109375
- w_gate: bfloat16 [8, 1536, 1024], P('mp'), may hold values from -0.15625 to 0.15625
- w_up: bfloat16 [8, 1536, 1024], P('mp'), may hold values from -0.15625 to 0.15625
- w_down: bfloat16 [8, 1024, 1536], P('mp'), may hold values from -0.1875 to 0.1875
- routes: int32 [5120, 2], P(('seq', 'ctx')), may hold values from 0 to 7, all different within a row; in each aligned block of 160 rows (0 to 159, 160 to 319, ...) at most 50 rows name the same one
- cotangent: bfloat16 [5120, 1536], P(('seq', 'ctx', 'mp')), may hold values from -6 to 6
Outputs:
- output: float32 [5120, 1536], P(('seq', 'ctx', 'mp'))
- grad_tokens: float32 [5120, 1536], P(('seq', 'ctx', 'mp'))
- grad_norm1: float32 [1536], replicated
- grad_query: float32 [1536, 1536], P(('seq', 'ctx'), 'mp')
- grad_key: float32 [1536, 512], P(('seq', 'ctx'), 'mp')
- grad_value: float32 [1536, 512], P(('seq', 'ctx'), 'mp')
- grad_out: float32 [1536, 1536], P('mp', ('seq', 'ctx'))
- grad_norm2: float32 [1536], replicated
- grad_router: float32 [1536, 8], replicated
- grad_gate: float32 [8, 1536, 1024], P('mp', ('seq', 'ctx'))
- grad_up: float32 [8, 1536, 1024], P('mp', ('seq', 'ctx'))
- grad_down: float32 [8, 1024, 1536], P('mp', ('seq', 'ctx'))
The draws below stay inside these ranges and needn't reach their ends.
Inputs may be any that keep to these rules, and one draw needn't show every extreme that they name: `routes`: the two experts of a row differ. Rows are taken in aligned blocks of 160; within one block no expert is named more than 50 times, a bound that some block reaches.
All inputs are finite; a program needn't handle non-finite values.
Results may differ from the reference program's by a relative error of at most 0.02.
Values may be sent and summed in bfloat16 or wider, within the bound.
A program may use at most 192 MiB of HBM per device.

```python
import math
import jax
import jax.numpy as jnp
import numpy as np
from jax import lax

MODEL_WIDTH = 1536
QUERY_HEADS = 24
KEY_VALUE_HEADS = 8
HEAD_SIZE = 64
FE = 1024
TOP = 2
TOK_DEV = 640
SEQUENCE_LENGTH = 2560
TOKENS = 5120
EXPERTS = 8
SHARE = 160
CAP = 50
N_SEQ = 2
N_MP = 4


def levels(stream_key, dims, split, least, high):
    def one(dim, shards_of):
        steps = jax.random.uniform(jax.random.fold_in(jax.random.fold_in(stream_key, 6), dim), (shards_of,), jnp.float32, least / len(split), high / len(split))
        return jnp.repeat(jnp.exp(steps), dims[dim] // shards_of).reshape((-1,) + (1,) * (len(dims) - dim - 1))

    level = one(*split[0])
    for cut in split[1:]:
        level = level * one(*cut)
    return level


def assign_block(own_key, own, number, rows, count, top, bound, slope):
    order = jax.random.permutation(own_key, count)
    heavy_load, ordinary = shares(count, rows * top, bound, slope, True), shares(count, rows * top, bound, slope, False)
    places = jnp.arange(count)

    def named(sizes, offset_by):
        used = int((sizes > 0).sum())
        fixed = max(1, used // 4)
        shifted = fixed + (places - fixed + offset_by * (used - fixed)) % max(1, count - fixed)
        return jnp.zeros((count,), jnp.int32).at[order[jnp.where(places < fixed, places, shifted)]].set(jnp.asarray(sizes, jnp.int32))

    sizes = jnp.where(number % 4 == 0, named(heavy_load, number // 4), named(ordinary, number - number // 4 - 1))
    mixed = jax.random.permutation(jax.random.fold_in(own, 3), count)
    donor, receiver = mixed[0:count // 2 * 2:2], mixed[1:count // 2 * 2:2]
    room = jnp.minimum(sizes[donor] - 1, bound - sizes[receiver]) // 2
    room = jnp.where((donor == order[0]) | (receiver == order[0]) | (sizes[receiver] == 0), 0, jnp.maximum(room, 0))
    shifted = jax.random.randint(jax.random.fold_in(own, 4), (count // 2,), 0, 1 << 20) % (room + 1)
    sizes = sizes.at[donor].add(-shifted).at[receiver].add(shifted)
    items = jnp.searchsorted(jnp.cumsum(sizes), jnp.arange(rows * top), side="right").astype(jnp.int32)
    listing = items.reshape(top, rows).T
    listing = listing[jax.random.permutation(jax.random.fold_in(own, 1), rows)]
    offset_by = jax.random.randint(jax.random.fold_in(own, 2), (rows, 1), 0, top)
    return jnp.take_along_axis(listing, (jnp.arange(top)[None, :] + offset_by) % top, axis=1)


def shares(amount, total, most, skew, full):
    loads = [(1 << 20) // math.isqrt(grade ** skew) + 1 for grade in range(1, amount + 1)]
    largest = most if full else min(most, max(-(-total // amount), total * loads[0] // sum(loads)))
    least = 1 if total - largest >= amount - 1 else 0
    holding, surplus = [largest] + [least] * (amount - 1), total - largest - least * (amount - 1)
    while surplus > 0:
        free = [i for i in range(1, amount) if holding[i] < largest] or [i for i in range(1, amount) if holding[i] < most]
        mass, remaining = sum([loads[i] for i in free]), surplus
        for i in free:
            addition = min(most - holding[i], max(1, remaining * loads[i] // mass), surplus)
            holding[i] = holding[i] + addition
            surplus = surplus - addition
    return np.array(holding)


def gaussian(key, extent, deviation, reach, split=(), held_as=jnp.bfloat16):
    result = deviation * jax.random.normal(key, extent, jnp.float32)
    if split:
        result = result * levels(key, extent, split, -0.22, 0.18)
    return jnp.clip(result, -reach, reach).astype(held_as)


def setup_inputs(seed: int = 0) -> dict:
    seeds = jax.random.split(jax.random.key(seed), 14)
    tokens = gaussian(seeds[0], (TOKENS, MODEL_WIDTH), 1.0, 6.0, ((0, 8),))
    norm1_gain = jnp.clip(1.0 + 0.1 * jax.random.normal(seeds[1], (MODEL_WIDTH,), jnp.float32), 0.5, 1.5)
    w_query = gaussian(seeds[2], (MODEL_WIDTH, QUERY_HEADS * HEAD_SIZE), MODEL_WIDTH ** -0.5, 0.15625, ((1, 4),))
    key_weight_matrix = gaussian(seeds[3], (MODEL_WIDTH, KEY_VALUE_HEADS * HEAD_SIZE), MODEL_WIDTH ** -0.5, 0.15625, ((1, 4),))
    value_weight_matrix = gaussian(seeds[4], (MODEL_WIDTH, KEY_VALUE_HEADS * HEAD_SIZE), MODEL_WIDTH ** -0.5, 0.15625, ((1, 4),))
    w_out = gaussian(seeds[5], (QUERY_HEADS * HEAD_SIZE, MODEL_WIDTH), (QUERY_HEADS * HEAD_SIZE // 16) ** -0.5, 0.625, ((0, 4),))
    norm2_gain = jnp.clip(1.0 + 0.1 * jax.random.normal(seeds[6], (MODEL_WIDTH,), jnp.float32), 0.5, 1.5)
    router = gaussian(seeds[7], (MODEL_WIDTH, EXPERTS), (2 * MODEL_WIDTH) ** -0.5, 0.109375, (), jnp.float32)
    w_gate = gaussian(seeds[8], (EXPERTS, MODEL_WIDTH, FE), MODEL_WIDTH ** -0.5, 0.15625, ((0, 4),))
    w_up = gaussian(seeds[9], (EXPERTS, MODEL_WIDTH, FE), MODEL_WIDTH ** -0.5, 0.15625, ((0, 4),))
    w_down = gaussian(seeds[10], (EXPERTS, FE, MODEL_WIDTH), FE ** -0.5, 0.1875, ((0, 4),))
    routes_keys = jax.random.split(jax.random.fold_in(seeds[11], 1), TOKENS // SHARE)
    routes_turns = jax.random.permutation(jax.random.fold_in(seeds[11], 3), TOKENS // SHARE)
    routes = jax.vmap(lambda own, number: assign_block(jax.random.fold_in(seeds[11], 2), own, number, SHARE, EXPERTS, TOP, CAP, 1))(routes_keys, routes_turns).reshape((TOKENS, TOP))
    cotangent = gaussian(seeds[12], (TOKENS, MODEL_WIDTH), 1.0, 6.0, ((0, 32),))
    return dict(tokens=tokens, norm1_gain=norm1_gain, w_query=w_query, key_weight_matrix=key_weight_matrix, value_weight_matrix=value_weight_matrix, w_out=w_out, norm2_gain=norm2_gain, router=router, w_gate=w_gate, w_up=w_up, w_down=w_down, routes=routes, cotangent=cotangent)


@jax.custom_vjp
def low(v):
    return lax.optimization_barrier(v.astype(jnp.bfloat16)).astype(jnp.float32)

@jax.custom_vjp
def low_back(v):
    return v

def low_keep(v):
    return (low(v), None)

def low_pass(kept, grad):
    return (grad,)

def back_keep(v):
    return (v, None)

def back_low(kept, grad):
    return (low(grad),)
low.defvjp(low_keep, low_pass)
low_back.defvjp(back_keep, back_low)
EPS = 1e-06

def rms_rows(rows):
    return rows * lax.rsqrt(lax.optimization_barrier(jnp.mean(rows * rows, axis=-1, keepdims=True)) + EPS)

def slot_targets(routes):
    share = TOK_DEV // N_MP
    blocks = routes.reshape(TOKENS // share, share * TOP)
    onehot = (blocks[:, :, None] == jnp.arange(EXPERTS, dtype=jnp.int32)[None, None, :]).astype(jnp.int32)
    ranks = lax.optimization_barrier(jnp.sum((jnp.cumsum(onehot, axis=1) - 1) * onehot, axis=2))
    return (blocks * CAP + ranks).astype(jnp.int32)

def attention(query_rows, key_rows, value_rows):
    query_group = QUERY_HEADS // KEY_VALUE_HEADS
    qblock = 512 if SEQUENCE_LENGTH % 512 == 0 else SEQUENCE_LENGTH
    per_seq = SEQUENCE_LENGTH // qblock
    hp = lax.Precision.HIGHEST
    query_rows_all = query_rows.reshape(N_SEQ, SEQUENCE_LENGTH, KEY_VALUE_HEADS, query_group, HEAD_SIZE)
    key_rows_all = key_rows.reshape(N_SEQ, SEQUENCE_LENGTH, KEY_VALUE_HEADS, HEAD_SIZE)
    value_rows_all = value_rows.reshape(N_SEQ, SEQUENCE_LENGTH, KEY_VALUE_HEADS, HEAD_SIZE)

    def one_block(index):
        sequence = index // per_seq
        first = (index % per_seq * qblock).astype(jnp.int32)
        q_seq = lax.dynamic_index_in_dim(query_rows_all, sequence, 0, keepdims=False)
        q_rows = lax.dynamic_slice_in_dim(q_seq, first, qblock, 0)
        k_seq = lax.dynamic_index_in_dim(key_rows_all, sequence, 0, keepdims=False)
        v_seq = lax.dynamic_index_in_dim(value_rows_all, sequence, 0, keepdims=False)
        scores = jnp.einsum('qhgd,khd->hgqk', q_rows, k_seq, precision=hp) * 0.125
        scores = low_back(scores)
        mask = jnp.arange(SEQUENCE_LENGTH, dtype=jnp.int32)[None, :] <= (first + jnp.arange(qblock, dtype=jnp.int32))[:, None]
        scores = jnp.where(mask, scores, -1e+30)
        peak = lax.optimization_barrier(jnp.max(scores, axis=-1, keepdims=True))
        weights = jnp.exp(scores - peak)
        probs = low(weights / lax.optimization_barrier(jnp.sum(weights, axis=-1, keepdims=True)))
        return jnp.einsum('hgqk,khd->qhgd', probs, v_seq, precision=hp)
    blocks = lax.map(jax.checkpoint(one_block), jnp.arange(N_SEQ * per_seq, dtype=jnp.int32))
    return blocks.reshape(TOKENS, QUERY_HEADS * HEAD_SIZE)

def forward(x, gain_one, w_query, key_weight_matrix, value_weight_matrix, w_out, gain_two, router, w_gate, w_up, w_down, dest, routes):
    hp = lax.Precision.HIGHEST
    h_one = low(rms_rows(x) * gain_one)
    query_rows = low_back(low(jnp.dot(h_one, w_query, precision=hp)))
    key_rows = low_back(low(jnp.dot(h_one, key_weight_matrix, precision=hp)))
    value_rows = low_back(low(jnp.dot(h_one, value_weight_matrix, precision=hp)))
    heads = low_back(low(attention(query_rows, key_rows, value_rows)))
    branch = low_back(jnp.dot(heads, w_out, precision=hp))
    resid = x + branch
    h_two = low(rms_rows(resid) * gain_two)
    logits = jnp.dot(h_two, router, precision=hp)
    onehot = (routes[:, :, None] == jnp.arange(EXPERTS, dtype=jnp.int32)[None, None, :]).astype(logits.dtype)
    chosen = lax.optimization_barrier(jnp.sum(logits[:, None, :] * onehot, axis=-1))
    gates = jax.nn.softmax(chosen, axis=-1)
    share = TOK_DEV // N_MP
    nblock = TOKENS // share
    rows = jnp.repeat(h_two.reshape(nblock, share, MODEL_WIDTH), TOP, axis=1)
    buffers = jax.vmap(lambda d, r: jnp.zeros((EXPERTS * CAP, MODEL_WIDTH), r.dtype).at[d].set(r))(dest, rows)
    buffers = low_back(buffers)
    expert_in = buffers.reshape(nblock, EXPERTS, CAP, MODEL_WIDTH).transpose(1, 0, 2, 3).reshape(EXPERTS, nblock * CAP, MODEL_WIDTH)
    gate_pre = low_back(jnp.einsum('erd,edf->erf', expert_in, w_gate, precision=hp))
    up_pre = low_back(jnp.einsum('erd,edf->erf', expert_in, w_up, precision=hp))
    hidden = low(jax.nn.silu(gate_pre) * up_pre)
    expert_out = low_back(low(jnp.einsum('erf,efd->erd', hidden, w_down, precision=hp)))
    back = expert_out.reshape(EXPERTS, nblock, CAP, MODEL_WIDTH).transpose(1, 0, 2, 3).reshape(nblock, EXPERTS * CAP, MODEL_WIDTH)
    picked = jax.vmap(lambda b, d: b[d])(back, dest).reshape(TOKENS, TOP, MODEL_WIDTH)
    return resid + lax.optimization_barrier(jnp.sum(gates[:, :, None] * picked, axis=1))

def reference(tokens, norm1_gain, w_query, key_weight_matrix, value_weight_matrix, w_out, norm2_gain, router, w_gate, w_up, w_down, routes, cotangent):
    dest = slot_targets(routes)
    floats = (tokens.astype(jnp.float32), norm1_gain.astype(jnp.float32), w_query.astype(jnp.float32), key_weight_matrix.astype(jnp.float32), value_weight_matrix.astype(jnp.float32), w_out.astype(jnp.float32), norm2_gain.astype(jnp.float32), router.astype(jnp.float32), w_gate.astype(jnp.float32), w_up.astype(jnp.float32), w_down.astype(jnp.float32))

    def wrapped(*params):
        return forward(*params, dest, routes)
    output, pull = jax.vjp(wrapped, *floats)
    grads = pull(cotangent.astype(jnp.float32))
    return (output, grads[0], grads[1], grads[2], grads[3], grads[4], grads[5], grads[6], grads[7], grads[8], grads[9], grads[10])
```

```python
import functools

import jax
import jax.numpy as jnp
from jax import lax
from jax.experimental import pallas as pl
from jax.experimental.pallas import tpu as pltpu
from jax.sharding import PartitionSpec as P

HEAD_SIZE = 64
EPS = 1e-06
MESH = pl.DeviceIdType.MESH
F32 = jnp.float32
BF16 = jnp.bfloat16
VMEM = pl.BlockSpec(memory_space=pltpu.VMEM)
DMA = pltpu.SemaphoreType.DMA
MIB = 2**20


def params(collective_id, mib=56):
    return pltpu.CompilerParams(
        collective_id=collective_id, has_side_effects=True, vmem_limit_bytes=mib * MIB
    )


def nt(a, b):
    return lax.dot_general(a, b, (((1,), (1,)), ((), ())), preferred_element_type=F32)


def nn(a, b):
    return jnp.dot(a, b, preferred_element_type=F32)


def line_barrier(c, n, up, down):
    sem = pltpu.get_barrier_semaphore()

    @pl.when(c > 0)
    def _():
        pl.semaphore_signal(sem, inc=1, device_id=down, device_id_type=MESH)

    @pl.when(c < n - 1)
    def _():
        pl.semaphore_signal(sem, inc=1, device_id=up, device_id_type=MESH)

    pl.semaphore_wait(sem, jnp.where(c > 0, 1, 0) + jnp.where(c < n - 1, 1, 0))


def pad_heads(src, dst, heads, group):
    dst[...] = jnp.zeros_like(dst)
    for h in range(heads):
        g = h // group
        rows = slice(g * HEAD_SIZE, (g + 1) * HEAD_SIZE)
        dst[h, rows, :] = src[h * HEAD_SIZE : (h + 1) * HEAD_SIZE, :]


def causal(t):
    keys = lax.broadcasted_iota(jnp.int32, (t, t), 0)
    queries = lax.broadcasted_iota(jnp.int32, (t, t), 1)
    return keys <= queries


def attend_kernel(n, q_ref, k_ref, v_ref, o_ref, heads_ref, lse_ref, kv_ref, qpad, vt, top, tot, send, recv):
    s, c, m = lax.axis_index("seq"), lax.axis_index("ctx"), lax.axis_index("mp")
    t, kvw = k_ref.shape
    heads = q_ref.shape[0] // HEAD_SIZE
    group = heads // (kvw // HEAD_SIZE)
    up, down = (s, lax.rem(c + 1, n), m), (s, lax.rem(c + n - 1, n), m)
    kv_ref[0, :, :kvw] = k_ref[...]
    kv_ref[0, :, kvw:] = v_ref[...]
    line_barrier(c, n, up, down)

    def pass_up(slot):
        return pltpu.make_async_remote_copy(
            src_ref=kv_ref.at[slot],
            dst_ref=kv_ref.at[slot + 1],
            send_sem=send.at[slot],
            recv_sem=recv.at[slot + 1],
            device_id=up,
            device_id_type=MESH,
        )

    def got(slot):
        return pltpu.make_async_remote_copy(
            src_ref=kv_ref.at[slot],
            dst_ref=kv_ref.at[slot],
            send_sem=send.at[slot],
            recv_sem=recv.at[slot],
            device_id=up,
            device_id_type=MESH,
        )

    @pl.when(c < n - 1)
    def _():
        pass_up(0).start()

    pad_heads(q_ref, qpad, heads, group)
    top[...] = jnp.full_like(top, -1e30)
    tot[...] = jnp.zeros_like(tot)
    o_ref[...] = jnp.zeros_like(o_ref)

    def block(slot, masked):
        vt[...] = kv_ref[slot, :, kvw:].T

        def head(h, carry):
            g = lax.div(h, group)
            scores = nn(kv_ref[slot, :, :kvw], qpad[h])
            if masked:
                scores = jnp.where(causal(t), scores, -1e30)
            old = top[h]
            new = jnp.maximum(old, jnp.max(scores, axis=0, keepdims=True))
            weights = jnp.exp(scores - new)
            factor = jnp.exp(old - new)
            top[h] = new
            tot[h] = tot[h] * factor + jnp.sum(weights, axis=0, keepdims=True)
            rows = pl.ds(pl.multiple_of(h * HEAD_SIZE, HEAD_SIZE), HEAD_SIZE)
            vrows = pl.ds(pl.multiple_of(g * HEAD_SIZE, HEAD_SIZE), HEAD_SIZE)
            o_ref[rows, :] = o_ref[rows, :] * factor + nn(vt[vrows, :], weights.astype(BF16))
            return carry

        lax.fori_loop(0, heads, head, 0)

    block(0, True)

    def earlier(slot, carry):
        got(slot).wait_recv()

        @pl.when(c < n - 1)
        def _():
            pass_up(slot).start()

        block(slot, False)
        return carry

    lax.fori_loop(1, c + 1, earlier, 0)
    for h in range(heads):
        rows = slice(h * HEAD_SIZE, (h + 1) * HEAD_SIZE)
        done = o_ref[rows, :] / tot[h]
        o_ref[rows, :] = done
        heads_ref[rows, :] = done.astype(BF16)
        lse_ref[h] = top[h] + jnp.log(tot[h])

    @pl.when(c < n - 1)
    def _():
        def sent(slot, carry):
            pass_up(slot).wait_send()
            return carry

        lax.fori_loop(0, c + 1, sent, 0)


def attend(n, qt, k, v):
    t, kvw = k.shape
    qw = qt.shape[0]
    heads = qw // HEAD_SIZE
    return pl.pallas_call(
        functools.partial(attend_kernel, n),
        out_shape=(
            jax.ShapeDtypeStruct((qw, t), F32),
            jax.ShapeDtypeStruct((qw, t), BF16),
            jax.ShapeDtypeStruct((heads, 1, t), F32),
            jax.ShapeDtypeStruct((n, t, 2 * kvw), BF16),
        ),
        in_specs=[VMEM] * 3,
        out_specs=(VMEM,) * 4,
        scratch_shapes=[
            pltpu.VMEM((heads, kvw, t), BF16),
            pltpu.VMEM((kvw, t), BF16),
            pltpu.VMEM((heads, 1, t), F32),
            pltpu.VMEM((heads, 1, t), F32),
            DMA((n,)),
            DMA((n,)),
        ],
        compiler_params=params(0),
        name="attend",
    )(qt, k, v)


def attend_back_kernel(
    n, q_ref, do_ref, o_ref, lse_ref, kv_ref, dq_ref, dkv_ref, qpad, dopad, delta, dq, kt, part, passing, send, recv
):
    s, c, m = lax.axis_index("seq"), lax.axis_index("ctx"), lax.axis_index("mp")
    _, t, kvw2 = kv_ref.shape
    kvw = kvw2 // 2
    heads = q_ref.shape[0] // HEAD_SIZE
    group = heads // (kvw // HEAD_SIZE)
    up, down = (s, lax.rem(c + 1, n), m), (s, lax.rem(c + n - 1, n), m)
    line_barrier(c, n, up, down)
    pad_heads(q_ref, qpad, heads, group)
    pad_heads(do_ref, dopad, heads, group)
    for h in range(heads):
        rows = slice(h * HEAD_SIZE, (h + 1) * HEAD_SIZE)
        delta[h] = jnp.sum(do_ref[rows, :].astype(F32) * o_ref[rows, :], axis=0, keepdims=True)
    dq[...] = jnp.zeros_like(dq)

    def block(j, masked):
        slot = c - j
        acc = part.at[lax.rem(j, 2)]
        acc[...] = jnp.zeros(acc.shape, F32)
        kt[...] = kv_ref[slot, :, :kvw].T

        def head(h, carry):
            g = lax.div(h, group)
            scores = nn(kv_ref[slot, :, :kvw], qpad[h])
            probs = jnp.exp(scores - lse_ref[h])
            if masked:
                probs = jnp.where(causal(t), probs, 0.0)
            dprobs = nn(kv_ref[slot, :, kvw:], dopad[h])
            ds = (probs * (dprobs - delta[h])).astype(BF16)
            rows = pl.ds(pl.multiple_of(h * HEAD_SIZE, HEAD_SIZE), HEAD_SIZE)
            krows = pl.ds(pl.multiple_of(g * HEAD_SIZE, HEAD_SIZE), HEAD_SIZE)
            dq[rows, :] = dq[rows, :] + nn(kt[krows, :], ds)
            acc[:, :kvw] = acc[:, :kvw] + nt(ds, qpad[h])
            acc[:, kvw:] = acc[:, kvw:] + nt(probs.astype(BF16), dopad[h])
            return carry

        lax.fori_loop(0, heads, head, 0)

    def pass_down(j):
        return pltpu.make_async_remote_copy(
            src_ref=passing.at[j],
            dst_ref=passing.at[j],
            send_sem=send.at[j],
            recv_sem=recv.at[j],
            device_id=down,
            device_id_type=MESH,
        )

    def gathered(j):
        acc = part.at[lax.rem(j, 2)]

        @pl.when(c < n - 1)
        def _():
            pass_down(j).wait_recv()
            acc[...] = acc[...] + passing[j].astype(F32)

        return acc

    def forward(j):
        acc = gathered(j)
        passing[j] = acc[...].astype(BF16)
        pass_down(j).start()

    def step(j, carry):
        block(j, False)

        @pl.when(jnp.logical_and(j > 0, c < n - 1))
        def _():
            forward(j - 1)

        @pl.when(c == n - 1)
        def _():
            forward(j)

        return carry

    lax.fori_loop(0, c, step, 0)
    block(c, True)

    @pl.when(jnp.logical_and(c > 0, c < n - 1))
    def _():
        forward(c - 1)

    dq_ref[...] = (dq[...] * 0.125).astype(BF16)
    acc = gathered(c)
    dkv_ref[...] = acc[...].astype(BF16)

    def sent(j, carry):
        pass_down(j).wait_send()
        return carry

    lax.fori_loop(0, c, sent, 0)


def attend_back(n, qt, dot, o, lse, kv):
    qw, t = qt.shape
    heads = qw // HEAD_SIZE
    kvw = kv.shape[2] // 2
    return pl.pallas_call(
        functools.partial(attend_back_kernel, n),
        out_shape=(
            jax.ShapeDtypeStruct((qw, t), BF16),
            jax.ShapeDtypeStruct((t, 2 * kvw), BF16),
        ),
        in_specs=[VMEM] * 5,
        out_specs=(VMEM,) * 2,
        scratch_shapes=[
            pltpu.VMEM((heads, kvw, t), BF16),
            pltpu.VMEM((heads, kvw, t), BF16),
            pltpu.VMEM((heads, 1, t), F32),
            pltpu.VMEM((qw, t), F32),
            pltpu.VMEM((kvw, t), BF16),
            pltpu.VMEM((2, t, 2 * kvw), F32),
            pltpu.VMEM((n, t, 2 * kvw), BF16),
            DMA((n,)),
            DMA((n,)),
        ],
        compiler_params=params(1),
        name="attend_back",
    )(qt, dot, o, lse, kv)


class Mp:
    def __init__(self, part, core_in, y_out, y_in, full, sems, chunks):
        self.part, self.core_in, self.y_out, self.y_in, self.full = part, core_in, y_out, y_in, full
        self.sems, self.chunks = sems, chunks
        s, c, m = lax.axis_index("seq"), lax.axis_index("ctx"), lax.axis_index("mp")
        self.m = m
        self.sib = m + 1 - 2 * lax.rem(m, 2)
        self.opp = lax.rem(m + 2, 4)
        self.diag = lax.rem(self.sib + 2, 4)
        self.sib_id, self.opp_id = (s, c, self.sib), (s, c, self.opp)
        share = (part if part is not None else full).shape[1]
        self.rows = share // chunks

    def barrier(self):
        sem = pltpu.get_barrier_semaphore()
        for d in (self.sib_id, self.opp_id):
            pl.semaphore_signal(sem, inc=1, device_id=d, device_id_type=MESH)
        pl.semaphore_wait(sem, 2)

    def copy(self, src, dst, i, dev):
        return pltpu.make_async_remote_copy(
            src_ref=src,
            dst_ref=dst,
            send_sem=self.sems.at[0, i],
            recv_sem=self.sems.at[1, i],
            device_id=dev,
            device_id_type=MESH,
        )

    def cut(self, i):
        return pl.ds(i * self.rows, self.rows)

    def rs_core(self, i):
        src = self.part.at[self.diag] if i == 0 else self.part.at[self.sib]
        return self.copy(src, self.core_in.at[i], i, self.sib_id)

    def rs_y(self, i):
        return self.copy(self.y_out.at[self.cut(i)], self.y_in.at[self.cut(i)], 2 + i, self.opp_id)

    def rs_begin(self):
        self.rs_core(0).start()
        self.rs_core(1).start()
        self.rs_core(0).wait_recv()
        for i in range(self.chunks):
            cut = self.cut(i)
            self.y_out[cut, :] = (
                self.part[self.opp, cut, :].astype(F32) + self.core_in[0, cut, :].astype(F32)
            ).astype(BF16)
            self.rs_y(i).start()
        self.rs_core(1).wait_recv()

    def rs_chunk(self, i):
        cut = self.cut(i)
        self.rs_y(i).wait_recv()
        return (
            self.part[self.m, cut, :].astype(F32) + self.core_in[1, cut, :].astype(F32)
        ) + self.y_in[cut, :].astype(F32)

    def rs_end(self):
        self.rs_core(0).wait_send()
        self.rs_core(1).wait_send()
        for i in range(self.chunks):
            self.rs_y(i).wait_send()

    def ag(self, kind, i, whose):
        block = self.full.at[whose, self.cut(i)]
        base = 2 + self.chunks
        dev = self.opp_id if kind == 0 else self.sib_id
        return self.copy(block, block, base + kind * self.chunks + i, dev)

    def ag_send(self, i):
        self.ag(0, i, self.m).start()
        self.ag(1, i, self.m).start()

    def ag_end(self):
        for i in range(self.chunks):
            self.ag(0, i, self.opp).wait_recv()
            self.ag(2, i, self.opp).start()
        for i in range(self.chunks):
            self.ag(1, i, self.sib).wait_recv()
            self.ag(2, i, self.diag).wait_recv()
            self.ag(0, i, self.m).wait_send()
            self.ag(1, i, self.m).wait_send()
            self.ag(2, i, self.opp).wait_send()


def mp_scratch(share, width, chunks):
    return [
        pltpu.VMEM((2, share, width), BF16),
        pltpu.VMEM((share, width), BF16),
        pltpu.VMEM((share, width), BF16),
        DMA((2, 2 + 4 * chunks)),
    ]


def rms_parts(rows):
    inverse = lax.rsqrt(jnp.mean(rows * rows, axis=-1, keepdims=True) + EPS)
    return rows * inverse, inverse


def rms_grad(grad_normed, normed, inverse):
    return inverse * (grad_normed - normed * jnp.mean(grad_normed * normed, axis=-1, keepdims=True))


def mid_forward_kernel(chunks, part, x_ref, gain, resid_ref, h_ref, core_in, y_out, y_in, sems):
    mp = Mp(part, core_in, y_out, y_in, h_ref, sems, chunks)
    mp.barrier()
    mp.rs_begin()
    for i in range(chunks):
        cut = mp.cut(i)
        resid = x_ref[cut, :].astype(F32) + mp.rs_chunk(i)
        resid_ref[cut, :] = resid
        normed, _ = rms_parts(resid)
        h_ref[mp.m, cut, :] = (normed * gain[...]).astype(BF16)
        mp.ag_send(i)
    mp.ag_end()
    mp.rs_end()


def mid_forward(part, x_mine, gain, chunks=2):
    _, share, width = part.shape
    return pl.pallas_call(
        functools.partial(mid_forward_kernel, chunks),
        out_shape=(jax.ShapeDtypeStruct((share, width), F32), jax.ShapeDtypeStruct(part.shape, BF16)),
        in_specs=[VMEM] * 3,
        out_specs=(VMEM,) * 2,
        scratch_shapes=mp_scratch(share, width, chunks),
        compiler_params=params(2),
        name="mid_forward",
    )(part, x_mine, gain)


def mid_back_kernel(
    chunks, part, resid_ref, gain, cot, gate_ref, router_ref, dresid_ref, db_ref, dlog_ref, gnorm_ref, core_in, y_out, y_in, sems
):
    mp = Mp(part, core_in, y_out, y_in, db_ref, sems, chunks)
    width = gain.shape[1]
    ex = gate_ref.shape[1]
    mp.barrier()
    mp.rs_begin()
    gnorm_ref[...] = jnp.zeros_like(gnorm_ref)
    for i in range(chunks):
        cut = mp.cut(i)
        both = mp.rs_chunk(i)
        dgate = both[:, width : width + ex] + both[:, width + ex :]
        gate = gate_ref[cut, :]
        dlog = gate * (dgate - jnp.sum(gate * dgate, axis=-1, keepdims=True))
        dlog_ref[cut, :] = dlog
        dh = both[:, :width] + jnp.dot(
            dlog, router_ref[...], precision=lax.Precision.HIGHEST, preferred_element_type=F32
        )
        normed, inverse = rms_parts(resid_ref[cut, :])
        gnorm_ref[0:1, :] = gnorm_ref[0:1, :] + jnp.sum(dh * normed, axis=0, keepdims=True)
        dresid = cot[cut, :].astype(F32) + rms_grad(dh * gain[...], normed, inverse)
        dresid_ref[cut, :] = dresid
        db_ref[mp.m, cut, :] = dresid.astype(BF16)
        mp.ag_send(i)
    mp.ag_end()
    mp.rs_end()


def mid_back(part, resid, gain, cot, gate, router_t, chunks=2):
    n, share, wide = part.shape
    width = gain.shape[1]
    return pl.pallas_call(
        functools.partial(mid_back_kernel, chunks),
        out_shape=(
            jax.ShapeDtypeStruct((share, width), F32),
            jax.ShapeDtypeStruct((n, share, width), BF16),
            jax.ShapeDtypeStruct(gate.shape, F32),
            jax.ShapeDtypeStruct((8, width), F32),
        ),
        in_specs=[VMEM] * 6,
        out_specs=(VMEM,) * 4,
        scratch_shapes=mp_scratch(share, wide, chunks),
        compiler_params=params(3),
        name="mid_back",
    )(part, resid, gain, cot, gate, router_t)


def last_kernel(chunks, part, x_ref, gain, dresid_ref, out_ref, core_in, y_out, y_in, sems):
    mp = Mp(part, core_in, y_out, y_in, None, sems, chunks)
    mp.barrier()
    mp.rs_begin()
    for i in range(chunks):
        cut = mp.cut(i)
        dh = mp.rs_chunk(i)
        normed, inverse = rms_parts(x_ref[cut, :].astype(F32))
        out_ref[cut, :] = dresid_ref[cut, :] + rms_grad(dh * gain[...], normed, inverse)
    mp.rs_end()


def last(part, x_mine, gain, dresid, chunks=2):
    _, share, width = part.shape
    return pl.pallas_call(
        functools.partial(last_kernel, chunks),
        out_shape=jax.ShapeDtypeStruct((share, width), F32),
        in_specs=[VMEM] * 4,
        out_specs=VMEM,
        scratch_shapes=mp_scratch(share, width, chunks),
        compiler_params=params(4),
        name="last",
    )(part, x_mine, gain, dresid)


def small_sum_kernel(sizes, x_ref, out_ref, *rest):
    bufs, sems = rest[:3], rest[3]
    axes = ("seq", "ctx", "mp")
    me = [lax.axis_index(a) for a in axes]

    def peer(axis, d):
        ids = list(me)
        ids[axis] = lax.rem(me[axis] + d, sizes[axis])
        return tuple(ids)

    bar = pltpu.get_barrier_semaphore()
    for axis in range(3):
        for d in range(1, sizes[axis]):
            pl.semaphore_signal(bar, inc=1, device_id=peer(axis, d), device_id_type=MESH)
    pl.semaphore_wait(bar, sum(sizes) - 3)
    out_ref[...] = x_ref[...]
    base = 0
    for axis in (2, 0, 1):
        n, buf = sizes[axis], bufs[axis]
        buf[0] = out_ref[...]
        copies = []
        for d in range(1, n):
            copy = pltpu.make_async_remote_copy(
                src_ref=buf.at[0],
                dst_ref=buf.at[d],
                send_sem=sems.at[0, base + d],
                recv_sem=sems.at[1, base + d],
                device_id=peer(axis, d),
                device_id_type=MESH,
            )
            copy.start()
            copies.append(copy)
        for copy in copies:
            copy.wait()
        total = jnp.zeros(out_ref.shape, F32)
        for i in range(n):
            total = total + buf[lax.rem(me[axis] - i + n, n)]
        out_ref[...] = total
        base += n


def small_sum(sizes, x):
    rows, width = x.shape
    return pl.pallas_call(
        functools.partial(small_sum_kernel, sizes),
        out_shape=jax.ShapeDtypeStruct(x.shape, F32),
        in_specs=[VMEM],
        out_specs=VMEM,
        scratch_shapes=[pltpu.VMEM((n, rows, width), F32) for n in sizes] + [DMA((2, sum(sizes)))],
        compiler_params=params(5),
        name="small_sum",
    )(x)


def line_sum(parts, n, dim):
    c = lax.axis_index("ctx")
    size = parts.shape[dim] // n

    def chunk(k):
        return lax.dynamic_slice_in_dim(parts, jnp.clip(k, 0, n - 1) * size, size, dim)

    total = chunk(c).astype(F32)
    for way in (1, -1):
        moving = None
        for t in range(1, n):
            mine = chunk(n - t + c if way == 1 else c - n + t)
            if moving is not None:
                mine = (mine.astype(F32) + moving.astype(F32)).astype(BF16)
            if way == 1:
                pairs = [(i, i + 1) for i in range(t)]
            else:
                pairs = [(i, i - 1) for i in range(n - t, n)]
            moving = lax.ppermute(mine, "ctx", pairs)
        total = total + moving.astype(F32)
    return total


def half(x, s, dim):
    size = x.shape[dim] // 2
    return lax.dynamic_slice_in_dim(x, s * size, size, dim)


SWAP = [(0, 1), (1, 0)]


def body(
    tokens,
    norm1_gain,
    w_query,
    key_weight_matrix,
    value_weight_matrix,
    w_out,
    norm2_gain,
    router,
    w_gate,
    w_up,
    w_down,
    routes,
    cotangent,
):
    n_seq, n_ctx, n_mp = (lax.axis_size(a) for a in ("seq", "ctx", "mp"))
    s, m = lax.axis_index("seq"), lax.axis_index("mp")
    tok, width = tokens.shape
    share = tok // n_mp
    experts_all = router.shape[1]
    exp_local = w_gate.shape[0]
    top = routes.shape[1]
    cap = share * top * 5 // (4 * experts_all)
    slots = n_mp * cap
    gain1 = norm1_gain.reshape(1, width)
    gain2 = norm2_gain.reshape(1, width)

    cot_all = lax.all_gather(cotangent, "mp", axis=0, tiled=True)
    x_mine = lax.dynamic_slice_in_dim(tokens, m * share, share, 0)

    normed_one, _ = rms_parts(tokens.astype(F32))
    h_one = (normed_one * gain1).astype(BF16)
    qt = (jnp.einsum("df,td->ft", w_query, h_one, preferred_element_type=F32).astype(BF16)) * BF16(0.125)
    k = nn(h_one, key_weight_matrix).astype(BF16)
    v = nn(h_one, value_weight_matrix).astype(BF16)
    o, heads_t, lse, kv = attend(n_ctx, qt, k, v)

    experts = jnp.arange(experts_all, dtype=jnp.int32)
    chosen = (routes[:, :, None] == experts[None, None, :]).any(axis=1)
    low = (jnp.arange(tok)[:, None] >= jnp.arange(tok)[None, :]).astype(BF16)
    rank = (nn(low, chosen.astype(BF16)) - 1.0).astype(jnp.int32)
    first = m * exp_local
    rank_t = lax.dynamic_slice_in_dim(rank.T, first, exp_local, 0)
    chosen_t = lax.dynamic_slice_in_dim(chosen.T, first, exp_local, 0)
    place = (
        (rank_t[:, None, :] == jnp.arange(slots, dtype=jnp.int32)[None, :, None]) & chosen_t[:, None, :]
    ).astype(BF16)
    dout_rows = jnp.einsum("ert,td->erd", place, cot_all, preferred_element_type=F32)
    dout_rows = dout_rows.astype(BF16).astype(F32)
    r_hi = router.astype(BF16)
    r_rest = router - r_hi.astype(F32)
    r_mid = r_rest.astype(BF16)
    r_low = (r_rest - r_mid.astype(F32)).astype(BF16)
    router3 = jnp.concatenate([r_hi, r_mid, r_low], axis=1)

    part = jnp.einsum("ft,fd->td", heads_t, w_out, preferred_element_type=F32).astype(BF16)
    resid, h_two = mid_forward(part.reshape(n_mp, share, width), x_mine, gain2)
    h_two = h_two.reshape(tok, width)

    logits3 = nn(h_two, router3)
    logits = (
        logits3[:, :experts_all]
        + logits3[:, experts_all : 2 * experts_all]
        + logits3[:, 2 * experts_all :]
    )
    peak = jnp.max(jnp.where(chosen, logits, -jnp.inf), axis=-1, keepdims=True)
    raised = jnp.where(chosen, jnp.exp(jnp.where(chosen, logits - peak, 0.0)), 0.0)
    gates = raised / jnp.sum(raised, axis=-1, keepdims=True)
    gates_mine = lax.dynamic_slice_in_dim(gates.T, first, exp_local, 0)
    gate_rows = jnp.sum(place.astype(F32) * gates_mine[:, None, :], axis=-1)[..., None]
    arrived = jnp.einsum("ert,td->erd", place, h_two, preferred_element_type=F32).astype(BF16)
    gate_pre = jnp.einsum("erd,edf->erf", arrived, w_gate, preferred_element_type=F32)
    up_pre = jnp.einsum("erd,edf->erf", arrived, w_up, preferred_element_type=F32)
    sigma = jax.nn.sigmoid(gate_pre)
    silu_gate = gate_pre * sigma
    hidden = (silu_gate * up_pre).astype(BF16)
    grad_made = (gate_rows * dout_rows).astype(BF16)
    grad_hidden = jnp.einsum("erd,efd->erf", grad_made, w_down, preferred_element_type=F32)
    grad_gate_pre = (grad_hidden * up_pre * sigma * (1.0 + gate_pre * (1.0 - sigma))).astype(BF16)
    grad_up_pre = (grad_hidden * silu_gate).astype(BF16)
    grad_arrived = jnp.einsum("erf,edf->erd", grad_gate_pre, w_gate, preferred_element_type=F32)
    grad_arrived = grad_arrived + jnp.einsum("erf,edf->erd", grad_up_pre, w_up, preferred_element_type=F32)
    grad_arrived = grad_arrived.astype(BF16)
    made = jnp.einsum("erf,efd->erd", hidden, w_down, preferred_element_type=F32).astype(BF16)
    made_f = made.astype(F32)
    gate_grads = jnp.sum(dout_rows * made_f, axis=-1)
    ex_pad = 64
    local_hot = (experts[None, :] == (first + jnp.arange(exp_local, dtype=jnp.int32))[:, None]).astype(F32)
    gate_grads = gate_grads[..., None] * local_hot[:, None, :]
    gate_grads = jnp.pad(gate_grads, ((0, 0), (0, 0), (0, ex_pad - experts_all)))
    gg_hi = gate_grads.astype(BF16)
    gg_low = (gate_grads - gg_hi.astype(F32)).astype(BF16)
    flat = place.reshape(exp_local * slots, tok)
    back_rows = jnp.concatenate([grad_arrived, gg_hi, gg_low], axis=-1).reshape(exp_local * slots, -1)
    back = jnp.einsum("rt,rd->td", flat, back_rows, preferred_element_type=F32).astype(BF16)
    comb_rows = (gate_rows * made_f).astype(BF16).reshape(exp_local * slots, width)
    comb = jnp.einsum("rt,rd->td", flat, comb_rows, preferred_element_type=F32).astype(BF16)
    output = resid + lax.psum_scatter(comb, "mp", scatter_dimension=0, tiled=True).astype(F32)

    gates_pad = jnp.pad(
        lax.dynamic_slice_in_dim(gates, m * share, share, 0), ((0, 0), (0, ex_pad - experts_all))
    )
    router_t = jnp.pad(router.T, ((0, ex_pad - experts_all), (0, 0)))
    dresid, db, dlog, gnorm2 = mid_back(
        back.reshape(n_mp, share, -1), resid, gain2, cotangent, gates_pad, router_t
    )
    db = db.reshape(tok, width)
    h_two_mine = lax.dynamic_slice_in_dim(h_two, m * share, share, 0).astype(F32)
    g_router = jnp.einsum("te,td->ed", dlog[:, :experts_all], h_two_mine, precision=lax.Precision.HIGHEST)

    def joined(x):
        return jnp.concatenate([x, lax.ppermute(x, "seq", SWAP)], axis=1)

    def joined_half(x):
        return jnp.concatenate([half(x, s, 2), lax.ppermute(half(x, 1 - s, 2), "seq", SWAP)], axis=1)

    arrived2 = joined_half(arrived)
    dg2, du2 = joined(grad_gate_pre), joined(grad_up_pre)
    g_gate = jnp.einsum("erd,erf->edf", arrived2, dg2, preferred_element_type=F32).astype(BF16)
    g_up = jnp.einsum("erd,erf->edf", arrived2, du2, preferred_element_type=F32).astype(BF16)
    hid2, dy2 = joined_half(hidden), joined(grad_made)
    g_down = jnp.einsum("erf,erd->efd", hid2, dy2, preferred_element_type=F32).astype(BF16)
    g_gate, g_up, g_down = (line_sum(g, n_ctx, 1) for g in (g_gate, g_up, g_down))

    dheads = jnp.einsum("fd,td->ft", w_out, db, preferred_element_type=F32).astype(BF16)
    g_out = jnp.einsum("td,ft->df", db, heads_t, preferred_element_type=F32).astype(BF16)

    def seq_half_sum(g):
        return (
            half(g, s, 0).astype(F32) + lax.ppermute(half(g, 1 - s, 0), "seq", SWAP).astype(F32)
        ).astype(BF16)

    g_out = line_sum(seq_half_sum(g_out), n_ctx, 0).T
    dq, dkv = attend_back(n_ctx, qt, dheads, o, lse, kv)
    kvw = dkv.shape[1] // 2
    dk, dv = dkv[:, :kvw], dkv[:, kvw:]
    dh = jnp.einsum("ft,df->td", dq, w_query, preferred_element_type=F32)
    dh = dh + jnp.einsum("tf,df->td", dk, key_weight_matrix, preferred_element_type=F32)
    dh = dh + jnp.einsum("tf,df->td", dv, value_weight_matrix, preferred_element_type=F32)
    gnorm1 = jnp.sum(dh * normed_one, axis=0, keepdims=True)
    grad_tokens = last(dh.astype(BF16).reshape(n_mp, share, width), x_mine, gain1, dresid)
    g_q = jnp.einsum("td,ft->df", h_one, dq, preferred_element_type=F32)
    g_kv = jnp.einsum("td,tf->df", h_one, dkv, preferred_element_type=F32)
    g_qkv = jnp.concatenate([g_q, g_kv], axis=1).astype(BF16)
    g_qkv = line_sum(seq_half_sum(g_qkv), n_ctx, 0)
    qw = w_query.shape[1]

    rows = 2 + experts_all
    small = jnp.concatenate(
        [gnorm1, gnorm2[:1], g_router, jnp.zeros((-rows % 8, width), F32)], axis=0
    )
    small = small_sum((n_seq, n_ctx, n_mp), small)
    return (
        output,
        grad_tokens,
        small[0],
        g_qkv[:, :qw],
        g_qkv[:, qw : qw + kvw],
        g_qkv[:, qw + kvw :],
        g_out,
        small[1],
        small[2:rows].T,
        g_gate,
        g_up,
        g_down,
    )


def solution(mesh):
    placed = (
        P(("seq", "ctx"), None),
        P(),
        P(None, "mp"),
        P(None, "mp"),
        P(None, "mp"),
        P("mp", None),
        P(),
        P(),
        P("mp", None, None),
        P("mp", None, None),
        P("mp", None, None),
        P(("seq", "ctx"), None),
        P(("seq", "ctx", "mp"), None),
    )
    return jax.shard_map(
        body,
        mesh=mesh,
        in_specs=placed,
        out_specs=(
            P(("seq", "ctx", "mp"), None),
            P(("seq", "ctx", "mp"), None),
            P(),
            P(("seq", "ctx"), "mp"),
            P(("seq", "ctx"), "mp"),
            P(("seq", "ctx"), "mp"),
            P("mp", ("seq", "ctx")),
            P(),
            P(),
            P("mp", ("seq", "ctx"), None),
            P("mp", ("seq", "ctx"), None),
            P("mp", ("seq", "ctx"), None),
        ),
        check_vma=False,
    )
```

```python
import functools

import jax
import jax.numpy as jnp
from jax import lax
from jax.experimental import pallas as pl
from jax.experimental.pallas import tpu as pltpu
from jax.sharding import PartitionSpec as P

HEAD_SIZE = 64
EPS = 1e-06
MESH = pl.DeviceIdType.MESH
F32 = jnp.float32
BF16 = jnp.bfloat16
VMEM = pl.BlockSpec(memory_space=pltpu.VMEM)
DMA = pltpu.SemaphoreType.DMA
MIB = 2**20


def cost(us):
    return pl.CostEstimate(flops=0, bytes_accessed=int(us * 3.6e6), transcendentals=0)


def params(collective_id, mib=56):
    return pltpu.CompilerParams(
        collective_id=collective_id, has_side_effects=True, vmem_limit_bytes=mib * MIB
    )


def nt(a, b):
    return lax.dot_general(a, b, (((1,), (1,)), ((), ())), preferred_element_type=F32)


def nn(a, b):
    return jnp.dot(a, b, preferred_element_type=F32)


class Spread:
    def __init__(self, n, own, below, above, all_ref, send, recv, local):
        self.n, self.own, self.below, self.above, self.all = n, own, below, above, all_ref
        self.send, self.recv, self.local = send, recv, local
        s, self.c, m = lax.axis_index("seq"), lax.axis_index("ctx"), lax.axis_index("mp")
        self.lower, self.upper = lax.rem(self.c + n - 1, n), lax.rem(self.c + 1, n)
        self.up, self.down = (s, self.upper, m), (s, self.lower, m)
        self.inner = jnp.logical_and(self.c > 0, self.c < n - 1)

    def move(self, b, src, device):
        return pltpu.make_async_remote_copy(
            src_ref=src,
            dst_ref=self.all.at[b],
            send_sem=self.send.at[b],
            recv_sem=self.recv.at[b],
            device_id=device,
            device_id_type=MESH,
        )

    def keep(self, i, src, b):
        return pltpu.make_async_copy(src, self.all.at[b], self.local.at[i])

    def start(self):
        @pl.when(self.inner)
        def _():
            self.move(self.lower, self.below, self.up).start()
            self.move(self.upper, self.above, self.down).start()

        self.keep(0, self.own, self.c).start()

        @pl.when(self.c > 0)
        def _():
            self.keep(1, self.below, self.lower).start()

        @pl.when(self.c < self.n - 1)
        def _():
            self.keep(2, self.above, self.upper).start()

    def tick(self, i):
        c, n = self.c, self.n

        @pl.when(c - 1 - i >= 0)
        def _():
            b = jnp.maximum(c - 1 - i, 0)
            self.move(b, self.all.at[b], self.up).wait_recv()

            @pl.when(c < n - 1)
            def _():
                self.move(b, self.all.at[b], self.up).start()

        @pl.when(c + 1 + i <= n - 1)
        def _():
            b = jnp.minimum(c + 1 + i, n - 1)
            self.move(b, self.all.at[b], self.down).wait_recv()

            @pl.when(c > 0)
            def _():
                self.move(b, self.all.at[b], self.down).start()

    def ticks(self, first):
        def later(i, carry):
            self.tick(i)
            return carry

        lax.fori_loop(first, self.n - 1, later, 0)

    def finish(self):
        self.keep(0, self.own, self.c).wait()

        @pl.when(self.c > 0)
        def _():
            self.keep(1, self.below, self.lower).wait()

        @pl.when(self.c < self.n - 1)
        def _():
            self.keep(2, self.above, self.upper).wait()

        @pl.when(self.inner)
        def _():
            def sent(b, carry):
                @pl.when(b != self.c)
                def _():
                    self.move(b, self.all.at[b], self.up).wait_send()

                return carry

            lax.fori_loop(0, self.n, sent, 0)


class Neighbours:
    def __init__(self, n, own, below, above, send, recv):
        self.n, self.own, self.below, self.above, self.send, self.recv = n, own, below, above, send, recv
        s, self.c, m = lax.axis_index("seq"), lax.axis_index("ctx"), lax.axis_index("mp")
        self.up, self.down = (s, lax.rem(self.c + 1, n), m), (s, lax.rem(self.c + n - 1, n), m)

    def move(self, way):
        return pltpu.make_async_remote_copy(
            src_ref=self.own,
            dst_ref=self.below if way == 0 else self.above,
            send_sem=self.send.at[way],
            recv_sem=self.recv.at[way],
            device_id=self.up if way == 0 else self.down,
            device_id_type=MESH,
        )

    def start_up(self):
        @pl.when(self.c < self.n - 1)
        def _():
            self.move(0).start()

    def start_down(self):
        @pl.when(self.c > 0)
        def _():
            self.move(1).start()

    def finish(self):
        @pl.when(self.c > 0)
        def _():
            self.move(0).wait_recv()
            self.move(1).wait_send()

        @pl.when(self.c < self.n - 1)
        def _():
            self.move(1).wait_recv()
            self.move(0).wait_send()


class Peers:
    def __init__(self, n, src_of, dst_of, send, recv):
        self.n, self.src_of, self.dst_of, self.send, self.recv = n, src_of, dst_of, send, recv
        self.s, self.c, self.m = lax.axis_index("seq"), lax.axis_index("ctx"), lax.axis_index("mp")

    def move(self, d):
        peer = lax.rem(self.c + d, self.n)
        return pltpu.make_async_remote_copy(
            src_ref=self.src_of(peer),
            dst_ref=self.dst_of(self.c),
            send_sem=self.send.at[d],
            recv_sem=self.recv.at[d],
            device_id=(self.s, peer, self.m),
            device_id_type=MESH,
        )

    def signal(self, sem):
        for d in range(1, self.n):
            pl.semaphore_signal(
                sem, inc=1, device_id=(self.s, lax.rem(self.c + d, self.n), self.m), device_id_type=MESH
            )

    def start(self):
        for d in range(1, self.n):
            self.move(d).start()

    def finish(self):
        for d in range(1, self.n):
            self.move(d).wait()


def signal_line(n, sem):
    s, c, m = lax.axis_index("seq"), lax.axis_index("ctx"), lax.axis_index("mp")

    @pl.when(c > 0)
    def _():
        pl.semaphore_signal(sem, inc=1, device_id=(s, lax.rem(c + n - 1, n), m), device_id_type=MESH)

    @pl.when(c < n - 1)
    def _():
        pl.semaphore_signal(sem, inc=1, device_id=(s, lax.rem(c + 1, n), m), device_id_type=MESH)


def line_degree(n):
    c = lax.axis_index("ctx")
    return jnp.where(c > 0, 1, 0) + jnp.where(c < n - 1, 1, 0)


def pad_heads(src, dst, heads, group):
    dst[...] = jnp.zeros_like(dst)
    for h in range(heads):
        g = h // group
        rows = slice(g * HEAD_SIZE, (g + 1) * HEAD_SIZE)
        dst[h, rows, :] = src[h * HEAD_SIZE : (h + 1) * HEAD_SIZE, :]


def causal(t):
    keys = lax.broadcasted_iota(jnp.int32, (t, t), 0)
    queries = lax.broadcasted_iota(jnp.int32, (t, t), 1)
    return keys <= queries


def attend_kernel(
    n,
    q_ref,
    k_ref,
    v_ref,
    cot_ref,
    routes_ref,
    o_ref,
    heads_ref,
    lse_ref,
    kv_ref,
    below_ref,
    above_ref,
    line_ref,
    qpad,
    vt,
    top,
    tot,
    send,
    recv,
    side,
    peers_sem,
):
    s, c, m = lax.axis_index("seq"), lax.axis_index("ctx"), lax.axis_index("mp")
    t, kvw = k_ref.shape
    heads = q_ref.shape[0] // HEAD_SIZE
    group = heads // (kvw // HEAD_SIZE)
    up, down = (s, lax.rem(c + 1, n), m), (s, lax.rem(c + n - 1, n), m)
    kv_ref[0, :, :kvw] = k_ref[...]
    kv_ref[0, :, kvw:] = v_ref[...]
    line_ref[c] = routes_ref[...]
    peers = Peers(n, lambda p: routes_ref, lambda i: line_ref.at[i], peers_sem.at[0], peers_sem.at[1])
    beside = Neighbours(n, cot_ref, below_ref, above_ref, side.at[0], side.at[1])
    sem = pltpu.get_barrier_semaphore()
    peers.signal(sem)
    pl.semaphore_wait(sem, n - 1)

    def pass_up(slot):
        return pltpu.make_async_remote_copy(
            src_ref=kv_ref.at[slot],
            dst_ref=kv_ref.at[slot + 1],
            send_sem=send.at[slot],
            recv_sem=recv.at[slot + 1],
            device_id=up,
            device_id_type=MESH,
        )

    def got(slot):
        return pltpu.make_async_remote_copy(
            src_ref=kv_ref.at[slot],
            dst_ref=kv_ref.at[slot],
            send_sem=send.at[slot],
            recv_sem=recv.at[slot],
            device_id=up,
            device_id_type=MESH,
        )

    @pl.when(c < n - 1)
    def _():
        pass_up(0).start()

    peers.start()
    beside.start_down()
    pad_heads(q_ref, qpad, heads, group)
    top[...] = jnp.full_like(top, -1e30)
    tot[...] = jnp.zeros_like(tot)
    o_ref[...] = jnp.zeros_like(o_ref)

    def block(slot, masked):
        vt[...] = kv_ref[slot, :, kvw:].T

        def head(h, carry):
            g = lax.div(h, group)
            scores = nn(kv_ref[slot, :, :kvw], qpad[h])
            if masked:
                scores = jnp.where(causal(t), scores, -1e30)
            old = top[h]
            new = jnp.maximum(old, jnp.max(scores, axis=0, keepdims=True))
            weights = jnp.exp(scores - new)
            factor = jnp.exp(old - new)
            top[h] = new
            tot[h] = tot[h] * factor + jnp.sum(weights, axis=0, keepdims=True)
            rows = pl.ds(pl.multiple_of(h * HEAD_SIZE, HEAD_SIZE), HEAD_SIZE)
            vrows = pl.ds(pl.multiple_of(g * HEAD_SIZE, HEAD_SIZE), HEAD_SIZE)
            o_ref[rows, :] = o_ref[rows, :] * factor + nn(vt[vrows, :], weights.astype(BF16))
            return carry

        lax.fori_loop(0, heads, head, 0)

    block(0, True)

    def earlier(slot, carry):
        got(slot).wait_recv()

        @pl.when(c < n - 1)
        def _():
            pass_up(slot).start()

        block(slot, False)
        return carry

    lax.fori_loop(1, c + 1, earlier, 0)
    beside.start_up()
    for h in range(heads):
        rows = slice(h * HEAD_SIZE, (h + 1) * HEAD_SIZE)
        done = o_ref[rows, :] / tot[h]
        o_ref[rows, :] = done
        heads_ref[rows, :] = done.astype(BF16)
        lse_ref[h] = top[h] + jnp.log(tot[h])

    @pl.when(c < n - 1)
    def _():
        def sent(slot, carry):
            pass_up(slot).wait_send()
            return carry

        lax.fori_loop(0, c + 1, sent, 0)

    peers.finish()
    beside.finish()


def attend(n, qt, k, v, cot, routes):
    t, kvw = k.shape
    qw = qt.shape[0]
    heads = qw // HEAD_SIZE
    return pl.pallas_call(
        functools.partial(attend_kernel, n),
        out_shape=(
            jax.ShapeDtypeStruct((qw, t), F32),
            jax.ShapeDtypeStruct((qw, t), BF16),
            jax.ShapeDtypeStruct((heads, 1, t), F32),
            jax.ShapeDtypeStruct((n, t, 2 * kvw), BF16),
            jax.ShapeDtypeStruct(cot.shape, BF16),
            jax.ShapeDtypeStruct(cot.shape, BF16),
            jax.ShapeDtypeStruct((n,) + routes.shape, jnp.int32),
        ),
        in_specs=[VMEM] * 5,
        out_specs=(VMEM,) * 7,
        scratch_shapes=[
            pltpu.VMEM((heads, kvw, t), BF16),
            pltpu.VMEM((kvw, t), BF16),
            pltpu.VMEM((heads, 1, t), F32),
            pltpu.VMEM((heads, 1, t), F32),
            DMA((n,)),
            DMA((n,)),
            DMA((2, 2)),
            DMA((2, n)),
        ],
        compiler_params=params(0),
        name="attend",
        cost_estimate=cost(30),
    )(qt, k, v, cot, routes)


def attend_back_kernel(
    n,
    q_ref,
    do_ref,
    o_ref,
    lse_ref,
    kv_ref,
    sum_ref,
    own_ref,
    below_ref,
    above_ref,
    dq_ref,
    dkv_ref,
    summed_ref,
    all_ref,
    qpad,
    dopad,
    delta,
    dq,
    kt,
    part,
    passing,
    from_below,
    from_above,
    send,
    recv,
    spread_sem,
    local,
):
    s, c, m = lax.axis_index("seq"), lax.axis_index("ctx"), lax.axis_index("mp")
    _, t, kvw2 = kv_ref.shape
    kvw = kvw2 // 2
    heads = q_ref.shape[0] // HEAD_SIZE
    group = heads // (kvw // HEAD_SIZE)
    ex = sum_ref.shape[0]
    chunk_rows = sum_ref.shape[1] // n
    up, down = (s, lax.rem(c + 1, n), m), (s, lax.rem(c + n - 1, n), m)
    spread = Spread(n, own_ref, below_ref, above_ref, all_ref, spread_sem.at[0], spread_sem.at[1], local)
    sem = pltpu.get_barrier_semaphore()
    signal_line(n, sem)
    pl.semaphore_wait(sem, line_degree(n))

    def remote(kind, i, src, dst, device):
        return pltpu.make_async_remote_copy(
            src_ref=src,
            dst_ref=dst,
            send_sem=send.at[kind, i],
            recv_sem=recv.at[kind, i],
            device_id=device,
            device_id_type=MESH,
        )

    def own_unit(k, e):
        return sum_ref.at[e, pl.ds(pl.multiple_of(k * chunk_rows, 16), chunk_rows), :]

    def sum_up(k, e, first=False):
        there = from_below.at[k, e]
        return remote(1, k * ex + e, own_unit(k, e) if first else there, there, up)

    def sum_down(k, e, first=False):
        there = from_above.at[k, e]
        return remote(2, k * ex + e, own_unit(k, e) if first else there, there, down)

    units = (n - 1) * ex
    ahead = 2

    def first_up(u):
        @pl.when(jnp.logical_and(c == 0, u < units))
        def _():
            @pl.when(u >= ahead)
            def _():
                v = jnp.maximum(u - ahead, 0)
                sum_up(n - 1 - lax.div(v, ex), lax.rem(v, ex), True).wait_send()

            w = jnp.minimum(u, units - 1)
            sum_up(n - 1 - lax.div(w, ex), lax.rem(w, ex), True).start()

    def first_down(u):
        @pl.when(jnp.logical_and(c == n - 1, u < units))
        def _():
            @pl.when(u >= ahead)
            def _():
                v = jnp.maximum(u - ahead, 0)
                sum_down(lax.div(v, ex), lax.rem(v, ex), True).wait_send()

            w = jnp.minimum(u, units - 1)
            sum_down(lax.div(w, ex), lax.rem(w, ex), True).start()

    first_up(0)
    first_down(0)
    spread.start()

    def tick(i):
        first_up(i + 1)
        first_down(i + 1)
        for hop in range(1, n - 1):

            @pl.when(i == hop * ex)
            def _():
                spread.tick(hop)

        u = i - c
        k = n - 1 - lax.div(jnp.maximum(u, 0), ex)
        e = lax.rem(jnp.maximum(u, 0), ex)

        @pl.when(jnp.logical_and(c > 0, jnp.logical_and(u >= 0, k > c)))
        def _():
            there = jnp.maximum(k, 0)
            sum_up(there, e).wait_recv()
            from_below[there, e] = (own_unit(there, e)[...].astype(F32) + from_below[there, e].astype(F32)).astype(BF16)
            sum_up(there, e).start()

        v = i - (n - 1 - c)
        kd = lax.div(jnp.maximum(v, 0), ex)
        ed = lax.rem(jnp.maximum(v, 0), ex)

        @pl.when(jnp.logical_and(c < n - 1, jnp.logical_and(v >= 0, kd < c)))
        def _():
            there = jnp.minimum(kd, n - 1)
            sum_down(there, ed).wait_recv()
            from_above[there, ed] = (own_unit(there, ed)[...].astype(F32) + from_above[there, ed].astype(F32)).astype(BF16)
            sum_down(there, ed).start()

    last_tick = units + n

    pad_heads(q_ref, qpad, heads, group)
    pad_heads(do_ref, dopad, heads, group)
    for h in range(heads):
        rows = slice(h * HEAD_SIZE, (h + 1) * HEAD_SIZE)
        delta[h] = jnp.sum(do_ref[rows, :].astype(F32) * o_ref[rows, :], axis=0, keepdims=True)
    dq[...] = jnp.zeros_like(dq)

    def block(j, masked):
        slot = c - j
        acc = part.at[lax.rem(j, 2)]
        acc[...] = jnp.zeros(acc.shape, F32)
        kt[...] = kv_ref[slot, :, :kvw].T

        def head(h, carry):
            g = lax.div(h, group)
            scores = nn(kv_ref[slot, :, :kvw], qpad[h])
            probs = jnp.exp(scores - lse_ref[h])
            if masked:
                probs = jnp.where(causal(t), probs, 0.0)
            dprobs = nn(kv_ref[slot, :, kvw:], dopad[h])
            ds = (probs * (dprobs - delta[h])).astype(BF16)
            rows = pl.ds(pl.multiple_of(h * HEAD_SIZE, HEAD_SIZE), HEAD_SIZE)
            krows = pl.ds(pl.multiple_of(g * HEAD_SIZE, HEAD_SIZE), HEAD_SIZE)
            dq[rows, :] = dq[rows, :] + nn(kt[krows, :], ds)
            acc[:, :kvw] = acc[:, :kvw] + nt(ds, qpad[h])
            acc[:, kvw:] = acc[:, kvw:] + nt(probs.astype(BF16), dopad[h])
            return carry

        lax.fori_loop(0, heads, head, 0)

    def pass_down(j):
        return remote(0, j, passing.at[j], passing.at[j], down)

    def gathered(j):
        acc = part.at[lax.rem(j, 2)]

        @pl.when(c < n - 1)
        def _():
            pass_down(j).wait_recv()
            acc[...] = acc[...] + passing[j].astype(F32)

        return acc

    def forward(j):
        acc = gathered(j)
        passing[j] = acc[...].astype(BF16)
        pass_down(j).start()

    def step(j, carry):
        block(j, False)

        @pl.when(jnp.logical_and(j > 0, c < n - 1))
        def _():
            forward(j - 1)

        @pl.when(c == n - 1)
        def _():
            forward(j)

        tick(j)
        return carry

    lax.fori_loop(0, c, step, 0)
    block(c, True)

    @pl.when(spread.inner)
    def _():
        forward(c - 1)

    dq_ref[...] = (dq[...] * 0.125).astype(BF16)

    def later(i, carry):
        tick(i)
        return carry

    lax.fori_loop(c, last_tick, later, 0)
    acc = gathered(c)
    dkv_ref[...] = acc[...].astype(BF16)
    for e in range(ex):
        summed_ref[e] = own_unit(c, e)[...].astype(F32)

        @pl.when(c > 0)
        def _():
            sum_up(c, e).wait_recv()
            summed_ref[e] = summed_ref[e] + from_below[c, e].astype(F32)

        @pl.when(c < n - 1)
        def _():
            sum_down(c, e).wait_recv()
            summed_ref[e] = summed_ref[e] + from_above[c, e].astype(F32)

    spread.finish()

    def sent_kv(j, carry):
        pass_down(j).wait_send()
        return carry

    lax.fori_loop(0, c, sent_kv, 0)

    done = jnp.where(c == 0, units - ahead, 0)

    @pl.when(c < n - 1)
    def _():
        def sent(u, carry):
            sum_up(n - 1 - lax.div(u, ex), lax.rem(u, ex)).wait_send()
            return carry

        lax.fori_loop(done, (n - 1 - c) * ex, sent, 0)

    done_down = jnp.where(c == n - 1, units - ahead, 0)

    @pl.when(c > 0)
    def _():
        def sent(u, carry):
            sum_down(lax.div(u, ex), lax.rem(u, ex)).wait_send()
            return carry

        lax.fori_loop(done_down, c * ex, sent, 0)


def attend_back(n, qt, dot, o, lse, kv, sums, own, below, above):
    qw, t = qt.shape
    heads = qw // HEAD_SIZE
    kvw = kv.shape[2] // 2
    ex, rows, cols = sums.shape
    chunk = (ex, rows // n, cols)
    return pl.pallas_call(
        functools.partial(attend_back_kernel, n),
        out_shape=(
            jax.ShapeDtypeStruct((qw, t), BF16),
            jax.ShapeDtypeStruct((t, 2 * kvw), BF16),
            jax.ShapeDtypeStruct(chunk, F32),
            jax.ShapeDtypeStruct((n,) + own.shape, BF16),
        ),
        in_specs=[VMEM] * 9,
        out_specs=(VMEM,) * 4,
        scratch_shapes=[
            pltpu.VMEM((heads, kvw, t), BF16),
            pltpu.VMEM((heads, kvw, t), BF16),
            pltpu.VMEM((heads, 1, t), F32),
            pltpu.VMEM((qw, t), F32),
            pltpu.VMEM((kvw, t), BF16),
            pltpu.VMEM((2, t, 2 * kvw), F32),
            pltpu.VMEM((n, t, 2 * kvw), BF16),
            pltpu.VMEM((n,) + chunk, BF16),
            pltpu.VMEM((n,) + chunk, BF16),
            DMA((3, n * ex)),
            DMA((3, n * ex)),
            DMA((2, n)),
            DMA((3,)),
        ],
        compiler_params=params(1),
        name="attend_back",
        cost_estimate=cost(75),
    )(qt, dot, o, lse, kv, sums, own, below, above)


class Mp:
    def __init__(self, part, core_in, y_out, y_in, full, sems, chunks):
        self.part, self.core_in, self.y_out, self.y_in, self.full = part, core_in, y_out, y_in, full
        self.sems, self.chunks = sems, chunks
        s, c, m = lax.axis_index("seq"), lax.axis_index("ctx"), lax.axis_index("mp")
        self.m = m
        self.sib = m + 1 - 2 * lax.rem(m, 2)
        self.opp = lax.rem(m + 2, 4)
        self.diag = lax.rem(self.sib + 2, 4)
        self.sib_id, self.opp_id = (s, c, self.sib), (s, c, self.opp)
        share = (part if part is not None else full).shape[1]
        self.rows = share // chunks

    def signal(self, sem):
        for d in (self.sib_id, self.opp_id):
            pl.semaphore_signal(sem, inc=1, device_id=d, device_id_type=MESH)

    def copy(self, src, dst, i, dev):
        return pltpu.make_async_remote_copy(
            src_ref=src,
            dst_ref=dst,
            send_sem=self.sems.at[0, i],
            recv_sem=self.sems.at[1, i],
            device_id=dev,
            device_id_type=MESH,
        )

    def cut(self, i):
        return pl.ds(i * self.rows, self.rows)

    def rs_core(self, i):
        src = self.part.at[self.diag] if i == 0 else self.part.at[self.sib]
        return self.copy(src, self.core_in.at[i], i, self.sib_id)

    def rs_y(self, i):
        return self.copy(self.y_out.at[self.cut(i)], self.y_in.at[self.cut(i)], 2 + i, self.opp_id)

    def rs_begin(self):
        self.rs_core(0).start()
        self.rs_core(1).start()
        self.rs_forward()

    def rs_forward(self):
        self.rs_core(0).wait_recv()
        for i in range(self.chunks):
            cut = self.cut(i)
            self.y_out[cut, :] = (
                self.part[self.opp, cut, :].astype(F32) + self.core_in[0, cut, :].astype(F32)
            ).astype(BF16)
            self.rs_y(i).start()
        self.rs_core(1).wait_recv()

    def rs_chunk(self, i):
        cut = self.cut(i)
        self.rs_y(i).wait_recv()
        return (
            self.part[self.m, cut, :].astype(F32) + self.core_in[1, cut, :].astype(F32)
        ) + self.y_in[cut, :].astype(F32)

    def rs_end(self):
        self.rs_core(0).wait_send()
        self.rs_core(1).wait_send()
        for i in range(self.chunks):
            self.rs_y(i).wait_send()

    def ag(self, kind, i, whose):
        block = self.full.at[whose, self.cut(i)]
        base = 2 + self.chunks
        dev = self.opp_id if kind == 0 else self.sib_id
        return self.copy(block, block, base + kind * self.chunks + i, dev)

    def ag_send(self, i):
        self.ag(0, i, self.m).start()
        self.ag(1, i, self.m).start()

    def ag_end(self):
        for i in range(self.chunks):
            self.ag(0, i, self.opp).wait_recv()
            self.ag(2, i, self.opp).start()
        for i in range(self.chunks):
            self.ag(1, i, self.sib).wait_recv()
            self.ag(2, i, self.diag).wait_recv()
            self.ag(0, i, self.m).wait_send()
            self.ag(1, i, self.m).wait_send()
            self.ag(2, i, self.opp).wait_send()


def mp_scratch(share, width, chunks):
    return [
        pltpu.VMEM((2, share, width), BF16),
        pltpu.VMEM((share, width), BF16),
        pltpu.VMEM((share, width), BF16),
        DMA((2, 2 + 4 * chunks)),
    ]


def rms_parts(rows):
    inverse = lax.rsqrt(jnp.mean(rows * rows, axis=-1, keepdims=True) + EPS)
    return rows * inverse, inverse


def rms_grad(grad_normed, normed, inverse):
    return inverse * (grad_normed - normed * jnp.mean(grad_normed * normed, axis=-1, keepdims=True))


def mid_forward_kernel(
    chunks, n, part, x_ref, gain, own, below, above, resid_ref, h_ref, line_ref, core_in, y_out, y_in, sems, send, recv, local
):
    mp = Mp(part, core_in, y_out, y_in, h_ref, sems, chunks)
    spread = Spread(n, own, below, above, line_ref, send, recv, local)
    sem = pltpu.get_barrier_semaphore()
    mp.signal(sem)
    signal_line(n, sem)
    pl.semaphore_wait(sem, 2 + line_degree(n))
    mp.rs_begin()
    spread.start()
    for i in range(chunks):
        cut = mp.cut(i)
        resid = x_ref[cut, :].astype(F32) + mp.rs_chunk(i)
        resid_ref[cut, :] = resid
        normed, _ = rms_parts(resid)
        h_ref[mp.m, cut, :] = (normed * gain[...]).astype(BF16)
        mp.ag_send(i)
    if n > 2:
        spread.tick(1)
    mp.ag_end()
    mp.rs_end()
    spread.ticks(2)
    spread.finish()


def mid_forward(n, part, x_mine, gain, own, below, above, chunks=2):
    _, share, width = part.shape
    return pl.pallas_call(
        functools.partial(mid_forward_kernel, chunks, n),
        out_shape=(
            jax.ShapeDtypeStruct((share, width), F32),
            jax.ShapeDtypeStruct(part.shape, BF16),
            jax.ShapeDtypeStruct((n,) + own.shape, BF16),
        ),
        in_specs=[VMEM] * 6,
        out_specs=(VMEM,) * 3,
        scratch_shapes=mp_scratch(share, width, chunks) + [DMA((n,)), DMA((n,)), DMA((3,))],
        compiler_params=params(2, 30),
        name="mid_forward",
        cost_estimate=cost(30),
    )(part, x_mine, gain, own, below, above)


def mid_back_kernel(
    chunks,
    n,
    part,
    resid_ref,
    gain,
    cot,
    gate_ref,
    router_ref,
    rows_ref,
    hid_ref,
    du_ref,
    dresid_ref,
    db_ref,
    dlog_ref,
    gnorm_ref,
    rows_line,
    hid_line,
    below_ref,
    above_ref,
    core_in,
    y_out,
    y_in,
    sems,
    side,
    peers_sem,
    local,
):
    c = lax.axis_index("ctx")
    mp = Mp(part, core_in, y_out, y_in, db_ref, sems, chunks)
    rows_peers = Peers(n, lambda p: rows_ref, lambda i: rows_line.at[i], peers_sem.at[0], peers_sem.at[1])
    hid_peers = Peers(n, lambda p: hid_ref.at[p], lambda i: hid_line.at[i], peers_sem.at[2], peers_sem.at[3])
    beside = Neighbours(n, du_ref, below_ref, above_ref, side.at[0], side.at[1])
    width = gain.shape[1]
    ex = gate_ref.shape[1]
    sem = pltpu.get_barrier_semaphore()
    mp.signal(sem)
    rows_peers.signal(sem)
    pl.semaphore_wait(sem, 2 + n - 1)
    mp.rs_begin()
    beside.start_up()
    beside.start_down()
    rows_peers.start()
    hid_peers.start()
    own_rows = pltpu.make_async_copy(rows_ref, rows_line.at[c], local.at[0])
    own_hid = pltpu.make_async_copy(hid_ref.at[c], hid_line.at[c], local.at[1])
    own_rows.start()
    own_hid.start()
    gnorm_ref[...] = jnp.zeros_like(gnorm_ref)
    for i in range(chunks):
        cut = mp.cut(i)
        both = mp.rs_chunk(i)
        dgate = both[:, width : width + ex] + both[:, width + ex :]
        gate = gate_ref[cut, :]
        dlog = gate * (dgate - jnp.sum(gate * dgate, axis=-1, keepdims=True))
        dlog_ref[cut, :] = dlog
        dh = both[:, :width] + jnp.dot(
            dlog, router_ref[...], precision=lax.Precision.HIGHEST, preferred_element_type=F32
        )
        normed, inverse = rms_parts(resid_ref[cut, :])
        gnorm_ref[0:1, :] = gnorm_ref[0:1, :] + jnp.sum(dh * normed, axis=0, keepdims=True)
        dresid = cot[cut, :].astype(F32) + rms_grad(dh * gain[...], normed, inverse)
        dresid_ref[cut, :] = dresid
        db_ref[mp.m, cut, :] = dresid.astype(BF16)
        mp.ag_send(i)
    mp.ag_end()
    mp.rs_end()
    own_rows.wait()
    own_hid.wait()
    rows_peers.finish()
    hid_peers.finish()
    beside.finish()


def mid_back(n, part, resid, gain, cot, gate, router_t, rows, hid, du, chunks=2):
    k, share, wide = part.shape
    width = gain.shape[1]
    return pl.pallas_call(
        functools.partial(mid_back_kernel, chunks, n),
        out_shape=(
            jax.ShapeDtypeStruct((share, width), F32),
            jax.ShapeDtypeStruct((k, share, width), BF16),
            jax.ShapeDtypeStruct(gate.shape, F32),
            jax.ShapeDtypeStruct((8, width), F32),
            jax.ShapeDtypeStruct((n,) + rows.shape, F32),
            jax.ShapeDtypeStruct(hid.shape, BF16),
            jax.ShapeDtypeStruct(du.shape, BF16),
            jax.ShapeDtypeStruct(du.shape, BF16),
        ),
        in_specs=[VMEM] * 9,
        out_specs=(VMEM,) * 8,
        scratch_shapes=mp_scratch(share, wide, chunks) + [DMA((2, 2)), DMA((4, n)), DMA((2,))],
        compiler_params=params(3, 36),
        name="mid_back",
        cost_estimate=cost(32),
    )(part, resid, gain, cot, gate, router_t, rows, hid, du)


class SmallSum:
    def __init__(self, sizes, x_ref, out_ref, bufs, sems):
        self.sizes, self.x, self.out, self.bufs, self.sems = sizes, x_ref, out_ref, bufs, sems
        self.me = [lax.axis_index(a) for a in ("seq", "ctx", "mp")]

    def peer(self, axis, d):
        ids = list(self.me)
        ids[axis] = lax.rem(self.me[axis] + d, self.sizes[axis])
        return tuple(ids)

    def signal(self, sem):
        for axis in range(3):
            for d in range(1, self.sizes[axis]):
                pl.semaphore_signal(sem, inc=1, device_id=self.peer(axis, d), device_id_type=MESH)
        return sum(self.sizes) - 3

    def move(self, axis, d):
        base = sum(self.sizes[:axis])
        buf = self.bufs[axis]
        return pltpu.make_async_remote_copy(
            src_ref=buf.at[0],
            dst_ref=buf.at[d],
            send_sem=self.sems.at[0, base + d],
            recv_sem=self.sems.at[1, base + d],
            device_id=self.peer(axis, d),
            device_id_type=MESH,
        )

    def begin(self, axis, value):
        self.bufs[axis][0] = value
        for d in range(1, self.sizes[axis]):
            self.move(axis, d).start()

    def end(self, axis):
        n = self.sizes[axis]
        for d in range(1, n):
            self.move(axis, d).wait()
        total = jnp.zeros(self.out.shape, F32)
        for i in range(n):
            total = total + self.bufs[axis][lax.rem(self.me[axis] - i + n, n)]
        return total


def last_kernel(
    chunks, sizes, part, x_ref, gain, dresid_ref, small_ref, out_ref, total_ref, core_in, y_out, y_in, sems, *rest
):
    mp = Mp(part, core_in, y_out, y_in, None, sems, chunks)
    small = SmallSum(sizes, small_ref, total_ref, rest[:3], rest[3])
    sem = pltpu.get_barrier_semaphore()
    pl.semaphore_wait(sem, small.signal(sem))
    mp.rs_core(0).start()
    mp.rs_core(1).start()
    small.begin(2, small_ref[...])
    mp.rs_forward()
    small.begin(0, small.end(2))
    order = (lambda: small.begin(1, small.end(0)),)
    for i in range(chunks):
        cut = mp.cut(i)
        if i < len(order):
            order[i]()
        dh = mp.rs_chunk(i)
        normed, inverse = rms_parts(x_ref[cut, :].astype(F32))
        out_ref[cut, :] = dresid_ref[cut, :] + rms_grad(dh * gain[...], normed, inverse)
    total_ref[...] = small.end(1)
    mp.rs_end()


def last(sizes, part, x_mine, gain, dresid, small, chunks=2):
    _, share, width = part.shape
    return pl.pallas_call(
        functools.partial(last_kernel, chunks, sizes),
        out_shape=(jax.ShapeDtypeStruct((share, width), F32), jax.ShapeDtypeStruct(small.shape, F32)),
        in_specs=[VMEM] * 5,
        out_specs=(VMEM,) * 2,
        scratch_shapes=mp_scratch(share, width, chunks)
        + [pltpu.VMEM((n,) + small.shape, F32) for n in sizes]
        + [DMA((2, sum(sizes)))],
        compiler_params=params(4, 20),
        name="last",
        cost_estimate=cost(20),
    )(part, x_mine, gain, dresid, small)


def line_sum(parts, n, dim):
    c = lax.axis_index("ctx")
    size = parts.shape[dim] // n

    def chunk(k):
        return lax.dynamic_slice_in_dim(parts, jnp.clip(k, 0, n - 1) * size, size, dim)

    total = chunk(c).astype(F32)
    for way in (1, -1):
        moving = None
        for t in range(1, n):
            mine = chunk(n - t + c if way == 1 else c - n + t)
            if moving is not None:
                mine = (mine.astype(F32) + moving.astype(F32)).astype(BF16)
            if way == 1:
                pairs = [(i, i + 1) for i in range(t)]
            else:
                pairs = [(i, i - 1) for i in range(n - t, n)]
            moving = lax.ppermute(mine, "ctx", pairs)
        total = total + moving.astype(F32)
    return total


def half(x, s, dim):
    size = x.shape[dim] // 2
    return lax.dynamic_slice_in_dim(x, s * size, size, dim)


SWAP = [(0, 1), (1, 0)]


def columns(x):
    n_seq, n_ctx = lax.axis_size("seq"), lax.axis_size("ctx")
    size = x.shape[2] // (n_seq * n_ctx)
    part = lambda i, j: x[:, :, (j * n_ctx + i) * size : (j * n_ctx + i + 1) * size]
    return jnp.stack([jnp.stack([part(i, j) for j in range(n_seq)]) for i in range(n_ctx)])


def body(
    tokens,
    norm1_gain,
    w_query,
    key_weight_matrix,
    value_weight_matrix,
    w_out,
    norm2_gain,
    router,
    w_gate,
    w_up,
    w_down,
    routes,
    cotangent,
):
    n_seq, n_ctx, n_mp = (lax.axis_size(a) for a in ("seq", "ctx", "mp"))
    s, c, m = (lax.axis_index(a) for a in ("seq", "ctx", "mp"))
    tok, width = tokens.shape
    share = tok // n_mp
    experts_all = router.shape[1]
    exp_local = w_gate.shape[0]
    top = routes.shape[1]
    cap = share * top * 5 // (4 * experts_all)
    slots = n_mp * cap
    gain1 = norm1_gain.reshape(1, width)
    gain2 = norm2_gain.reshape(1, width)

    cot_all = lax.all_gather(cotangent, "mp", axis=0, tiled=True)
    x_mine = lax.dynamic_slice_in_dim(tokens, m * share, share, 0)

    normed_one, _ = rms_parts(tokens.astype(F32))
    h_one = (normed_one * gain1).astype(BF16)
    qt = (jnp.einsum("df,td->ft", w_query, h_one, preferred_element_type=F32).astype(BF16)) * BF16(0.125)
    k = nn(h_one, key_weight_matrix).astype(BF16)
    v = nn(h_one, value_weight_matrix).astype(BF16)
    o, heads_t, lse, kv, cot_below, cot_above, routes_line = attend(n_ctx, qt, k, v, cotangent, routes.T)

    experts = jnp.arange(experts_all, dtype=jnp.int32)
    first = m * exp_local
    local = first + jnp.arange(exp_local, dtype=jnp.int32)
    chosen_line = (routes_line[:, None, :, :] == local[None, :, None, None]).any(axis=2)
    low = (jnp.arange(tok)[:, None] <= jnp.arange(tok)[None, :]).astype(BF16)
    rank_line = (
        jnp.einsum("cet,tu->ceu", chosen_line.astype(BF16), low, preferred_element_type=F32) - 1.0
    ).astype(jnp.int32)
    place_line = (
        (rank_line[:, :, None, :] == jnp.arange(slots, dtype=jnp.int32)[None, None, :, None])
        & chosen_line[:, :, None, :]
    ).astype(BF16)
    chosen = (routes[:, :, None] == experts[None, None, :]).any(axis=1)
    place = lax.dynamic_index_in_dim(place_line, c, 0, keepdims=False)
    dout_rows = jnp.einsum("ert,td->erd", place, cot_all, preferred_element_type=F32)
    dout_rows = dout_rows.astype(BF16).astype(F32)
    r_hi = router.astype(BF16)
    r_rest = router - r_hi.astype(F32)
    r_mid = r_rest.astype(BF16)
    r_low = (r_rest - r_mid.astype(F32)).astype(BF16)
    router3 = jnp.concatenate([r_hi, r_mid, r_low], axis=1)

    part = jnp.einsum("ft,fd->td", heads_t, w_out, preferred_element_type=F32).astype(BF16)
    resid, h_two, cot_mine = mid_forward(
        n_ctx, part.reshape(n_mp, share, width), x_mine, gain2, cotangent, cot_below, cot_above
    )
    h_two = h_two.reshape(tok, width)

    logits3 = nn(h_two, router3)
    logits = (
        logits3[:, :experts_all]
        + logits3[:, experts_all : 2 * experts_all]
        + logits3[:, 2 * experts_all :]
    )
    peak = jnp.max(jnp.where(chosen, logits, -jnp.inf), axis=-1, keepdims=True)
    raised = jnp.where(chosen, jnp.exp(jnp.where(chosen, logits - peak, 0.0)), 0.0)
    gates = raised / jnp.sum(raised, axis=-1, keepdims=True)
    gates_mine = lax.dynamic_slice_in_dim(gates.T, first, exp_local, 0)
    gate_rows = jnp.sum(place.astype(F32) * gates_mine[:, None, :], axis=-1)[..., None]
    arrived = jnp.einsum("ert,td->erd", place, h_two, preferred_element_type=F32).astype(BF16)
    gate_pre = jnp.einsum("erd,edf->erf", arrived, w_gate, preferred_element_type=F32)
    up_pre = jnp.einsum("erd,edf->erf", arrived, w_up, preferred_element_type=F32)
    sigma = jax.nn.sigmoid(gate_pre)
    silu_gate = gate_pre * sigma
    hidden = (silu_gate * up_pre).astype(BF16)
    grad_made = (gate_rows * dout_rows).astype(BF16)
    grad_hidden = jnp.einsum("erd,efd->erf", grad_made, w_down, preferred_element_type=F32)
    grad_gate_pre = (grad_hidden * up_pre * sigma * (1.0 + gate_pre * (1.0 - sigma))).astype(BF16)
    grad_up_pre = (grad_hidden * silu_gate).astype(BF16)
    grad_arrived = jnp.einsum("erf,edf->erd", grad_gate_pre, w_gate, preferred_element_type=F32)
    grad_arrived = grad_arrived + jnp.einsum("erf,edf->erd", grad_up_pre, w_up, preferred_element_type=F32)
    grad_arrived = grad_arrived.astype(BF16)
    made = jnp.einsum("erf,efd->erd", hidden, w_down, preferred_element_type=F32).astype(BF16)
    made_f = made.astype(F32)
    gate_grads = jnp.sum(dout_rows * made_f, axis=-1)
    ex_pad = 64
    local_hot = (experts[None, :] == (first + jnp.arange(exp_local, dtype=jnp.int32))[:, None]).astype(F32)
    gate_grads = gate_grads[..., None] * local_hot[:, None, :]
    gate_grads = jnp.pad(gate_grads, ((0, 0), (0, 0), (0, ex_pad - experts_all)))
    gg_hi = gate_grads.astype(BF16)
    gg_low = (gate_grads - gg_hi.astype(F32)).astype(BF16)
    flat = place.reshape(exp_local * slots, tok)
    back_rows = jnp.concatenate([grad_arrived, gg_hi, gg_low], axis=-1).reshape(exp_local * slots, -1)
    back = jnp.einsum("rt,rd->td", flat, back_rows, preferred_element_type=F32).astype(BF16)
    comb_rows = (gate_rows * made_f).astype(BF16).reshape(exp_local * slots, width)
    comb = jnp.einsum("rt,rd->td", flat, comb_rows, preferred_element_type=F32).astype(BF16)
    output = resid + lax.psum_scatter(comb, "mp", scatter_dimension=0, tiled=True).astype(F32)

    gates_pad = jnp.pad(
        lax.dynamic_slice_in_dim(gates, m * share, share, 0), ((0, 0), (0, ex_pad - experts_all))
    )
    router_t = jnp.pad(router.T, ((0, ex_pad - experts_all), (0, 0)))
    hidden_parts = columns(hidden)
    dresid, db, dlog, gnorm2, gate_rows_line, hidden_line, du_below, du_above = mid_back(
        n_ctx,
        back.reshape(n_mp, share, -1),
        resid,
        gain2,
        cotangent,
        gates_pad,
        router_t,
        gate_rows[..., 0],
        hidden_parts,
        grad_up_pre,
    )
    db = db.reshape(tok, width)
    h_two_mine = lax.dynamic_slice_in_dim(h_two, m * share, share, 0).astype(F32)
    g_router = jnp.einsum("te,td->ed", dlog[:, :experts_all], h_two_mine, precision=lax.Precision.HIGHEST)

    arrived2 = jnp.concatenate([half(arrived, s, 2), lax.ppermute(half(arrived, 1 - s, 2), "seq", SWAP)], axis=1)
    dg2 = jnp.concatenate([grad_gate_pre, lax.ppermute(grad_gate_pre, "seq", SWAP)], axis=1)
    g_gate = jnp.einsum("erd,erf->edf", arrived2, dg2, preferred_element_type=F32).astype(BF16)
    arrived_line = lax.all_to_all(columns(arrived), "ctx", split_axis=0, concat_axis=0, tiled=True)
    opp = [(i, (i + n_mp // 2) % n_mp) for i in range(n_mp)]
    sib = [(i, i + 1 - 2 * (i % 2)) for i in range(n_mp)]
    cot_opp = lax.ppermute(cot_mine, "mp", opp)
    cot_sib, cot_diag = lax.ppermute(cot_mine, "mp", sib), lax.ppermute(cot_opp, "mp", sib)
    by_mp = jnp.stack([cot_mine, cot_sib, cot_opp, cot_diag])
    where = jnp.arange(n_mp)
    flip = (where & 1) ^ (m & 1) | (where & 2) ^ (m & 2)
    cot_line = by_mp[flip].transpose(1, 0, 2, 3).reshape(n_ctx, tok, width)
    dout_line = jnp.einsum("cert,ctd->cerd", place_line, cot_line, preferred_element_type=F32)
    dy_line = (gate_rows_line[..., None] * dout_line.astype(BF16).astype(F32)).astype(BF16)

    def seq_sum(g):
        mine = lax.dynamic_index_in_dim(g, s, 0, keepdims=False)
        theirs = lax.dynamic_index_in_dim(g, 1 - s, 0, keepdims=False).astype(BF16)
        return mine.astype(F32) + lax.ppermute(theirs, "seq", SWAP).astype(F32)

    g_down = seq_sum(jnp.einsum("csera,cerd->sead", hidden_line, dy_line, preferred_element_type=F32))

    dheads = jnp.einsum("fd,td->ft", w_out, db, preferred_element_type=F32).astype(BF16)
    g_out = jnp.einsum("td,ft->df", db, heads_t, preferred_element_type=F32).astype(BF16)

    def seq_half_sum(g):
        return (
            half(g, s, 0).astype(F32) + lax.ppermute(half(g, 1 - s, 0), "seq", SWAP).astype(F32)
        ).astype(BF16)

    g_out = line_sum(seq_half_sum(g_out), n_ctx, 0).T
    dq, dkv, g_gate, du_line = attend_back(
        n_ctx, qt, dheads, o, lse, kv, g_gate, grad_up_pre, du_below, du_above
    )
    g_up = seq_sum(jnp.einsum("csera,cerf->seaf", arrived_line, du_line, preferred_element_type=F32))
    kvw = dkv.shape[1] // 2
    dk, dv = dkv[:, :kvw], dkv[:, kvw:]
    dh = jnp.einsum("ft,df->td", dq, w_query, preferred_element_type=F32)
    dh = dh + jnp.einsum("tf,df->td", dk, key_weight_matrix, preferred_element_type=F32)
    dh = dh + jnp.einsum("tf,df->td", dv, value_weight_matrix, preferred_element_type=F32)
    gnorm1 = jnp.sum(dh * normed_one, axis=0, keepdims=True)
    rows = 2 + experts_all
    small = jnp.concatenate([gnorm1, gnorm2[:1], g_router, jnp.zeros((-rows % 8, width), F32)], axis=0)
    grad_tokens, small = last(
        (n_seq, n_ctx, n_mp), dh.astype(BF16).reshape(n_mp, share, width), x_mine, gain1, dresid, small
    )
    g_q = jnp.einsum("td,ft->df", h_one, dq, preferred_element_type=F32)
    g_kv = jnp.einsum("td,tf->df", h_one, dkv, preferred_element_type=F32)
    g_qkv = jnp.concatenate([g_q, g_kv], axis=1).astype(BF16)
    g_qkv = line_sum(seq_half_sum(g_qkv), n_ctx, 0)
    qw = w_query.shape[1]

    return (
        output,
        grad_tokens,
        small[0],
        g_qkv[:, :qw],
        g_qkv[:, qw : qw + kvw],
        g_qkv[:, qw + kvw :],
        g_out,
        small[1],
        small[2:rows].T,
        g_gate,
        g_up,
        g_down,
    )


def solution(mesh):
    placed = (
        P(("seq", "ctx"), None),
        P(),
        P(None, "mp"),
        P(None, "mp"),
        P(None, "mp"),
        P("mp", None),
        P(),
        P(),
        P("mp", None, None),
        P("mp", None, None),
        P("mp", None, None),
        P(("seq", "ctx"), None),
        P(("seq", "ctx", "mp"), None),
    )
    return jax.shard_map(
        body,
        mesh=mesh,
        in_specs=placed,
        out_specs=(
            P(("seq", "ctx", "mp"), None),
            P(("seq", "ctx", "mp"), None),
            P(),
            P(("seq", "ctx"), "mp"),
            P(("seq", "ctx"), "mp"),
            P(("seq", "ctx"), "mp"),
            P("mp", ("seq", "ctx")),
            P(),
            P(),
            P("mp", ("seq", "ctx"), None),
            P("mp", ("seq", "ctx"), None),
            P("mp", ("seq", "ctx"), None),
        ),
        check_vma=False,
    )
```

```python
import functools

import jax
import jax.numpy as jnp
from jax import lax
from jax.experimental import pallas as pl
from jax.experimental.pallas import tpu as pltpu
from jax.sharding import PartitionSpec as P

HEAD_SIZE = 64
EPS = 1e-06
MESH = pl.DeviceIdType.MESH
F32 = jnp.float32
BF16 = jnp.bfloat16
VMEM = pl.BlockSpec(memory_space=pltpu.VMEM)
DMA = pltpu.SemaphoreType.DMA
MIB = 2**20


def cost(us):
    return pl.CostEstimate(flops=0, bytes_accessed=int(us * 3.6e6), transcendentals=0)


def params(collective_id, mib=56):
    return pltpu.CompilerParams(
        collective_id=collective_id, has_side_effects=True, vmem_limit_bytes=mib * MIB
    )


def nt(a, b):
    return lax.dot_general(a, b, (((1,), (1,)), ((), ())), preferred_element_type=F32)


def nn(a, b):
    return jnp.dot(a, b, preferred_element_type=F32)


class Spread:
    def __init__(self, n, own, below, above, all_ref, send, recv, local):
        self.n, self.own, self.below, self.above, self.all = n, own, below, above, all_ref
        self.send, self.recv, self.local = send, recv, local
        s, self.c, m = lax.axis_index("seq"), lax.axis_index("ctx"), lax.axis_index("mp")
        self.lower, self.upper = lax.rem(self.c + n - 1, n), lax.rem(self.c + 1, n)
        self.up, self.down = (s, self.upper, m), (s, self.lower, m)
        self.inner = jnp.logical_and(self.c > 0, self.c < n - 1)

    def move(self, b, src, device):
        return pltpu.make_async_remote_copy(
            src_ref=src,
            dst_ref=self.all.at[b],
            send_sem=self.send.at[b],
            recv_sem=self.recv.at[b],
            device_id=device,
            device_id_type=MESH,
        )

    def keep(self, i, src, b):
        return pltpu.make_async_copy(src, self.all.at[b], self.local.at[i])

    def start(self):
        @pl.when(self.inner)
        def _():
            self.move(self.lower, self.below, self.up).start()
            self.move(self.upper, self.above, self.down).start()

        self.keep(0, self.own, self.c).start()

        @pl.when(self.c > 0)
        def _():
            self.keep(1, self.below, self.lower).start()

        @pl.when(self.c < self.n - 1)
        def _():
            self.keep(2, self.above, self.upper).start()

    def tick(self, i):
        c, n = self.c, self.n

        @pl.when(c - 1 - i >= 0)
        def _():
            b = jnp.maximum(c - 1 - i, 0)
            self.move(b, self.all.at[b], self.up).wait_recv()

            @pl.when(c < n - 1)
            def _():
                self.move(b, self.all.at[b], self.up).start()

        @pl.when(c + 1 + i <= n - 1)
        def _():
            b = jnp.minimum(c + 1 + i, n - 1)
            self.move(b, self.all.at[b], self.down).wait_recv()

            @pl.when(c > 0)
            def _():
                self.move(b, self.all.at[b], self.down).start()

    def ticks(self, first):
        def later(i, carry):
            self.tick(i)
            return carry

        lax.fori_loop(first, self.n - 1, later, 0)

    def finish(self):
        self.keep(0, self.own, self.c).wait()

        @pl.when(self.c > 0)
        def _():
            self.keep(1, self.below, self.lower).wait()

        @pl.when(self.c < self.n - 1)
        def _():
            self.keep(2, self.above, self.upper).wait()

        @pl.when(self.inner)
        def _():
            def sent(b, carry):
                @pl.when(b != self.c)
                def _():
                    self.move(b, self.all.at[b], self.up).wait_send()

                return carry

            lax.fori_loop(0, self.n, sent, 0)


class Neighbours:
    def __init__(self, n, own, below, above, send, recv):
        self.n, self.own, self.below, self.above, self.send, self.recv = n, own, below, above, send, recv
        s, self.c, m = lax.axis_index("seq"), lax.axis_index("ctx"), lax.axis_index("mp")
        self.up, self.down = (s, lax.rem(self.c + 1, n), m), (s, lax.rem(self.c + n - 1, n), m)

    def move(self, way):
        return pltpu.make_async_remote_copy(
            src_ref=self.own,
            dst_ref=self.below if way == 0 else self.above,
            send_sem=self.send.at[way],
            recv_sem=self.recv.at[way],
            device_id=self.up if way == 0 else self.down,
            device_id_type=MESH,
        )

    def start_up(self):
        @pl.when(self.c < self.n - 1)
        def _():
            self.move(0).start()

    def start_down(self):
        @pl.when(self.c > 0)
        def _():
            self.move(1).start()

    def finish(self):
        @pl.when(self.c > 0)
        def _():
            self.move(0).wait_recv()
            self.move(1).wait_send()

        @pl.when(self.c < self.n - 1)
        def _():
            self.move(1).wait_recv()
            self.move(0).wait_send()


class Peers:
    def __init__(self, n, src_of, dst_of, send, recv):
        self.n, self.src_of, self.dst_of, self.send, self.recv = n, src_of, dst_of, send, recv
        self.s, self.c, self.m = lax.axis_index("seq"), lax.axis_index("ctx"), lax.axis_index("mp")

    def move(self, d):
        peer = lax.rem(self.c + d, self.n)
        return pltpu.make_async_remote_copy(
            src_ref=self.src_of(peer),
            dst_ref=self.dst_of(self.c),
            send_sem=self.send.at[d],
            recv_sem=self.recv.at[d],
            device_id=(self.s, peer, self.m),
            device_id_type=MESH,
        )

    def signal(self, sem):
        for d in range(1, self.n):
            pl.semaphore_signal(
                sem, inc=1, device_id=(self.s, lax.rem(self.c + d, self.n), self.m), device_id_type=MESH
            )

    def start(self):
        for d in range(1, self.n):
            self.move(d).start()

    def finish(self):
        for d in range(1, self.n):
            self.move(d).wait()


class CotExchange:
    def __init__(self, line_ref, full, first, count, sems, local):
        self.line, self.full, self.first, self.count, self.sems, self.local = line_ref, full, first, count, sems, local
        s, c, m = lax.axis_index("seq"), lax.axis_index("ctx"), lax.axis_index("mp")
        self.m = m
        self.share = line_ref.shape[1]
        self.sib = m + 1 - 2 * lax.rem(m, 2)
        self.opp = lax.rem(m + 2, 4)
        self.sib_id, self.opp_id = (s, c, self.sib), (s, c, self.opp)

    def signal(self, sem):
        for d in (self.sib_id, self.opp_id):
            pl.semaphore_signal(sem, inc=1, device_id=d, device_id_type=MESH)

    def place(self, who):
        return self.full.at[:, pl.ds(pl.multiple_of(who * self.share, 16), self.share), :]

    def move(self, i):
        mine = self.line.at[pl.ds(self.first, self.count)]
        src = self.place(self.opp) if i == 2 else mine
        whose = self.opp if i == 2 else self.m
        return pltpu.make_async_remote_copy(
            src_ref=src,
            dst_ref=self.place(whose),
            send_sem=self.sems.at[0, i],
            recv_sem=self.sems.at[1, i],
            device_id=self.opp_id if i == 0 else self.sib_id,
            device_id_type=MESH,
        )

    def own(self):
        return pltpu.make_async_copy(
            self.line.at[pl.ds(self.first, self.count)], self.place(self.m), self.local.at[0]
        )

    def start(self):
        self.move(0).start()
        self.move(1).start()
        self.own().start()

    def finish(self):
        self.move(0).wait_recv()
        self.move(2).start()
        self.own().wait()
        self.move(1).wait_recv()
        self.move(2).wait_recv()
        for i in range(3):
            self.move(i).wait_send()


def signal_line(n, sem):
    s, c, m = lax.axis_index("seq"), lax.axis_index("ctx"), lax.axis_index("mp")

    @pl.when(c > 0)
    def _():
        pl.semaphore_signal(sem, inc=1, device_id=(s, lax.rem(c + n - 1, n), m), device_id_type=MESH)

    @pl.when(c < n - 1)
    def _():
        pl.semaphore_signal(sem, inc=1, device_id=(s, lax.rem(c + 1, n), m), device_id_type=MESH)


def line_degree(n):
    c = lax.axis_index("ctx")
    return jnp.where(c > 0, 1, 0) + jnp.where(c < n - 1, 1, 0)


def pad_heads(src, dst, heads, group):
    dst[...] = jnp.zeros_like(dst)
    for h in range(heads):
        g = h // group
        rows = slice(g * HEAD_SIZE, (g + 1) * HEAD_SIZE)
        dst[h, rows, :] = src[h * HEAD_SIZE : (h + 1) * HEAD_SIZE, :]


def causal(t):
    keys = lax.broadcasted_iota(jnp.int32, (t, t), 0)
    queries = lax.broadcasted_iota(jnp.int32, (t, t), 1)
    return keys <= queries


def attend_kernel(
    n,
    q_ref,
    k_ref,
    v_ref,
    cot_ref,
    routes_ref,
    o_ref,
    heads_ref,
    lse_ref,
    kv_ref,
    below_ref,
    above_ref,
    line_ref,
    qpad,
    vt,
    top,
    tot,
    send,
    recv,
    side,
    peers_sem,
):
    s, c, m = lax.axis_index("seq"), lax.axis_index("ctx"), lax.axis_index("mp")
    t, kvw = k_ref.shape
    heads = q_ref.shape[0] // HEAD_SIZE
    group = heads // (kvw // HEAD_SIZE)
    up, down = (s, lax.rem(c + 1, n), m), (s, lax.rem(c + n - 1, n), m)
    kv_ref[0, :, :kvw] = k_ref[...]
    kv_ref[0, :, kvw:] = v_ref[...]
    line_ref[c] = routes_ref[...]
    peers = Peers(n, lambda p: routes_ref, lambda i: line_ref.at[i], peers_sem.at[0], peers_sem.at[1])
    beside = Neighbours(n, cot_ref, below_ref, above_ref, side.at[0], side.at[1])
    sem = pltpu.get_barrier_semaphore()
    peers.signal(sem)
    pl.semaphore_wait(sem, n - 1)

    def pass_up(slot):
        return pltpu.make_async_remote_copy(
            src_ref=kv_ref.at[slot],
            dst_ref=kv_ref.at[slot + 1],
            send_sem=send.at[slot],
            recv_sem=recv.at[slot + 1],
            device_id=up,
            device_id_type=MESH,
        )

    def got(slot):
        return pltpu.make_async_remote_copy(
            src_ref=kv_ref.at[slot],
            dst_ref=kv_ref.at[slot],
            send_sem=send.at[slot],
            recv_sem=recv.at[slot],
            device_id=up,
            device_id_type=MESH,
        )

    @pl.when(c < n - 1)
    def _():
        pass_up(0).start()

    peers.start()
    beside.start_down()
    pad_heads(q_ref, qpad, heads, group)
    top[...] = jnp.full_like(top, -1e30)
    tot[...] = jnp.zeros_like(tot)
    o_ref[...] = jnp.zeros_like(o_ref)

    def block(slot, masked):
        vt[...] = kv_ref[slot, :, kvw:].T

        def head(h, carry):
            g = lax.div(h, group)
            scores = nn(kv_ref[slot, :, :kvw], qpad[h])
            if masked:
                scores = jnp.where(causal(t), scores, -1e30)
            old = top[h]
            new = jnp.maximum(old, jnp.max(scores, axis=0, keepdims=True))
            weights = jnp.exp(scores - new)
            factor = jnp.exp(old - new)
            top[h] = new
            tot[h] = tot[h] * factor + jnp.sum(weights, axis=0, keepdims=True)
            rows = pl.ds(pl.multiple_of(h * HEAD_SIZE, HEAD_SIZE), HEAD_SIZE)
            vrows = pl.ds(pl.multiple_of(g * HEAD_SIZE, HEAD_SIZE), HEAD_SIZE)
            o_ref[rows, :] = o_ref[rows, :] * factor + nn(vt[vrows, :], weights.astype(BF16))
            return carry

        lax.fori_loop(0, heads, head, 0)

    block(0, True)

    def earlier(slot, carry):
        got(slot).wait_recv()

        @pl.when(c < n - 1)
        def _():
            pass_up(slot).start()

        @pl.when(slot == c)
        def _():
            beside.start_up()

        block(slot, False)
        return carry

    @pl.when(c == 0)
    def _():
        beside.start_up()

    lax.fori_loop(1, c + 1, earlier, 0)
    for h in range(heads):
        rows = slice(h * HEAD_SIZE, (h + 1) * HEAD_SIZE)
        done = o_ref[rows, :] / tot[h]
        o_ref[rows, :] = done
        heads_ref[rows, :] = done.astype(BF16)
        lse_ref[h] = top[h] + jnp.log(tot[h])

    @pl.when(c < n - 1)
    def _():
        def sent(slot, carry):
            pass_up(slot).wait_send()
            return carry

        lax.fori_loop(0, c + 1, sent, 0)

    peers.finish()
    beside.finish()


def attend(n, qt, k, v, cot, routes):
    t, kvw = k.shape
    qw = qt.shape[0]
    heads = qw // HEAD_SIZE
    return pl.pallas_call(
        functools.partial(attend_kernel, n),
        out_shape=(
            jax.ShapeDtypeStruct((qw, t), F32),
            jax.ShapeDtypeStruct((qw, t), BF16),
            jax.ShapeDtypeStruct((heads, 1, t), F32),
            jax.ShapeDtypeStruct((n, t, 2 * kvw), BF16),
            jax.ShapeDtypeStruct(cot.shape, BF16),
            jax.ShapeDtypeStruct(cot.shape, BF16),
            jax.ShapeDtypeStruct((n,) + routes.shape, jnp.int32),
        ),
        in_specs=[VMEM] * 5,
        out_specs=(VMEM,) * 7,
        scratch_shapes=[
            pltpu.VMEM((heads, kvw, t), BF16),
            pltpu.VMEM((kvw, t), BF16),
            pltpu.VMEM((heads, 1, t), F32),
            pltpu.VMEM((heads, 1, t), F32),
            DMA((n,)),
            DMA((n,)),
            DMA((2, 2)),
            DMA((2, n)),
        ],
        compiler_params=params(0),
        name="attend",
        cost_estimate=cost(30),
    )(qt, k, v, cot, routes)


def attend_back_kernel(
    n,
    n_seq,
    q_ref,
    db_ref,
    wout_ref,
    o_ref,
    lse_ref,
    kv_ref,
    arr_ref,
    arr_other,
    dg_ref,
    dg_other,
    own_ref,
    below_ref,
    above_ref,
    rows_line,
    hid_line,
    arr_line,
    place_hbm,
    line_hbm,
    first_hbm,
    dq_ref,
    dkv_ref,
    summed_ref,
    up_ref,
    down_ref,
    all_ref,
    rest_hbm,
    do_ref,
    qpad,
    dopad,
    delta,
    dq,
    kt,
    part,
    passing,
    sum_ref,
    from_below,
    from_above,
    place_buf,
    cot_buf,
    du_buf,
    dy,
    d_acc,
    u_acc,
    d_out,
    d_in,
    u_out,
    u_in,
    send,
    recv,
    spread_sem,
    local,
    ysem,
    cot_local,
    load_sem,
    swap_sem,
):
    s, c, m = lax.axis_index("seq"), lax.axis_index("ctx"), lax.axis_index("mp")
    _, t, kvw2 = kv_ref.shape
    kvw = kvw2 // 2
    heads = q_ref.shape[0] // HEAD_SIZE
    group = heads // (kvw // HEAD_SIZE)
    ex = sum_ref.shape[0]
    half_width = sum_ref.shape[1]
    chunk_rows = half_width // n
    slots = arr_ref.shape[1]
    width = db_ref.shape[1]
    up, down = (s, lax.rem(c + 1, n), m), (s, lax.rem(c + n - 1, n), m)
    spread = Spread(n, own_ref, below_ref, above_ref, all_ref, spread_sem.at[0], spread_sem.at[1], local)
    done_blocks = first_hbm.shape[0]
    cots = CotExchange(line_hbm, rest_hbm, done_blocks, n - done_blocks, ysem, cot_local)
    sem = pltpu.get_barrier_semaphore()
    signal_line(n, sem)
    cots.signal(sem)
    pl.semaphore_signal(sem, inc=1, device_id=swap_partner(), device_id_type=MESH)
    pl.semaphore_wait(sem, line_degree(n) + 3)
    cots.start()
    spread.start()

    def gate_part(i):
        e, r = lax.div(i, half_width // 256), lax.rem(i, half_width // 256)
        mine = pl.ds(pl.multiple_of(s * half_width + r * 256, 128), 256)
        cut = pl.ds(pl.multiple_of(r * 256, 256), 256)
        sum_ref[e, cut, :] = (
            tn(arr_ref[e, :, mine], dg_ref[e]) + tn(arr_other[e, :, cut], dg_other[e])
        ).astype(BF16)

    loop(ex * (half_width // 256), gate_part)

    def remote(kind, i, src, dst, device):
        return pltpu.make_async_remote_copy(
            src_ref=src,
            dst_ref=dst,
            send_sem=send.at[kind, i],
            recv_sem=recv.at[kind, i],
            device_id=device,
            device_id_type=MESH,
        )

    def own_unit(k, e):
        return sum_ref.at[e, pl.ds(pl.multiple_of(k * chunk_rows, 16), chunk_rows), :]

    def sum_up(k, e, first=False):
        there = from_below.at[k, e]
        return remote(1, k * ex + e, own_unit(k, e) if first else there, there, up)

    def sum_down(k, e, first=False):
        there = from_above.at[k, e]
        return remote(2, k * ex + e, own_unit(k, e) if first else there, there, down)

    units = (n - 1) * ex
    ahead = 2

    def first_up(u):
        @pl.when(jnp.logical_and(c == 0, u < units))
        def _():
            @pl.when(u >= ahead)
            def _():
                v = jnp.maximum(u - ahead, 0)
                sum_up(n - 1 - lax.div(v, ex), lax.rem(v, ex), True).wait_send()

            w = jnp.minimum(u, units - 1)
            sum_up(n - 1 - lax.div(w, ex), lax.rem(w, ex), True).start()

    def first_down(u):
        @pl.when(jnp.logical_and(c == n - 1, u < units))
        def _():
            @pl.when(u >= ahead)
            def _():
                v = jnp.maximum(u - ahead, 0)
                sum_down(lax.div(v, ex), lax.rem(v, ex), True).wait_send()

            w = jnp.minimum(u, units - 1)
            sum_down(lax.div(w, ex), lax.rem(w, ex), True).start()

    first_up(0)
    first_down(0)
    do_ref[...] = nt(wout_ref[...], db_ref[...]).astype(BF16)

    def tick(i):
        first_up(i + 1)
        first_down(i + 1)
        for hop in range(1, n - 1):

            @pl.when(i == hop * ex)
            def _():
                spread.tick(hop)

        u = i - c
        k = n - 1 - lax.div(jnp.maximum(u, 0), ex)
        e = lax.rem(jnp.maximum(u, 0), ex)

        @pl.when(jnp.logical_and(c > 0, jnp.logical_and(u >= 0, k > c)))
        def _():
            there = jnp.maximum(k, 0)
            sum_up(there, e).wait_recv()
            from_below[there, e] = (own_unit(there, e)[...].astype(F32) + from_below[there, e].astype(F32)).astype(BF16)
            sum_up(there, e).start()

        v = i - (n - 1 - c)
        kd = lax.div(jnp.maximum(v, 0), ex)
        ed = lax.rem(jnp.maximum(v, 0), ex)

        @pl.when(jnp.logical_and(c < n - 1, jnp.logical_and(v >= 0, kd < c)))
        def _():
            there = jnp.minimum(kd, n - 1)
            sum_down(there, ed).wait_recv()
            from_above[there, ed] = (own_unit(there, ed)[...].astype(F32) + from_above[there, ed].astype(F32)).astype(BF16)
            sum_down(there, ed).start()

    last_tick = units + n

    pad_heads(q_ref, qpad, heads, group)
    pad_heads(do_ref, dopad, heads, group)
    for h in range(heads):
        rows = slice(h * HEAD_SIZE, (h + 1) * HEAD_SIZE)
        delta[h] = jnp.sum(do_ref[rows, :].astype(F32) * o_ref[rows, :], axis=0, keepdims=True)
    dq[...] = jnp.zeros_like(dq)

    def block(j, masked):
        slot = c - j
        acc = part.at[lax.rem(j, 2)]
        acc[...] = jnp.zeros(acc.shape, F32)
        kt[...] = kv_ref[slot, :, :kvw].T

        def head(h, carry):
            g = lax.div(h, group)
            scores = nn(kv_ref[slot, :, :kvw], qpad[h])
            probs = jnp.exp(scores - lse_ref[h])
            if masked:
                probs = jnp.where(causal(t), probs, 0.0)
            dprobs = nn(kv_ref[slot, :, kvw:], dopad[h])
            ds = (probs * (dprobs - delta[h])).astype(BF16)
            rows = pl.ds(pl.multiple_of(h * HEAD_SIZE, HEAD_SIZE), HEAD_SIZE)
            krows = pl.ds(pl.multiple_of(g * HEAD_SIZE, HEAD_SIZE), HEAD_SIZE)
            dq[rows, :] = dq[rows, :] + nn(kt[krows, :], ds)
            acc[:, :kvw] = acc[:, :kvw] + nt(ds, qpad[h])
            acc[:, kvw:] = acc[:, kvw:] + nt(probs.astype(BF16), dopad[h])
            return carry

        lax.fori_loop(0, heads, head, 0)

    def pass_down(j):
        return remote(0, j, passing.at[j], passing.at[j], down)

    def gathered(j):
        acc = part.at[lax.rem(j, 2)]

        @pl.when(c < n - 1)
        def _():
            pass_down(j).wait_recv()
            acc[...] = acc[...] + passing[j].astype(F32)

        return acc

    def forward(j):
        acc = gathered(j)
        passing[j] = acc[...].astype(BF16)
        pass_down(j).start()

    def step(j, carry):
        block(j, False)

        @pl.when(jnp.logical_and(j > 0, c < n - 1))
        def _():
            forward(j - 1)

        @pl.when(c == n - 1)
        def _():
            forward(j)

        tick(j)
        return carry

    lax.fori_loop(0, c, step, 0)
    block(c, True)

    @pl.when(spread.inner)
    def _():
        forward(c - 1)

    dq_ref[...] = (dq[...] * 0.125).astype(BF16)

    def later(i, carry):
        tick(i)
        return carry

    pause = jnp.maximum(c, 2 * ex)
    lax.fori_loop(c, pause, later, 0)
    acc = gathered(c)
    dkv_ref[...] = acc[...].astype(BF16)

    cots.finish()

    def load_block(b, slot, start):
        place_copy = pltpu.make_async_copy(place_hbm.at[b], place_buf.at[slot], load_sem.at[0, slot])
        first_copy = pltpu.make_async_copy(
            first_hbm.at[jnp.minimum(b, done_blocks - 1)], cot_buf.at[slot], load_sem.at[1, slot]
        )
        rest_copy = pltpu.make_async_copy(
            rest_hbm.at[jnp.maximum(b - done_blocks, 0)], cot_buf.at[slot], load_sem.at[1, slot]
        )
        if start:
            place_copy.start()

            @pl.when(b < done_blocks)
            def _():
                first_copy.start()

            @pl.when(b >= done_blocks)
            def _():
                rest_copy.start()
        else:
            place_copy.wait()
            first_copy.wait()

    d_acc[...] = jnp.zeros_like(d_acc)
    load_block(0, 0, True)
    wide = 512

    def down_block(b):
        slot = lax.rem(b, 2)
        load_block(b, slot, False)

        @pl.when(b < n - 1)
        def _():
            load_block(b + 1, 1 - slot, True)

        cols = rows_line[b].T
        for e in range(ex):

            def dys(i):
                cut = pl.ds(pl.multiple_of(i * wide, wide), wide)
                dy[:, cut] = (
                    cols[:slots, e : e + 1] * nn(place_buf[slot, e * slots : (e + 1) * slots, :], cot_buf[slot, :, cut])
                ).astype(BF16)

            loop(width // wide, dys)
            for j in range(n_seq):
                d_acc[j, e] = d_acc[j, e] + tn(hid_line[b, j, e], dy[...])

    loop(n, down_block)
    d_out[...] = d_acc[1 - s].astype(BF16)
    d_swap = swap(d_out, d_in, swap_sem, 0)
    d_swap.start()
    lax.fori_loop(pause, last_tick, later, 0)

    spread.finish()
    u_acc[...] = jnp.zeros_like(u_acc)

    def load_du(b, slot):
        return pltpu.make_async_copy(all_ref.at[b], du_buf.at[slot], load_sem.at[2, slot])

    load_du(0, 0).start()

    def up_block(b):
        slot = lax.rem(b, 2)
        load_du(b, slot).wait()

        @pl.when(b < n - 1)
        def _():
            load_du(b + 1, 1 - slot).start()

        for e in range(ex):
            for j in range(n_seq):
                u_acc[j, e] = u_acc[j, e] + tn(arr_line[b, j, e], du_buf[slot, e])

    loop(n, up_block)
    u_out[...] = u_acc[1 - s].astype(BF16)
    u_swap = swap(u_out, u_in, swap_sem, 1)
    u_swap.start()
    for e in range(ex):
        summed_ref[e] = own_unit(c, e)[...].astype(F32)

        @pl.when(c > 0)
        def _():
            sum_up(c, e).wait_recv()
            summed_ref[e] = summed_ref[e] + from_below[c, e].astype(F32)

        @pl.when(c < n - 1)
        def _():
            sum_down(c, e).wait_recv()
            summed_ref[e] = summed_ref[e] + from_above[c, e].astype(F32)

    d_swap.wait()
    down_ref[...] = d_acc[s] + d_in[...].astype(F32)
    u_swap.wait()
    up_ref[...] = u_acc[s] + u_in[...].astype(F32)

    def sent_kv(j, carry):
        pass_down(j).wait_send()
        return carry

    lax.fori_loop(0, c, sent_kv, 0)

    done = jnp.where(c == 0, units - ahead, 0)

    @pl.when(c < n - 1)
    def _():
        def sent(u, carry):
            sum_up(n - 1 - lax.div(u, ex), lax.rem(u, ex)).wait_send()
            return carry

        lax.fori_loop(done, (n - 1 - c) * ex, sent, 0)

    done_down = jnp.where(c == n - 1, units - ahead, 0)

    @pl.when(c > 0)
    def _():
        def sent(u, carry):
            sum_down(lax.div(u, ex), lax.rem(u, ex)).wait_send()
            return carry

        lax.fori_loop(done_down, c * ex, sent, 0)


def attend_back(n, n_seq, qt, db, w_out, o, lse, kv, arr, arr_other, dg, dg_other, du, below, above, rows, hid, arr_line, place, line, first):
    qw, t = qt.shape
    heads = qw // HEAD_SIZE
    kvw = kv.shape[2] // 2
    ex, slots, width = arr.shape
    ff = dg.shape[2]
    half_width = width // 2
    chunk = (ex, half_width // n, ff)
    down_chunk = (ex, hid.shape[4], width)
    any_ = pl.BlockSpec(memory_space=pl.ANY)
    sds = jax.ShapeDtypeStruct
    return pl.pallas_call(
        functools.partial(attend_back_kernel, n, n_seq),
        out_shape=(
            sds((qw, t), BF16),
            sds((t, 2 * kvw), BF16),
            sds(chunk, F32),
            sds(chunk, F32),
            sds(down_chunk, F32),
            sds((n,) + du.shape, BF16),
            sds((n - first.shape[0],) + first.shape[1:], BF16),
        ),
        in_specs=[VMEM] * 16 + [any_] * 3,
        out_specs=(VMEM,) * 5 + (any_,) * 2,
        scratch_shapes=[
            pltpu.VMEM((qw, t), BF16),
            pltpu.VMEM((heads, kvw, t), BF16),
            pltpu.VMEM((heads, kvw, t), BF16),
            pltpu.VMEM((heads, 1, t), F32),
            pltpu.VMEM((qw, t), F32),
            pltpu.VMEM((kvw, t), BF16),
            pltpu.VMEM((2, t, 2 * kvw), F32),
            pltpu.VMEM((n, t, 2 * kvw), BF16),
            pltpu.VMEM((ex, half_width, ff), BF16),
            pltpu.VMEM((n,) + chunk, BF16),
            pltpu.VMEM((n,) + chunk, BF16),
            pltpu.VMEM((2,) + place.shape[1:], BF16),
            pltpu.VMEM((2,) + first.shape[1:], BF16),
            pltpu.VMEM((2,) + du.shape, BF16),
            pltpu.VMEM((slots, width), BF16),
            pltpu.VMEM((n_seq,) + down_chunk, F32),
            pltpu.VMEM((n_seq,) + chunk, F32),
            pltpu.VMEM(down_chunk, BF16),
            pltpu.VMEM(down_chunk, BF16),
            pltpu.VMEM(chunk, BF16),
            pltpu.VMEM(chunk, BF16),
            DMA((3, n * ex)),
            DMA((3, n * ex)),
            DMA((2, n)),
            DMA((3,)),
            DMA((2, 3)),
            DMA((1,)),
            DMA((3, 2)),
            DMA((2, 2)),
        ],
        compiler_params=params(1, 63),
        name="attend_back",
        cost_estimate=cost(80),
    )(qt, db, w_out, o, lse, kv, arr, arr_other, dg, dg_other, du, below, above, rows, hid, arr_line, place, line, first)


def tn(a, b):
    return lax.dot_general(a, b, (((0,), (0,)), ((), ())), preferred_element_type=F32)


def loop(n, f):
    def step(i, carry):
        f(i)
        return carry

    lax.fori_loop(0, n, step, 0)


def moe_kernel(
    n,
    n_seq,
    experts_all,
    h_ref,
    cot_ref,
    place_ref,
    place_t_ref,
    sel_ref,
    router_ref,
    wg_hbm,
    wu_hbm,
    wd_hbm,
    line_hbm,
    gates_ref,
    rows_ref,
    arr_ref,
    hid_ref,
    dg_ref,
    du_ref,
    back_ref,
    comb_ref,
    arr_line,
    cot_first,
    wg,
    wu,
    wd,
    dout,
    dy,
    hid,
    back_rows,
    comb_rows,
    parts,
    cols,
    wsem,
    peers_sem,
    ysem,
    local,
):
    s, c, m = lax.axis_index("seq"), lax.axis_index("ctx"), lax.axis_index("mp")
    ex, width, ff = wg.shape
    slots = place_ref.shape[0] // ex
    first = m * ex
    lanes = gates_ref.shape[1]
    peers = Peers(n, lambda p: parts.at[p], lambda i: arr_line.at[i], peers_sem.at[0], peers_sem.at[1])
    cots = CotExchange(line_hbm, cot_first, 0, cot_first.shape[0], ysem, local)
    sem = pltpu.get_barrier_semaphore()
    peers.signal(sem)
    cots.signal(sem)
    weights = {}
    for e in range(ex):
        for i, (src, dst) in enumerate(((wg_hbm, wg), (wu_hbm, wu), (wd_hbm, wd))):
            weights[i, e] = pltpu.make_async_copy(src.at[e], dst.at[e], wsem.at[i, e])
            weights[i, e].start()

    def rows_of(e):
        return slice(e * slots, (e + 1) * slots)

    def arrive(i):
        cut = pl.ds(pl.multiple_of(i * slots, 16), slots)
        arr_ref[i] = nn(place_ref[cut, :], h_ref[...]).astype(BF16)

    loop(ex, arrive)
    size = width // (n * n_seq)
    for e in range(ex):
        for i in range(n):
            for j in range(n_seq):
                at = (j * n + i) * size
                parts[i, j, e] = arr_ref[e, :, at : at + size]
    pl.semaphore_wait(sem, n - 1 + 2)
    peers.start()
    cots.start()
    own = pltpu.make_async_copy(parts.at[c], arr_line.at[c], local.at[1])
    own.start()

    three = nn(h_ref[...], router_ref[...])
    logits = three + pltpu.roll(three, lanes - experts_all, 1) + pltpu.roll(three, lanes - 2 * experts_all, 1)
    chosen = sel_ref[...] > 0.0
    peak = jnp.max(jnp.where(chosen, logits, -1e30), axis=1, keepdims=True)
    raised = jnp.where(chosen, jnp.exp(jnp.where(chosen, logits - peak, 0.0)), 0.0)
    gates = raised / jnp.sum(raised, axis=1, keepdims=True)
    gates_ref[...] = gates
    g1 = gates.astype(BF16)
    rest = gates - g1.astype(F32)
    g2 = rest.astype(BF16)
    g3 = (rest - g2.astype(F32)).astype(BF16)
    lane = lax.broadcasted_iota(jnp.int32, (slots, lanes), 1)
    cols[...] = jnp.zeros_like(cols)
    gate_col = []
    for e in range(ex):
        pe = place_ref[rows_of(e), :]
        got = nn(pe, g1) + nn(pe, g2) + nn(pe, g3)
        col = jnp.sum(jnp.where(lane == first + e, got, 0.0), axis=1, keepdims=True)
        gate_col.append(col)
        cols[:slots, :] = cols[:slots, :] + jnp.where(lane == e, col, 0.0)

    rows_ref[...] = cols[...].T[:8, :]
    wide = 512
    for e in range(ex):
        col = gate_col[e]

        def douts(i):
            cut = pl.ds(pl.multiple_of(i * wide, wide), wide)
            d = nn(place_ref[rows_of(e), :], cot_ref[:, cut])
            dout[e, :, cut] = d.astype(BF16)
            dy[e, :, cut] = (col * d).astype(BF16)

        loop(width // wide, douts)
        for i in range(3):
            weights[i, e].wait()

        def hidden(i):
            cut = pl.ds(pl.multiple_of(i * 256, 256), 256)
            g = nn(arr_ref[e], wg[e, :, cut])
            u = nn(arr_ref[e], wu[e, :, cut])
            dh = nt(dy[e], wd[e, cut, :])
            sigma = jax.nn.sigmoid(g)
            silu = g * sigma
            hid[:, cut] = (silu * u).astype(BF16)
            dg_ref[e, :, cut] = (dh * u * sigma * (1.0 + g * (1.0 - sigma))).astype(BF16)
            du_ref[e, :, cut] = (dh * silu).astype(BF16)

        loop(ff // 256, hidden)
        size = ff // (n * n_seq)
        for i in range(n):
            for j in range(n_seq):
                at = (j * n + i) * size
                hid_ref[i, j, e] = hid[:, at : at + size]

        def outs(i, grads):
            cut = pl.ds(pl.multiple_of(i * wide, wide), wide)
            y = nn(hid[...], wd[e, :, cut]).astype(BF16).astype(F32)
            comb_rows[rows_of(e), cut] = (col * y).astype(BF16)
            back_rows[rows_of(e), cut] = (nt(dg_ref[e], wg[e, cut, :]) + nt(du_ref[e], wu[e, cut, :])).astype(BF16)
            return grads + jnp.sum(dout[e, :, cut].astype(F32) * y, axis=1, keepdims=True)

        grads = lax.fori_loop(0, width // wide, outs, jnp.zeros((slots, 1), F32))
        high = grads.astype(BF16).astype(F32)
        here = jnp.where(lane == first + e, high, jnp.where(lane == lanes // 2 + first + e, grads - high, 0.0))
        back_rows[rows_of(e), width:] = here.astype(BF16)

    def scatter(i):
        cut = pl.ds(pl.multiple_of(i * 256, 256), 256)
        back_ref[:, cut] = nn(place_t_ref[...], back_rows[:, cut]).astype(BF16)
        comb_ref[:, cut] = nn(place_t_ref[...], comb_rows[:, cut]).astype(BF16)

    loop(width // 256, scatter)
    back_ref[:, width:] = nn(place_t_ref[...], back_rows[:, width:]).astype(BF16)
    own.wait()
    peers.finish()
    cots.finish()


def moe(n, n_seq, experts_all, h, cot, place, place_t, sel, router3, wg, wu, wd, line):
    ex, width, ff = wg.shape
    tok = h.shape[0]
    slots = place.shape[0] // ex
    share = line.shape[1]
    blocks = n // 2
    size = width // (n * n_seq)
    any_ = pl.BlockSpec(memory_space=pl.ANY)
    sds = jax.ShapeDtypeStruct
    return pl.pallas_call(
        functools.partial(moe_kernel, n, n_seq, experts_all),
        out_shape=(
            sds((tok, 128), F32),
            sds((8, 256), F32),
            sds((ex, slots, width), BF16),
            sds((n, n_seq, ex, slots, ff // (n * n_seq)), BF16),
            sds((ex, slots, ff), BF16),
            sds((ex, slots, ff), BF16),
            sds((tok, width + 128), BF16),
            sds((tok, width), BF16),
            sds((n, n_seq, ex, slots, size), BF16),
            sds((blocks, tok, width), BF16),
        ),
        in_specs=[VMEM] * 6 + [any_] * 4,
        out_specs=(VMEM,) * 8 + (VMEM, any_),
        scratch_shapes=[
            pltpu.VMEM(wg.shape, BF16),
            pltpu.VMEM(wu.shape, BF16),
            pltpu.VMEM(wd.shape, BF16),
            pltpu.VMEM((ex, slots, width), BF16),
            pltpu.VMEM((ex, slots, width), BF16),
            pltpu.VMEM((slots, ff), BF16),
            pltpu.VMEM((ex * slots, width + 128), BF16),
            pltpu.VMEM((ex * slots, width), BF16),
            pltpu.VMEM((n, n_seq, ex, slots, size), BF16),
            pltpu.VMEM((256, 128), F32),
            DMA((3, ex)),
            DMA((2, n)),
            DMA((2, 3)),
            DMA((2,)),
        ],
        compiler_params=params(6, 60),
        name="moe",
        cost_estimate=cost(30),
    )(h, cot, place, place_t, sel, router3, wg, wu, wd, line)


class Mp:
    def __init__(self, part, core_in, y_out, y_in, full, sems, chunks):
        self.part, self.core_in, self.y_out, self.y_in, self.full = part, core_in, y_out, y_in, full
        self.sems, self.chunks = sems, chunks
        s, c, m = lax.axis_index("seq"), lax.axis_index("ctx"), lax.axis_index("mp")
        self.m = m
        self.sib = m + 1 - 2 * lax.rem(m, 2)
        self.opp = lax.rem(m + 2, 4)
        self.diag = lax.rem(self.sib + 2, 4)
        self.sib_id, self.opp_id = (s, c, self.sib), (s, c, self.opp)
        share = (part if part is not None else full).shape[1]
        self.rows = share // chunks

    def signal(self, sem):
        for d in (self.sib_id, self.opp_id):
            pl.semaphore_signal(sem, inc=1, device_id=d, device_id_type=MESH)

    def copy(self, src, dst, i, dev):
        return pltpu.make_async_remote_copy(
            src_ref=src,
            dst_ref=dst,
            send_sem=self.sems.at[0, i],
            recv_sem=self.sems.at[1, i],
            device_id=dev,
            device_id_type=MESH,
        )

    def cut(self, i):
        return pl.ds(i * self.rows, self.rows)

    def rs_core(self, i):
        src = self.part.at[self.diag] if i == 0 else self.part.at[self.sib]
        return self.copy(src, self.core_in.at[i], i, self.sib_id)

    def rs_y(self, i):
        return self.copy(self.y_out.at[self.cut(i)], self.y_in.at[self.cut(i)], 2 + i, self.opp_id)

    def rs_begin(self):
        self.rs_core(0).start()
        self.rs_core(1).start()
        self.rs_forward()

    def rs_forward(self):
        self.rs_core(0).wait_recv()
        for i in range(self.chunks):
            cut = self.cut(i)
            self.y_out[cut, :] = (
                self.part[self.opp, cut, :].astype(F32) + self.core_in[0, cut, :].astype(F32)
            ).astype(BF16)
            self.rs_y(i).start()
        self.rs_core(1).wait_recv()

    def rs_chunk(self, i):
        cut = self.cut(i)
        self.rs_y(i).wait_recv()
        return (
            self.part[self.m, cut, :].astype(F32) + self.core_in[1, cut, :].astype(F32)
        ) + self.y_in[cut, :].astype(F32)

    def rs_end(self):
        self.rs_core(0).wait_send()
        self.rs_core(1).wait_send()
        for i in range(self.chunks):
            self.rs_y(i).wait_send()

    def ag(self, kind, i, whose):
        block = self.full.at[whose, self.cut(i)]
        base = 2 + self.chunks
        dev = self.opp_id if kind == 0 else self.sib_id
        return self.copy(block, block, base + kind * self.chunks + i, dev)

    def ag_send(self, i):
        self.ag(0, i, self.m).start()
        self.ag(1, i, self.m).start()

    def ag_end(self):
        for i in range(self.chunks):
            self.ag(0, i, self.opp).wait_recv()
            self.ag(2, i, self.opp).start()
        for i in range(self.chunks):
            self.ag(1, i, self.sib).wait_recv()
            self.ag(2, i, self.diag).wait_recv()
            self.ag(0, i, self.m).wait_send()
            self.ag(1, i, self.m).wait_send()
            self.ag(2, i, self.opp).wait_send()


def mp_scratch(share, width, chunks):
    return [
        pltpu.VMEM((2, share, width), BF16),
        pltpu.VMEM((share, width), BF16),
        pltpu.VMEM((share, width), BF16),
        DMA((2, 2 + 4 * chunks)),
    ]


def rms_parts(rows):
    inverse = lax.rsqrt(jnp.mean(rows * rows, axis=-1, keepdims=True) + EPS)
    return rows * inverse, inverse


def rms_grad(grad_normed, normed, inverse):
    return inverse * (grad_normed - normed * jnp.mean(grad_normed * normed, axis=-1, keepdims=True))


def mid_forward_kernel(
    chunks, n, part, x_ref, gain, own, below, above, resid_ref, h_ref, line_ref, core_in, y_out, y_in, sems, send, recv, local
):
    mp = Mp(part, core_in, y_out, y_in, h_ref, sems, chunks)
    spread = Spread(n, own, below, above, line_ref, send, recv, local)
    sem = pltpu.get_barrier_semaphore()
    mp.signal(sem)
    signal_line(n, sem)
    pl.semaphore_wait(sem, 2 + line_degree(n))
    mp.rs_begin()
    spread.start()
    for i in range(chunks):
        cut = mp.cut(i)
        resid = x_ref[cut, :].astype(F32) + mp.rs_chunk(i)
        resid_ref[cut, :] = resid
        normed, _ = rms_parts(resid)
        h_ref[mp.m, cut, :] = (normed * gain[...]).astype(BF16)
        mp.ag_send(i)
    if n > 2:
        spread.tick(1)
    mp.ag_end()
    mp.rs_end()
    spread.ticks(2)
    spread.finish()


def mid_forward(n, part, x_mine, gain, own, below, above, chunks=2):
    _, share, width = part.shape
    return pl.pallas_call(
        functools.partial(mid_forward_kernel, chunks, n),
        out_shape=(
            jax.ShapeDtypeStruct((share, width), F32),
            jax.ShapeDtypeStruct(part.shape, BF16),
            jax.ShapeDtypeStruct((n,) + own.shape, BF16),
        ),
        in_specs=[VMEM] * 6,
        out_specs=(VMEM,) * 3,
        scratch_shapes=mp_scratch(share, width, chunks) + [DMA((n,)), DMA((n,)), DMA((3,))],
        compiler_params=params(2, 30),
        name="mid_forward",
        cost_estimate=cost(30),
    )(part, x_mine, gain, own, below, above)


def mid_back_kernel(
    chunks,
    n,
    part,
    resid_ref,
    gain,
    cot,
    gate_ref,
    router_ref,
    rows_ref,
    hid_ref,
    du_ref,
    arr_ref,
    dg_ref,
    dresid_ref,
    db_ref,
    dlog_ref,
    gnorm_ref,
    rows_line,
    hid_line,
    below_ref,
    above_ref,
    arr_other,
    dg_other,
    core_in,
    y_out,
    y_in,
    sems,
    side,
    peers_sem,
    local,
    swap_sem,
):
    c = lax.axis_index("ctx")
    mp = Mp(part, core_in, y_out, y_in, db_ref, sems, chunks)
    rows_peers = Peers(n, lambda p: rows_ref, lambda i: rows_line.at[i], peers_sem.at[0], peers_sem.at[1])
    hid_peers = Peers(n, lambda p: hid_ref.at[p], lambda i: hid_line.at[i], peers_sem.at[2], peers_sem.at[3])
    beside = Neighbours(n, du_ref, below_ref, above_ref, side.at[0], side.at[1])
    width = gain.shape[1]
    ex = gate_ref.shape[1]
    sem = pltpu.get_barrier_semaphore()
    mp.signal(sem)
    rows_peers.signal(sem)
    partner = swap_partner()
    pl.semaphore_signal(sem, inc=1, device_id=partner, device_id_type=MESH)
    pl.semaphore_wait(sem, 2 + n - 1 + 1)
    mp.rs_begin()
    half_width = width // 2
    theirs = pl.ds(pl.multiple_of((1 - lax.axis_index("seq")) * half_width, 128), half_width)
    swaps = [
        swap(arr_ref.at[:, :, theirs], arr_other, swap_sem, 0),
        swap(dg_ref, dg_other, swap_sem, 1),
    ]
    for sw in swaps:
        sw.start()
    beside.start_up()
    beside.start_down()
    rows_peers.start()
    hid_peers.start()
    own_rows = pltpu.make_async_copy(rows_ref, rows_line.at[c], local.at[0])
    own_hid = pltpu.make_async_copy(hid_ref.at[c], hid_line.at[c], local.at[1])
    own_rows.start()
    own_hid.start()
    gnorm_ref[...] = jnp.zeros_like(gnorm_ref)
    for i in range(chunks):
        cut = mp.cut(i)
        both = mp.rs_chunk(i)
        dgate = both[:, width : width + ex] + both[:, width + ex :]
        gate = gate_ref[cut, :]
        dlog = gate * (dgate - jnp.sum(gate * dgate, axis=-1, keepdims=True))
        dlog_ref[cut, :] = dlog
        dh = both[:, :width] + jnp.dot(
            dlog, router_ref[...], precision=lax.Precision.HIGHEST, preferred_element_type=F32
        )
        normed, inverse = rms_parts(resid_ref[cut, :])
        gnorm_ref[0:1, :] = gnorm_ref[0:1, :] + jnp.sum(dh * normed, axis=0, keepdims=True)
        dresid = cot[cut, :].astype(F32) + rms_grad(dh * gain[...], normed, inverse)
        dresid_ref[cut, :] = dresid
        db_ref[mp.m, cut, :] = dresid.astype(BF16)
        mp.ag_send(i)
    mp.ag_end()
    mp.rs_end()
    own_rows.wait()
    own_hid.wait()
    rows_peers.finish()
    hid_peers.finish()
    beside.finish()
    for sw in swaps:
        sw.wait()


def swap_partner():
    return (1 - lax.axis_index("seq"), lax.axis_index("ctx"), lax.axis_index("mp"))


def swap(src, dst, sems, i):
    return pltpu.make_async_remote_copy(
        src_ref=src,
        dst_ref=dst,
        send_sem=sems.at[0, i],
        recv_sem=sems.at[1, i],
        device_id=swap_partner(),
        device_id_type=MESH,
    )


def mid_back(n, part, resid, gain, cot, gate, router_t, rows, hid, du, arr, dg, chunks=2):
    k, share, wide = part.shape
    width = gain.shape[1]
    return pl.pallas_call(
        functools.partial(mid_back_kernel, chunks, n),
        out_shape=(
            jax.ShapeDtypeStruct((share, width), F32),
            jax.ShapeDtypeStruct((k, share, width), BF16),
            jax.ShapeDtypeStruct(gate.shape, F32),
            jax.ShapeDtypeStruct((8, width), F32),
            jax.ShapeDtypeStruct((n,) + rows.shape, F32),
            jax.ShapeDtypeStruct(hid.shape, BF16),
            jax.ShapeDtypeStruct(du.shape, BF16),
            jax.ShapeDtypeStruct(du.shape, BF16),
            jax.ShapeDtypeStruct(arr.shape[:2] + (arr.shape[2] // 2,), BF16),
            jax.ShapeDtypeStruct(dg.shape, BF16),
        ),
        in_specs=[VMEM] * 11,
        out_specs=(VMEM,) * 10,
        scratch_shapes=mp_scratch(share, wide, chunks) + [DMA((2, 2)), DMA((4, n)), DMA((2,)), DMA((2, 2))],
        compiler_params=params(3, 40),
        name="mid_back",
        cost_estimate=cost(32),
    )(part, resid, gain, cot, gate, router_t, rows, hid, du, arr, dg)


class SmallSum:
    def __init__(self, sizes, x_ref, out_ref, bufs, sems):
        self.sizes, self.x, self.out, self.bufs, self.sems = sizes, x_ref, out_ref, bufs, sems
        self.me = [lax.axis_index(a) for a in ("seq", "ctx", "mp")]

    def peer(self, axis, d):
        ids = list(self.me)
        ids[axis] = lax.rem(self.me[axis] + d, self.sizes[axis])
        return tuple(ids)

    def signal(self, sem):
        for axis in range(3):
            for d in range(1, self.sizes[axis]):
                pl.semaphore_signal(sem, inc=1, device_id=self.peer(axis, d), device_id_type=MESH)
        return sum(self.sizes) - 3

    def move(self, axis, d):
        base = sum(self.sizes[:axis])
        buf = self.bufs[axis]
        return pltpu.make_async_remote_copy(
            src_ref=buf.at[0],
            dst_ref=buf.at[d],
            send_sem=self.sems.at[0, base + d],
            recv_sem=self.sems.at[1, base + d],
            device_id=self.peer(axis, d),
            device_id_type=MESH,
        )

    def begin(self, axis, value):
        self.bufs[axis][0] = value
        for d in range(1, self.sizes[axis]):
            self.move(axis, d).start()

    def end(self, axis):
        n = self.sizes[axis]
        for d in range(1, n):
            self.move(axis, d).wait()
        total = jnp.zeros(self.out.shape, F32)
        for i in range(n):
            total = total + self.bufs[axis][lax.rem(self.me[axis] - i + n, n)]
        return total


def last_kernel(
    chunks,
    sizes,
    part,
    x_ref,
    gain,
    dresid_ref,
    small_ref,
    wout_ref,
    qkv_ref,
    out_ref,
    total_ref,
    gout_ref,
    gqkv_ref,
    core_in,
    y_out,
    y_in,
    sems,
    swapped,
    summed,
    wout_in,
    qkv_in,
    swap_sem,
    peers_sem,
    *rest,
):
    n = sizes[1]
    s, c = lax.axis_index("seq"), lax.axis_index("ctx")
    mp = Mp(part, core_in, y_out, y_in, None, sems, chunks)
    small = SmallSum(sizes, small_ref, total_ref, rest[:3], rest[3])
    half_rows = swapped.shape[0]
    rows = half_rows // n
    wout_peers = Peers(
        n, lambda p: wout_ref.at[cut_of(p, rows)], lambda i: wout_in.at[i], peers_sem.at[0], peers_sem.at[1]
    )
    qkv_peers = Peers(
        n, lambda p: summed.at[cut_of(p, rows)], lambda i: qkv_in.at[i], peers_sem.at[2], peers_sem.at[3]
    )
    sem = pltpu.get_barrier_semaphore()
    pl.semaphore_wait(sem, small.signal(sem))
    qkv_swap = swap(qkv_ref.at[cut_of(1 - s, half_rows)], swapped, swap_sem, 0)
    qkv_swap.start()
    mp.rs_core(0).start()
    mp.rs_core(1).start()
    small.begin(2, small_ref[...])
    wout_peers.start()
    mp.rs_forward()
    small.begin(0, small.end(2))
    for i in range(chunks):
        cut = mp.cut(i)
        if i == 1:
            small.begin(1, small.end(0))
        dh = mp.rs_chunk(i)
        normed, inverse = rms_parts(x_ref[cut, :].astype(F32))
        out_ref[cut, :] = dresid_ref[cut, :] + rms_grad(dh * gain[...], normed, inverse)
    qkv_swap.wait()

    def add(i):
        here = cut_of(i, rows)
        summed[here, :] = (
            qkv_ref[cut_of(s * n + i, rows), :].astype(F32) + swapped[here, :].astype(F32)
        ).astype(BF16)

    loop(n, add)
    qkv_peers.start()
    total_ref[...] = small.end(1)
    wout_peers.finish()
    wout_in[c] = wout_ref[cut_of(c, rows), :]
    total = jnp.zeros(gout_ref.shape, F32)
    for i in range(n):
        total = total + wout_in[i].astype(F32)
    gout_ref[...] = total
    mp.rs_end()
    qkv_peers.finish()
    qkv_in[c] = summed[cut_of(c, rows), :]
    total = jnp.zeros(gqkv_ref.shape, F32)
    for i in range(n):
        total = total + qkv_in[i].astype(F32)
    gqkv_ref[...] = total


def cut_of(i, rows):
    return pl.ds(pl.multiple_of(i * rows, 16), rows)


def last(sizes, part, x_mine, gain, dresid, small, wout, qkv, chunks=2):
    _, share, width = part.shape
    n = sizes[1]
    half_rows, fo = wout.shape
    fq = qkv.shape[1]
    rows = half_rows // n
    sds = jax.ShapeDtypeStruct
    return pl.pallas_call(
        functools.partial(last_kernel, chunks, sizes),
        out_shape=(sds((share, width), F32), sds(small.shape, F32), sds((rows, fo), F32), sds((rows, fq), F32)),
        in_specs=[VMEM] * 7,
        out_specs=(VMEM,) * 4,
        scratch_shapes=mp_scratch(share, width, chunks)
        + [
            pltpu.VMEM((half_rows, fq), BF16),
            pltpu.VMEM((half_rows, fq), BF16),
            pltpu.VMEM((n, rows, fo), BF16),
            pltpu.VMEM((n, rows, fq), BF16),
            DMA((2, 1)),
            DMA((4, n)),
        ]
        + [pltpu.VMEM((k,) + small.shape, F32) for k in sizes]
        + [DMA((2, sum(sizes)))],
        compiler_params=params(4, 24),
        name="last",
        cost_estimate=cost(45),
    )(part, x_mine, gain, dresid, small, wout, qkv)


def half(x, s, dim):
    size = x.shape[dim] // 2
    return lax.dynamic_slice_in_dim(x, s * size, size, dim)


SWAP = [(0, 1), (1, 0)]


def body(
    tokens,
    norm1_gain,
    w_query,
    key_weight_matrix,
    value_weight_matrix,
    w_out,
    norm2_gain,
    router,
    w_gate,
    w_up,
    w_down,
    routes,
    cotangent,
):
    n_seq, n_ctx, n_mp = (lax.axis_size(a) for a in ("seq", "ctx", "mp"))
    s, c, m = (lax.axis_index(a) for a in ("seq", "ctx", "mp"))
    tok, width = tokens.shape
    share = tok // n_mp
    experts_all = router.shape[1]
    exp_local = w_gate.shape[0]
    top = routes.shape[1]
    cap = share * top * 5 // (4 * experts_all)
    slots = -(-n_mp * cap // 16) * 16
    gain1 = norm1_gain.reshape(1, width)
    gain2 = norm2_gain.reshape(1, width)

    cot_all = lax.all_gather(cotangent, "mp", axis=0, tiled=True)
    x_mine = lax.dynamic_slice_in_dim(tokens, m * share, share, 0)

    normed_one, _ = rms_parts(tokens.astype(F32))
    h_one = (normed_one * gain1).astype(BF16)
    qt = (jnp.einsum("df,td->ft", w_query, h_one, preferred_element_type=F32).astype(BF16)) * BF16(0.125)
    k = nn(h_one, key_weight_matrix).astype(BF16)
    v = nn(h_one, value_weight_matrix).astype(BF16)
    o, heads_t, lse, kv, cot_below, cot_above, routes_line = attend(n_ctx, qt, k, v, cotangent, routes.T)

    experts = jnp.arange(experts_all, dtype=jnp.int32)
    first = m * exp_local
    local = first + jnp.arange(exp_local, dtype=jnp.int32)
    chosen_line = (routes_line[:, None, :, :] == local[None, :, None, None]).any(axis=2)
    low = (jnp.arange(tok)[:, None] <= jnp.arange(tok)[None, :]).astype(BF16)
    rank_line = (
        jnp.einsum("cet,tu->ceu", chosen_line.astype(BF16), low, preferred_element_type=F32) - 1.0
    ).astype(jnp.int32)
    place_line = (
        (rank_line[:, :, None, :] == jnp.arange(slots, dtype=jnp.int32)[None, None, :, None])
        & chosen_line[:, :, None, :]
    ).astype(BF16)
    chosen = (routes[:, :, None] == experts[None, None, :]).any(axis=1)
    place_line = place_line.reshape(n_ctx, exp_local * slots, tok)
    place = lax.dynamic_index_in_dim(place_line, c, 0, keepdims=False)
    place_t = place.T
    lanes = 128
    chosen_pad = jnp.pad(chosen.astype(F32), ((0, 0), (0, lanes - experts_all)))
    r_hi = router.astype(BF16)
    r_rest = router - r_hi.astype(F32)
    r_mid = r_rest.astype(BF16)
    r_low = (r_rest - r_mid.astype(F32)).astype(BF16)
    router3 = jnp.pad(jnp.concatenate([r_hi, r_mid, r_low], axis=1), ((0, 0), (0, lanes - 3 * experts_all)))
    router_t = jnp.pad(router.T, ((0, lanes // 2 - experts_all), (0, 0)))

    part = jnp.einsum("ft,fd->td", heads_t, w_out, preferred_element_type=F32).astype(BF16)
    resid, h_two, cot_line = mid_forward(
        n_ctx, part.reshape(n_mp, share, width), x_mine, gain2, cotangent, cot_below, cot_above
    )
    h_two = h_two.reshape(tok, width)

    gates, gate_rows, arrived, hidden, dg, du, back, comb, arrived_line, cot_first = moe(
        n_ctx, n_seq, experts_all, h_two, cot_all, place, place_t, chosen_pad, router3, w_gate, w_up, w_down, cot_line
    )
    output = resid + lax.psum_scatter(comb, "mp", scatter_dimension=0, tiled=True).astype(F32)
    gates_mine = lax.dynamic_slice_in_dim(gates, m * share, share, 0)[:, : lanes // 2]
    dresid, db, dlog, gnorm2, gate_rows_line, hidden_line, du_below, du_above, arrived_other, dg_other = mid_back(
        n_ctx,
        back.reshape(n_mp, share, -1),
        resid,
        gain2,
        cotangent,
        gates_mine,
        router_t,
        gate_rows,
        hidden,
        du,
        arrived,
        dg,
    )
    db = db.reshape(tok, width)
    h_two_mine = lax.dynamic_slice_in_dim(h_two, m * share, share, 0).astype(F32)
    g_router = jnp.einsum("te,td->ed", dlog[:, :experts_all], h_two_mine, precision=lax.Precision.HIGHEST)
    g_out = jnp.einsum("td,ft->df", db, heads_t, preferred_element_type=F32).astype(BF16)
    g_out = (
        half(g_out, s, 0).astype(F32) + lax.ppermute(half(g_out, 1 - s, 0), "seq", SWAP).astype(F32)
    ).astype(BF16)

    dq, dkv, g_gate, g_up, g_down, _, _ = attend_back(
        n_ctx,
        n_seq,
        qt,
        db,
        w_out,
        o,
        lse,
        kv,
        arrived,
        arrived_other,
        dg,
        dg_other,
        du,
        du_below,
        du_above,
        gate_rows_line,
        hidden_line,
        arrived_line,
        place_line,
        cot_line,
        cot_first,
    )
    kvw = dkv.shape[1] // 2
    dk, dv = dkv[:, :kvw], dkv[:, kvw:]
    g_q = jnp.einsum("td,ft->df", h_one, dq, preferred_element_type=F32)
    g_kv = jnp.einsum("td,tf->df", h_one, dkv, preferred_element_type=F32)
    g_qkv = jnp.concatenate([g_q, g_kv], axis=1).astype(BF16)
    dh = jnp.einsum("ft,df->td", dq, w_query, preferred_element_type=F32)
    dh = dh + jnp.einsum("tf,df->td", dk, key_weight_matrix, preferred_element_type=F32)
    dh = dh + jnp.einsum("tf,df->td", dv, value_weight_matrix, preferred_element_type=F32)
    gnorm1 = jnp.sum(dh * normed_one, axis=0, keepdims=True)
    rows = 2 + experts_all
    small = jnp.concatenate([gnorm1, gnorm2[:1], g_router, jnp.zeros((-rows % 8, width), F32)], axis=0)
    grad_tokens, small, g_out, g_qkv = last(
        (n_seq, n_ctx, n_mp), dh.astype(BF16).reshape(n_mp, share, width), x_mine, gain1, dresid, small, g_out, g_qkv
    )
    qw = w_query.shape[1]
    return (
        output,
        grad_tokens,
        small[0],
        g_qkv[:, :qw],
        g_qkv[:, qw : qw + kvw],
        g_qkv[:, qw + kvw :],
        g_out.T,
        small[1],
        small[2:rows].T,
        g_gate,
        g_up,
        g_down,
    )


def solution(mesh):
    placed = (
        P(("seq", "ctx"), None),
        P(),
        P(None, "mp"),
        P(None, "mp"),
        P(None, "mp"),
        P("mp", None),
        P(),
        P(),
        P("mp", None, None),
        P("mp", None, None),
        P("mp", None, None),
        P(("seq", "ctx"), None),
        P(("seq", "ctx", "mp"), None),
    )
    return jax.shard_map(
        body,
        mesh=mesh,
        in_specs=placed,
        out_specs=(
            P(("seq", "ctx", "mp"), None),
            P(("seq", "ctx", "mp"), None),
            P(),
            P(("seq", "ctx"), "mp"),
            P(("seq", "ctx"), "mp"),
            P(("seq", "ctx"), "mp"),
            P("mp", ("seq", "ctx")),
            P(),
            P(),
            P("mp", ("seq", "ctx"), None),
            P("mp", ("seq", "ctx"), None),
            P("mp", ("seq", "ctx"), None),
        ),
        check_vma=False,
    )
```

```python
import functools

import jax
import jax.numpy as jnp
from jax import lax
from jax.experimental import pallas as pl
from jax.experimental.pallas import tpu as pltpu
from jax.sharding import PartitionSpec as P

HEAD_SIZE = 64
EPS = 1e-06
MESH = pl.DeviceIdType.MESH
F32 = jnp.float32
BF16 = jnp.bfloat16
VMEM = pl.BlockSpec(memory_space=pltpu.VMEM)
HBM = pl.BlockSpec(memory_space=pl.ANY)
DMA = pltpu.SemaphoreType.DMA
MIB = 2**20


def cost(us):
    return pl.CostEstimate(flops=0, bytes_accessed=int(us * 3.6e6), transcendentals=0)


def params(collective_id, mib=56):
    return pltpu.CompilerParams(
        collective_id=collective_id, has_side_effects=True, vmem_limit_bytes=mib * MIB
    )


def nt(a, b):
    return lax.dot_general(a, b, (((1,), (1,)), ((), ())), preferred_element_type=F32)


def nn(a, b):
    return jnp.dot(a, b, preferred_element_type=F32)


class Staged:
    def __init__(self, pairs, sems):
        self.copies = [pltpu.make_async_copy(src, dst, sems.at[i]) for i, (src, dst) in enumerate(pairs)]

    def start(self):
        for copy in self.copies:
            copy.start()

    def wait(self, *which):
        for i in which:
            self.copies[i].wait()


class Spread:
    def __init__(self, n, own, below, above, all_ref, send, recv, local, short=False):
        self.n, self.own, self.below, self.above, self.all = n, own, below, above, all_ref
        self.send, self.recv, self.local = send, recv, local
        self.top = n - 2 if short else n - 1
        s, self.c, m = lax.axis_index("seq"), lax.axis_index("ctx"), lax.axis_index("mp")
        self.lower, self.upper = lax.rem(self.c + n - 1, n), lax.rem(self.c + 1, n)
        self.up, self.down = (s, self.upper, m), (s, self.lower, m)
        self.inner = jnp.logical_and(self.c > 0, self.c < n - 1)

    def move(self, b, src, device):
        return pltpu.make_async_remote_copy(
            src_ref=src,
            dst_ref=self.all.at[b],
            send_sem=self.send.at[b],
            recv_sem=self.recv.at[b],
            device_id=device,
            device_id_type=MESH,
        )

    def keep(self, i, src, b):
        return pltpu.make_async_copy(src, self.all.at[b], self.local.at[i])

    def goes_up(self, b):
        return jnp.logical_and(self.c < self.n - 1, self.c - b < self.top)

    def start(self):
        if self.below is None:

            @pl.when(self.c < self.n - 1)
            def _():
                self.move(self.c, self.own, self.up).start()
        else:

            @pl.when(jnp.logical_and(self.inner, self.goes_up(self.lower)))
            def _():
                self.move(self.lower, self.below, self.up).start()

            @pl.when(self.c > 0)
            def _():
                self.keep(1, self.below, self.lower).start()

        @pl.when(self.inner)
        def _():
            self.move(self.upper, self.above, self.down).start()

        self.keep(0, self.own, self.c).start()

        @pl.when(self.c < self.n - 1)
        def _():
            self.keep(2, self.above, self.upper).start()

    def tick(self, i):
        c, n = self.c, self.n
        off = i if self.below is None else i + 1

        @pl.when(jnp.logical_and(c - off >= 0, off <= self.top))
        def _():
            b = jnp.maximum(c - off, 0)
            self.move(b, self.all.at[b], self.up).wait_recv()

            @pl.when(self.goes_up(b))
            def _():
                self.move(b, self.all.at[b], self.up).start()

        @pl.when(c + 1 + i <= n - 1)
        def _():
            b = jnp.minimum(c + 1 + i, n - 1)
            self.move(b, self.all.at[b], self.down).wait_recv()

            @pl.when(c > 0)
            def _():
                self.move(b, self.all.at[b], self.down).start()

    def ticks(self, first):
        def later(i, carry):
            self.tick(i)
            return carry

        lax.fori_loop(first, self.n if self.below is None else self.n - 1, later, 0)

    def finish(self):
        self.keep(0, self.own, self.c).wait()

        if self.below is not None:

            @pl.when(self.c > 0)
            def _():
                self.keep(1, self.below, self.lower).wait()

        @pl.when(self.c < self.n - 1)
        def _():
            self.keep(2, self.above, self.upper).wait()

        def sent(b, carry):
            if self.below is None:
                sent_up = jnp.logical_and(b <= self.c, self.goes_up(b))
            else:
                sent_up = jnp.logical_and(b < self.c, self.goes_up(b))

            @pl.when(jnp.logical_or(sent_up, jnp.logical_and(b > self.c, self.c > 0)))
            def _():
                self.move(b, self.all.at[b], self.up).wait_send()

            return carry

        lax.fori_loop(0, self.n, sent, 0)


class Neighbours:
    def __init__(self, n, own, below, above, send, recv):
        self.n, self.own, self.below, self.above, self.send, self.recv = n, own, below, above, send, recv
        s, self.c, m = lax.axis_index("seq"), lax.axis_index("ctx"), lax.axis_index("mp")
        self.up, self.down = (s, lax.rem(self.c + 1, n), m), (s, lax.rem(self.c + n - 1, n), m)

    def move(self, way):
        return pltpu.make_async_remote_copy(
            src_ref=self.own,
            dst_ref=self.below if way == 0 else self.above,
            send_sem=self.send.at[way],
            recv_sem=self.recv.at[way],
            device_id=self.up if way == 0 else self.down,
            device_id_type=MESH,
        )

    def start_up(self):
        @pl.when(self.c < self.n - 1)
        def _():
            self.move(0).start()

    def start_down(self):
        @pl.when(self.c > 0)
        def _():
            self.move(1).start()

    def finish(self, up=True):
        @pl.when(self.c > 0)
        def _():
            if up:
                self.move(0).wait_recv()
            self.move(1).wait_send()

        @pl.when(self.c < self.n - 1)
        def _():
            self.move(1).wait_recv()
            if up:
                self.move(0).wait_send()


class LineSum:
    ahead = 2

    def __init__(self, n, parts, from_below, from_above, send, recv):
        self.n, self.parts, self.from_below, self.from_above, self.send, self.recv = n, parts, from_below, from_above, send, recv
        s, self.c, m = lax.axis_index("seq"), lax.axis_index("ctx"), lax.axis_index("mp")
        self.up, self.down = (s, lax.rem(self.c + 1, n), m), (s, lax.rem(self.c + n - 1, n), m)
        self.rows = from_below.shape[1]

    def own(self, k):
        return self.parts.at[pl.ds(pl.multiple_of(k * self.rows, 16), self.rows), :]

    def move(self, way, k, first=False):
        there = (self.from_below if way == 0 else self.from_above).at[k]
        return pltpu.make_async_remote_copy(
            src_ref=self.own(k) if first else there,
            dst_ref=there,
            send_sem=self.send.at[way, k],
            recv_sem=self.recv.at[way, k],
            device_id=self.up if way == 0 else self.down,
            device_id_type=MESH,
        )

    def chunk(self, way, u):
        return self.n - 1 - u if way == 0 else u

    def first(self, u):
        units = self.n - 1
        for way, end in ((0, 0), (1, self.n - 1)):

            @pl.when(jnp.logical_and(self.c == end, u < units))
            def _():
                @pl.when(u >= self.ahead)
                def _():
                    self.move(way, self.chunk(way, jnp.maximum(u - self.ahead, 0)), True).wait_send()

                self.move(way, self.chunk(way, jnp.minimum(u, units - 1)), True).start()

    def tick(self, i):
        self.first(i + 1)
        for way, far in ((0, self.c), (1, self.n - 1 - self.c)):
            u = i - far
            buf = self.from_below if way == 0 else self.from_above

            @pl.when(jnp.logical_and(far > 0, jnp.logical_and(u >= 0, u < self.n - 1 - far)))
            def _():
                k = self.chunk(way, jnp.clip(u, 0, self.n - 2))
                self.move(way, k).wait_recv()
                buf[k] = (self.own(k)[...].astype(F32) + buf[k].astype(F32)).astype(BF16)
                self.move(way, k).start()

    def finish(self, out):
        c = self.c
        out[...] = self.own(c)[...].astype(F32)
        for way, far in ((0, c), (1, self.n - 1 - c)):
            buf = self.from_below if way == 0 else self.from_above

            @pl.when(far > 0)
            def _():
                self.move(way, c).wait_recv()
                out[...] = out[...] + buf[c].astype(F32)

            done = jnp.where(far == 0, max(self.n - 1 - self.ahead, 0), 0)

            def sent(u, carry):
                self.move(way, self.chunk(way, u)).wait_send()
                return carry

            lax.fori_loop(done, self.n - 1 - far, sent, 0)


class Peers:
    def __init__(self, n, src_of, dst_of, send, recv):
        self.n, self.src_of, self.dst_of, self.send, self.recv = n, src_of, dst_of, send, recv
        self.s, self.c, self.m = lax.axis_index("seq"), lax.axis_index("ctx"), lax.axis_index("mp")

    def move(self, d):
        peer = lax.rem(self.c + d, self.n)
        return pltpu.make_async_remote_copy(
            src_ref=self.src_of(peer),
            dst_ref=self.dst_of(self.c),
            send_sem=self.send.at[d],
            recv_sem=self.recv.at[d],
            device_id=(self.s, peer, self.m),
            device_id_type=MESH,
        )

    def signal(self, sem):
        for d in range(1, self.n):
            pl.semaphore_signal(
                sem, inc=1, device_id=(self.s, lax.rem(self.c + d, self.n), self.m), device_id_type=MESH
            )

    def start(self):
        for d in range(1, self.n):
            self.move(d).start()

    def finish(self):
        for d in range(1, self.n):
            self.move(d).wait()


class CotExchange:
    def __init__(self, n, line_ref, full, first, sems):
        self.n, self.line, self.full, self.first, self.sems = n, line_ref, full, first, sems
        self.count = full.shape[0]
        s, self.c, m = lax.axis_index("seq"), lax.axis_index("ctx"), lax.axis_index("mp")
        self.m = m
        self.share = line_ref.shape[1]
        self.sib = m + 1 - 2 * lax.rem(m, 2)
        self.opp = lax.rem(m + 2, 4)
        self.sib_id, self.opp_id = (s, self.c, self.sib), (s, self.c, self.opp)

    def signal(self, sem):
        for d in (self.sib_id, self.opp_id):
            pl.semaphore_signal(sem, inc=1, device_id=d, device_id_type=MESH)

    def place(self, i, who):
        return self.full.at[i, pl.ds(pl.multiple_of(who * self.share, 16), self.share), :]

    def mine(self, i):
        return self.line.at[lax.rem(self.c - self.first - i + 2 * self.n, self.n)]

    def move(self, kind, i):
        whose = self.opp if kind == 2 else self.m
        return pltpu.make_async_remote_copy(
            src_ref=self.place(i, self.opp) if kind == 2 else self.mine(i),
            dst_ref=self.place(i, whose),
            send_sem=self.sems.at[0, kind, i],
            recv_sem=self.sems.at[1, kind, i],
            device_id=self.opp_id if kind == 0 else self.sib_id,
            device_id_type=MESH,
        )

    def start(self):
        for i in range(self.count):
            self.move(0, i).start()
            self.move(1, i).start()

    def finish(self):
        for i in range(self.count):
            self.move(0, i).wait_recv()
            self.move(2, i).start()
        for i in range(self.count):
            self.move(1, i).wait_recv()
            self.move(2, i).wait_recv()
            for kind in range(3):
                self.move(kind, i).wait_send()


def signal_line(n, sem):
    s, c, m = lax.axis_index("seq"), lax.axis_index("ctx"), lax.axis_index("mp")

    @pl.when(c > 0)
    def _():
        pl.semaphore_signal(sem, inc=1, device_id=(s, lax.rem(c + n - 1, n), m), device_id_type=MESH)

    @pl.when(c < n - 1)
    def _():
        pl.semaphore_signal(sem, inc=1, device_id=(s, lax.rem(c + 1, n), m), device_id_type=MESH)


def line_degree(n):
    c = lax.axis_index("ctx")
    return jnp.where(c > 0, 1, 0) + jnp.where(c < n - 1, 1, 0)


def pad_heads(src, dst, heads, group):
    dst[...] = jnp.zeros_like(dst)
    for h in range(heads):
        g = h // group
        rows = slice(g * HEAD_SIZE, (g + 1) * HEAD_SIZE)
        dst[h, rows, :] = src[h * HEAD_SIZE : (h + 1) * HEAD_SIZE, :]


def causal(t):
    keys = lax.broadcasted_iota(jnp.int32, (t, t), 0)
    queries = lax.broadcasted_iota(jnp.int32, (t, t), 1)
    return keys <= queries


def attend_kernel(
    n,
    q_ref,
    k_ref,
    v_ref,
    cot_ref,
    routes_ref,
    o_ref,
    heads_ref,
    lse_ref,
    kv_ref,
    above_ref,
    line_ref,
    qpad,
    vt,
    top,
    tot,
    send,
    recv,
    side,
    peers_sem,
):
    s, c, m = lax.axis_index("seq"), lax.axis_index("ctx"), lax.axis_index("mp")
    t, kvw = k_ref.shape
    heads = q_ref.shape[0] // HEAD_SIZE
    group = heads // (kvw // HEAD_SIZE)
    up, down = (s, lax.rem(c + 1, n), m), (s, lax.rem(c + n - 1, n), m)
    kv_ref[0, :, :kvw] = k_ref[...]
    kv_ref[0, :, kvw:] = v_ref[...]
    line_ref[c] = routes_ref[...]
    peers = Peers(n, lambda p: routes_ref, lambda i: line_ref.at[i], peers_sem.at[0], peers_sem.at[1])
    beside = Neighbours(n, cot_ref, None, above_ref, side.at[0], side.at[1])
    sem = pltpu.get_barrier_semaphore()
    peers.signal(sem)
    pl.semaphore_wait(sem, n - 1)

    def pass_up(slot):
        return pltpu.make_async_remote_copy(
            src_ref=kv_ref.at[slot],
            dst_ref=kv_ref.at[slot + 1],
            send_sem=send.at[slot],
            recv_sem=recv.at[slot + 1],
            device_id=up,
            device_id_type=MESH,
        )

    def got(slot):
        return pltpu.make_async_remote_copy(
            src_ref=kv_ref.at[slot],
            dst_ref=kv_ref.at[slot],
            send_sem=send.at[slot],
            recv_sem=recv.at[slot],
            device_id=up,
            device_id_type=MESH,
        )

    @pl.when(c < n - 1)
    def _():
        pass_up(0).start()

    peers.start()
    beside.start_down()
    pad_heads(q_ref, qpad, heads, group)
    top[...] = jnp.full_like(top, -1e30)
    tot[...] = jnp.zeros_like(tot)
    o_ref[...] = jnp.zeros_like(o_ref)

    def block(slot, masked):
        vt[...] = kv_ref[slot, :, kvw:].T

        def head(h, carry):
            g = lax.div(h, group)
            scores = nn(kv_ref[slot, :, :kvw], qpad[h])
            if masked:
                scores = jnp.where(causal(t), scores, -1e30)
            old = top[h]
            new = jnp.maximum(old, jnp.max(scores, axis=0, keepdims=True))
            weights = jnp.exp(scores - new)
            factor = jnp.exp(old - new)
            top[h] = new
            tot[h] = tot[h] * factor + jnp.sum(weights, axis=0, keepdims=True)
            rows = pl.ds(pl.multiple_of(h * HEAD_SIZE, HEAD_SIZE), HEAD_SIZE)
            vrows = pl.ds(pl.multiple_of(g * HEAD_SIZE, HEAD_SIZE), HEAD_SIZE)
            o_ref[rows, :] = o_ref[rows, :] * factor + nn(vt[vrows, :], weights.astype(BF16))
            return carry

        lax.fori_loop(0, heads, head, 0)

    block(0, True)

    def earlier(slot, carry):
        got(slot).wait_recv()

        @pl.when(c < n - 1)
        def _():
            pass_up(slot).start()

        block(slot, False)
        return carry

    lax.fori_loop(1, c + 1, earlier, 0)
    for h in range(heads):
        rows = slice(h * HEAD_SIZE, (h + 1) * HEAD_SIZE)
        done = o_ref[rows, :] / tot[h]
        o_ref[rows, :] = done
        heads_ref[rows, :] = done.astype(BF16)
        lse_ref[h] = top[h] + jnp.log(tot[h])

    @pl.when(c < n - 1)
    def _():
        def sent(slot, carry):
            pass_up(slot).wait_send()
            return carry

        lax.fori_loop(0, c + 1, sent, 0)

    peers.finish()
    beside.finish(up=False)


def attend(n, qt, k, v, cot, routes):
    t, kvw = k.shape
    qw = qt.shape[0]
    heads = qw // HEAD_SIZE
    return pl.pallas_call(
        functools.partial(attend_kernel, n),
        out_shape=(
            jax.ShapeDtypeStruct((qw, t), F32),
            jax.ShapeDtypeStruct((qw, t), BF16),
            jax.ShapeDtypeStruct((heads, 1, t), F32),
            jax.ShapeDtypeStruct((n, t, 2 * kvw), BF16),
            jax.ShapeDtypeStruct(cot.shape, BF16),
            jax.ShapeDtypeStruct((n,) + routes.shape, jnp.int32),
        ),
        in_specs=[VMEM] * 3 + [HBM, VMEM],
        out_specs=(VMEM,) * 4 + (HBM, VMEM),
        scratch_shapes=[
            pltpu.VMEM((heads, kvw, t), BF16),
            pltpu.VMEM((kvw, t), BF16),
            pltpu.VMEM((heads, 1, t), F32),
            pltpu.VMEM((heads, 1, t), F32),
            DMA((n,)),
            DMA((n,)),
            DMA((2, 2)),
            DMA((2, n)),
        ],
        compiler_params=params(0),
        name="attend",
        cost_estimate=cost(30),
    )(qt, k, v, cot, routes)


def attend_back_kernel(
    n,
    q_ref,
    db_ref,
    wout_ref,
    o_ref,
    lse_ref,
    kv_ref,
    arr_ref,
    arr_other,
    dg_ref,
    dg_other,
    rows_line,
    own_ref,
    below_ref,
    above_ref,
    hid_hbm,
    hid_own,
    arr_hbm,
    place_hbm,
    line_hbm,
    first_hbm,
    dqkv_ref,
    gate_ref,
    gate_parts,
    down_ref,
    down_other,
    up_ref,
    up_other,
    all_hbm,
    rest_hbm,
    do_ref,
    qpad,
    dopad,
    delta,
    dq,
    kt,
    part,
    passing,
    sum_ref,
    from_below,
    from_above,
    place_buf,
    cot_buf,
    hid_buf,
    arr_buf,
    du_buf,
    dy,
    acc_ref,
    kv_sem,
    sum_sem,
    spread_sem,
    local,
    ysem,
    load_sem,
):
    s, c, m = lax.axis_index("seq"), lax.axis_index("ctx"), lax.axis_index("mp")
    _, t, kvw2 = kv_ref.shape
    kvw = kvw2 // 2
    heads = q_ref.shape[0] // HEAD_SIZE
    group = heads // (kvw // HEAD_SIZE)
    ex, slots, width = arr_ref.shape
    half_width = width // 2
    down = (s, lax.rem(c + n - 1, n), m)
    spread = Spread(n, own_ref, below_ref, above_ref, all_hbm, spread_sem.at[0], spread_sem.at[1], local)
    done_blocks = first_hbm.shape[0]
    cots = CotExchange(n, line_hbm, rest_hbm, done_blocks, ysem)
    line = LineSum(n, sum_ref, from_below, from_above, sum_sem.at[0], sum_sem.at[1])
    sem = pltpu.get_barrier_semaphore()
    signal_line(n, sem)
    cots.signal(sem)
    pl.semaphore_wait(sem, line_degree(n) + 2)
    spread.start()
    cots.start()

    def gate_part(e, out):
        def piece(r):
            mine = pl.ds(pl.multiple_of(s * half_width + r * 256, 128), 256)
            cut = pl.ds(pl.multiple_of(r * 256, 256), 256)
            out[cut, :] = (tn(arr_ref[e, :, mine], dg_ref[e]) + tn(arr_other[e, :, cut], dg_other[e])).astype(BF16)

        loop(half_width // 256, piece)

    gate_part(0, sum_ref)
    line.first(0)
    do_ref[...] = nt(wout_ref[...], db_ref[...]).astype(BF16)

    def tick(i):
        line.tick(i)
        for hop in range(1, n - 1):

            @pl.when(i == 2 * hop)
            def _():
                spread.tick(hop)

    ticks = 2 * (n - 2) + 1
    pad_heads(q_ref, qpad, heads, group)
    pad_heads(do_ref, dopad, heads, group)
    for h in range(heads):
        rows = slice(h * HEAD_SIZE, (h + 1) * HEAD_SIZE)
        delta[h] = jnp.sum(do_ref[rows, :].astype(F32) * o_ref[rows, :], axis=0, keepdims=True)
    dq[...] = jnp.zeros_like(dq)

    def block(j, masked):
        slot = c - j
        acc = part.at[lax.rem(j, 2)]
        acc[...] = jnp.zeros(acc.shape, F32)
        kt[...] = kv_ref[slot, :, :kvw].T

        def head(h, carry):
            g = lax.div(h, group)
            scores = nn(kv_ref[slot, :, :kvw], qpad[h])
            probs = jnp.exp(scores - lse_ref[h])
            if masked:
                probs = jnp.where(causal(t), probs, 0.0)
            dprobs = nn(kv_ref[slot, :, kvw:], dopad[h])
            ds = (probs * (dprobs - delta[h])).astype(BF16)
            rows = pl.ds(pl.multiple_of(h * HEAD_SIZE, HEAD_SIZE), HEAD_SIZE)
            krows = pl.ds(pl.multiple_of(g * HEAD_SIZE, HEAD_SIZE), HEAD_SIZE)
            dq[rows, :] = dq[rows, :] + nn(kt[krows, :], ds)
            acc[:, :kvw] = acc[:, :kvw] + nt(ds, qpad[h])
            acc[:, kvw:] = acc[:, kvw:] + nt(probs.astype(BF16), dopad[h])
            return carry

        lax.fori_loop(0, heads, head, 0)

    def pass_down(j):
        return pltpu.make_async_remote_copy(
            src_ref=passing.at[j],
            dst_ref=passing.at[j],
            send_sem=kv_sem.at[0, j],
            recv_sem=kv_sem.at[1, j],
            device_id=down,
            device_id_type=MESH,
        )

    def gathered(j):
        acc = part.at[lax.rem(j, 2)]

        @pl.when(c < n - 1)
        def _():
            pass_down(j).wait_recv()
            acc[...] = acc[...] + passing[j].astype(F32)

        return acc

    def forward(j):
        acc = gathered(j)
        passing[j] = acc[...].astype(BF16)
        pass_down(j).start()

    def step(j, carry):
        block(j, False)

        @pl.when(jnp.logical_and(j > 0, c < n - 1))
        def _():
            forward(j - 1)

        @pl.when(c == n - 1)
        def _():
            forward(j)

        tick(j)
        return carry

    lax.fori_loop(0, c, step, 0)
    block(c, True)

    @pl.when(jnp.logical_and(c > 0, c < n - 1))
    def _():
        forward(c - 1)

    qw = dq.shape[0]
    dqkv_ref[:, :qw] = (dq[...] * 0.125).astype(BF16).T
    for e in range(1, ex):
        gate_part(e, gate_parts.at[e - 1])

    def later(i, carry):
        tick(i)
        return carry

    middle = jnp.maximum(c, min(3, ticks))
    lax.fori_loop(c, middle, later, 0)

    cots.finish()

    def load_block(i, slot, start):
        b = lax.rem(c - i + n, n)
        share = line_hbm.shape[1]
        place_copy = pltpu.make_async_copy(place_hbm.at[b], place_buf.at[slot], load_sem.at[0, slot])
        hid_copy = pltpu.make_async_copy(hid_hbm.at[b], hid_buf.at[slot], load_sem.at[1, slot])
        hid_mine = pltpu.make_async_copy(hid_own.at[b], hid_buf.at[slot], load_sem.at[1, slot])

        def rows(who):
            return pl.ds(pl.multiple_of(who * share, 16), share)

        def piece(k, who, full, at):
            return pltpu.make_async_copy(
                full.at[at, rows(who), :], cot_buf.at[slot, rows(who), :], load_sem.at[2 + k, slot]
            )

        others = (cots.sib, cots.opp, lax.rem(cots.sib + 2, 4))
        mine = pltpu.make_async_copy(line_hbm.at[b], cot_buf.at[slot, rows(m), :], load_sem.at[5, slot])
        first = [piece(k, who, first_hbm, jnp.minimum(i, done_blocks - 1)) for k, who in enumerate(others)]
        if not start:
            for copy in [place_copy, hid_copy, mine] + first:
                copy.wait()
            return
        rest = [piece(k, who, rest_hbm, jnp.maximum(i - done_blocks, 0)) for k, who in enumerate(others)]
        place_copy.start()
        mine.start()

        @pl.when(b == c)
        def _():
            hid_mine.start()

        @pl.when(b != c)
        def _():
            hid_copy.start()

        @pl.when(i < done_blocks)
        def _():
            for copy in first:
                copy.start()

        @pl.when(i >= done_blocks)
        def _():
            for copy in rest:
                copy.start()

    fa, ua = hid_hbm.shape[3], arr_hbm.shape[3]
    ff = dg_ref.shape[2]
    acc_ref[...] = jnp.zeros_like(acc_ref)
    load_block(0, 0, True)
    wide = 512

    def down_block(i):
        slot = lax.rem(i, 2)
        load_block(i, slot, False)

        @pl.when(i < n - 1)
        def _():
            load_block(i + 1, 1 - slot, True)

        cols = rows_line[lax.rem(c - i + n, n)].T
        for e in range(ex):

            def dys(k):
                cut = pl.ds(pl.multiple_of(k * wide, wide), wide)
                dy[:, cut] = (
                    cols[:slots, e : e + 1] * nn(place_buf[slot, e * slots : (e + 1) * slots, :], cot_buf[slot, :, cut])
                ).astype(BF16)

            loop(width // wide, dys)
            acc_ref[e, :fa, :] = acc_ref[e, :fa, :] + tn(hid_buf[slot, e], dy[...])

    loop(n, down_block)
    mine, other = (pl.ds(pl.multiple_of(k * (fa // 2), 16), fa // 2) for k in (s, 1 - s))
    down_ref[...] = acc_ref[:, mine, :]
    down_other[...] = acc_ref[:, other, :].astype(BF16)

    lax.fori_loop(middle, ticks, later, 0)

    spread.finish()
    acc_ref[...] = jnp.zeros_like(acc_ref)

    def load_du(b, slot):
        return (
            pltpu.make_async_copy(all_hbm.at[b], du_buf.at[slot], load_sem.at[6, slot]),
            pltpu.make_async_copy(arr_hbm.at[b], arr_buf.at[slot], load_sem.at[7, slot]),
        )

    for copy in load_du(0, 0):
        copy.start()

    def up_block(b):
        slot = lax.rem(b, 2)
        for copy in load_du(b, slot):
            copy.wait()

        @pl.when(b < n - 1)
        def _():
            for copy in load_du(b + 1, 1 - slot):
                copy.start()

        for e in range(ex):
            acc_ref[e, :ua, :ff] = acc_ref[e, :ua, :ff] + tn(arr_buf[slot, e], du_buf[slot, e])

    loop(n, up_block)
    mine, other = (pl.ds(pl.multiple_of(k * (ua // 2), 16), ua // 2) for k in (s, 1 - s))
    up_ref[...] = acc_ref[:, mine, :ff]
    up_other[...] = acc_ref[:, other, :ff].astype(BF16)

    acc = gathered(c)
    dqkv_ref[:, qw:] = acc[...].astype(BF16)
    line.finish(gate_ref)

    def sent_kv(j, carry):
        pass_down(j).wait_send()
        return carry

    lax.fori_loop(0, c, sent_kv, 0)


def attend_back(n, qt, db, w_out, o, lse, kv, arr, arr_other, dg, dg_other, rows, du, below, above, hid, hid_own, arr_line, place, line, first):
    qw, t = qt.shape
    heads = qw // HEAD_SIZE
    kvw = kv.shape[2] // 2
    ex, slots, width = arr.shape
    ff = dg.shape[2]
    half_width = width // 2
    chunk = (half_width // n, ff)
    fa, ua = hid.shape[3], arr_line.shape[3]
    blocks = first.shape[0]
    sds = jax.ShapeDtypeStruct
    return pl.pallas_call(
        functools.partial(attend_back_kernel, n),
        out_shape=(
            sds((t, qw + 2 * kvw), BF16),
            sds(chunk, F32),
            sds((ex - 1, half_width, ff), BF16),
            sds((ex, fa // 2, width), F32),
            sds((ex, fa // 2, width), BF16),
            sds((ex, ua // 2, ff), F32),
            sds((ex, ua // 2, ff), BF16),
            sds((n,) + du.shape, BF16),
            sds((n - blocks,) + first.shape[1:], BF16),
        ),
        in_specs=[VMEM] * 14 + [HBM] * 6,
        out_specs=(VMEM,) * 7 + (HBM,) * 2,
        scratch_shapes=[
            pltpu.VMEM((qw, t), BF16),
            pltpu.VMEM((heads, kvw, t), BF16),
            pltpu.VMEM((heads, kvw, t), BF16),
            pltpu.VMEM((heads, 1, t), F32),
            pltpu.VMEM((qw, t), F32),
            pltpu.VMEM((kvw, t), BF16),
            pltpu.VMEM((2, t, 2 * kvw), F32),
            pltpu.VMEM((n, t, 2 * kvw), BF16),
            pltpu.VMEM((half_width, ff), BF16),
            pltpu.VMEM((n,) + chunk, BF16),
            pltpu.VMEM((n,) + chunk, BF16),
            pltpu.VMEM((2,) + place.shape[1:], BF16),
            pltpu.VMEM((2,) + first.shape[1:], BF16),
            pltpu.VMEM((2, ex, slots, fa), BF16),
            pltpu.VMEM((2, ex, slots, ua), BF16),
            pltpu.VMEM((2,) + du.shape, BF16),
            pltpu.VMEM((slots, width), BF16),
            pltpu.VMEM((ex, max(fa, ua), width), F32),
            DMA((2, n)),
            DMA((2, 2, n)),
            DMA((2, n)),
            DMA((3,)),
            DMA((2, 3, n - blocks)),
            DMA((8, 2)),
        ],
        compiler_params=params(1, 60),
        name="attend_back",
        cost_estimate=cost(60),
    )(qt, db, w_out, o, lse, kv, arr, arr_other, dg, dg_other, rows, du, below, above, hid, hid_own, arr_line, place, line, first)


def tn(a, b):
    return lax.dot_general(a, b, (((0,), (0,)), ((), ())), preferred_element_type=F32)


def loop(n, f):
    def step(i, carry):
        f(i)
        return carry

    lax.fori_loop(0, n, step, 0)


def moe_kernel(
    n,
    n_seq,
    experts_all,
    h_ref,
    cot_ref,
    place_ref,
    place_t_ref,
    routes_ref,
    router_ref,
    wg_hbm,
    wu_hbm,
    wd_hbm,
    line_hbm,
    gates_ref,
    rows_ref,
    arr_ref,
    hid_ref,
    dg_ref,
    du_ref,
    back_ref,
    comb_ref,
    arr_line,
    cot_first,
    line_out,
    wg,
    wu,
    wd,
    dout,
    dy,
    hid,
    back_rows,
    comb_rows,
    parts,
    cols,
    wsem,
    peers_sem,
    ysem,
    local,
    far_sem,
    router3,
):
    s, c, m = lax.axis_index("seq"), lax.axis_index("ctx"), lax.axis_index("mp")
    ex, width, ff = wg.shape
    slots = place_ref.shape[0] // ex
    first = m * ex
    lanes = gates_ref.shape[1]
    peers = Peers(n, lambda p: parts.at[p], lambda i: arr_line.at[i], peers_sem.at[0], peers_sem.at[1])
    cots = CotExchange(n, line_hbm, cot_first, 0, ysem)
    far = pltpu.make_async_remote_copy(
        src_ref=line_hbm.at[0],
        dst_ref=line_out.at[0],
        send_sem=far_sem.at[0],
        recv_sem=far_sem.at[1],
        device_id=(s, lax.rem(c + 1, n), m),
        device_id_type=MESH,
    )
    sem = pltpu.get_barrier_semaphore()
    peers.signal(sem)
    cots.signal(sem)
    weights = {}
    for e in range(ex):
        for i, (src, dst) in enumerate(((wg_hbm, wg), (wu_hbm, wu), (wd_hbm, wd))):
            weights[i, e] = pltpu.make_async_copy(src.at[e], dst.at[e], wsem.at[i, e])
            weights[i, e].start()

    def rows_of(e):
        return slice(e * slots, (e + 1) * slots)

    def arrive(i):
        cut = pl.ds(pl.multiple_of(i * slots, 16), slots)
        arr_ref[i] = nn(place_ref[cut, :], h_ref[...]).astype(BF16)

    loop(ex, arrive)
    size = width // (n * n_seq)
    for e in range(ex):
        for i in range(n):
            for j in range(n_seq):
                at = (j * n + i) * size
                parts[i, e, :, j * size : (j + 1) * size] = arr_ref[e, :, at : at + size]
    pl.semaphore_wait(sem, n - 1 + 2)
    peers.start()
    cots.start()

    @pl.when(c == n - 2)
    def _():
        far.start()

    own = pltpu.make_async_copy(parts.at[c], arr_line.at[c], local.at[0])
    own.start()

    router3[...] = jnp.zeros_like(router3)
    left = router_ref[...]
    for i in range(3):
        piece = left.astype(BF16)
        router3[:, i * experts_all : (i + 1) * experts_all] = piece
        left = left - piece.astype(F32)
    three = nn(h_ref[...], router3[...])
    logits = three + pltpu.roll(three, lanes - experts_all, 1) + pltpu.roll(three, lanes - 2 * experts_all, 1)
    which = lax.broadcasted_iota(jnp.int32, three.shape, 1)
    chosen = which == routes_ref[:, 0:1]
    for k in range(1, routes_ref.shape[1]):
        chosen = jnp.logical_or(chosen, which == routes_ref[:, k : k + 1])
    peak = jnp.max(jnp.where(chosen, logits, -1e30), axis=1, keepdims=True)
    raised = jnp.where(chosen, jnp.exp(jnp.where(chosen, logits - peak, 0.0)), 0.0)
    gates = raised / jnp.sum(raised, axis=1, keepdims=True)
    gates_ref[...] = gates
    g1 = gates.astype(BF16)
    rest = gates - g1.astype(F32)
    g2 = rest.astype(BF16)
    g3 = (rest - g2.astype(F32)).astype(BF16)
    lane = lax.broadcasted_iota(jnp.int32, (slots, lanes), 1)
    cols[...] = jnp.zeros_like(cols)
    gate_col = []
    for e in range(ex):
        pe = place_ref[rows_of(e), :]
        got = nn(pe, g1) + nn(pe, g2) + nn(pe, g3)
        col = jnp.sum(jnp.where(lane == first + e, got, 0.0), axis=1, keepdims=True)
        gate_col.append(col)
        cols[:slots, :] = cols[:slots, :] + jnp.where(lane == e, col, 0.0)

    rows_ref[...] = cols[...].T[:8, :]
    wide = 512
    for e in range(ex):
        col = gate_col[e]

        def douts(i):
            cut = pl.ds(pl.multiple_of(i * wide, wide), wide)
            d = nn(place_ref[rows_of(e), :], cot_ref[:, cut])
            dout[e, :, cut] = d.astype(BF16)
            dy[e, :, cut] = (col * d).astype(BF16)

        loop(width // wide, douts)
        for i in range(3):
            weights[i, e].wait()

        def hidden(i):
            cut = pl.ds(pl.multiple_of(i * 256, 256), 256)
            g = nn(arr_ref[e], wg[e, :, cut])
            u = nn(arr_ref[e], wu[e, :, cut])
            dh = nt(dy[e], wd[e, cut, :])
            sigma = jax.nn.sigmoid(g)
            silu = g * sigma
            hid[:, cut] = (silu * u).astype(BF16)
            dg_ref[e, :, cut] = (dh * u * sigma * (1.0 + g * (1.0 - sigma))).astype(BF16)
            du_ref[e, :, cut] = (dh * silu).astype(BF16)

        loop(ff // 256, hidden)
        size = ff // (n * n_seq)
        for i in range(n):
            for j in range(n_seq):
                at = (j * n + i) * size
                hid_ref[i, e, :, j * size : (j + 1) * size] = hid[:, at : at + size]

        def outs(i, grads):
            cut = pl.ds(pl.multiple_of(i * wide, wide), wide)
            y = nn(hid[...], wd[e, :, cut]).astype(BF16).astype(F32)
            comb_rows[rows_of(e), cut] = (col * y).astype(BF16)
            back_rows[rows_of(e), cut] = (nt(dg_ref[e], wg[e, cut, :]) + nt(du_ref[e], wu[e, cut, :])).astype(BF16)
            return grads + jnp.sum(dout[e, :, cut].astype(F32) * y, axis=1, keepdims=True)

        grads = lax.fori_loop(0, width // wide, outs, jnp.zeros((slots, 1), F32))
        high = grads.astype(BF16).astype(F32)
        here = jnp.where(lane == first + e, high, jnp.where(lane == lanes // 2 + first + e, grads - high, 0.0))
        back_rows[rows_of(e), width:] = here.astype(BF16)

    def scatter(i):
        cut = pl.ds(pl.multiple_of(i * 256, 256), 256)
        back_ref[:, cut] = nn(place_t_ref[...], back_rows[:, cut]).astype(BF16)
        comb_ref[:, cut] = nn(place_t_ref[...], comb_rows[:, cut]).astype(BF16)

    loop(width // 256, scatter)
    back_ref[:, width:] = nn(place_t_ref[...], back_rows[:, width:]).astype(BF16)
    own.wait()
    cots.finish()
    peers.finish()

    @pl.when(c == n - 2)
    def _():
        far.wait_send()

    @pl.when(c == n - 1)
    def _():
        far.wait_recv()


def moe(n, n_seq, experts_all, h, cot, place, place_t, routes, router, wg, wu, wd, line):
    ex, width, ff = wg.shape
    tok = h.shape[0]
    slots = place.shape[0] // ex
    blocks = n // 2
    sds = jax.ShapeDtypeStruct
    return pl.pallas_call(
        functools.partial(moe_kernel, n, n_seq, experts_all),
        out_shape=(
            sds((tok, 128), F32),
            sds((8, 256), F32),
            sds((ex, slots, width), BF16),
            sds((n, ex, slots, ff // n), BF16),
            sds((ex, slots, ff), BF16),
            sds((ex, slots, ff), BF16),
            sds((tok, width + 128), BF16),
            sds((tok, width), BF16),
            sds((n, ex, slots, width // n), BF16),
            sds((blocks, tok, width), BF16),
            sds(line.shape, BF16),
        ),
        in_specs=[VMEM] * 6 + [HBM] * 4,
        out_specs=(VMEM,) * 8 + (HBM,) * 3,
        scratch_shapes=[
            pltpu.VMEM(wg.shape, BF16),
            pltpu.VMEM(wu.shape, BF16),
            pltpu.VMEM(wd.shape, BF16),
            pltpu.VMEM((ex, slots, width), BF16),
            pltpu.VMEM((ex, slots, width), BF16),
            pltpu.VMEM((slots, ff), BF16),
            pltpu.VMEM((ex * slots, width + 128), BF16),
            pltpu.VMEM((ex * slots, width), BF16),
            pltpu.VMEM((n, ex, slots, width // n), BF16),
            pltpu.VMEM((256, 128), F32),
            DMA((3, ex)),
            DMA((2, n)),
            DMA((2, 3, blocks)),
            DMA((1,)),
            DMA((2,)),
            pltpu.VMEM((width, 128), BF16),
        ],
        input_output_aliases={9: 10},
        compiler_params=params(6, 60),
        name="moe",
        cost_estimate=cost(30),
    )(h, cot, place, place_t, routes, router, wg, wu, wd, line)


class Mp:
    def __init__(self, part, core_in, y_out, y_in, full, sems, chunks):
        self.part, self.core_in, self.y_out, self.y_in, self.full = part, core_in, y_out, y_in, full
        self.sems, self.chunks = sems, chunks
        s, c, m = lax.axis_index("seq"), lax.axis_index("ctx"), lax.axis_index("mp")
        self.m = m
        self.sib = m + 1 - 2 * lax.rem(m, 2)
        self.opp = lax.rem(m + 2, 4)
        self.diag = lax.rem(self.sib + 2, 4)
        self.sib_id, self.opp_id = (s, c, self.sib), (s, c, self.opp)
        share = (part if part is not None else full).shape[1]
        self.rows = share // chunks

    def signal(self, sem):
        for d in (self.sib_id, self.opp_id):
            pl.semaphore_signal(sem, inc=1, device_id=d, device_id_type=MESH)

    def copy(self, src, dst, i, dev):
        return pltpu.make_async_remote_copy(
            src_ref=src,
            dst_ref=dst,
            send_sem=self.sems.at[0, i],
            recv_sem=self.sems.at[1, i],
            device_id=dev,
            device_id_type=MESH,
        )

    def cut(self, i):
        return pl.ds(i * self.rows, self.rows)

    def rs_core(self, i):
        src = self.part.at[self.diag] if i == 0 else self.part.at[self.sib]
        return self.copy(src, self.core_in.at[i], i, self.sib_id)

    def rs_y(self, i):
        return self.copy(self.y_out.at[self.cut(i)], self.y_in.at[self.cut(i)], 2 + i, self.opp_id)

    def rs_begin(self):
        self.rs_core(0).start()
        self.rs_core(1).start()
        self.rs_forward()

    def rs_forward(self):
        self.rs_core(0).wait_recv()
        for i in range(self.chunks):
            cut = self.cut(i)
            self.y_out[cut, :] = (
                self.part[self.opp, cut, :].astype(F32) + self.core_in[0, cut, :].astype(F32)
            ).astype(BF16)
            self.rs_y(i).start()
        self.rs_core(1).wait_recv()

    def rs_chunk(self, i):
        cut = self.cut(i)
        self.rs_y(i).wait_recv()
        return (
            self.part[self.m, cut, :].astype(F32) + self.core_in[1, cut, :].astype(F32)
        ) + self.y_in[cut, :].astype(F32)

    def rs_end(self):
        self.rs_core(0).wait_send()
        self.rs_core(1).wait_send()
        for i in range(self.chunks):
            self.rs_y(i).wait_send()

    def ag(self, kind, i, whose):
        block = self.full.at[whose, self.cut(i)]
        base = 2 + self.chunks
        dev = self.opp_id if kind == 0 else self.sib_id
        return self.copy(block, block, base + kind * self.chunks + i, dev)

    def ag_send(self, i):
        self.ag(0, i, self.m).start()
        self.ag(1, i, self.m).start()

    def ag_end(self):
        for i in range(self.chunks):
            self.ag(0, i, self.opp).wait_recv()
            self.ag(2, i, self.opp).start()
        for i in range(self.chunks):
            self.ag(1, i, self.sib).wait_recv()
            self.ag(2, i, self.diag).wait_recv()
            self.ag(0, i, self.m).wait_send()
            self.ag(1, i, self.m).wait_send()
            self.ag(2, i, self.opp).wait_send()


def mp_scratch(share, width, chunks):
    return [
        pltpu.VMEM((2, share, width), BF16),
        pltpu.VMEM((share, width), BF16),
        pltpu.VMEM((share, width), BF16),
        DMA((2, 2 + 4 * chunks)),
    ]


def rms_parts(rows):
    inverse = lax.rsqrt(jnp.mean(rows * rows, axis=-1, keepdims=True) + EPS)
    return rows * inverse, inverse


def rms_grad(grad_normed, normed, inverse):
    return inverse * (grad_normed - normed * jnp.mean(grad_normed * normed, axis=-1, keepdims=True))


def mid_forward_kernel(
    chunks,
    n,
    ex,
    part,
    gain,
    own,
    above,
    routes_ref,
    tok_hbm,
    resid_ref,
    h_ref,
    place_ref,
    place_t,
    place_line,
    line_ref,
    core_in,
    y_out,
    y_in,
    sems,
    send,
    recv,
    local,
    x_ref,
    x_sem,
    ranks,
):
    c = lax.axis_index("ctx")
    mp = Mp(part, core_in, y_out, y_in, h_ref, sems, chunks)
    spread = Spread(n, own, None, above, line_ref, send, recv, local, short=True)
    x_copy = pltpu.make_async_copy(tok_hbm.at[mp.m], x_ref, x_sem.at[0])
    x_copy.start()
    sem = pltpu.get_barrier_semaphore()
    mp.signal(sem)
    signal_line(n, sem)
    pl.semaphore_wait(sem, 2 + line_degree(n))
    mp.rs_core(0).start()
    mp.rs_core(1).start()
    spread.start()
    mp.rs_forward()
    tok = routes_ref.shape[2]
    slots = place_ref.shape[0] // ex
    before = (
        lax.broadcasted_iota(jnp.int32, (tok, tok), 0) <= lax.broadcasted_iota(jnp.int32, (tok, tok), 1)
    ).astype(BF16)

    def places(b):
        at = b * ex
        ranks[...] = jnp.zeros_like(ranks)
        for e in range(ex):
            hit = routes_ref[b] == mp.m * ex + e
            ranks[e : e + 1, :] = jnp.max(hit.astype(F32), axis=0, keepdims=True)
        sel = ranks[...]
        order = nn(sel.astype(BF16), before) - 1.0
        rows = lax.broadcasted_iota(jnp.int32, (slots, tok), 0).astype(F32)
        for e in range(ex):
            one = jnp.where(rows == order[e : e + 1, :], 1.0, 0.0) * sel[e : e + 1, :]
            place_line[b, e * slots : (e + 1) * slots, :] = one.astype(BF16)

    x_copy.wait()
    for i in range(chunks):
        cut = mp.cut(i)
        resid = x_ref[cut, :].astype(F32) + mp.rs_chunk(i)
        resid_ref[cut, :] = resid
        normed, _ = rms_parts(resid)
        h_ref[mp.m, cut, :] = (normed * gain[...]).astype(BF16)
        mp.ag_send(i)
    places(c)
    place_ref[...] = place_line[c]
    place_t[...] = place_ref[...].T
    spread.tick(1)
    loop(n - 1, lambda i: places(lax.rem(c + 1 + i, n)))
    mp.ag_end()
    mp.rs_end()
    spread.ticks(2)
    spread.finish()


def mid_forward(n, ex, slots, part, gain, own, above, routes_line, tokens, chunks=2):
    k, share, width = part.shape
    tok = k * share
    sds = jax.ShapeDtypeStruct
    return pl.pallas_call(
        functools.partial(mid_forward_kernel, chunks, n, ex),
        out_shape=(
            sds((share, width), F32),
            sds(part.shape, BF16),
            sds((ex * slots, tok), BF16),
            sds((tok, ex * slots), BF16),
            sds((n, ex * slots, tok), BF16),
            sds((n,) + own.shape, BF16),
        ),
        in_specs=[VMEM] * 5 + [HBM],
        out_specs=(VMEM,) * 5 + (HBM,),
        scratch_shapes=mp_scratch(share, width, chunks)
        + [DMA((n,)), DMA((n,)), DMA((3,)), pltpu.VMEM((share, width), BF16), DMA((1,)), pltpu.VMEM((8, tok), F32)],
        compiler_params=params(2, 58),
        name="mid_forward",
        cost_estimate=cost(30),
    )(part, gain, own, above, routes_line, tokens)


def mid_back_kernel(
    chunks,
    n,
    part,
    resid_ref,
    gain,
    cot,
    gate_ref,
    router_ref,
    rows_ref,
    hid_ref,
    du_ref,
    arr_ref,
    dg_ref,
    dresid_ref,
    db_ref,
    small_ref,
    rows_line,
    hid_line,
    below_ref,
    above_ref,
    arr_other,
    dg_other,
    core_in,
    y_out,
    y_in,
    sems,
    side,
    peers_sem,
    swap_sem,
):
    c = lax.axis_index("ctx")
    mp = Mp(part, core_in, y_out, y_in, db_ref, sems, chunks)
    rows_peers = Peers(n, lambda p: rows_ref, lambda i: rows_line.at[i], peers_sem.at[0], peers_sem.at[1])
    hid_peers = Peers(n, lambda p: hid_ref.at[p], lambda i: hid_line.at[i], peers_sem.at[2], peers_sem.at[3])
    beside = Neighbours(n, du_ref, below_ref, above_ref, side.at[0], side.at[1])
    width = gain.shape[1]
    ex = router_ref.shape[0]
    lanes = gate_ref.shape[2]
    sem = pltpu.get_barrier_semaphore()
    mp.signal(sem)
    rows_peers.signal(sem)
    partner = swap_partner()
    pl.semaphore_signal(sem, inc=1, device_id=partner, device_id_type=MESH)
    pl.semaphore_wait(sem, 2 + n - 1 + 1)
    mp.rs_core(0).start()
    mp.rs_core(1).start()
    half_width = width // 2
    theirs = pl.ds(pl.multiple_of((1 - lax.axis_index("seq")) * half_width, 128), half_width)
    swaps = [
        swap(arr_ref.at[:, :, theirs], arr_other, swap_sem, 0),
        swap(dg_ref, dg_other, swap_sem, 1),
    ]
    for sw in swaps:
        sw.start()
    beside.start_up()
    beside.start_down()
    rows_peers.start()
    hid_peers.start()
    mp.rs_forward()
    rows_line[c] = rows_ref[...]
    small_ref[...] = jnp.zeros_like(small_ref)
    for i in range(chunks):
        cut = mp.cut(i)
        both = mp.rs_chunk(i)
        dgate = both[:, width : width + ex] + both[:, width + lanes // 2 : width + lanes // 2 + ex]
        gate = gate_ref[mp.m, cut, :ex]
        dlog = gate * (dgate - jnp.sum(gate * dgate, axis=-1, keepdims=True))
        dh = both[:, :width] + jnp.dot(
            dlog, router_ref[...], precision=lax.Precision.HIGHEST, preferred_element_type=F32
        )
        normed, inverse = rms_parts(resid_ref[cut, :])
        small_ref[1:2, :] = small_ref[1:2, :] + jnp.sum(dh * normed, axis=0, keepdims=True)
        h_two = (normed * gain[...]).astype(BF16).astype(F32)
        small_ref[8 : 8 + ex, :] = small_ref[8 : 8 + ex, :] + lax.dot_general(
            dlog, h_two, (((0,), (0,)), ((), ())), precision=lax.Precision.HIGHEST, preferred_element_type=F32
        )
        dresid = cot[cut, :].astype(F32) + rms_grad(dh * gain[...], normed, inverse)
        dresid_ref[cut, :] = dresid
        db_ref[mp.m, cut, :] = dresid.astype(BF16)
        mp.ag_send(i)
    mp.ag_end()
    mp.rs_end()
    rows_peers.finish()
    hid_peers.finish()
    beside.finish()
    for sw in swaps:
        sw.wait()


def swap_partner():
    return (1 - lax.axis_index("seq"), lax.axis_index("ctx"), lax.axis_index("mp"))


def swap(src, dst, sems, i):
    return pltpu.make_async_remote_copy(
        src_ref=src,
        dst_ref=dst,
        send_sem=sems.at[0, i],
        recv_sem=sems.at[1, i],
        device_id=swap_partner(),
        device_id_type=MESH,
    )


def mid_back(n, part, resid, gain, cot, gate, router_t, rows, hid, du, arr, dg, chunks=2):
    k, share, wide = part.shape
    width = gain.shape[1]
    return pl.pallas_call(
        functools.partial(mid_back_kernel, chunks, n),
        out_shape=(
            jax.ShapeDtypeStruct((share, width), F32),
            jax.ShapeDtypeStruct((k, share, width), BF16),
            jax.ShapeDtypeStruct((8 + router_t.shape[0], width), F32),
            jax.ShapeDtypeStruct((n,) + rows.shape, F32),
            jax.ShapeDtypeStruct(hid.shape, BF16),
            jax.ShapeDtypeStruct(du.shape, BF16),
            jax.ShapeDtypeStruct(du.shape, BF16),
            jax.ShapeDtypeStruct(arr.shape[:2] + (arr.shape[2] // 2,), BF16),
            jax.ShapeDtypeStruct(dg.shape, BF16),
        ),
        in_specs=[VMEM] * 7 + [HBM] * 4,
        out_specs=(VMEM,) * 4 + (HBM,) * 5,
        scratch_shapes=mp_scratch(share, wide, chunks) + [DMA((2, 2)), DMA((4, n)), DMA((2, 2))],
        compiler_params=params(3, 60),
        name="mid_back",
        cost_estimate=cost(32),
    )(part, resid, gain, cot, gate, router_t, rows, hid, du, arr, dg)


class SmallSum:
    def __init__(self, sizes, x_ref, out_ref, bufs, sems):
        self.sizes, self.x, self.out, self.bufs, self.sems = sizes, x_ref, out_ref, bufs, sems
        self.me = [lax.axis_index(a) for a in ("seq", "ctx", "mp")]

    def peer(self, axis, d):
        ids = list(self.me)
        ids[axis] = lax.rem(self.me[axis] + d, self.sizes[axis])
        return tuple(ids)

    def signal(self, sem):
        for axis in range(3):
            for d in range(1, self.sizes[axis]):
                pl.semaphore_signal(sem, inc=1, device_id=self.peer(axis, d), device_id_type=MESH)
        return sum(self.sizes) - 3

    def move(self, axis, d):
        base = sum(self.sizes[:axis])
        buf = self.bufs[axis]
        return pltpu.make_async_remote_copy(
            src_ref=buf.at[0],
            dst_ref=buf.at[d],
            send_sem=self.sems.at[0, base + d],
            recv_sem=self.sems.at[1, base + d],
            device_id=self.peer(axis, d),
            device_id_type=MESH,
        )

    def begin(self, axis, value):
        self.bufs[axis][0] = value
        for d in range(1, self.sizes[axis]):
            self.move(axis, d).start()

    def end(self, axis):
        n = self.sizes[axis]
        for d in range(1, n):
            self.move(axis, d).wait()
        total = jnp.zeros(self.out.shape, F32)
        for i in range(n):
            total = total + self.bufs[axis][lax.rem(self.me[axis] - i + n, n)]
        return total


def last_kernel(
    chunks,
    sizes,
    dqkv_ref,
    h_hbm,
    wq_hbm,
    wk_hbm,
    wv_hbm,
    tok_hbm,
    gain,
    dresid_hbm,
    small_ref,
    wout_ref,
    gate0_hbm,
    parts_ref,
    down0_hbm,
    down_other,
    up0_hbm,
    up_other,
    comb_hbm,
    resid_hbm,
    out_ref,
    final_ref,
    total_ref,
    gout_ref,
    gqkv_ref,
    gate_ref,
    down_ref,
    up_ref,
    core_in,
    y_out,
    y_in,
    sems,
    core_in2,
    y_out2,
    y_in2,
    sems2,
    h_ref,
    wq_ref,
    wk_ref,
    wv_ref,
    tok_ref,
    dresid_ref,
    comb,
    resid_ref,
    part,
    dh_ref,
    qkv_ref,
    swapped,
    summed,
    wout_in,
    qkv_in,
    down_in,
    up_in,
    from_below,
    from_above,
    load_sem,
    swap_sem,
    peers_sem,
    sum_sem,
    *rest,
):
    n = sizes[1]
    s, c = lax.axis_index("seq"), lax.axis_index("ctx")
    load = Staged(
        (
            (h_hbm, h_ref),
            (wq_hbm, wq_ref),
            (wk_hbm, wk_ref),
            (wv_hbm, wv_ref),
            (tok_hbm, tok_ref),
            (comb_hbm, comb),
            (dresid_hbm, dresid_ref),
            (resid_hbm, resid_ref),
            (gate0_hbm, gate_ref.at[0]),
            (down0_hbm, down_ref),
            (up0_hbm, up_ref),
        ),
        load_sem,
    )
    load.start()
    mp = Mp(part, core_in, y_out, y_in, None, sems, chunks)
    mp2 = Mp(comb, core_in2, y_out2, y_in2, None, sems2, chunks)
    small = SmallSum(sizes, small_ref, total_ref, rest[:3], rest[3])
    half_rows = swapped.shape[0]
    rows = half_rows // n
    wout_peers = Peers(
        n, lambda p: wout_ref.at[cut_of(p, rows)], lambda i: wout_in.at[i], peers_sem.at[0], peers_sem.at[1]
    )
    qkv_peers = Peers(
        n, lambda p: summed.at[cut_of(p, rows)], lambda i: qkv_in.at[i], peers_sem.at[2], peers_sem.at[3]
    )
    ex = gate_ref.shape[0]
    lines = [
        LineSum(n, parts_ref.at[e], from_below.at[e], from_above.at[e], sum_sem.at[e, 0], sum_sem.at[e, 1])
        for e in range(ex - 1)
    ]
    sem = pltpu.get_barrier_semaphore()
    pl.semaphore_wait(sem, small.signal(sem))
    for line in lines:
        line.first(0)
    wout_peers.start()
    load.wait(0)

    def weight_rows(first):
        def piece(r):
            at = pl.ds(pl.multiple_of(first + r * 256, 256), 256)
            qkv_ref[at, :] = tn(h_ref[:, at], dqkv_ref[...]).astype(BF16)

        loop(half_rows // 256, piece)

    weight_rows((1 - s) * half_rows)
    qkv_swap = swap(qkv_ref.at[cut_of(1 - s, half_rows)], swapped, swap_sem, 0)
    qkv_swap.start()
    load.wait(1, 2, 3)
    share, width = out_ref.shape
    qw, kw = wq_ref.shape[1], wk_ref.shape[1]

    def token_rows(i):
        at = pl.ds(pl.multiple_of(i * 512, 512), 512)
        dh = nt(dqkv_ref[:, :qw], wq_ref[at, :])
        dh = dh + nt(dqkv_ref[:, qw : qw + kw], wk_ref[at, :])
        dh = dh + nt(dqkv_ref[:, qw + kw :], wv_ref[at, :])
        for p in range(part.shape[0]):
            dh_ref[p, :, at] = dh[p * share : (p + 1) * share, :]
            part[p, :, at] = dh[p * share : (p + 1) * share, :].astype(BF16)

    loop(width // 512, token_rows)
    mp.rs_core(0).start()
    mp.rs_core(1).start()
    load.wait(5)
    mp2.rs_core(0).start()
    mp2.rs_core(1).start()
    weight_rows(s * half_rows)
    mp.rs_forward()
    load.wait(4)
    total_ref[...] = small_ref[...]

    def norm_rows(p):
        normed, _ = rms_parts(tok_ref[p].astype(F32))
        total_ref[0:1, :] = total_ref[0:1, :] + jnp.sum(dh_ref[p] * normed, axis=0, keepdims=True)

    loop(part.shape[0], norm_rows)
    small.begin(2, total_ref[...])
    for line in lines:
        line.tick(0)
    mp2.rs_forward()
    small.begin(0, small.end(2))
    load.wait(6)
    for i in range(chunks):
        cut = mp.cut(i)
        dh = mp.rs_chunk(i)
        normed, inverse = rms_parts(tok_ref[mp.m, cut, :].astype(F32))
        final_ref[cut, :] = dresid_ref[cut, :] + rms_grad(dh * gain[...], normed, inverse)
        for line in lines:
            line.tick(1 + i)
    for line in lines:
        loop(max(2 * n - 4 - chunks, 0), lambda i: line.tick(i + 1 + chunks))
    small.begin(1, small.end(0))
    qkv_swap.wait()
    down_swap = swap(down_other, down_in, swap_sem, 1)
    up_swap = swap(up_other, up_in, swap_sem, 2)
    down_swap.start()
    up_swap.start()

    def add(i):
        here = cut_of(i, rows)
        summed[here, :] = (
            qkv_ref[cut_of(s * n + i, rows), :].astype(F32) + swapped[here, :].astype(F32)
        ).astype(BF16)

    loop(n, add)
    qkv_peers.start()
    load.wait(7)
    for i in range(chunks):
        cut = mp.cut(i)
        out_ref[cut, :] = resid_ref[cut, :] + mp2.rs_chunk(i)
    total_ref[...] = small.end(1)
    wout_peers.finish()
    wout_in[c] = wout_ref[cut_of(c, rows), :]
    total = jnp.zeros(gout_ref.shape, F32)
    for i in range(n):
        total = total + wout_in[i].astype(F32)
    gout_ref[...] = total
    mp.rs_end()
    mp2.rs_end()
    load.wait(8, 9, 10)
    for e in range(1, ex):
        lines[e - 1].finish(gate_ref.at[e])
    down_swap.wait()
    down_ref[...] = down_ref[...] + down_in[...].astype(F32)
    qkv_peers.finish()
    qkv_in[c] = summed[cut_of(c, rows), :]
    total = jnp.zeros(gqkv_ref.shape, F32)
    for i in range(n):
        total = total + qkv_in[i].astype(F32)
    gqkv_ref[...] = total
    up_swap.wait()
    up_ref[...] = up_ref[...] + up_in[...].astype(F32)


def cut_of(i, rows):
    return pl.ds(pl.multiple_of(i * rows, 16), rows)


def last(sizes, dqkv, h, wq, wk, wv, tokens, gain, dresid, small, wout, gate0, parts, down0, down_other, up0, up_other, comb, resid, chunks=2):
    k, share, width = comb.shape
    n = sizes[1]
    half_rows, fo = wout.shape
    fq = dqkv.shape[1]
    rows = half_rows // n
    sds = jax.ShapeDtypeStruct
    vm = lambda x: pltpu.VMEM(x.shape, x.dtype)
    return pl.pallas_call(
        functools.partial(last_kernel, chunks, sizes),
        out_shape=(
            sds((share, width), F32),
            sds((share, width), F32),
            sds(small.shape, F32),
            sds((rows, fo), F32),
            sds((rows, fq), F32),
            sds((parts.shape[0] + 1,) + gate0.shape, F32),
            sds(down0.shape, F32),
            sds(up0.shape, F32),
        ),
        in_specs=[VMEM] + [HBM] * 5 + [VMEM, HBM, VMEM, VMEM, HBM, VMEM, HBM, VMEM, HBM, VMEM, HBM, HBM],
        out_specs=(VMEM,) * 8,
        scratch_shapes=mp_scratch(share, width, chunks)
        + mp_scratch(share, width, chunks)
        + [vm(h), vm(wq), vm(wk), vm(wv), vm(tokens), vm(dresid), vm(comb), vm(resid)]
        + [
            pltpu.VMEM(comb.shape, BF16),
            pltpu.VMEM(comb.shape, F32),
            pltpu.VMEM((2 * half_rows, fq), BF16),
            pltpu.VMEM((half_rows, fq), BF16),
            pltpu.VMEM((half_rows, fq), BF16),
            pltpu.VMEM((n, rows, fo), BF16),
            pltpu.VMEM((n, rows, fq), BF16),
            pltpu.VMEM(down0.shape, BF16),
            pltpu.VMEM(up0.shape, BF16),
            pltpu.VMEM((parts.shape[0], n) + gate0.shape, BF16),
            pltpu.VMEM((parts.shape[0], n) + gate0.shape, BF16),
            DMA((11,)),
            DMA((2, 3)),
            DMA((4, n)),
            DMA((parts.shape[0], 2, 2, n)),
        ]
        + [pltpu.VMEM((d,) + small.shape, F32) for d in sizes]
        + [DMA((2, sum(sizes)))],
        compiler_params=params(4, 60),
        name="last",
        cost_estimate=cost(60),
    )(dqkv, h, wq, wk, wv, tokens, gain, dresid, small, wout, gate0, parts, down0, down_other, up0, up_other, comb, resid)


def half(x, s, dim):
    size = x.shape[dim] // 2
    return lax.dynamic_slice_in_dim(x, s * size, size, dim)


SWAP = [(0, 1), (1, 0)]


def body(
    tokens,
    norm1_gain,
    w_query,
    key_weight_matrix,
    value_weight_matrix,
    w_out,
    norm2_gain,
    router,
    w_gate,
    w_up,
    w_down,
    routes,
    cotangent,
):
    n_seq, n_ctx, n_mp = (lax.axis_size(a) for a in ("seq", "ctx", "mp"))
    s, c, m = (lax.axis_index(a) for a in ("seq", "ctx", "mp"))
    tok, width = tokens.shape
    share = tok // n_mp
    experts_all = router.shape[1]
    exp_local = w_gate.shape[0]
    top = routes.shape[1]
    cap = share * top * 5 // (4 * experts_all)
    slots = -(-n_mp * cap // 16) * 16
    gain1 = norm1_gain.reshape(1, width)
    gain2 = norm2_gain.reshape(1, width)

    cot_all = lax.all_gather(cotangent, "mp", axis=0, tiled=True)
    by_share = tokens.reshape(n_mp, share, width)

    normed_one, _ = rms_parts(tokens.astype(F32))
    h_one = (normed_one * gain1).astype(BF16)
    qt = (jnp.einsum("df,td->ft", w_query, h_one, preferred_element_type=F32).astype(BF16)) * BF16(0.125)
    k = nn(h_one, key_weight_matrix).astype(BF16)
    v = nn(h_one, value_weight_matrix).astype(BF16)
    o, heads_t, lse, kv, cot_above, routes_line = attend(n_ctx, qt, k, v, cotangent, routes.T)
    part = jnp.einsum("ft,fd->td", heads_t, w_out, preferred_element_type=F32).astype(BF16)
    resid, h_two, place, place_t, place_line, cot_line = mid_forward(
        n_ctx, exp_local, slots, part.reshape(n_mp, share, width), gain2, cotangent, cot_above, routes_line, by_share
    )
    h_two = h_two.reshape(tok, width)

    gates, gate_rows, arrived, hidden, dg, du, back, comb, arrived_line, cot_first, cot_line = moe(
        n_ctx, n_seq, experts_all, h_two, cot_all, place, place_t, routes, router, w_gate, w_up, w_down, cot_line
    )
    dresid, db, small, gate_rows_line, hidden_line, du_below, du_above, arrived_other, dg_other = mid_back(
        n_ctx,
        back.reshape(n_mp, share, -1),
        resid,
        gain2,
        cotangent,
        gates.reshape(n_mp, share, -1),
        router.T,
        gate_rows,
        hidden,
        du,
        arrived,
        dg,
    )

    db = db.reshape(tok, width)
    g_out = jnp.einsum("td,ft->df", db, heads_t, preferred_element_type=F32).astype(BF16)
    g_out = (
        half(g_out, s, 0).astype(F32) + lax.ppermute(half(g_out, 1 - s, 0), "seq", SWAP).astype(F32)
    ).astype(BF16)
    dqkv, gate0, gate_parts, down0, down_other, up0, up_other, _, _ = attend_back(
        n_ctx,
        qt,
        db,
        w_out,
        o,
        lse,
        kv,
        arrived,
        arrived_other,
        dg,
        dg_other,
        gate_rows_line,
        du,
        du_below,
        du_above,
        hidden_line,
        hidden,
        arrived_line,
        place_line,
        cot_line,
        cot_first,
    )
    output, grad_tokens, small, g_out, g_qkv, g_gate, g_down, g_up = last(
        (n_seq, n_ctx, n_mp),
        dqkv,
        h_one,
        w_query,
        key_weight_matrix,
        value_weight_matrix,
        by_share,
        gain1,
        dresid,
        small,
        g_out,
        gate0,
        gate_parts,
        down0,
        down_other,
        up0,
        up_other,
        comb.reshape(n_mp, share, width),
        resid,
    )
    qw, kvw = w_query.shape[1], key_weight_matrix.shape[1]
    return (
        output,
        grad_tokens,
        small[0],
        g_qkv[:, :qw],
        g_qkv[:, qw : qw + kvw],
        g_qkv[:, qw + kvw :],
        g_out.T,
        small[1],
        small[8 : 8 + experts_all].T,
        g_gate,
        g_up,
        g_down,
    )


def solution(mesh):
    placed = (
        P(("seq", "ctx"), None),
        P(),
        P(None, "mp"),
        P(None, "mp"),
        P(None, "mp"),
        P("mp", None),
        P(),
        P(),
        P("mp", None, None),
        P("mp", None, None),
        P("mp", None, None),
        P(("seq", "ctx"), None),
        P(("seq", "ctx", "mp"), None),
    )
    return jax.shard_map(
        body,
        mesh=mesh,
        in_specs=placed,
        out_specs=(
            P(("seq", "ctx", "mp"), None),
            P(("seq", "ctx", "mp"), None),
            P(),
            P(("seq", "ctx"), "mp"),
            P(("seq", "ctx"), "mp"),
            P(("seq", "ctx"), "mp"),
            P("mp", ("seq", "ctx")),
            P(),
            P(),
            P("mp", ("seq", "ctx"), None),
            P("mp", ("seq", "ctx"), None),
            P("mp", ("seq", "ctx"), None),
        ),
        check_vma=False,
    )
```

```python
import functools

import jax
import jax.numpy as jnp
from jax import lax
from jax.experimental import pallas as pl
from jax.experimental.pallas import tpu as pltpu
from jax.sharding import PartitionSpec as P

HEAD_SIZE = 64
EPS = 1e-06
MESH = pl.DeviceIdType.MESH
F32 = jnp.float32
BF16 = jnp.bfloat16
VMEM = pl.BlockSpec(memory_space=pltpu.VMEM)
HBM = pl.BlockSpec(memory_space=pl.ANY)
DMA = pltpu.SemaphoreType.DMA
MIB = 2**20


def cost(us):
    return pl.CostEstimate(flops=0, bytes_accessed=int(us * 3.6e6), transcendentals=0)


def params(collective_id, mib=56):
    return pltpu.CompilerParams(
        collective_id=collective_id, has_side_effects=True, vmem_limit_bytes=mib * MIB
    )


def nt(a, b):
    return lax.dot_general(a, b, (((1,), (1,)), ((), ())), preferred_element_type=F32)


def nn(a, b):
    return jnp.dot(a, b, preferred_element_type=F32)


class Staged:
    def __init__(self, pairs, sems):
        self.copies = [pltpu.make_async_copy(src, dst, sems.at[i]) for i, (src, dst) in enumerate(pairs)]

    def start(self):
        for copy in self.copies:
            copy.start()

    def wait(self, *which):
        for i in which:
            self.copies[i].wait()


class Spread:
    def __init__(self, n, own, below, above, all_ref, send, recv, local, short=False):
        self.n, self.own, self.below, self.above, self.all = n, own, below, above, all_ref
        self.send, self.recv, self.local = send, recv, local
        self.top = n - 2 if short else n - 1
        s, self.c, m = lax.axis_index("seq"), lax.axis_index("ctx"), lax.axis_index("mp")
        self.lower, self.upper = lax.rem(self.c + n - 1, n), lax.rem(self.c + 1, n)
        self.up, self.down = (s, self.upper, m), (s, self.lower, m)
        self.inner = jnp.logical_and(self.c > 0, self.c < n - 1)

    def move(self, b, src, device):
        return pltpu.make_async_remote_copy(
            src_ref=src,
            dst_ref=self.all.at[b],
            send_sem=self.send.at[b],
            recv_sem=self.recv.at[b],
            device_id=device,
            device_id_type=MESH,
        )

    def keep(self, i, src, b):
        return pltpu.make_async_copy(src, self.all.at[b], self.local.at[i])

    def goes_up(self, b):
        return jnp.logical_and(self.c < self.n - 1, self.c - b < self.top)

    def start(self):
        if self.below is None:

            @pl.when(self.c < self.n - 1)
            def _():
                self.move(self.c, self.own, self.up).start()
        else:

            @pl.when(jnp.logical_and(self.inner, self.goes_up(self.lower)))
            def _():
                self.move(self.lower, self.below, self.up).start()

            @pl.when(self.c > 0)
            def _():
                self.keep(1, self.below, self.lower).start()

        @pl.when(self.inner)
        def _():
            self.move(self.upper, self.above, self.down).start()

        self.keep(0, self.own, self.c).start()

        @pl.when(self.c < self.n - 1)
        def _():
            self.keep(2, self.above, self.upper).start()

    def tick(self, i):
        c, n = self.c, self.n
        off = i if self.below is None else i + 1

        @pl.when(jnp.logical_and(c - off >= 0, off <= self.top))
        def _():
            b = jnp.maximum(c - off, 0)
            self.move(b, self.all.at[b], self.up).wait_recv()

            @pl.when(self.goes_up(b))
            def _():
                self.move(b, self.all.at[b], self.up).start()

        @pl.when(c + 1 + i <= n - 1)
        def _():
            b = jnp.minimum(c + 1 + i, n - 1)
            self.move(b, self.all.at[b], self.down).wait_recv()

            @pl.when(c > 0)
            def _():
                self.move(b, self.all.at[b], self.down).start()

    def ticks(self, first):
        def later(i, carry):
            self.tick(i)
            return carry

        lax.fori_loop(first, self.n if self.below is None else self.n - 1, later, 0)

    def finish(self):
        self.keep(0, self.own, self.c).wait()

        if self.below is not None:

            @pl.when(self.c > 0)
            def _():
                self.keep(1, self.below, self.lower).wait()

        @pl.when(self.c < self.n - 1)
        def _():
            self.keep(2, self.above, self.upper).wait()

        def sent(b, carry):
            if self.below is None:
                sent_up = jnp.logical_and(b <= self.c, self.goes_up(b))
            else:
                sent_up = jnp.logical_and(b < self.c, self.goes_up(b))

            @pl.when(jnp.logical_or(sent_up, jnp.logical_and(b > self.c, self.c > 0)))
            def _():
                self.move(b, self.all.at[b], self.up).wait_send()

            return carry

        lax.fori_loop(0, self.n, sent, 0)


class Neighbours:
    def __init__(self, n, own, below, above, send, recv):
        self.n, self.own, self.below, self.above, self.send, self.recv = n, own, below, above, send, recv
        s, self.c, m = lax.axis_index("seq"), lax.axis_index("ctx"), lax.axis_index("mp")
        self.up, self.down = (s, lax.rem(self.c + 1, n), m), (s, lax.rem(self.c + n - 1, n), m)

    def move(self, way):
        return pltpu.make_async_remote_copy(
            src_ref=self.own,
            dst_ref=self.below if way == 0 else self.above,
            send_sem=self.send.at[way],
            recv_sem=self.recv.at[way],
            device_id=self.up if way == 0 else self.down,
            device_id_type=MESH,
        )

    def start_up(self):
        @pl.when(self.c < self.n - 1)
        def _():
            self.move(0).start()

    def start_down(self):
        @pl.when(self.c > 0)
        def _():
            self.move(1).start()

    def finish(self, up=True):
        @pl.when(self.c > 0)
        def _():
            if up:
                self.move(0).wait_recv()
            self.move(1).wait_send()

        @pl.when(self.c < self.n - 1)
        def _():
            self.move(1).wait_recv()
            if up:
                self.move(0).wait_send()


class LineSum:
    ahead = 2

    def __init__(self, n, parts, from_below, from_above, send, recv):
        self.n, self.parts, self.bufs, self.send, self.recv = n, parts, (from_below, from_above), send, recv
        s, self.c, m = lax.axis_index("seq"), lax.axis_index("ctx"), lax.axis_index("mp")
        self.up, self.down = (s, lax.rem(self.c + 1, n), m), (s, lax.rem(self.c + n - 1, n), m)
        self.ex, self.rows = from_below.shape[1], from_below.shape[2]
        self.units = (n - 1) * self.ex
        self.ticks = self.units + n - 3

    def own(self, k, e):
        return self.parts.at[e, pl.ds(pl.multiple_of(k * self.rows, 16), self.rows), :]

    def move(self, way, k, e, first=False):
        there = self.bufs[way].at[k, e]
        return pltpu.make_async_remote_copy(
            src_ref=self.own(k, e) if first else there,
            dst_ref=there,
            send_sem=self.send.at[way, k, e],
            recv_sem=self.recv.at[way, k, e],
            device_id=self.up if way == 0 else self.down,
            device_id_type=MESH,
        )

    def unit(self, way, u):
        k = lax.div(u, self.ex)
        return (self.n - 1 - k if way == 0 else k), lax.rem(u, self.ex)

    def first(self, u):
        for way, end in ((0, 0), (1, self.n - 1)):

            @pl.when(jnp.logical_and(self.c == end, u < self.units))
            def _():
                @pl.when(u >= self.ahead)
                def _():
                    self.move(way, *self.unit(way, jnp.maximum(u - self.ahead, 0)), True).wait_send()

                self.move(way, *self.unit(way, jnp.minimum(u, self.units - 1)), True).start()

    def tick(self, i):
        self.first(i + 1)
        for way, far in ((0, self.c), (1, self.n - 1 - self.c)):
            u = i - far

            @pl.when(jnp.logical_and(far > 0, jnp.logical_and(u >= 0, u < (self.n - 1 - far) * self.ex)))
            def _():
                k, e = self.unit(way, jnp.clip(u, 0, self.units - 1))
                self.move(way, k, e).wait_recv()
                self.bufs[way][k, e] = (
                    self.own(k, e)[...].astype(F32) + self.bufs[way][k, e].astype(F32)
                ).astype(BF16)
                self.move(way, k, e).start()

    def finish(self, out):
        c = self.c
        for e in range(self.ex):
            out[e] = self.own(c, e)[...].astype(F32)
        for way, far in ((0, c), (1, self.n - 1 - c)):

            @pl.when(far > 0)
            def _():
                for e in range(self.ex):
                    self.move(way, c, e).wait_recv()
                    out[e] = out[e] + self.bufs[way][c, e].astype(F32)

            done = jnp.where(far == 0, max(self.units - self.ahead, 0), 0)

            def sent(u, carry):
                self.move(way, *self.unit(way, u)).wait_send()
                return carry

            lax.fori_loop(done, (self.n - 1 - far) * self.ex, sent, 0)


class Peers:
    def __init__(self, n, src_of, dst_of, send, recv):
        self.n, self.src_of, self.dst_of, self.send, self.recv = n, src_of, dst_of, send, recv
        self.s, self.c, self.m = lax.axis_index("seq"), lax.axis_index("ctx"), lax.axis_index("mp")

    def move(self, d):
        peer = lax.rem(self.c + d, self.n)
        return pltpu.make_async_remote_copy(
            src_ref=self.src_of(peer),
            dst_ref=self.dst_of(self.c),
            send_sem=self.send.at[d],
            recv_sem=self.recv.at[d],
            device_id=(self.s, peer, self.m),
            device_id_type=MESH,
        )

    def signal(self, sem):
        for d in range(1, self.n):
            pl.semaphore_signal(
                sem, inc=1, device_id=(self.s, lax.rem(self.c + d, self.n), self.m), device_id_type=MESH
            )

    def start(self):
        for d in range(1, self.n):
            self.move(d).start()

    def finish(self):
        for d in range(1, self.n):
            self.move(d).wait()


class CotExchange:
    def __init__(self, n, line_ref, full, first, sems):
        self.n, self.line, self.full, self.first, self.sems = n, line_ref, full, first, sems
        self.count = full.shape[0]
        s, self.c, m = lax.axis_index("seq"), lax.axis_index("ctx"), lax.axis_index("mp")
        self.m = m
        self.share = line_ref.shape[1]
        self.sib = m + 1 - 2 * lax.rem(m, 2)
        self.opp = lax.rem(m + 2, 4)
        self.sib_id, self.opp_id = (s, self.c, self.sib), (s, self.c, self.opp)

    def signal(self, sem):
        for d in (self.sib_id, self.opp_id):
            pl.semaphore_signal(sem, inc=1, device_id=d, device_id_type=MESH)

    def place(self, i, who):
        return self.full.at[i, pl.ds(pl.multiple_of(who * self.share, 16), self.share), :]

    def mine(self, i):
        return self.line.at[lax.rem(self.c - self.first - i + 2 * self.n, self.n)]

    def move(self, kind, i):
        whose = self.opp if kind == 2 else self.m
        return pltpu.make_async_remote_copy(
            src_ref=self.place(i, self.opp) if kind == 2 else self.mine(i),
            dst_ref=self.place(i, whose),
            send_sem=self.sems.at[0, kind, i],
            recv_sem=self.sems.at[1, kind, i],
            device_id=self.opp_id if kind == 0 else self.sib_id,
            device_id_type=MESH,
        )

    def start(self):
        for i in range(self.count):
            self.move(0, i).start()
            self.move(1, i).start()

    def finish(self):
        for i in range(self.count):
            self.move(0, i).wait_recv()
            self.move(2, i).start()
        for i in range(self.count):
            self.move(1, i).wait_recv()
            self.move(2, i).wait_recv()
            for kind in range(3):
                self.move(kind, i).wait_send()


def signal_line(n, sem):
    s, c, m = lax.axis_index("seq"), lax.axis_index("ctx"), lax.axis_index("mp")

    @pl.when(c > 0)
    def _():
        pl.semaphore_signal(sem, inc=1, device_id=(s, lax.rem(c + n - 1, n), m), device_id_type=MESH)

    @pl.when(c < n - 1)
    def _():
        pl.semaphore_signal(sem, inc=1, device_id=(s, lax.rem(c + 1, n), m), device_id_type=MESH)


def line_degree(n):
    c = lax.axis_index("ctx")
    return jnp.where(c > 0, 1, 0) + jnp.where(c < n - 1, 1, 0)


def pad_heads(src, dst, heads, group):
    dst[...] = jnp.zeros_like(dst)
    for h in range(heads):
        g = h // group
        rows = slice(g * HEAD_SIZE, (g + 1) * HEAD_SIZE)
        dst[h, rows, :] = src[h * HEAD_SIZE : (h + 1) * HEAD_SIZE, :]


def causal(t):
    keys = lax.broadcasted_iota(jnp.int32, (t, t), 0)
    queries = lax.broadcasted_iota(jnp.int32, (t, t), 1)
    return keys <= queries


def attend_kernel(
    n,
    q_ref,
    k_ref,
    v_ref,
    cot_ref,
    routes_ref,
    o_ref,
    heads_ref,
    lse_ref,
    kv_ref,
    above_ref,
    line_ref,
    qpad,
    vt,
    top,
    tot,
    send,
    recv,
    side,
    peers_sem,
):
    s, c, m = lax.axis_index("seq"), lax.axis_index("ctx"), lax.axis_index("mp")
    t, kvw = k_ref.shape
    heads = q_ref.shape[0] // HEAD_SIZE
    group = heads // (kvw // HEAD_SIZE)
    up, down = (s, lax.rem(c + 1, n), m), (s, lax.rem(c + n - 1, n), m)
    kv_ref[0, :, :kvw] = k_ref[...]
    kv_ref[0, :, kvw:] = v_ref[...]
    line_ref[c] = routes_ref[...]
    peers = Peers(n, lambda p: routes_ref, lambda i: line_ref.at[i], peers_sem.at[0], peers_sem.at[1])
    beside = Neighbours(n, cot_ref, None, above_ref, side.at[0], side.at[1])
    sem = pltpu.get_barrier_semaphore()
    peers.signal(sem)
    pl.semaphore_wait(sem, n - 1)

    def pass_up(slot):
        return pltpu.make_async_remote_copy(
            src_ref=kv_ref.at[slot],
            dst_ref=kv_ref.at[slot + 1],
            send_sem=send.at[slot],
            recv_sem=recv.at[slot + 1],
            device_id=up,
            device_id_type=MESH,
        )

    def got(slot):
        return pltpu.make_async_remote_copy(
            src_ref=kv_ref.at[slot],
            dst_ref=kv_ref.at[slot],
            send_sem=send.at[slot],
            recv_sem=recv.at[slot],
            device_id=up,
            device_id_type=MESH,
        )

    @pl.when(c < n - 1)
    def _():
        pass_up(0).start()

    peers.start()
    beside.start_down()
    pad_heads(q_ref, qpad, heads, group)
    top[...] = jnp.full_like(top, -1e30)
    tot[...] = jnp.zeros_like(tot)
    o_ref[...] = jnp.zeros_like(o_ref)

    def block(slot, masked):
        vt[...] = kv_ref[slot, :, kvw:].T

        def head(h, carry):
            g = lax.div(h, group)
            scores = nn(kv_ref[slot, :, :kvw], qpad[h])
            if masked:
                scores = jnp.where(causal(t), scores, -1e30)
            old = top[h]
            new = jnp.maximum(old, jnp.max(scores, axis=0, keepdims=True))
            weights = jnp.exp(scores - new)
            factor = jnp.exp(old - new)
            top[h] = new
            tot[h] = tot[h] * factor + jnp.sum(weights, axis=0, keepdims=True)
            rows = pl.ds(pl.multiple_of(h * HEAD_SIZE, HEAD_SIZE), HEAD_SIZE)
            vrows = pl.ds(pl.multiple_of(g * HEAD_SIZE, HEAD_SIZE), HEAD_SIZE)
            o_ref[rows, :] = o_ref[rows, :] * factor + nn(vt[vrows, :], weights.astype(BF16))
            return carry

        lax.fori_loop(0, heads, head, 0)

    block(0, True)

    def earlier(slot, carry):
        got(slot).wait_recv()

        @pl.when(c < n - 1)
        def _():
            pass_up(slot).start()

        block(slot, False)
        return carry

    lax.fori_loop(1, c + 1, earlier, 0)
    for h in range(heads):
        rows = slice(h * HEAD_SIZE, (h + 1) * HEAD_SIZE)
        done = o_ref[rows, :] / tot[h]
        o_ref[rows, :] = done
        heads_ref[rows, :] = done.astype(BF16)
        lse_ref[h] = top[h] + jnp.log(tot[h])

    @pl.when(c < n - 1)
    def _():
        def sent(slot, carry):
            pass_up(slot).wait_send()
            return carry

        lax.fori_loop(0, c + 1, sent, 0)

    peers.finish()
    beside.finish(up=False)


def attend(n, qt, k, v, cot, routes):
    t, kvw = k.shape
    qw = qt.shape[0]
    heads = qw // HEAD_SIZE
    return pl.pallas_call(
        functools.partial(attend_kernel, n),
        out_shape=(
            jax.ShapeDtypeStruct((qw, t), F32),
            jax.ShapeDtypeStruct((qw, t), BF16),
            jax.ShapeDtypeStruct((heads, 1, t), F32),
            jax.ShapeDtypeStruct((n, t, 2 * kvw), BF16),
            jax.ShapeDtypeStruct(cot.shape, BF16),
            jax.ShapeDtypeStruct((n,) + routes.shape, jnp.int32),
        ),
        in_specs=[VMEM] * 3 + [HBM, VMEM],
        out_specs=(VMEM,) * 4 + (HBM, VMEM),
        scratch_shapes=[
            pltpu.VMEM((heads, kvw, t), BF16),
            pltpu.VMEM((kvw, t), BF16),
            pltpu.VMEM((heads, 1, t), F32),
            pltpu.VMEM((heads, 1, t), F32),
            DMA((n,)),
            DMA((n,)),
            DMA((2, 2)),
            DMA((2, n)),
        ],
        compiler_params=params(0),
        name="attend",
        cost_estimate=cost(30),
    )(qt, k, v, cot, routes)


def attend_back_kernel(
    n,
    q_ref,
    db_ref,
    wout_ref,
    o_ref,
    lse_ref,
    kv_ref,
    arr_ref,
    arr_other,
    dg_ref,
    dg_other,
    rows_line,
    own_ref,
    below_ref,
    above_ref,
    hid_hbm,
    hid_own,
    heads_ref,
    arr_hbm,
    place_hbm,
    line_hbm,
    first_hbm,
    dqkv_ref,
    gate_ref,
    down_ref,
    up_ref,
    up_other,
    wsum_ref,
    all_hbm,
    rest_hbm,
    do_ref,
    qpad,
    dopad,
    delta,
    dq,
    kt,
    part,
    passing,
    sum_ref,
    from_below,
    from_above,
    place_buf,
    cot_buf,
    hid_buf,
    arr_buf,
    du_buf,
    dy,
    acc_ref,
    kv_sem,
    sum_sem,
    spread_sem,
    local,
    ysem,
    load_sem,
    swap_sem,
    wout_part,
    wout_in,
    down_out,
    down_in,
):
    s, c, m = lax.axis_index("seq"), lax.axis_index("ctx"), lax.axis_index("mp")
    _, t, kvw2 = kv_ref.shape
    kvw = kvw2 // 2
    heads = q_ref.shape[0] // HEAD_SIZE
    group = heads // (kvw // HEAD_SIZE)
    ex, slots, width = arr_ref.shape
    half_width = width // 2
    down = (s, lax.rem(c + n - 1, n), m)
    spread = Spread(n, own_ref, below_ref, above_ref, all_hbm, spread_sem.at[0], spread_sem.at[1], local)
    done_blocks = first_hbm.shape[0]
    cots = CotExchange(n, line_hbm, rest_hbm, done_blocks, ysem)
    line = LineSum(n, sum_ref, from_below, from_above, sum_sem.at[0], sum_sem.at[1])
    sem = pltpu.get_barrier_semaphore()
    signal_line(n, sem)
    cots.signal(sem)
    pl.semaphore_signal(sem, inc=1, device_id=swap_partner(), device_id_type=MESH)
    pl.semaphore_wait(sem, line_degree(n) + 3)
    spread.start()
    cots.start()

    def gate_part(e, out):
        def piece(r):
            mine = pl.ds(pl.multiple_of(s * half_width + r * 256, 128), 256)
            cut = pl.ds(pl.multiple_of(r * 256, 256), 256)
            out[cut, :] = (tn(arr_ref[e, :, mine], dg_ref[e]) + tn(arr_other[e, :, cut], dg_other[e])).astype(BF16)

        loop(half_width // 256, piece)

    for e in range(ex):
        gate_part(e, sum_ref.at[e])
        if e == 0:
            line.first(0)
    do_ref[...] = nt(wout_ref[...], db_ref[...]).astype(BF16)

    def wout_piece(r):
        at = pl.ds(pl.multiple_of(r * 512, 512), 512)
        wout_part[:, at] = nn(heads_ref[...], db_ref[:, at]).astype(BF16)

    loop(width // 512, wout_piece)
    own_half, other_half = (pl.ds(pl.multiple_of(k * half_width, 128), half_width) for k in (s, 1 - s))
    wout_swap = swap(wout_part.at[:, other_half], wout_in, swap_sem, 0)
    wout_swap.start()

    def tick(i):
        line.tick(i)
        for hop in range(1, n - 1):

            @pl.when(i == 2 * hop - 1)
            def _():
                spread.tick(hop)

    ticks = max(line.ticks, 2 * (n - 2)) + 1
    pad_heads(q_ref, qpad, heads, group)
    pad_heads(do_ref, dopad, heads, group)
    for h in range(heads):
        rows = slice(h * HEAD_SIZE, (h + 1) * HEAD_SIZE)
        delta[h] = jnp.sum(do_ref[rows, :].astype(F32) * o_ref[rows, :], axis=0, keepdims=True)
    dq[...] = jnp.zeros_like(dq)

    def block(j, masked):
        slot = c - j
        acc = part.at[lax.rem(j, 2)]
        acc[...] = jnp.zeros(acc.shape, F32)
        kt[...] = kv_ref[slot, :, :kvw].T

        def head(h, carry):
            g = lax.div(h, group)
            scores = nn(kv_ref[slot, :, :kvw], qpad[h])
            probs = jnp.exp(scores - lse_ref[h])
            if masked:
                probs = jnp.where(causal(t), probs, 0.0)
            dprobs = nn(kv_ref[slot, :, kvw:], dopad[h])
            ds = (probs * (dprobs - delta[h])).astype(BF16)
            rows = pl.ds(pl.multiple_of(h * HEAD_SIZE, HEAD_SIZE), HEAD_SIZE)
            krows = pl.ds(pl.multiple_of(g * HEAD_SIZE, HEAD_SIZE), HEAD_SIZE)
            dq[rows, :] = dq[rows, :] + nn(kt[krows, :], ds)
            acc[:, :kvw] = acc[:, :kvw] + nt(ds, qpad[h])
            acc[:, kvw:] = acc[:, kvw:] + nt(probs.astype(BF16), dopad[h])
            return carry

        lax.fori_loop(0, heads, head, 0)

    def pass_down(j):
        return pltpu.make_async_remote_copy(
            src_ref=passing.at[j],
            dst_ref=passing.at[j],
            send_sem=kv_sem.at[0, j],
            recv_sem=kv_sem.at[1, j],
            device_id=down,
            device_id_type=MESH,
        )

    def gathered(j):
        acc = part.at[lax.rem(j, 2)]

        @pl.when(c < n - 1)
        def _():
            pass_down(j).wait_recv()
            acc[...] = acc[...] + passing[j].astype(F32)

        return acc

    def forward(j):
        acc = gathered(j)
        passing[j] = acc[...].astype(BF16)
        pass_down(j).start()

    def step(j, carry):
        block(j, False)

        @pl.when(jnp.logical_and(j > 0, c < n - 1))
        def _():
            forward(j - 1)

        @pl.when(c == n - 1)
        def _():
            forward(j)

        tick(j)
        return carry

    lax.fori_loop(0, c, step, 0)
    def later(i, carry):
        tick(i)
        return carry

    middle = jnp.maximum(c, min(2, ticks))
    lax.fori_loop(c, middle, later, 0)

    cots.finish()

    def load_block(i, slot, start):
        b = lax.rem(c - i + n, n)
        share = line_hbm.shape[1]
        place_copy = pltpu.make_async_copy(place_hbm.at[b], place_buf.at[slot], load_sem.at[0, slot])
        hid_copy = pltpu.make_async_copy(hid_hbm.at[b], hid_buf.at[slot], load_sem.at[1, slot])
        hid_mine = pltpu.make_async_copy(hid_own.at[b], hid_buf.at[slot], load_sem.at[1, slot])

        def rows(who):
            return pl.ds(pl.multiple_of(who * share, 16), share)

        def piece(k, who, full, at):
            return pltpu.make_async_copy(
                full.at[at, rows(who), :], cot_buf.at[slot, rows(who), :], load_sem.at[2 + k, slot]
            )

        others = (cots.sib, cots.opp, lax.rem(cots.sib + 2, 4))
        mine = pltpu.make_async_copy(line_hbm.at[b], cot_buf.at[slot, rows(m), :], load_sem.at[5, slot])
        first = [piece(k, who, first_hbm, jnp.minimum(i, done_blocks - 1)) for k, who in enumerate(others)]
        if not start:
            for copy in [place_copy, hid_copy, mine] + first:
                copy.wait()
            return
        rest = [piece(k, who, rest_hbm, jnp.maximum(i - done_blocks, 0)) for k, who in enumerate(others)]
        place_copy.start()
        mine.start()

        @pl.when(b == c)
        def _():
            hid_mine.start()

        @pl.when(b != c)
        def _():
            hid_copy.start()

        @pl.when(i < done_blocks)
        def _():
            for copy in first:
                copy.start()

        @pl.when(i >= done_blocks)
        def _():
            for copy in rest:
                copy.start()

    fa, ua = hid_hbm.shape[3], arr_hbm.shape[3]
    ff = dg_ref.shape[2]
    acc_ref[...] = jnp.zeros_like(acc_ref)
    load_block(0, 0, True)
    wide = 512

    def down_block(i):
        slot = lax.rem(i, 2)
        load_block(i, slot, False)

        @pl.when(i < n - 1)
        def _():
            load_block(i + 1, 1 - slot, True)

        cols = rows_line[lax.rem(c - i + n, n)].T
        for e in range(ex):

            def dys(k):
                cut = pl.ds(pl.multiple_of(k * wide, wide), wide)
                dy[:, cut] = (
                    cols[:slots, e : e + 1] * nn(place_buf[slot, e * slots : (e + 1) * slots, :], cot_buf[slot, :, cut])
                ).astype(BF16)

            loop(width // wide, dys)
            acc_ref[e, :fa, :] = acc_ref[e, :fa, :] + tn(hid_buf[slot, e], dy[...])

    loop(n, down_block)
    mine, other = (pl.ds(pl.multiple_of(k * (fa // 2), 16), fa // 2) for k in (s, 1 - s))
    down_ref[...] = acc_ref[:, mine, :]
    down_out[...] = acc_ref[:, other, :].astype(BF16)
    wout_swap.wait()
    down_swap = swap(down_out, down_in, swap_sem, 1)
    down_swap.start()
    wsum_ref[...] = (wout_part[:, own_half].astype(F32) + wout_in[...].astype(F32)).astype(BF16).T

    after = jnp.minimum(middle + 1, ticks)
    lax.fori_loop(middle, after, later, 0)
    block(c, True)

    @pl.when(jnp.logical_and(c > 0, c < n - 1))
    def _():
        forward(c - 1)

    qw = dq.shape[0]
    dqkv_ref[:, :qw] = (dq[...] * 0.125).astype(BF16).T
    lax.fori_loop(after, ticks, later, 0)

    spread.finish()
    acc_ref[...] = jnp.zeros_like(acc_ref)

    def load_du(b, slot):
        return (
            pltpu.make_async_copy(all_hbm.at[b], du_buf.at[slot], load_sem.at[6, slot]),
            pltpu.make_async_copy(arr_hbm.at[b], arr_buf.at[slot], load_sem.at[7, slot]),
        )

    for copy in load_du(0, 0):
        copy.start()

    def up_block(b):
        slot = lax.rem(b, 2)
        for copy in load_du(b, slot):
            copy.wait()

        @pl.when(b < n - 1)
        def _():
            for copy in load_du(b + 1, 1 - slot):
                copy.start()

        for e in range(ex):
            acc_ref[e, :ua, :ff] = acc_ref[e, :ua, :ff] + tn(arr_buf[slot, e], du_buf[slot, e])

    loop(n, up_block)
    mine, other = (pl.ds(pl.multiple_of(k * (ua // 2), 16), ua // 2) for k in (s, 1 - s))
    up_ref[...] = acc_ref[:, mine, :ff]
    up_other[...] = acc_ref[:, other, :ff].astype(BF16)

    acc = gathered(c)
    dqkv_ref[:, qw:] = acc[...].astype(BF16)
    line.finish(gate_ref)
    down_swap.wait()
    down_ref[...] = down_ref[...] + down_in[...].astype(F32)

    def sent_kv(j, carry):
        pass_down(j).wait_send()
        return carry

    lax.fori_loop(0, c, sent_kv, 0)


def attend_back(n, qt, db, w_out, o, lse, kv, arr, arr_other, dg, dg_other, rows, du, below, above, hid, hid_own, heads_t, arr_line, place, line, first):
    qw, t = qt.shape
    heads = qw // HEAD_SIZE
    kvw = kv.shape[2] // 2
    ex, slots, width = arr.shape
    ff = dg.shape[2]
    half_width = width // 2
    chunk = (ex, half_width // n, ff)
    fa, ua = hid.shape[3], arr_line.shape[3]
    blocks = first.shape[0]
    sds = jax.ShapeDtypeStruct
    return pl.pallas_call(
        functools.partial(attend_back_kernel, n),
        out_shape=(
            sds((t, qw + 2 * kvw), BF16),
            sds(chunk, F32),
            sds((ex, fa // 2, width), F32),
            sds((ex, ua // 2, ff), F32),
            sds((ex, ua // 2, ff), BF16),
            sds((half_width, qw), BF16),
            sds((n,) + du.shape, BF16),
            sds((n - blocks,) + first.shape[1:], BF16),
        ),
        in_specs=[VMEM] * 14 + [HBM] * 2 + [VMEM] + [HBM] * 4,
        out_specs=(VMEM,) * 6 + (HBM,) * 2,
        scratch_shapes=[
            pltpu.VMEM((qw, t), BF16),
            pltpu.VMEM((heads, kvw, t), BF16),
            pltpu.VMEM((heads, kvw, t), BF16),
            pltpu.VMEM((heads, 1, t), F32),
            pltpu.VMEM((qw, t), F32),
            pltpu.VMEM((kvw, t), BF16),
            pltpu.VMEM((2, t, 2 * kvw), F32),
            pltpu.VMEM((n, t, 2 * kvw), BF16),
            pltpu.VMEM((ex, half_width, ff), BF16),
            pltpu.VMEM((n,) + chunk, BF16),
            pltpu.VMEM((n,) + chunk, BF16),
            pltpu.VMEM((2,) + place.shape[1:], BF16),
            pltpu.VMEM((2,) + first.shape[1:], BF16),
            pltpu.VMEM((2, ex, slots, fa), BF16),
            pltpu.VMEM((2, ex, slots, ua), BF16),
            pltpu.VMEM((2,) + du.shape, BF16),
            pltpu.VMEM((slots, width), BF16),
            pltpu.VMEM((ex, max(fa, ua), width), F32),
            DMA((2, n)),
            DMA((2, 2, n, ex)),
            DMA((2, n)),
            DMA((3,)),
            DMA((2, 3, n - blocks)),
            DMA((8, 2)),
            DMA((2, 2)),
            pltpu.VMEM((qw, width), BF16),
            pltpu.VMEM((qw, half_width), BF16),
            pltpu.VMEM((ex, fa // 2, width), BF16),
            pltpu.VMEM((ex, fa // 2, width), BF16),
        ],
        compiler_params=params(1, 62),
        name="attend_back",
        cost_estimate=cost(60),
    )(qt, db, w_out, o, lse, kv, arr, arr_other, dg, dg_other, rows, du, below, above, hid, hid_own, heads_t, arr_line, place, line, first)


def tn(a, b):
    return lax.dot_general(a, b, (((0,), (0,)), ((), ())), preferred_element_type=F32)


def loop(n, f):
    def step(i, carry):
        f(i)
        return carry

    lax.fori_loop(0, n, step, 0)


def moe_kernel(
    n,
    n_seq,
    experts_all,
    h_ref,
    cot_ref,
    place_ref,
    place_t_ref,
    routes_ref,
    router_ref,
    wg_hbm,
    wu_hbm,
    wd_hbm,
    line_hbm,
    gates_ref,
    rows_ref,
    arr_ref,
    hid_ref,
    dg_ref,
    du_ref,
    back_ref,
    comb_ref,
    arr_line,
    cot_first,
    line_out,
    wg,
    wu,
    wd,
    dout,
    dy,
    hid,
    back_rows,
    comb_rows,
    parts,
    cols,
    wsem,
    peers_sem,
    ysem,
    local,
    far_sem,
    router3,
    named,
):
    s, c, m = lax.axis_index("seq"), lax.axis_index("ctx"), lax.axis_index("mp")
    ex, width, ff = wg.shape
    slots = place_ref.shape[0] // ex
    first = m * ex
    lanes = gates_ref.shape[1]
    peers = Peers(n, lambda p: parts.at[p], lambda i: arr_line.at[i], peers_sem.at[0], peers_sem.at[1])
    cots = CotExchange(n, line_hbm, cot_first, 0, ysem)
    far = pltpu.make_async_remote_copy(
        src_ref=line_hbm.at[0],
        dst_ref=line_out.at[0],
        send_sem=far_sem.at[0],
        recv_sem=far_sem.at[1],
        device_id=(s, lax.rem(c + 1, n), m),
        device_id_type=MESH,
    )
    sem = pltpu.get_barrier_semaphore()
    peers.signal(sem)
    cots.signal(sem)
    weights = {}
    for e in range(ex):
        for i, (src, dst) in enumerate(((wg_hbm, wg), (wu_hbm, wu), (wd_hbm, wd))):
            weights[i, e] = pltpu.make_async_copy(src.at[e], dst.at[e], wsem.at[i, e])
            weights[i, e].start()

    pl.semaphore_wait(sem, n - 1 + 2)
    cots.start()

    @pl.when(c == n - 2)
    def _():
        far.start()

    def rows_of(e):
        return slice(e * slots, (e + 1) * slots)

    def arrive(i):
        cut = pl.ds(pl.multiple_of(i * slots, 16), slots)
        arr_ref[i] = nn(place_ref[cut, :], h_ref[...]).astype(BF16)

    loop(ex, arrive)
    size = width // (n * n_seq)
    for e in range(ex):
        for i in range(n):
            for j in range(n_seq):
                at = (j * n + i) * size
                parts[i, e, :, j * size : (j + 1) * size] = arr_ref[e, :, at : at + size]
    peers.start()
    own = pltpu.make_async_copy(parts.at[c], arr_line.at[c], local.at[0])
    own.start()

    router3[...] = jnp.zeros_like(router3)
    left = router_ref[...]
    for i in range(3):
        piece = left.astype(BF16)
        router3[i * experts_all : (i + 1) * experts_all, :] = piece
        left = left - piece.astype(F32)
    three = nt(h_ref[...], router3[...])
    logits = three + pltpu.roll(three, lanes - experts_all, 1) + pltpu.roll(three, lanes - 2 * experts_all, 1)
    which = lax.broadcasted_iota(jnp.int32, three.shape, 1)
    top = routes_ref.shape[0]
    named[...] = jnp.zeros_like(named)
    named[:top, :] = routes_ref[...].astype(F32)
    columns = named[...].T
    which = which.astype(F32)
    chosen = which == columns[:, 0:1]
    for k in range(1, top):
        chosen = jnp.logical_or(chosen, which == columns[:, k : k + 1])
    peak = jnp.max(jnp.where(chosen, logits, -1e30), axis=1, keepdims=True)
    raised = jnp.where(chosen, jnp.exp(jnp.where(chosen, logits - peak, 0.0)), 0.0)
    gates = raised / jnp.sum(raised, axis=1, keepdims=True)
    gates_ref[...] = gates
    g1 = gates.astype(BF16)
    rest = gates - g1.astype(F32)
    g2 = rest.astype(BF16)
    g3 = (rest - g2.astype(F32)).astype(BF16)
    lane = lax.broadcasted_iota(jnp.int32, (slots, lanes), 1)
    cols[...] = jnp.zeros_like(cols)
    gate_col = []
    for e in range(ex):
        pe = place_ref[rows_of(e), :]
        got = nn(pe, g1) + nn(pe, g2) + nn(pe, g3)
        col = jnp.sum(jnp.where(lane == first + e, got, 0.0), axis=1, keepdims=True)
        gate_col.append(col)
        cols[:slots, :] = cols[:slots, :] + jnp.where(lane == e, col, 0.0)

    rows_ref[...] = cols[...].T[:8, :]
    wide = 512
    for e in range(ex):
        col = gate_col[e]

        def douts(i):
            cut = pl.ds(pl.multiple_of(i * wide, wide), wide)
            d = nn(place_ref[rows_of(e), :], cot_ref[:, cut])
            dout[e, :, cut] = d.astype(BF16)
            dy[e, :, cut] = (col * d).astype(BF16)

        loop(width // wide, douts)
        for i in range(3):
            weights[i, e].wait()

        def hidden(i):
            cut = pl.ds(pl.multiple_of(i * 256, 256), 256)
            g = nn(arr_ref[e], wg[e, :, cut])
            u = nn(arr_ref[e], wu[e, :, cut])
            dh = nt(dy[e], wd[e, cut, :])
            sigma = jax.nn.sigmoid(g)
            silu = g * sigma
            hid[:, cut] = (silu * u).astype(BF16)
            dg_ref[e, :, cut] = (dh * u * sigma * (1.0 + g * (1.0 - sigma))).astype(BF16)
            du_ref[e, :, cut] = (dh * silu).astype(BF16)

        loop(ff // 256, hidden)
        size = ff // (n * n_seq)
        for i in range(n):
            for j in range(n_seq):
                at = (j * n + i) * size
                hid_ref[i, e, :, j * size : (j + 1) * size] = hid[:, at : at + size]

        def outs(i, grads):
            cut = pl.ds(pl.multiple_of(i * wide, wide), wide)
            y = nn(hid[...], wd[e, :, cut]).astype(BF16).astype(F32)
            comb_rows[rows_of(e), cut] = (col * y).astype(BF16)
            back_rows[rows_of(e), cut] = (nt(dg_ref[e], wg[e, cut, :]) + nt(du_ref[e], wu[e, cut, :])).astype(BF16)
            return grads + jnp.sum(dout[e, :, cut].astype(F32) * y, axis=1, keepdims=True)

        grads = lax.fori_loop(0, width // wide, outs, jnp.zeros((slots, 1), F32))
        high = grads.astype(BF16).astype(F32)
        here = jnp.where(lane == first + e, high, jnp.where(lane == lanes // 2 + first + e, grads - high, 0.0))
        back_rows[rows_of(e), width:] = here.astype(BF16)

    def scatter(i):
        cut = pl.ds(pl.multiple_of(i * 256, 256), 256)
        back_ref[:, cut] = nn(place_t_ref[...], back_rows[:, cut]).astype(BF16)
        comb_ref[:, cut] = nn(place_t_ref[...], comb_rows[:, cut]).astype(BF16)

    loop(width // 256, scatter)
    back_ref[:, width:] = nn(place_t_ref[...], back_rows[:, width:]).astype(BF16)
    own.wait()
    cots.finish()
    peers.finish()

    @pl.when(c == n - 2)
    def _():
        far.wait_send()

    @pl.when(c == n - 1)
    def _():
        far.wait_recv()


def moe(n, n_seq, experts_all, h, cot, place, place_t, routes, router, wg, wu, wd, line):
    ex, width, ff = wg.shape
    tok = h.shape[0]
    slots = place.shape[0] // ex
    blocks = n // 2
    sds = jax.ShapeDtypeStruct
    return pl.pallas_call(
        functools.partial(moe_kernel, n, n_seq, experts_all),
        out_shape=(
            sds((tok, 128), F32),
            sds((8, 256), F32),
            sds((ex, slots, width), BF16),
            sds((n, ex, slots, ff // n), BF16),
            sds((ex, slots, ff), BF16),
            sds((ex, slots, ff), BF16),
            sds((tok, width + 128), BF16),
            sds((tok, width), BF16),
            sds((n, ex, slots, width // n), BF16),
            sds((blocks, tok, width), BF16),
            sds(line.shape, BF16),
        ),
        in_specs=[VMEM] * 6 + [HBM] * 4,
        out_specs=(VMEM,) * 8 + (HBM,) * 3,
        scratch_shapes=[
            pltpu.VMEM(wg.shape, BF16),
            pltpu.VMEM(wu.shape, BF16),
            pltpu.VMEM(wd.shape, BF16),
            pltpu.VMEM((ex, slots, width), BF16),
            pltpu.VMEM((ex, slots, width), BF16),
            pltpu.VMEM((slots, ff), BF16),
            pltpu.VMEM((ex * slots, width + 128), BF16),
            pltpu.VMEM((ex * slots, width), BF16),
            pltpu.VMEM((n, ex, slots, width // n), BF16),
            pltpu.VMEM((256, 128), F32),
            DMA((3, ex)),
            DMA((2, n)),
            DMA((2, 3, blocks)),
            DMA((1,)),
            DMA((2,)),
            pltpu.VMEM((128, width), BF16),
            pltpu.VMEM((8, tok), F32),
        ],
        input_output_aliases={9: 10},
        compiler_params=params(6, 60),
        name="moe",
        cost_estimate=cost(30),
    )(h, cot, place, place_t, routes, router, wg, wu, wd, line)


class Mp:
    def __init__(self, part, core_in, y_out, y_in, full, sems, chunks):
        self.part, self.core_in, self.y_out, self.y_in, self.full = part, core_in, y_out, y_in, full
        self.sems, self.chunks = sems, chunks
        s, c, m = lax.axis_index("seq"), lax.axis_index("ctx"), lax.axis_index("mp")
        self.m = m
        self.sib = m + 1 - 2 * lax.rem(m, 2)
        self.opp = lax.rem(m + 2, 4)
        self.diag = lax.rem(self.sib + 2, 4)
        self.sib_id, self.opp_id = (s, c, self.sib), (s, c, self.opp)
        share = (part if part is not None else full).shape[1]
        self.rows = share // chunks

    def signal(self, sem):
        for d in (self.sib_id, self.opp_id):
            pl.semaphore_signal(sem, inc=1, device_id=d, device_id_type=MESH)

    def copy(self, src, dst, i, dev):
        return pltpu.make_async_remote_copy(
            src_ref=src,
            dst_ref=dst,
            send_sem=self.sems.at[0, i],
            recv_sem=self.sems.at[1, i],
            device_id=dev,
            device_id_type=MESH,
        )

    def cut(self, i):
        return pl.ds(i * self.rows, self.rows)

    def rs_core(self, i):
        src = self.part.at[self.diag] if i == 0 else self.part.at[self.sib]
        return self.copy(src, self.core_in.at[i], i, self.sib_id)

    def rs_y(self, i):
        return self.copy(self.y_out.at[self.cut(i)], self.y_in.at[self.cut(i)], 2 + i, self.opp_id)

    def rs_begin(self):
        self.rs_core(0).start()
        self.rs_core(1).start()
        self.rs_forward()

    def rs_forward(self):
        self.rs_core(0).wait_recv()
        for i in range(self.chunks):
            cut = self.cut(i)
            self.y_out[cut, :] = (
                self.part[self.opp, cut, :].astype(F32) + self.core_in[0, cut, :].astype(F32)
            ).astype(BF16)
            self.rs_y(i).start()
        self.rs_core(1).wait_recv()

    def rs_chunk(self, i):
        cut = self.cut(i)
        self.rs_y(i).wait_recv()
        return (
            self.part[self.m, cut, :].astype(F32) + self.core_in[1, cut, :].astype(F32)
        ) + self.y_in[cut, :].astype(F32)

    def rs_end(self):
        self.rs_core(0).wait_send()
        self.rs_core(1).wait_send()
        for i in range(self.chunks):
            self.rs_y(i).wait_send()

    def ag(self, kind, i, whose):
        block = self.full.at[whose, self.cut(i)]
        base = 2 + self.chunks
        dev = self.opp_id if kind == 0 else self.sib_id
        return self.copy(block, block, base + kind * self.chunks + i, dev)

    def ag_send(self, i):
        self.ag(0, i, self.m).start()
        self.ag(1, i, self.m).start()

    def ag_end(self):
        for i in range(self.chunks):
            self.ag(0, i, self.opp).wait_recv()
            self.ag(2, i, self.opp).start()
        for i in range(self.chunks):
            self.ag(1, i, self.sib).wait_recv()
            self.ag(2, i, self.diag).wait_recv()
            self.ag(0, i, self.m).wait_send()
            self.ag(1, i, self.m).wait_send()
            self.ag(2, i, self.opp).wait_send()


def mp_scratch(share, width, chunks):
    return [
        pltpu.VMEM((2, share, width), BF16),
        pltpu.VMEM((share, width), BF16),
        pltpu.VMEM((share, width), BF16),
        DMA((2, 2 + 4 * chunks)),
    ]


def rms_parts(rows):
    inverse = lax.rsqrt(jnp.mean(rows * rows, axis=-1, keepdims=True) + EPS)
    return rows * inverse, inverse


def rms_grad(grad_normed, normed, inverse):
    return inverse * (grad_normed - normed * jnp.mean(grad_normed * normed, axis=-1, keepdims=True))


def mid_forward_kernel(
    chunks,
    n,
    ex,
    heads_ref,
    wout_ref,
    gain,
    own,
    above,
    routes_ref,
    tok_hbm,
    resid_ref,
    h_ref,
    place_ref,
    place_t,
    place_line,
    line_ref,
    core_in,
    y_out,
    y_in,
    sems,
    send,
    recv,
    local,
    x_ref,
    x_sem,
    ranks,
    part,
):
    c = lax.axis_index("ctx")
    mp = Mp(part, core_in, y_out, y_in, h_ref, sems, chunks)
    spread = Spread(n, own, None, above, line_ref, send, recv, local, short=True)
    x_copy = pltpu.make_async_copy(tok_hbm.at[mp.m], x_ref, x_sem.at[0])
    x_copy.start()
    sem = pltpu.get_barrier_semaphore()
    mp.signal(sem)
    signal_line(n, sem)
    share, width = x_ref.shape

    def outs(i):
        at = pl.ds(pl.multiple_of(i * 512, 512), 512)
        rows = tn(heads_ref[...], wout_ref[:, at]).astype(BF16)
        for p in range(part.shape[0]):
            part[p, :, at] = rows[p * share : (p + 1) * share, :]

    loop(width // 512, outs)
    pl.semaphore_wait(sem, 2 + line_degree(n))
    mp.rs_core(0).start()
    mp.rs_core(1).start()
    spread.start()
    mp.rs_forward()
    tok = routes_ref.shape[2]
    slots = place_ref.shape[0] // ex
    before = (
        lax.broadcasted_iota(jnp.int32, (tok, tok), 0) <= lax.broadcasted_iota(jnp.int32, (tok, tok), 1)
    ).astype(BF16)

    def places(b):
        at = b * ex
        ranks[...] = jnp.zeros_like(ranks)
        for e in range(ex):
            hit = routes_ref[b] == mp.m * ex + e
            ranks[e : e + 1, :] = jnp.max(hit.astype(F32), axis=0, keepdims=True)
        sel = ranks[...]
        order = nn(sel.astype(BF16), before) - 1.0
        rows = lax.broadcasted_iota(jnp.int32, (slots, tok), 0).astype(F32)
        for e in range(ex):
            one = jnp.where(rows == order[e : e + 1, :], 1.0, 0.0) * sel[e : e + 1, :]
            place_line[b, e * slots : (e + 1) * slots, :] = one.astype(BF16)

    places(c)
    place_ref[...] = place_line[c]
    place_t[...] = place_ref[...].T
    x_copy.wait()
    for i in range(chunks):
        cut = mp.cut(i)
        resid = x_ref[cut, :].astype(F32) + mp.rs_chunk(i)
        resid_ref[cut, :] = resid
        normed, _ = rms_parts(resid)
        h_ref[mp.m, cut, :] = (normed * gain[...].reshape(1, -1)).astype(BF16)
        mp.ag_send(i)
    spread.tick(1)
    loop(n - 1, lambda i: places(lax.rem(c + 1 + i, n)))
    mp.ag_end()
    mp.rs_end()
    spread.ticks(2)
    spread.finish()


def mid_forward(n, ex, slots, heads_t, w_out, gain, own, above, routes_line, tokens, chunks=2):
    k, share, width = tokens.shape
    tok = k * share
    sds = jax.ShapeDtypeStruct
    return pl.pallas_call(
        functools.partial(mid_forward_kernel, chunks, n, ex),
        out_shape=(
            sds((share, width), F32),
            sds(tokens.shape, BF16),
            sds((ex * slots, tok), BF16),
            sds((tok, ex * slots), BF16),
            sds((n, ex * slots, tok), BF16),
            sds((n,) + own.shape, BF16),
        ),
        in_specs=[VMEM] * 6 + [HBM],
        out_specs=(VMEM,) * 5 + (HBM,),
        scratch_shapes=mp_scratch(share, width, chunks)
        + [DMA((n,)), DMA((n,)), DMA((3,)), pltpu.VMEM((share, width), BF16), DMA((1,)), pltpu.VMEM((8, tok), F32)]
        + [pltpu.VMEM(tokens.shape, BF16)],
        compiler_params=params(2, 58),
        name="mid_forward",
        cost_estimate=cost(30),
    )(heads_t, w_out, gain, own, above, routes_line, tokens)


def mid_back_kernel(
    chunks,
    n,
    part,
    resid_ref,
    gain,
    cot,
    gate_ref,
    router_ref,
    rows_ref,
    hid_ref,
    du_ref,
    arr_ref,
    dg_ref,
    dresid_ref,
    db_ref,
    small_ref,
    rows_line,
    hid_line,
    below_ref,
    above_ref,
    arr_other,
    dg_other,
    core_in,
    y_out,
    y_in,
    sems,
    side,
    peers_sem,
    swap_sem,
):
    c = lax.axis_index("ctx")
    mp = Mp(part, core_in, y_out, y_in, db_ref, sems, chunks)
    rows_peers = Peers(n, lambda p: rows_ref, lambda i: rows_line.at[i], peers_sem.at[0], peers_sem.at[1])
    hid_peers = Peers(n, lambda p: hid_ref.at[p], lambda i: hid_line.at[i], peers_sem.at[2], peers_sem.at[3])
    beside = Neighbours(n, du_ref, below_ref, above_ref, side.at[0], side.at[1])
    width = gain.shape[0]
    ex = router_ref.shape[0]
    lanes = gate_ref.shape[2]
    sem = pltpu.get_barrier_semaphore()
    mp.signal(sem)
    rows_peers.signal(sem)
    partner = swap_partner()
    pl.semaphore_signal(sem, inc=1, device_id=partner, device_id_type=MESH)
    pl.semaphore_wait(sem, 2 + n - 1 + 1)
    mp.rs_core(0).start()
    mp.rs_core(1).start()
    half_width = width // 2
    theirs = pl.ds(pl.multiple_of((1 - lax.axis_index("seq")) * half_width, 128), half_width)
    swaps = [
        swap(arr_ref.at[:, :, theirs], arr_other, swap_sem, 0),
        swap(dg_ref, dg_other, swap_sem, 1),
    ]
    for sw in swaps:
        sw.start()
    beside.start_up()
    beside.start_down()
    rows_peers.start()
    hid_peers.start()
    mp.rs_forward()
    rows_line[c] = rows_ref[...]
    small_ref[...] = jnp.zeros_like(small_ref)
    for i in range(chunks):
        cut = mp.cut(i)
        both = mp.rs_chunk(i)
        dgate = both[:, width : width + ex] + both[:, width + lanes // 2 : width + lanes // 2 + ex]
        gate = gate_ref[mp.m, cut, :ex]
        dlog = gate * (dgate - jnp.sum(gate * dgate, axis=-1, keepdims=True))
        dh = both[:, :width] + jnp.dot(
            dlog, router_ref[...], precision=lax.Precision.HIGHEST, preferred_element_type=F32
        )
        normed, inverse = rms_parts(resid_ref[cut, :])
        small_ref[1:2, :] = small_ref[1:2, :] + jnp.sum(dh * normed, axis=0, keepdims=True)
        h_two = (normed * gain[...].reshape(1, -1)).astype(BF16).astype(F32)
        small_ref[8 : 8 + ex, :] = small_ref[8 : 8 + ex, :] + lax.dot_general(
            dlog, h_two, (((0,), (0,)), ((), ())), precision=lax.Precision.HIGHEST, preferred_element_type=F32
        )
        dresid = cot[cut, :].astype(F32) + rms_grad(dh * gain[...].reshape(1, -1), normed, inverse)
        dresid_ref[cut, :] = dresid
        db_ref[mp.m, cut, :] = dresid.astype(BF16)
        mp.ag_send(i)
    mp.ag_end()
    mp.rs_end()
    rows_peers.finish()
    hid_peers.finish()
    beside.finish()
    for sw in swaps:
        sw.wait()


def swap_partner():
    return (1 - lax.axis_index("seq"), lax.axis_index("ctx"), lax.axis_index("mp"))


def swap(src, dst, sems, i):
    return pltpu.make_async_remote_copy(
        src_ref=src,
        dst_ref=dst,
        send_sem=sems.at[0, i],
        recv_sem=sems.at[1, i],
        device_id=swap_partner(),
        device_id_type=MESH,
    )


def mid_back(n, part, resid, gain, cot, gate, router_t, rows, hid, du, arr, dg, chunks=2):
    k, share, wide = part.shape
    width = gain.shape[0]
    return pl.pallas_call(
        functools.partial(mid_back_kernel, chunks, n),
        out_shape=(
            jax.ShapeDtypeStruct((share, width), F32),
            jax.ShapeDtypeStruct((k, share, width), BF16),
            jax.ShapeDtypeStruct((8 + router_t.shape[0], width), F32),
            jax.ShapeDtypeStruct((n,) + rows.shape, F32),
            jax.ShapeDtypeStruct(hid.shape, BF16),
            jax.ShapeDtypeStruct(du.shape, BF16),
            jax.ShapeDtypeStruct(du.shape, BF16),
            jax.ShapeDtypeStruct(arr.shape[:2] + (arr.shape[2] // 2,), BF16),
            jax.ShapeDtypeStruct(dg.shape, BF16),
        ),
        in_specs=[VMEM] * 7 + [HBM] * 4,
        out_specs=(VMEM,) * 4 + (HBM,) * 5,
        scratch_shapes=mp_scratch(share, wide, chunks) + [DMA((2, 2)), DMA((4, n)), DMA((2, 2))],
        compiler_params=params(3, 60),
        name="mid_back",
        cost_estimate=cost(32),
    )(part, resid, gain, cot, gate, router_t, rows, hid, du, arr, dg)


class SmallSum:
    def __init__(self, sizes, x_ref, out_ref, bufs, sems):
        self.sizes, self.x, self.out, self.bufs, self.sems = sizes, x_ref, out_ref, bufs, sems
        self.me = [lax.axis_index(a) for a in ("seq", "ctx", "mp")]

    def peer(self, axis, d):
        ids = list(self.me)
        ids[axis] = lax.rem(self.me[axis] + d, self.sizes[axis])
        return tuple(ids)

    def signal(self, sem):
        for axis in range(3):
            for d in range(1, self.sizes[axis]):
                pl.semaphore_signal(sem, inc=1, device_id=self.peer(axis, d), device_id_type=MESH)
        return sum(self.sizes) - 3

    def move(self, axis, d):
        base = sum(self.sizes[:axis])
        buf = self.bufs[axis]
        return pltpu.make_async_remote_copy(
            src_ref=buf.at[0],
            dst_ref=buf.at[d],
            send_sem=self.sems.at[0, base + d],
            recv_sem=self.sems.at[1, base + d],
            device_id=self.peer(axis, d),
            device_id_type=MESH,
        )

    def begin(self, axis, value):
        self.bufs[axis][0] = value
        for d in range(1, self.sizes[axis]):
            self.move(axis, d).start()

    def end(self, axis):
        n = self.sizes[axis]
        for d in range(1, n):
            self.move(axis, d).wait()
        total = jnp.zeros(self.out.shape, F32)
        for i in range(n):
            total = total + self.bufs[axis][lax.rem(self.me[axis] - i + n, n)]
        return total


def last_kernel(
    chunks,
    sizes,
    dqkv_ref,
    h_hbm,
    wq_hbm,
    wk_hbm,
    wv_hbm,
    tok_hbm,
    gain,
    dresid_hbm,
    small_ref,
    wout_ref,
    up0_hbm,
    up_other,
    comb_hbm,
    resid_hbm,
    out_ref,
    final_ref,
    total_ref,
    gout_ref,
    gqkv_ref,
    up_ref,
    core_in,
    y_out,
    y_in,
    sems,
    core_in2,
    y_out2,
    y_in2,
    sems2,
    h_ref,
    wq_ref,
    wk_ref,
    wv_ref,
    tok_ref,
    dresid_ref,
    comb,
    resid_ref,
    part,
    dh_ref,
    qkv_ref,
    swapped,
    summed,
    wout_in,
    qkv_in,
    up_in,
    load_sem,
    swap_sem,
    peers_sem,
    *rest,
):
    n = sizes[1]
    s, c = lax.axis_index("seq"), lax.axis_index("ctx")
    load = Staged(
        (
            (h_hbm, h_ref),
            (wq_hbm, wq_ref),
            (wk_hbm, wk_ref),
            (wv_hbm, wv_ref),
            (tok_hbm, tok_ref),
            (comb_hbm, comb),
            (dresid_hbm, dresid_ref),
            (resid_hbm, resid_ref),
            (up0_hbm, up_ref),
        ),
        load_sem,
    )
    load.start()
    mp = Mp(part, core_in, y_out, y_in, None, sems, chunks)
    mp2 = Mp(comb, core_in2, y_out2, y_in2, None, sems2, chunks)
    small = SmallSum(sizes, small_ref, total_ref, rest[:3], rest[3])
    half_rows = swapped.shape[0]
    rows = half_rows // n
    wout_peers = Peers(
        n, lambda p: wout_ref.at[cut_of(p, rows)], lambda i: wout_in.at[i], peers_sem.at[0], peers_sem.at[1]
    )
    qkv_peers = Peers(
        n, lambda p: summed.at[cut_of(p, rows)], lambda i: qkv_in.at[i], peers_sem.at[2], peers_sem.at[3]
    )
    sem = pltpu.get_barrier_semaphore()
    pl.semaphore_wait(sem, small.signal(sem))
    wout_peers.start()
    load.wait(0)

    def weight_rows(first):
        def piece(r):
            at = pl.ds(pl.multiple_of(first + r * 256, 256), 256)
            qkv_ref[at, :] = tn(h_ref[:, at], dqkv_ref[...]).astype(BF16)

        loop(half_rows // 256, piece)

    weight_rows((1 - s) * half_rows)

    def chunk_swap(k):
        p = lax.rem(c + 1 + k, n)
        return swap(qkv_ref.at[cut_of((1 - s) * n + p, rows)], swapped.at[cut_of(p, rows)], swap_sem, k)

    up_swap = swap(up_other, up_in, swap_sem, n)

    def chunk_arrived(k):
        chunk_swap(k).wait_recv()
        if k + 2 < n:
            chunk_swap(k + 2).start()
        if k + 2 == n:
            up_swap.start()
        p = lax.rem(c + 1 + k, n)
        here = cut_of(p, rows)
        summed[here, :] = (
            qkv_ref[cut_of(s * n + p, rows), :].astype(F32) + swapped[here, :].astype(F32)
        ).astype(BF16)
        if k < n - 1:
            qkv_peers.move(k + 1).start()

    for k in range(min(2, n)):
        chunk_swap(k).start()
    load.wait(1, 2, 3)
    share, width = out_ref.shape
    qw, kw = wq_ref.shape[1], wk_ref.shape[1]

    def token_rows(i):
        at = pl.ds(pl.multiple_of(i * 512, 512), 512)
        dh = nt(dqkv_ref[:, :qw], wq_ref[at, :])
        dh = dh + nt(dqkv_ref[:, qw : qw + kw], wk_ref[at, :])
        dh = dh + nt(dqkv_ref[:, qw + kw :], wv_ref[at, :])
        for p in range(part.shape[0]):
            dh_ref[p, :, at] = dh[p * share : (p + 1) * share, :]
            part[p, :, at] = dh[p * share : (p + 1) * share, :].astype(BF16)

    loop(width // 512, token_rows)
    mp.rs_core(0).start()
    mp.rs_core(1).start()
    load.wait(5)
    mp2.rs_core(0).start()
    mp2.rs_core(1).start()
    weight_rows(s * half_rows)
    mp.rs_forward()
    load.wait(4)
    total_ref[...] = small_ref[...]

    def norm_rows(p):
        normed, _ = rms_parts(tok_ref[p].astype(F32))
        total_ref[0:1, :] = total_ref[0:1, :] + jnp.sum(dh_ref[p] * normed, axis=0, keepdims=True)

    loop(part.shape[0], norm_rows)
    small.begin(1, total_ref[...])
    chunk_arrived(0)
    mp2.rs_forward()
    chunk_arrived(1)
    load.wait(6)
    for i in range(chunks):
        cut = mp.cut(i)
        dh = mp.rs_chunk(i)
        normed, inverse = rms_parts(tok_ref[mp.m, cut, :].astype(F32))
        final_ref[cut, :] = dresid_ref[cut, :] + rms_grad(dh * gain[...].reshape(1, -1), normed, inverse)
        if i + 2 < n:
            chunk_arrived(i + 2)
        if i == 0:
            small.begin(0, small.end(1))
    for k in range(chunks + 2, n):
        chunk_arrived(k)
    small.begin(2, small.end(0))
    load.wait(7)
    for i in range(chunks):
        cut = mp.cut(i)
        out_ref[cut, :] = resid_ref[cut, :] + mp2.rs_chunk(i)
    total_ref[...] = small.end(2)
    wout_peers.finish()
    wout_in[c] = wout_ref[cut_of(c, rows), :]
    total = jnp.zeros(gout_ref.shape, F32)
    for i in range(n):
        total = total + wout_in[i].astype(F32)
    gout_ref[...] = total
    mp.rs_end()
    mp2.rs_end()
    load.wait(8)
    for k in range(n):
        chunk_swap(k).wait_send()
    qkv_peers.finish()
    qkv_in[c] = summed[cut_of(c, rows), :]
    total = jnp.zeros(gqkv_ref.shape, F32)
    for i in range(n):
        total = total + qkv_in[i].astype(F32)
    gqkv_ref[...] = total
    up_swap.wait()
    up_ref[...] = up_ref[...] + up_in[...].astype(F32)


def cut_of(i, rows):
    return pl.ds(pl.multiple_of(i * rows, 16), rows)


def last(sizes, dqkv, h, wq, wk, wv, tokens, gain, dresid, small, wout, up0, up_other, comb, resid, chunks=2):
    k, share, width = comb.shape
    n = sizes[1]
    half_rows, fo = wout.shape
    fq = dqkv.shape[1]
    rows = half_rows // n
    sds = jax.ShapeDtypeStruct
    vm = lambda x: pltpu.VMEM(x.shape, x.dtype)
    return pl.pallas_call(
        functools.partial(last_kernel, chunks, sizes),
        out_shape=(
            sds((share, width), F32),
            sds((share, width), F32),
            sds(small.shape, F32),
            sds((rows, fo), F32),
            sds((rows, fq), F32),
            sds(up0.shape, F32),
        ),
        in_specs=[VMEM] + [HBM] * 5 + [VMEM, HBM, VMEM, VMEM, HBM, VMEM, HBM, HBM],
        out_specs=(VMEM,) * 6,
        scratch_shapes=mp_scratch(share, width, chunks)
        + mp_scratch(share, width, chunks)
        + [vm(h), vm(wq), vm(wk), vm(wv), vm(tokens), vm(dresid), vm(comb), vm(resid)]
        + [
            pltpu.VMEM(comb.shape, BF16),
            pltpu.VMEM(comb.shape, F32),
            pltpu.VMEM((2 * half_rows, fq), BF16),
            pltpu.VMEM((half_rows, fq), BF16),
            pltpu.VMEM((half_rows, fq), BF16),
            pltpu.VMEM((n, rows, fo), BF16),
            pltpu.VMEM((n, rows, fq), BF16),
            pltpu.VMEM(up0.shape, BF16),
            DMA((9,)),
            DMA((2, n + 1)),
            DMA((4, n)),
        ]
        + [pltpu.VMEM((d,) + small.shape, F32) for d in sizes]
        + [DMA((2, sum(sizes)))],
        compiler_params=params(4, 60),
        name="last",
        cost_estimate=cost(60),
    )(dqkv, h, wq, wk, wv, tokens, gain, dresid, small, wout, up0, up_other, comb, resid)


def finish_kernel(*refs):
    n_in = 8
    total, gout, gqkv = refs[5:n_in]
    outs = refs[n_in : n_in + 12]
    sems = refs[n_in + 12]
    output, tokens, norm1, gq, gk, gv, go, norm2, router, gate, up, down = outs
    large = Staged(tuple(zip(refs[:5], (output, tokens, gate, up, down))), sems)
    large.start()
    norm1[...] = total[0, :]
    norm2[...] = total[1, :]
    router[...] = total[8 : 8 + router.shape[0], :]
    qw, kw = gq.shape[1], gk.shape[1]
    gq[...] = gqkv[:, :qw]
    gk[...] = gqkv[:, qw : qw + kw]
    gv[...] = gqkv[:, qw + kw :]
    go[...] = gout[...].T
    large.wait(0, 1, 2, 3, 4)


def finish(experts_all, qw, output, tokens, gate, up, down, total, gout, gqkv):
    sds = jax.ShapeDtypeStruct
    width = total.shape[1]
    rows = gqkv.shape[0]
    kw = (gqkv.shape[1] - qw) // 2
    shapes = (
        output.shape,
        tokens.shape,
        (width,),
        (rows, qw),
        (rows, kw),
        (rows, kw),
        gout.shape[::-1],
        (width,),
        (experts_all, width),
        gate.shape,
        up.shape,
        down.shape,
    )
    return pl.pallas_call(
        finish_kernel,
        out_shape=tuple(sds(x, F32) for x in shapes),
        in_specs=[HBM] * 5 + [VMEM] * 3,
        out_specs=(VMEM,) * 12,
        scratch_shapes=[DMA((5,))],
        compiler_params=pltpu.CompilerParams(vmem_limit_bytes=60 * MIB),
        name="finish",
        cost_estimate=cost(6),
    )(output, tokens, gate, up, down, total, gout, gqkv)


def body(
    tokens,
    norm1_gain,
    w_query,
    key_weight_matrix,
    value_weight_matrix,
    w_out,
    norm2_gain,
    router,
    w_gate,
    w_up,
    w_down,
    routes,
    cotangent,
):
    n_seq, n_ctx, n_mp = (lax.axis_size(a) for a in ("seq", "ctx", "mp"))
    s, c, m = (lax.axis_index(a) for a in ("seq", "ctx", "mp"))
    tok, width = tokens.shape
    share = tok // n_mp
    experts_all = router.shape[1]
    exp_local = w_gate.shape[0]
    top = routes.shape[1]
    cap = share * top * 5 // (4 * experts_all)
    slots = -(-n_mp * cap // 16) * 16

    cot_all = lax.all_gather(cotangent, "mp", axis=0, tiled=True)
    by_share = tokens.reshape(n_mp, share, width)

    normed_one, _ = rms_parts(tokens.astype(F32))
    h_one = (normed_one * norm1_gain[None, :]).astype(BF16)
    qt = (jnp.einsum("df,td->ft", w_query, h_one, preferred_element_type=F32).astype(BF16)) * BF16(0.125)
    k = nn(h_one, key_weight_matrix).astype(BF16)
    v = nn(h_one, value_weight_matrix).astype(BF16)
    o, heads_t, lse, kv, cot_above, routes_line = attend(n_ctx, qt, k, v, cotangent, routes.T)
    resid, h_two, place, place_t, place_line, cot_line = mid_forward(
        n_ctx, exp_local, slots, heads_t, w_out, norm2_gain, cotangent, cot_above, routes_line, by_share
    )
    h_two = h_two.reshape(tok, width)

    gates, gate_rows, arrived, hidden, dg, du, back, comb, arrived_line, cot_first, cot_line = moe(
        n_ctx, n_seq, experts_all, h_two, cot_all, place, place_t, routes.T, router.T, w_gate, w_up, w_down, cot_line
    )
    dresid, db, small, gate_rows_line, hidden_line, du_below, du_above, arrived_other, dg_other = mid_back(
        n_ctx,
        back.reshape(n_mp, share, -1),
        resid,
        norm2_gain,
        cotangent,
        gates.reshape(n_mp, share, -1),
        router.T,
        gate_rows,
        hidden,
        du,
        arrived,
        dg,
    )

    db = db.reshape(tok, width)
    dqkv, g_gate, g_down, up0, up_other, g_out, _, _ = attend_back(
        n_ctx,
        qt,
        db,
        w_out,
        o,
        lse,
        kv,
        arrived,
        arrived_other,
        dg,
        dg_other,
        gate_rows_line,
        du,
        du_below,
        du_above,
        hidden_line,
        hidden,
        heads_t,
        arrived_line,
        place_line,
        cot_line,
        cot_first,
    )
    output, grad_tokens, small, g_out, g_qkv, g_up = last(
        (n_seq, n_ctx, n_mp),
        dqkv,
        h_one,
        w_query,
        key_weight_matrix,
        value_weight_matrix,
        by_share,
        norm1_gain,
        dresid,
        small,
        g_out,
        up0,
        up_other,
        comb.reshape(n_mp, share, width),
        resid,
    )
    outs = finish(experts_all, w_query.shape[1], output, grad_tokens, g_gate, g_up, g_down, small, g_out, g_qkv)
    return outs[:8] + (outs[8].T,) + outs[9:]


def solution(mesh):
    placed = (
        P(("seq", "ctx"), None),
        P(),
        P(None, "mp"),
        P(None, "mp"),
        P(None, "mp"),
        P("mp", None),
        P(),
        P(),
        P("mp", None, None),
        P("mp", None, None),
        P("mp", None, None),
        P(("seq", "ctx"), None),
        P(("seq", "ctx", "mp"), None),
    )
    return jax.shard_map(
        body,
        mesh=mesh,
        in_specs=placed,
        out_specs=(
            P(("seq", "ctx", "mp"), None),
            P(("seq", "ctx", "mp"), None),
            P(),
            P(("seq", "ctx"), "mp"),
            P(("seq", "ctx"), "mp"),
            P(("seq", "ctx"), "mp"),
            P("mp", ("seq", "ctx")),
            P(),
            P(),
            P("mp", ("seq", "ctx"), None),
            P("mp", ("seq", "ctx"), None),
            P("mp", ("seq", "ctx"), None),
        ),
        check_vma=False,
    )
```

```python
import functools

import jax
import jax.numpy as jnp
from jax import lax
from jax.experimental import pallas as pl
from jax.experimental.pallas import tpu as pltpu
from jax.sharding import PartitionSpec as P

HEAD_SIZE = 64
EPS = 1e-06
MESH = pl.DeviceIdType.MESH
F32 = jnp.float32
BF16 = jnp.bfloat16
VMEM = pl.BlockSpec(memory_space=pltpu.VMEM)
HBM = pl.BlockSpec(memory_space=pl.ANY)
DMA = pltpu.SemaphoreType.DMA
MIB = 2**20


def cost(us):
    return pl.CostEstimate(flops=0, bytes_accessed=int(us * 3.6e6), transcendentals=0)


def params(collective_id, mib=56):
    return pltpu.CompilerParams(
        collective_id=collective_id, has_side_effects=True, vmem_limit_bytes=mib * MIB
    )


def nt(a, b):
    return lax.dot_general(a, b, (((1,), (1,)), ((), ())), preferred_element_type=F32)


def nn(a, b):
    return jnp.dot(a, b, preferred_element_type=F32)


class Staged:
    def __init__(self, pairs, sems):
        self.copies = [pltpu.make_async_copy(src, dst, sems.at[i]) for i, (src, dst) in enumerate(pairs)]

    def start(self):
        for copy in self.copies:
            copy.start()

    def wait(self, *which):
        for i in which:
            self.copies[i].wait()


class Spread:
    def __init__(self, n, own, below, above, all_ref, send, recv, local, short=False):
        self.n, self.own, self.below, self.above, self.all = n, own, below, above, all_ref
        self.send, self.recv, self.local = send, recv, local
        self.top = n - 2 if short else n - 1
        s, self.c, m = lax.axis_index("seq"), lax.axis_index("ctx"), lax.axis_index("mp")
        self.lower, self.upper = lax.rem(self.c + n - 1, n), lax.rem(self.c + 1, n)
        self.up, self.down = (s, self.upper, m), (s, self.lower, m)
        self.inner = jnp.logical_and(self.c > 0, self.c < n - 1)

    def move(self, b, src, device):
        return pltpu.make_async_remote_copy(
            src_ref=src,
            dst_ref=self.all.at[b],
            send_sem=self.send.at[b],
            recv_sem=self.recv.at[b],
            device_id=device,
            device_id_type=MESH,
        )

    def keep(self, i, src, b):
        return pltpu.make_async_copy(src, self.all.at[b], self.local.at[i])

    def goes_up(self, b):
        return jnp.logical_and(self.c < self.n - 1, self.c - b < self.top)

    def start(self):
        if self.below is None:

            @pl.when(self.c < self.n - 1)
            def _():
                self.move(self.c, self.own, self.up).start()
        else:

            @pl.when(jnp.logical_and(self.inner, self.goes_up(self.lower)))
            def _():
                self.move(self.lower, self.below, self.up).start()

            @pl.when(self.c > 0)
            def _():
                self.keep(1, self.below, self.lower).start()

        @pl.when(self.inner)
        def _():
            self.move(self.upper, self.above, self.down).start()

        self.keep(0, self.own, self.c).start()

        @pl.when(self.c < self.n - 1)
        def _():
            self.keep(2, self.above, self.upper).start()

    def tick(self, i):
        c, n = self.c, self.n
        off = i if self.below is None else i + 1

        @pl.when(jnp.logical_and(c - off >= 0, off <= self.top))
        def _():
            b = jnp.maximum(c - off, 0)
            self.move(b, self.all.at[b], self.up).wait_recv()

            @pl.when(self.goes_up(b))
            def _():
                self.move(b, self.all.at[b], self.up).start()

        @pl.when(c + 1 + i <= n - 1)
        def _():
            b = jnp.minimum(c + 1 + i, n - 1)
            self.move(b, self.all.at[b], self.down).wait_recv()

            @pl.when(c > 0)
            def _():
                self.move(b, self.all.at[b], self.down).start()

    def ticks(self, first):
        def later(i, carry):
            self.tick(i)
            return carry

        lax.fori_loop(first, self.n if self.below is None else self.n - 1, later, 0)

    def finish(self):
        self.keep(0, self.own, self.c).wait()

        if self.below is not None:

            @pl.when(self.c > 0)
            def _():
                self.keep(1, self.below, self.lower).wait()

        @pl.when(self.c < self.n - 1)
        def _():
            self.keep(2, self.above, self.upper).wait()

        def sent(b, carry):
            if self.below is None:
                sent_up = jnp.logical_and(b <= self.c, self.goes_up(b))
            else:
                sent_up = jnp.logical_and(b < self.c, self.goes_up(b))

            @pl.when(jnp.logical_or(sent_up, jnp.logical_and(b > self.c, self.c > 0)))
            def _():
                self.move(b, self.all.at[b], self.up).wait_send()

            return carry

        lax.fori_loop(0, self.n, sent, 0)


class Neighbours:
    def __init__(self, n, own, below, above, send, recv):
        self.n, self.own, self.below, self.above, self.send, self.recv = n, own, below, above, send, recv
        s, self.c, m = lax.axis_index("seq"), lax.axis_index("ctx"), lax.axis_index("mp")
        self.up, self.down = (s, lax.rem(self.c + 1, n), m), (s, lax.rem(self.c + n - 1, n), m)

    def move(self, way):
        return pltpu.make_async_remote_copy(
            src_ref=self.own,
            dst_ref=self.below if way == 0 else self.above,
            send_sem=self.send.at[way],
            recv_sem=self.recv.at[way],
            device_id=self.up if way == 0 else self.down,
            device_id_type=MESH,
        )

    def start_up(self):
        @pl.when(self.c < self.n - 1)
        def _():
            self.move(0).start()

    def start_down(self):
        @pl.when(self.c > 0)
        def _():
            self.move(1).start()

    def finish(self, up=True):
        @pl.when(self.c > 0)
        def _():
            if up:
                self.move(0).wait_recv()
            self.move(1).wait_send()

        @pl.when(self.c < self.n - 1)
        def _():
            self.move(1).wait_recv()
            if up:
                self.move(0).wait_send()


class LineSum:
    ahead = 2

    def __init__(self, n, parts, from_below, from_above, send, recv):
        self.n, self.parts, self.bufs, self.send, self.recv = n, parts, (from_below, from_above), send, recv
        s, self.c, m = lax.axis_index("seq"), lax.axis_index("ctx"), lax.axis_index("mp")
        self.up, self.down = (s, lax.rem(self.c + 1, n), m), (s, lax.rem(self.c + n - 1, n), m)
        self.ex, self.rows = from_below.shape[1], from_below.shape[2]
        self.units = (n - 1) * self.ex
        self.ticks = self.units + n - 3

    def own(self, k, e):
        return self.parts.at[e, pl.ds(pl.multiple_of(k * self.rows, 16), self.rows), :]

    def move(self, way, k, e, first=False):
        there = self.bufs[way].at[k, e]
        return pltpu.make_async_remote_copy(
            src_ref=self.own(k, e) if first else there,
            dst_ref=there,
            send_sem=self.send.at[way, k, e],
            recv_sem=self.recv.at[way, k, e],
            device_id=self.up if way == 0 else self.down,
            device_id_type=MESH,
        )

    def unit(self, way, u):
        k = lax.div(u, self.ex)
        return (self.n - 1 - k if way == 0 else k), lax.rem(u, self.ex)

    def first(self, u):
        for way, end in ((0, 0), (1, self.n - 1)):

            @pl.when(jnp.logical_and(self.c == end, u < self.units))
            def _():
                @pl.when(u >= self.ahead)
                def _():
                    self.move(way, *self.unit(way, jnp.maximum(u - self.ahead, 0)), True).wait_send()

                self.move(way, *self.unit(way, jnp.minimum(u, self.units - 1)), True).start()

    def tick(self, i):
        self.first(i + 1)
        for way, far in ((0, self.c), (1, self.n - 1 - self.c)):
            u = i - far

            @pl.when(jnp.logical_and(far > 0, jnp.logical_and(u >= 0, u < (self.n - 1 - far) * self.ex)))
            def _():
                k, e = self.unit(way, jnp.clip(u, 0, self.units - 1))
                self.move(way, k, e).wait_recv()
                self.bufs[way][k, e] = (
                    self.own(k, e)[...].astype(F32) + self.bufs[way][k, e].astype(F32)
                ).astype(BF16)
                self.move(way, k, e).start()

    def finish(self, out):
        c = self.c
        for e in range(self.ex):
            out[e] = self.own(c, e)[...].astype(F32)
        for way, far in ((0, c), (1, self.n - 1 - c)):

            @pl.when(far > 0)
            def _():
                for e in range(self.ex):
                    self.move(way, c, e).wait_recv()
                    out[e] = out[e] + self.bufs[way][c, e].astype(F32)

            done = jnp.where(far == 0, max(self.units - self.ahead, 0), 0)

            def sent(u, carry):
                self.move(way, *self.unit(way, u)).wait_send()
                return carry

            lax.fori_loop(done, (self.n - 1 - far) * self.ex, sent, 0)


class Peers:
    def __init__(self, n, src_of, dst_of, send, recv):
        self.n, self.src_of, self.dst_of, self.send, self.recv = n, src_of, dst_of, send, recv
        self.s, self.c, self.m = lax.axis_index("seq"), lax.axis_index("ctx"), lax.axis_index("mp")

    def move(self, d):
        peer = lax.rem(self.c + d, self.n)
        return pltpu.make_async_remote_copy(
            src_ref=self.src_of(peer),
            dst_ref=self.dst_of(self.c),
            send_sem=self.send.at[d],
            recv_sem=self.recv.at[d],
            device_id=(self.s, peer, self.m),
            device_id_type=MESH,
        )

    def signal(self, sem):
        for d in range(1, self.n):
            pl.semaphore_signal(
                sem, inc=1, device_id=(self.s, lax.rem(self.c + d, self.n), self.m), device_id_type=MESH
            )

    def start(self):
        for d in range(1, self.n):
            self.move(d).start()

    def finish(self):
        for d in range(1, self.n):
            self.move(d).wait()


class CotExchange:
    def __init__(self, n, line_ref, full, first, sems):
        self.n, self.line, self.full, self.first, self.sems = n, line_ref, full, first, sems
        self.count = full.shape[0]
        s, self.c, m = lax.axis_index("seq"), lax.axis_index("ctx"), lax.axis_index("mp")
        self.m = m
        self.share = line_ref.shape[1]
        self.sib = m + 1 - 2 * lax.rem(m, 2)
        self.opp = lax.rem(m + 2, 4)
        self.sib_id, self.opp_id = (s, self.c, self.sib), (s, self.c, self.opp)

    def signal(self, sem):
        for d in (self.sib_id, self.opp_id):
            pl.semaphore_signal(sem, inc=1, device_id=d, device_id_type=MESH)

    def place(self, i, who):
        return self.full.at[i, pl.ds(pl.multiple_of(who * self.share, 16), self.share), :]

    def mine(self, i):
        return self.line.at[lax.rem(self.c - self.first - i + 2 * self.n, self.n)]

    def move(self, kind, i):
        whose = self.opp if kind == 2 else self.m
        return pltpu.make_async_remote_copy(
            src_ref=self.place(i, self.opp) if kind == 2 else self.mine(i),
            dst_ref=self.place(i, whose),
            send_sem=self.sems.at[0, kind, i],
            recv_sem=self.sems.at[1, kind, i],
            device_id=self.opp_id if kind == 0 else self.sib_id,
            device_id_type=MESH,
        )

    def start(self):
        for i in range(self.count):
            self.move(0, i).start()
            self.move(1, i).start()

    def finish(self):
        for i in range(self.count):
            self.move(0, i).wait_recv()
            self.move(2, i).start()
        for i in range(self.count):
            self.move(1, i).wait_recv()
            self.move(2, i).wait_recv()
            for kind in range(3):
                self.move(kind, i).wait_send()


def signal_line(n, sem):
    s, c, m = lax.axis_index("seq"), lax.axis_index("ctx"), lax.axis_index("mp")

    @pl.when(c > 0)
    def _():
        pl.semaphore_signal(sem, inc=1, device_id=(s, lax.rem(c + n - 1, n), m), device_id_type=MESH)

    @pl.when(c < n - 1)
    def _():
        pl.semaphore_signal(sem, inc=1, device_id=(s, lax.rem(c + 1, n), m), device_id_type=MESH)


def line_degree(n):
    c = lax.axis_index("ctx")
    return jnp.where(c > 0, 1, 0) + jnp.where(c < n - 1, 1, 0)


def pad_heads(src, dst, heads, group):
    dst[...] = jnp.zeros_like(dst)
    for h in range(heads):
        g = h // group
        rows = slice(g * HEAD_SIZE, (g + 1) * HEAD_SIZE)
        dst[h, rows, :] = src[h * HEAD_SIZE : (h + 1) * HEAD_SIZE, :]


def causal(t):
    keys = lax.broadcasted_iota(jnp.int32, (t, t), 0)
    queries = lax.broadcasted_iota(jnp.int32, (t, t), 1)
    return keys <= queries


def attend_kernel(
    n,
    tok_ref,
    gain,
    wq_ref,
    wk_ref,
    wv_ref,
    cot_ref,
    routes_ref,
    q_ref,
    h_ref,
    o_ref,
    heads_ref,
    lse_ref,
    kv_ref,
    above_ref,
    line_ref,
    qpad,
    vt,
    top,
    tot,
    send,
    recv,
    side,
    peers_sem,
):
    s, c, m = lax.axis_index("seq"), lax.axis_index("ctx"), lax.axis_index("mp")
    t, kvw = tok_ref.shape[0], wk_ref.shape[1]
    heads = q_ref.shape[0] // HEAD_SIZE
    group = heads // (kvw // HEAD_SIZE)
    up, down = (s, lax.rem(c + 1, n), m), (s, lax.rem(c + n - 1, n), m)

    def norm_rows(i):
        rows = pl.ds(pl.multiple_of(i * 128, 128), 128)
        normed, _ = rms_parts(tok_ref[rows, :].astype(F32))
        h_ref[rows, :] = (normed * gain[...].reshape(1, -1)).astype(BF16)

    loop(t // 128, norm_rows)
    kv_ref[0, :, :kvw] = nn(h_ref[...], wk_ref[...]).astype(BF16)
    kv_ref[0, :, kvw:] = nn(h_ref[...], wv_ref[...]).astype(BF16)
    line_ref[c] = routes_ref[...]
    peers = Peers(n, lambda p: routes_ref, lambda i: line_ref.at[i], peers_sem.at[0], peers_sem.at[1])
    beside = Neighbours(n, cot_ref, None, above_ref, side.at[0], side.at[1])
    sem = pltpu.get_barrier_semaphore()
    peers.signal(sem)
    pl.semaphore_wait(sem, n - 1)

    def pass_up(slot):
        return pltpu.make_async_remote_copy(
            src_ref=kv_ref.at[slot],
            dst_ref=kv_ref.at[slot + 1],
            send_sem=send.at[slot],
            recv_sem=recv.at[slot + 1],
            device_id=up,
            device_id_type=MESH,
        )

    def got(slot):
        return pltpu.make_async_remote_copy(
            src_ref=kv_ref.at[slot],
            dst_ref=kv_ref.at[slot],
            send_sem=send.at[slot],
            recv_sem=recv.at[slot],
            device_id=up,
            device_id_type=MESH,
        )

    @pl.when(c < n - 1)
    def _():
        pass_up(0).start()

    peers.start()
    beside.start_down()
    q_ref[...] = (nn(h_ref[...], wq_ref[...]) * 0.125).astype(BF16).T
    pad_heads(q_ref, qpad, heads, group)
    top[...] = jnp.full_like(top, -1e30)
    tot[...] = jnp.zeros_like(tot)
    o_ref[...] = jnp.zeros_like(o_ref)

    def block(slot, masked):
        vt[...] = kv_ref[slot, :, kvw:].T

        def head(h, carry):
            g = lax.div(h, group)
            scores = nn(kv_ref[slot, :, :kvw], qpad[h])
            if masked:
                scores = jnp.where(causal(t), scores, -1e30)
            old = top[h]
            new = jnp.maximum(old, jnp.max(scores, axis=0, keepdims=True))
            weights = jnp.exp(scores - new)
            factor = jnp.exp(old - new)
            top[h] = new
            tot[h] = tot[h] * factor + jnp.sum(weights, axis=0, keepdims=True)
            rows = pl.ds(pl.multiple_of(h * HEAD_SIZE, HEAD_SIZE), HEAD_SIZE)
            vrows = pl.ds(pl.multiple_of(g * HEAD_SIZE, HEAD_SIZE), HEAD_SIZE)
            o_ref[rows, :] = o_ref[rows, :] * factor + nn(vt[vrows, :], weights.astype(BF16))
            return carry

        lax.fori_loop(0, heads, head, 0)

    block(0, True)

    def earlier(slot, carry):
        got(slot).wait_recv()

        @pl.when(c < n - 1)
        def _():
            pass_up(slot).start()

        block(slot, False)
        return carry

    lax.fori_loop(1, c + 1, earlier, 0)
    for h in range(heads):
        rows = slice(h * HEAD_SIZE, (h + 1) * HEAD_SIZE)
        done = o_ref[rows, :] / tot[h]
        o_ref[rows, :] = done
        heads_ref[rows, :] = done.astype(BF16)
        lse_ref[h] = top[h] + jnp.log(tot[h])

    @pl.when(c < n - 1)
    def _():
        def sent(slot, carry):
            pass_up(slot).wait_send()
            return carry

        lax.fori_loop(0, c + 1, sent, 0)

    peers.finish()
    beside.finish(up=False)


def attend(n, tokens, gain, wq, wk, wv, cot, routes):
    t, kvw = tokens.shape[0], wk.shape[1]
    qw = wq.shape[1]
    heads = qw // HEAD_SIZE
    return pl.pallas_call(
        functools.partial(attend_kernel, n),
        out_shape=(
            jax.ShapeDtypeStruct((qw, t), BF16),
            jax.ShapeDtypeStruct(tokens.shape, BF16),
            jax.ShapeDtypeStruct((qw, t), F32),
            jax.ShapeDtypeStruct((qw, t), BF16),
            jax.ShapeDtypeStruct((heads, 1, t), F32),
            jax.ShapeDtypeStruct((n, t, 2 * kvw), BF16),
            jax.ShapeDtypeStruct(cot.shape, BF16),
            jax.ShapeDtypeStruct((n,) + routes.shape, jnp.int32),
        ),
        in_specs=[VMEM] * 5 + [HBM, VMEM],
        out_specs=(VMEM,) * 6 + (HBM, VMEM),
        scratch_shapes=[
            pltpu.VMEM((heads, kvw, t), BF16),
            pltpu.VMEM((kvw, t), BF16),
            pltpu.VMEM((heads, 1, t), F32),
            pltpu.VMEM((heads, 1, t), F32),
            DMA((n,)),
            DMA((n,)),
            DMA((2, 2)),
            DMA((2, n)),
        ],
        compiler_params=params(0),
        name="attend",
        cost_estimate=cost(30),
    )(tokens, gain, wq, wk, wv, cot, routes)


def attend_back_kernel(
    n,
    q_ref,
    db_ref,
    wout_ref,
    o_ref,
    lse_ref,
    kv_ref,
    arr_ref,
    arr_other,
    dg_ref,
    dg_other,
    rows_line,
    own_ref,
    below_ref,
    above_ref,
    hid_hbm,
    hid_own,
    heads_ref,
    arr_hbm,
    place_hbm,
    line_hbm,
    first_hbm,
    dqkv_ref,
    gate_ref,
    down_ref,
    up_ref,
    up_other,
    wsum_ref,
    all_hbm,
    rest_hbm,
    do_ref,
    qpad,
    dopad,
    delta,
    dq,
    kt,
    part,
    passing,
    sum_ref,
    from_below,
    from_above,
    place_buf,
    cot_buf,
    hid_buf,
    arr_buf,
    du_buf,
    dy,
    acc_ref,
    kv_sem,
    sum_sem,
    spread_sem,
    local,
    ysem,
    load_sem,
    swap_sem,
    wout_part,
    wout_in,
    down_out,
    down_in,
):
    s, c, m = lax.axis_index("seq"), lax.axis_index("ctx"), lax.axis_index("mp")
    _, t, kvw2 = kv_ref.shape
    kvw = kvw2 // 2
    heads = q_ref.shape[0] // HEAD_SIZE
    group = heads // (kvw // HEAD_SIZE)
    ex, slots, width = arr_ref.shape
    half_width = width // 2
    down = (s, lax.rem(c + n - 1, n), m)
    spread = Spread(n, own_ref, below_ref, above_ref, all_hbm, spread_sem.at[0], spread_sem.at[1], local)
    done_blocks = first_hbm.shape[0]
    cots = CotExchange(n, line_hbm, rest_hbm, done_blocks, ysem)
    line = LineSum(n, sum_ref, from_below, from_above, sum_sem.at[0], sum_sem.at[1])
    sem = pltpu.get_barrier_semaphore()
    signal_line(n, sem)
    cots.signal(sem)
    pl.semaphore_signal(sem, inc=1, device_id=swap_partner(), device_id_type=MESH)
    pl.semaphore_wait(sem, line_degree(n) + 3)
    spread.start()
    cots.start()

    def gate_part(e, out):
        def piece(r):
            mine = pl.ds(pl.multiple_of(s * half_width + r * 256, 128), 256)
            cut = pl.ds(pl.multiple_of(r * 256, 256), 256)
            out[cut, :] = (tn(arr_ref[e, :, mine], dg_ref[e]) + tn(arr_other[e, :, cut], dg_other[e])).astype(BF16)

        loop(half_width // 256, piece)

    for e in range(ex):
        gate_part(e, sum_ref.at[e])
        if e == 0:
            line.first(0)
    do_ref[...] = nt(wout_ref[...], db_ref[...]).astype(BF16)

    def wout_piece(r):
        at = pl.ds(pl.multiple_of(r * 512, 512), 512)
        wout_part[:, at] = nn(heads_ref[...], db_ref[:, at]).astype(BF16)

    loop(width // 512, wout_piece)
    own_half, other_half = (pl.ds(pl.multiple_of(k * half_width, 128), half_width) for k in (s, 1 - s))
    wout_swap = swap(wout_part.at[:, other_half], wout_in, swap_sem, 0)
    wout_swap.start()

    def tick(i):
        line.tick(i)
        for hop in range(1, n - 1):

            @pl.when(i == 2 * hop - 1)
            def _():
                spread.tick(hop)

    ticks = max(line.ticks, 2 * (n - 2)) + 1
    pad_heads(q_ref, qpad, heads, group)
    pad_heads(do_ref, dopad, heads, group)
    for h in range(heads):
        rows = slice(h * HEAD_SIZE, (h + 1) * HEAD_SIZE)
        delta[h] = jnp.sum(do_ref[rows, :].astype(F32) * o_ref[rows, :], axis=0, keepdims=True)
    dq[...] = jnp.zeros_like(dq)

    def block(j, masked):
        slot = c - j
        acc = part.at[lax.rem(j, 2)]
        acc[...] = jnp.zeros(acc.shape, F32)
        kt[...] = kv_ref[slot, :, :kvw].T

        def head(h, carry):
            g = lax.div(h, group)
            scores = nn(kv_ref[slot, :, :kvw], qpad[h])
            probs = jnp.exp(scores - lse_ref[h])
            if masked:
                probs = jnp.where(causal(t), probs, 0.0)
            dprobs = nn(kv_ref[slot, :, kvw:], dopad[h])
            ds = (probs * (dprobs - delta[h])).astype(BF16)
            rows = pl.ds(pl.multiple_of(h * HEAD_SIZE, HEAD_SIZE), HEAD_SIZE)
            krows = pl.ds(pl.multiple_of(g * HEAD_SIZE, HEAD_SIZE), HEAD_SIZE)
            dq[rows, :] = dq[rows, :] + nn(kt[krows, :], ds)
            acc[:, :kvw] = acc[:, :kvw] + nt(ds, qpad[h])
            acc[:, kvw:] = acc[:, kvw:] + nt(probs.astype(BF16), dopad[h])
            return carry

        lax.fori_loop(0, heads, head, 0)

    def pass_down(j):
        return pltpu.make_async_remote_copy(
            src_ref=passing.at[j],
            dst_ref=passing.at[j],
            send_sem=kv_sem.at[0, j],
            recv_sem=kv_sem.at[1, j],
            device_id=down,
            device_id_type=MESH,
        )

    def gathered(j):
        acc = part.at[lax.rem(j, 2)]

        @pl.when(c < n - 1)
        def _():
            pass_down(j).wait_recv()
            acc[...] = acc[...] + passing[j].astype(F32)

        return acc

    def forward(j):
        acc = gathered(j)
        passing[j] = acc[...].astype(BF16)
        pass_down(j).start()

    def step(j, carry):
        block(j, False)

        @pl.when(jnp.logical_and(j > 0, c < n - 1))
        def _():
            forward(j - 1)

        @pl.when(c == n - 1)
        def _():
            forward(j)

        tick(j)
        return carry

    lax.fori_loop(0, c, step, 0)
    def later(i, carry):
        tick(i)
        return carry

    middle = jnp.maximum(c, min(2, ticks))
    lax.fori_loop(c, middle, later, 0)

    cots.finish()

    def load_block(i, slot, start):
        b = lax.rem(c - i + n, n)
        share = line_hbm.shape[1]
        place_copy = pltpu.make_async_copy(place_hbm.at[b], place_buf.at[slot], load_sem.at[0, slot])
        hid_copy = pltpu.make_async_copy(hid_hbm.at[b], hid_buf.at[slot], load_sem.at[1, slot])
        hid_mine = pltpu.make_async_copy(hid_own.at[b], hid_buf.at[slot], load_sem.at[1, slot])

        def rows(who):
            return pl.ds(pl.multiple_of(who * share, 16), share)

        def piece(k, who, full, at):
            return pltpu.make_async_copy(
                full.at[at, rows(who), :], cot_buf.at[slot, rows(who), :], load_sem.at[2 + k, slot]
            )

        others = (cots.sib, cots.opp, lax.rem(cots.sib + 2, 4))
        mine = pltpu.make_async_copy(line_hbm.at[b], cot_buf.at[slot, rows(m), :], load_sem.at[5, slot])
        first = [piece(k, who, first_hbm, jnp.minimum(i, done_blocks - 1)) for k, who in enumerate(others)]
        if not start:
            for copy in [place_copy, hid_copy, mine] + first:
                copy.wait()
            return
        rest = [piece(k, who, rest_hbm, jnp.maximum(i - done_blocks, 0)) for k, who in enumerate(others)]
        place_copy.start()
        mine.start()

        @pl.when(b == c)
        def _():
            hid_mine.start()

        @pl.when(b != c)
        def _():
            hid_copy.start()

        @pl.when(i < done_blocks)
        def _():
            for copy in first:
                copy.start()

        @pl.when(i >= done_blocks)
        def _():
            for copy in rest:
                copy.start()

    fa, ua = hid_hbm.shape[3], arr_hbm.shape[3]
    ff = dg_ref.shape[2]
    acc_ref[...] = jnp.zeros_like(acc_ref)
    load_block(0, 0, True)
    wide = 512

    def down_block(i):
        slot = lax.rem(i, 2)
        load_block(i, slot, False)

        @pl.when(i < n - 1)
        def _():
            load_block(i + 1, 1 - slot, True)

        cols = rows_line[lax.rem(c - i + n, n)].T
        for e in range(ex):

            def dys(k):
                cut = pl.ds(pl.multiple_of(k * wide, wide), wide)
                dy[:, cut] = (
                    cols[:slots, e : e + 1] * nn(place_buf[slot, e * slots : (e + 1) * slots, :], cot_buf[slot, :, cut])
                ).astype(BF16)

            loop(width // wide, dys)
            acc_ref[e, :fa, :] = acc_ref[e, :fa, :] + tn(hid_buf[slot, e], dy[...])

    loop(n, down_block)
    mine, other = (pl.ds(pl.multiple_of(k * (fa // 2), 16), fa // 2) for k in (s, 1 - s))
    down_ref[...] = acc_ref[:, mine, :]
    down_out[...] = acc_ref[:, other, :].astype(BF16)
    wout_swap.wait()
    down_swap = swap(down_out, down_in, swap_sem, 1)
    down_swap.start()
    wsum_ref[...] = (wout_part[:, own_half].astype(F32) + wout_in[...].astype(F32)).astype(BF16).T

    after = jnp.minimum(middle + 1, ticks)
    lax.fori_loop(middle, after, later, 0)
    block(c, True)

    @pl.when(jnp.logical_and(c > 0, c < n - 1))
    def _():
        forward(c - 1)

    qw = dq.shape[0]
    dqkv_ref[:, :qw] = (dq[...] * 0.125).astype(BF16).T
    lax.fori_loop(after, ticks, later, 0)

    spread.finish()
    acc_ref[...] = jnp.zeros_like(acc_ref)

    def load_du(b, slot):
        return (
            pltpu.make_async_copy(all_hbm.at[b], du_buf.at[slot], load_sem.at[6, slot]),
            pltpu.make_async_copy(arr_hbm.at[b], arr_buf.at[slot], load_sem.at[7, slot]),
        )

    for copy in load_du(0, 0):
        copy.start()

    def up_block(b):
        slot = lax.rem(b, 2)
        for copy in load_du(b, slot):
            copy.wait()

        @pl.when(b < n - 1)
        def _():
            for copy in load_du(b + 1, 1 - slot):
                copy.start()

        for e in range(ex):
            acc_ref[e, :ua, :ff] = acc_ref[e, :ua, :ff] + tn(arr_buf[slot, e], du_buf[slot, e])

    loop(n, up_block)
    mine, other = (pl.ds(pl.multiple_of(k * (ua // 2), 16), ua // 2) for k in (s, 1 - s))
    up_ref[...] = acc_ref[:, mine, :ff]
    up_other[...] = acc_ref[:, other, :ff].astype(BF16)

    acc = gathered(c)
    dqkv_ref[:, qw:] = acc[...].astype(BF16)
    line.finish(gate_ref)
    down_swap.wait()
    down_ref[...] = down_ref[...] + down_in[...].astype(F32)

    def sent_kv(j, carry):
        pass_down(j).wait_send()
        return carry

    lax.fori_loop(0, c, sent_kv, 0)


def attend_back(n, qt, db, w_out, o, lse, kv, arr, arr_other, dg, dg_other, rows, du, below, above, hid, hid_own, heads_t, arr_line, place, line, first):
    qw, t = qt.shape
    heads = qw // HEAD_SIZE
    kvw = kv.shape[2] // 2
    ex, slots, width = arr.shape
    ff = dg.shape[2]
    half_width = width // 2
    chunk = (ex, half_width // n, ff)
    fa, ua = hid.shape[3], arr_line.shape[3]
    blocks = first.shape[0]
    sds = jax.ShapeDtypeStruct
    return pl.pallas_call(
        functools.partial(attend_back_kernel, n),
        out_shape=(
            sds((t, qw + 2 * kvw), BF16),
            sds(chunk, F32),
            sds((ex, fa // 2, width), F32),
            sds((ex, ua // 2, ff), F32),
            sds((ex, ua // 2, ff), BF16),
            sds((half_width, qw), BF16),
            sds((n,) + du.shape, BF16),
            sds((n - blocks,) + first.shape[1:], BF16),
        ),
        in_specs=[VMEM] * 14 + [HBM] * 2 + [VMEM] + [HBM] * 4,
        out_specs=(VMEM,) * 6 + (HBM,) * 2,
        scratch_shapes=[
            pltpu.VMEM((qw, t), BF16),
            pltpu.VMEM((heads, kvw, t), BF16),
            pltpu.VMEM((heads, kvw, t), BF16),
            pltpu.VMEM((heads, 1, t), F32),
            pltpu.VMEM((qw, t), F32),
            pltpu.VMEM((kvw, t), BF16),
            pltpu.VMEM((2, t, 2 * kvw), F32),
            pltpu.VMEM((n, t, 2 * kvw), BF16),
            pltpu.VMEM((ex, half_width, ff), BF16),
            pltpu.VMEM((n,) + chunk, BF16),
            pltpu.VMEM((n,) + chunk, BF16),
            pltpu.VMEM((2,) + place.shape[1:], BF16),
            pltpu.VMEM((2,) + first.shape[1:], BF16),
            pltpu.VMEM((2, ex, slots, fa), BF16),
            pltpu.VMEM((2, ex, slots, ua), BF16),
            pltpu.VMEM((2,) + du.shape, BF16),
            pltpu.VMEM((slots, width), BF16),
            pltpu.VMEM((ex, max(fa, ua), width), F32),
            DMA((2, n)),
            DMA((2, 2, n, ex)),
            DMA((2, n)),
            DMA((3,)),
            DMA((2, 3, n - blocks)),
            DMA((8, 2)),
            DMA((2, 2)),
            pltpu.VMEM((qw, width), BF16),
            pltpu.VMEM((qw, half_width), BF16),
            pltpu.VMEM((ex, fa // 2, width), BF16),
            pltpu.VMEM((ex, fa // 2, width), BF16),
        ],
        compiler_params=params(1, 62),
        name="attend_back",
        cost_estimate=cost(60),
    )(qt, db, w_out, o, lse, kv, arr, arr_other, dg, dg_other, rows, du, below, above, hid, hid_own, heads_t, arr_line, place, line, first)


def tn(a, b):
    return lax.dot_general(a, b, (((0,), (0,)), ((), ())), preferred_element_type=F32)


def loop(n, f):
    def step(i, carry):
        f(i)
        return carry

    lax.fori_loop(0, n, step, 0)


def moe_kernel(
    n,
    n_seq,
    experts_all,
    h_ref,
    cot_ref,
    place_ref,
    place_t_ref,
    routes_ref,
    router_ref,
    wg_hbm,
    wu_hbm,
    wd_hbm,
    line_hbm,
    gates_ref,
    rows_ref,
    arr_ref,
    hid_ref,
    dg_ref,
    du_ref,
    back_ref,
    comb_ref,
    arr_line,
    cot_first,
    line_out,
    wg,
    wu,
    wd,
    dout,
    dy,
    hid,
    back_rows,
    comb_rows,
    parts,
    cols,
    wsem,
    peers_sem,
    ysem,
    local,
    far_sem,
    router3,
    named,
):
    s, c, m = lax.axis_index("seq"), lax.axis_index("ctx"), lax.axis_index("mp")
    ex, width, ff = wg.shape
    slots = place_ref.shape[0] // ex
    first = m * ex
    lanes = gates_ref.shape[1]
    peers = Peers(n, lambda p: parts.at[p], lambda i: arr_line.at[i], peers_sem.at[0], peers_sem.at[1])
    cots = CotExchange(n, line_hbm, cot_first, 0, ysem)
    far = pltpu.make_async_remote_copy(
        src_ref=line_hbm.at[0],
        dst_ref=line_out.at[0],
        send_sem=far_sem.at[0],
        recv_sem=far_sem.at[1],
        device_id=(s, lax.rem(c + 1, n), m),
        device_id_type=MESH,
    )
    sem = pltpu.get_barrier_semaphore()
    peers.signal(sem)
    cots.signal(sem)
    weights = {}
    for e in range(ex):
        for i, (src, dst) in enumerate(((wg_hbm, wg), (wu_hbm, wu), (wd_hbm, wd))):
            weights[i, e] = pltpu.make_async_copy(src.at[e], dst.at[e], wsem.at[i, e])
            weights[i, e].start()

    pl.semaphore_wait(sem, n - 1 + 2)
    cots.start()

    @pl.when(c == n - 2)
    def _():
        far.start()

    def rows_of(e):
        return slice(e * slots, (e + 1) * slots)

    def arrive(i):
        cut = pl.ds(pl.multiple_of(i * slots, 16), slots)
        arr_ref[i] = nn(place_ref[cut, :], h_ref[...]).astype(BF16)

    loop(ex, arrive)
    size = width // (n * n_seq)
    for e in range(ex):
        for i in range(n):
            for j in range(n_seq):
                at = (j * n + i) * size
                parts[i, e, :, j * size : (j + 1) * size] = arr_ref[e, :, at : at + size]
    peers.start()
    own = pltpu.make_async_copy(parts.at[c], arr_line.at[c], local.at[0])
    own.start()

    router3[...] = jnp.zeros_like(router3)
    left = router_ref[...]
    for i in range(3):
        piece = left.astype(BF16)
        router3[i * experts_all : (i + 1) * experts_all, :] = piece
        left = left - piece.astype(F32)
    three = nt(h_ref[...], router3[...])
    logits = three + pltpu.roll(three, lanes - experts_all, 1) + pltpu.roll(three, lanes - 2 * experts_all, 1)
    which = lax.broadcasted_iota(jnp.int32, three.shape, 1)
    top = routes_ref.shape[0]
    named[...] = jnp.zeros_like(named)
    named[:top, :] = routes_ref[...].astype(F32)
    columns = named[...].T
    which = which.astype(F32)
    chosen = which == columns[:, 0:1]
    for k in range(1, top):
        chosen = jnp.logical_or(chosen, which == columns[:, k : k + 1])
    peak = jnp.max(jnp.where(chosen, logits, -1e30), axis=1, keepdims=True)
    raised = jnp.where(chosen, jnp.exp(jnp.where(chosen, logits - peak, 0.0)), 0.0)
    gates = raised / jnp.sum(raised, axis=1, keepdims=True)
    gates_ref[...] = gates
    g1 = gates.astype(BF16)
    rest = gates - g1.astype(F32)
    g2 = rest.astype(BF16)
    g3 = (rest - g2.astype(F32)).astype(BF16)
    lane = lax.broadcasted_iota(jnp.int32, (slots, lanes), 1)
    cols[...] = jnp.zeros_like(cols)
    gate_col = []
    for e in range(ex):
        pe = place_ref[rows_of(e), :]
        got = nn(pe, g1) + nn(pe, g2) + nn(pe, g3)
        col = jnp.sum(jnp.where(lane == first + e, got, 0.0), axis=1, keepdims=True)
        gate_col.append(col)
        cols[:slots, :] = cols[:slots, :] + jnp.where(lane == e, col, 0.0)

    rows_ref[...] = cols[...].T[:8, :]
    wide = 512
    for e in range(ex):
        col = gate_col[e]

        def douts(i):
            cut = pl.ds(pl.multiple_of(i * wide, wide), wide)
            d = nn(place_ref[rows_of(e), :], cot_ref[:, cut])
            dout[e, :, cut] = d.astype(BF16)
            dy[e, :, cut] = (col * d).astype(BF16)

        loop(width // wide, douts)
        for i in range(3):
            weights[i, e].wait()

        def hidden(i):
            cut = pl.ds(pl.multiple_of(i * 256, 256), 256)
            g = nn(arr_ref[e], wg[e, :, cut])
            u = nn(arr_ref[e], wu[e, :, cut])
            dh = nt(dy[e], wd[e, cut, :])
            sigma = jax.nn.sigmoid(g)
            silu = g * sigma
            hid[:, cut] = (silu * u).astype(BF16)
            dg_ref[e, :, cut] = (dh * u * sigma * (1.0 + g * (1.0 - sigma))).astype(BF16)
            du_ref[e, :, cut] = (dh * silu).astype(BF16)

        loop(ff // 256, hidden)
        size = ff // (n * n_seq)
        for i in range(n):
            for j in range(n_seq):
                at = (j * n + i) * size
                hid_ref[i, e, :, j * size : (j + 1) * size] = hid[:, at : at + size]

        def outs(i, grads):
            cut = pl.ds(pl.multiple_of(i * wide, wide), wide)
            y = nn(hid[...], wd[e, :, cut]).astype(BF16).astype(F32)
            comb_rows[rows_of(e), cut] = (col * y).astype(BF16)
            back_rows[rows_of(e), cut] = (nt(dg_ref[e], wg[e, cut, :]) + nt(du_ref[e], wu[e, cut, :])).astype(BF16)
            return grads + jnp.sum(dout[e, :, cut].astype(F32) * y, axis=1, keepdims=True)

        grads = lax.fori_loop(0, width // wide, outs, jnp.zeros((slots, 1), F32))
        high = grads.astype(BF16).astype(F32)
        here = jnp.where(lane == first + e, high, jnp.where(lane == lanes // 2 + first + e, grads - high, 0.0))
        back_rows[rows_of(e), width:] = here.astype(BF16)

    def scatter(i):
        cut = pl.ds(pl.multiple_of(i * 256, 256), 256)
        back_ref[:, cut] = nn(place_t_ref[...], back_rows[:, cut]).astype(BF16)
        comb_ref[:, cut] = nn(place_t_ref[...], comb_rows[:, cut]).astype(BF16)

    loop(width // 256, scatter)
    back_ref[:, width:] = nn(place_t_ref[...], back_rows[:, width:]).astype(BF16)
    own.wait()
    cots.finish()
    peers.finish()

    @pl.when(c == n - 2)
    def _():
        far.wait_send()

    @pl.when(c == n - 1)
    def _():
        far.wait_recv()


def moe(n, n_seq, experts_all, h, cot, place, place_t, routes, router, wg, wu, wd, line):
    ex, width, ff = wg.shape
    tok = h.shape[0]
    slots = place.shape[0] // ex
    blocks = n // 2
    sds = jax.ShapeDtypeStruct
    return pl.pallas_call(
        functools.partial(moe_kernel, n, n_seq, experts_all),
        out_shape=(
            sds((tok, 128), F32),
            sds((8, 256), F32),
            sds((ex, slots, width), BF16),
            sds((n, ex, slots, ff // n), BF16),
            sds((ex, slots, ff), BF16),
            sds((ex, slots, ff), BF16),
            sds((tok, width + 128), BF16),
            sds((tok, width), BF16),
            sds((n, ex, slots, width // n), BF16),
            sds((blocks, tok, width), BF16),
            sds(line.shape, BF16),
        ),
        in_specs=[VMEM] * 6 + [HBM] * 4,
        out_specs=(VMEM,) * 8 + (HBM,) * 3,
        scratch_shapes=[
            pltpu.VMEM(wg.shape, BF16),
            pltpu.VMEM(wu.shape, BF16),
            pltpu.VMEM(wd.shape, BF16),
            pltpu.VMEM((ex, slots, width), BF16),
            pltpu.VMEM((ex, slots, width), BF16),
            pltpu.VMEM((slots, ff), BF16),
            pltpu.VMEM((ex * slots, width + 128), BF16),
            pltpu.VMEM((ex * slots, width), BF16),
            pltpu.VMEM((n, ex, slots, width // n), BF16),
            pltpu.VMEM((256, 128), F32),
            DMA((3, ex)),
            DMA((2, n)),
            DMA((2, 3, blocks)),
            DMA((1,)),
            DMA((2,)),
            pltpu.VMEM((128, width), BF16),
            pltpu.VMEM((8, tok), F32),
        ],
        input_output_aliases={9: 10},
        compiler_params=params(6, 60),
        name="moe",
        cost_estimate=cost(30),
    )(h, cot, place, place_t, routes, router, wg, wu, wd, line)


class Mp:
    def __init__(self, part, core_in, y_out, y_in, full, sems, chunks):
        self.part, self.core_in, self.y_out, self.y_in, self.full = part, core_in, y_out, y_in, full
        self.sems, self.chunks = sems, chunks
        s, c, m = lax.axis_index("seq"), lax.axis_index("ctx"), lax.axis_index("mp")
        self.m = m
        self.sib = m + 1 - 2 * lax.rem(m, 2)
        self.opp = lax.rem(m + 2, 4)
        self.diag = lax.rem(self.sib + 2, 4)
        self.sib_id, self.opp_id = (s, c, self.sib), (s, c, self.opp)
        share = (part if part is not None else full).shape[1]
        self.rows = share // chunks

    def signal(self, sem):
        for d in (self.sib_id, self.opp_id):
            pl.semaphore_signal(sem, inc=1, device_id=d, device_id_type=MESH)

    def copy(self, src, dst, i, dev):
        return pltpu.make_async_remote_copy(
            src_ref=src,
            dst_ref=dst,
            send_sem=self.sems.at[0, i],
            recv_sem=self.sems.at[1, i],
            device_id=dev,
            device_id_type=MESH,
        )

    def cut(self, i):
        return pl.ds(i * self.rows, self.rows)

    def rs_core(self, i):
        src = self.part.at[self.diag] if i == 0 else self.part.at[self.sib]
        return self.copy(src, self.core_in.at[i], i, self.sib_id)

    def rs_y(self, i):
        return self.copy(self.y_out.at[self.cut(i)], self.y_in.at[self.cut(i)], 2 + i, self.opp_id)

    def rs_begin(self):
        self.rs_core(0).start()
        self.rs_core(1).start()
        self.rs_forward()

    def rs_forward(self):
        self.rs_core(0).wait_recv()
        for i in range(self.chunks):
            cut = self.cut(i)
            self.y_out[cut, :] = (
                self.part[self.opp, cut, :].astype(F32) + self.core_in[0, cut, :].astype(F32)
            ).astype(BF16)
            self.rs_y(i).start()
        self.rs_core(1).wait_recv()

    def rs_chunk(self, i):
        cut = self.cut(i)
        self.rs_y(i).wait_recv()
        return (
            self.part[self.m, cut, :].astype(F32) + self.core_in[1, cut, :].astype(F32)
        ) + self.y_in[cut, :].astype(F32)

    def rs_end(self):
        self.rs_core(0).wait_send()
        self.rs_core(1).wait_send()
        for i in range(self.chunks):
            self.rs_y(i).wait_send()

    def ag(self, kind, i, whose):
        block = self.full.at[whose, self.cut(i)]
        base = 2 + self.chunks
        dev = self.opp_id if kind == 0 else self.sib_id
        return self.copy(block, block, base + kind * self.chunks + i, dev)

    def ag_send(self, i):
        self.ag(0, i, self.m).start()
        self.ag(1, i, self.m).start()

    def ag_end(self):
        for i in range(self.chunks):
            self.ag(0, i, self.opp).wait_recv()
            self.ag(2, i, self.opp).start()
        for i in range(self.chunks):
            self.ag(1, i, self.sib).wait_recv()
            self.ag(2, i, self.diag).wait_recv()
            self.ag(0, i, self.m).wait_send()
            self.ag(1, i, self.m).wait_send()
            self.ag(2, i, self.opp).wait_send()


def mp_scratch(share, width, chunks):
    return [
        pltpu.VMEM((2, share, width), BF16),
        pltpu.VMEM((share, width), BF16),
        pltpu.VMEM((share, width), BF16),
        DMA((2, 2 + 4 * chunks)),
    ]


def rms_parts(rows):
    inverse = lax.rsqrt(jnp.mean(rows * rows, axis=-1, keepdims=True) + EPS)
    return rows * inverse, inverse


def rms_grad(grad_normed, normed, inverse):
    return inverse * (grad_normed - normed * jnp.mean(grad_normed * normed, axis=-1, keepdims=True))


def mid_forward_kernel(
    chunks,
    n,
    ex,
    heads_ref,
    wout_ref,
    gain,
    own,
    above,
    routes_ref,
    tok_hbm,
    resid_ref,
    h_ref,
    place_ref,
    place_t,
    place_line,
    line_ref,
    core_in,
    y_out,
    y_in,
    sems,
    send,
    recv,
    local,
    x_ref,
    x_sem,
    ranks,
    part,
):
    c = lax.axis_index("ctx")
    mp = Mp(part, core_in, y_out, y_in, h_ref, sems, chunks)
    spread = Spread(n, own, None, above, line_ref, send, recv, local, short=True)
    x_copy = pltpu.make_async_copy(tok_hbm.at[mp.m], x_ref, x_sem.at[0])
    x_copy.start()
    sem = pltpu.get_barrier_semaphore()
    mp.signal(sem)
    signal_line(n, sem)
    share, width = x_ref.shape

    def outs(i):
        at = pl.ds(pl.multiple_of(i * 512, 512), 512)
        rows = tn(heads_ref[...], wout_ref[:, at]).astype(BF16)
        for p in range(part.shape[0]):
            part[p, :, at] = rows[p * share : (p + 1) * share, :]

    loop(width // 512, outs)
    pl.semaphore_wait(sem, 2 + line_degree(n))
    mp.rs_core(0).start()
    mp.rs_core(1).start()
    spread.start()
    mp.rs_forward()
    tok = routes_ref.shape[2]
    slots = place_ref.shape[0] // ex
    before = (
        lax.broadcasted_iota(jnp.int32, (tok, tok), 0) <= lax.broadcasted_iota(jnp.int32, (tok, tok), 1)
    ).astype(BF16)

    def places(b):
        at = b * ex
        ranks[...] = jnp.zeros_like(ranks)
        for e in range(ex):
            hit = routes_ref[b] == mp.m * ex + e
            ranks[e : e + 1, :] = jnp.max(hit.astype(F32), axis=0, keepdims=True)
        sel = ranks[...]
        order = nn(sel.astype(BF16), before) - 1.0
        rows = lax.broadcasted_iota(jnp.int32, (slots, tok), 0).astype(F32)
        for e in range(ex):
            one = jnp.where(rows == order[e : e + 1, :], 1.0, 0.0) * sel[e : e + 1, :]
            place_line[b, e * slots : (e + 1) * slots, :] = one.astype(BF16)

    places(c)
    place_ref[...] = place_line[c]
    place_t[...] = place_ref[...].T
    x_copy.wait()
    for i in range(chunks):
        cut = mp.cut(i)
        resid = x_ref[cut, :].astype(F32) + mp.rs_chunk(i)
        resid_ref[cut, :] = resid
        normed, _ = rms_parts(resid)
        h_ref[mp.m, cut, :] = (normed * gain[...].reshape(1, -1)).astype(BF16)
        mp.ag_send(i)
    spread.tick(1)
    loop(n - 1, lambda i: places(lax.rem(c + 1 + i, n)))
    mp.ag_end()
    mp.rs_end()
    spread.ticks(2)
    spread.finish()


def mid_forward(n, ex, slots, heads_t, w_out, gain, own, above, routes_line, tokens, chunks=2):
    k, share, width = tokens.shape
    tok = k * share
    sds = jax.ShapeDtypeStruct
    return pl.pallas_call(
        functools.partial(mid_forward_kernel, chunks, n, ex),
        out_shape=(
            sds((share, width), F32),
            sds(tokens.shape, BF16),
            sds((ex * slots, tok), BF16),
            sds((tok, ex * slots), BF16),
            sds((n, ex * slots, tok), BF16),
            sds((n,) + own.shape, BF16),
        ),
        in_specs=[VMEM] * 6 + [HBM],
        out_specs=(VMEM,) * 5 + (HBM,),
        scratch_shapes=mp_scratch(share, width, chunks)
        + [DMA((n,)), DMA((n,)), DMA((3,)), pltpu.VMEM((share, width), BF16), DMA((1,)), pltpu.VMEM((8, tok), F32)]
        + [pltpu.VMEM(tokens.shape, BF16)],
        compiler_params=params(2, 58),
        name="mid_forward",
        cost_estimate=cost(30),
    )(heads_t, w_out, gain, own, above, routes_line, tokens)


def mid_back_kernel(
    chunks,
    n,
    part,
    resid_ref,
    gain,
    cot,
    gate_ref,
    router_ref,
    rows_ref,
    hid_ref,
    du_ref,
    arr_ref,
    dg_ref,
    dresid_ref,
    db_ref,
    small_ref,
    rows_line,
    hid_line,
    below_ref,
    above_ref,
    arr_other,
    dg_other,
    core_in,
    y_out,
    y_in,
    sems,
    side,
    peers_sem,
    swap_sem,
):
    c = lax.axis_index("ctx")
    mp = Mp(part, core_in, y_out, y_in, db_ref, sems, chunks)
    rows_peers = Peers(n, lambda p: rows_ref, lambda i: rows_line.at[i], peers_sem.at[0], peers_sem.at[1])
    hid_peers = Peers(n, lambda p: hid_ref.at[p], lambda i: hid_line.at[i], peers_sem.at[2], peers_sem.at[3])
    beside = Neighbours(n, du_ref, below_ref, above_ref, side.at[0], side.at[1])
    width = gain.shape[0]
    ex = router_ref.shape[0]
    lanes = gate_ref.shape[2]
    sem = pltpu.get_barrier_semaphore()
    mp.signal(sem)
    rows_peers.signal(sem)
    partner = swap_partner()
    pl.semaphore_signal(sem, inc=1, device_id=partner, device_id_type=MESH)
    pl.semaphore_wait(sem, 2 + n - 1 + 1)
    mp.rs_core(0).start()
    mp.rs_core(1).start()
    half_width = width // 2
    theirs = pl.ds(pl.multiple_of((1 - lax.axis_index("seq")) * half_width, 128), half_width)
    swaps = [
        swap(arr_ref.at[:, :, theirs], arr_other, swap_sem, 0),
        swap(dg_ref, dg_other, swap_sem, 1),
    ]
    for sw in swaps:
        sw.start()
    beside.start_up()
    beside.start_down()
    rows_peers.start()
    hid_peers.start()
    mp.rs_forward()
    rows_line[c] = rows_ref[...]
    small_ref[...] = jnp.zeros_like(small_ref)
    for i in range(chunks):
        cut = mp.cut(i)
        both = mp.rs_chunk(i)
        dgate = both[:, width : width + ex] + both[:, width + lanes // 2 : width + lanes // 2 + ex]
        gate = gate_ref[mp.m, cut, :ex]
        dlog = gate * (dgate - jnp.sum(gate * dgate, axis=-1, keepdims=True))
        dh = both[:, :width] + jnp.dot(
            dlog, router_ref[...], precision=lax.Precision.HIGHEST, preferred_element_type=F32
        )
        normed, inverse = rms_parts(resid_ref[cut, :])
        small_ref[1:2, :] = small_ref[1:2, :] + jnp.sum(dh * normed, axis=0, keepdims=True)
        h_two = (normed * gain[...].reshape(1, -1)).astype(BF16).astype(F32)
        small_ref[8 : 8 + ex, :] = small_ref[8 : 8 + ex, :] + lax.dot_general(
            dlog, h_two, (((0,), (0,)), ((), ())), precision=lax.Precision.HIGHEST, preferred_element_type=F32
        )
        dresid = cot[cut, :].astype(F32) + rms_grad(dh * gain[...].reshape(1, -1), normed, inverse)
        dresid_ref[cut, :] = dresid
        db_ref[mp.m, cut, :] = dresid.astype(BF16)
        mp.ag_send(i)
    mp.ag_end()
    mp.rs_end()
    rows_peers.finish()
    hid_peers.finish()
    beside.finish()
    for sw in swaps:
        sw.wait()


def swap_partner():
    return (1 - lax.axis_index("seq"), lax.axis_index("ctx"), lax.axis_index("mp"))


def swap(src, dst, sems, i):
    return pltpu.make_async_remote_copy(
        src_ref=src,
        dst_ref=dst,
        send_sem=sems.at[0, i],
        recv_sem=sems.at[1, i],
        device_id=swap_partner(),
        device_id_type=MESH,
    )


def mid_back(n, part, resid, gain, cot, gate, router_t, rows, hid, du, arr, dg, chunks=2):
    k, share, wide = part.shape
    width = gain.shape[0]
    return pl.pallas_call(
        functools.partial(mid_back_kernel, chunks, n),
        out_shape=(
            jax.ShapeDtypeStruct((share, width), F32),
            jax.ShapeDtypeStruct((k, share, width), BF16),
            jax.ShapeDtypeStruct((8 + router_t.shape[0], width), F32),
            jax.ShapeDtypeStruct((n,) + rows.shape, F32),
            jax.ShapeDtypeStruct(hid.shape, BF16),
            jax.ShapeDtypeStruct(du.shape, BF16),
            jax.ShapeDtypeStruct(du.shape, BF16),
            jax.ShapeDtypeStruct(arr.shape[:2] + (arr.shape[2] // 2,), BF16),
            jax.ShapeDtypeStruct(dg.shape, BF16),
        ),
        in_specs=[VMEM] * 7 + [HBM] * 4,
        out_specs=(VMEM,) * 4 + (HBM,) * 5,
        scratch_shapes=mp_scratch(share, wide, chunks) + [DMA((2, 2)), DMA((4, n)), DMA((2, 2))],
        compiler_params=params(3, 60),
        name="mid_back",
        cost_estimate=cost(32),
    )(part, resid, gain, cot, gate, router_t, rows, hid, du, arr, dg)


class SmallSum:
    def __init__(self, sizes, x_ref, out_ref, bufs, sems):
        self.sizes, self.x, self.out, self.bufs, self.sems = sizes, x_ref, out_ref, bufs, sems
        self.me = [lax.axis_index(a) for a in ("seq", "ctx", "mp")]

    def peer(self, axis, d):
        ids = list(self.me)
        ids[axis] = lax.rem(self.me[axis] + d, self.sizes[axis])
        return tuple(ids)

    def signal(self, sem):
        for axis in range(3):
            for d in range(1, self.sizes[axis]):
                pl.semaphore_signal(sem, inc=1, device_id=self.peer(axis, d), device_id_type=MESH)
        return sum(self.sizes) - 3

    def move(self, axis, d):
        base = sum(self.sizes[:axis])
        buf = self.bufs[axis]
        return pltpu.make_async_remote_copy(
            src_ref=buf.at[0],
            dst_ref=buf.at[d],
            send_sem=self.sems.at[0, base + d],
            recv_sem=self.sems.at[1, base + d],
            device_id=self.peer(axis, d),
            device_id_type=MESH,
        )

    def begin(self, axis, value):
        self.bufs[axis][0] = value
        for d in range(1, self.sizes[axis]):
            self.move(axis, d).start()

    def end(self, axis):
        n = self.sizes[axis]
        for d in range(1, n):
            self.move(axis, d).wait()
        total = jnp.zeros(self.out.shape, F32)
        for i in range(n):
            total = total + self.bufs[axis][lax.rem(self.me[axis] - i + n, n)]
        return total


def last_kernel(
    chunks,
    sizes,
    dqkv_ref,
    h_hbm,
    wq_hbm,
    wk_hbm,
    wv_hbm,
    tok_hbm,
    gain,
    dresid_hbm,
    small_ref,
    wout_ref,
    up0_hbm,
    up_other,
    comb_hbm,
    resid_hbm,
    out_ref,
    final_ref,
    total_ref,
    gout_ref,
    gqkv_ref,
    up_ref,
    core_in,
    y_out,
    y_in,
    sems,
    core_in2,
    y_out2,
    y_in2,
    sems2,
    h_ref,
    wq_ref,
    wk_ref,
    wv_ref,
    tok_ref,
    dresid_ref,
    comb,
    resid_ref,
    part,
    dh_ref,
    qkv_ref,
    swapped,
    summed,
    wout_in,
    qkv_in,
    up_in,
    load_sem,
    swap_sem,
    peers_sem,
    *rest,
):
    n = sizes[1]
    s, c = lax.axis_index("seq"), lax.axis_index("ctx")
    load = Staged(
        (
            (h_hbm, h_ref),
            (wq_hbm, wq_ref),
            (wk_hbm, wk_ref),
            (wv_hbm, wv_ref),
            (tok_hbm, tok_ref),
            (comb_hbm, comb),
            (dresid_hbm, dresid_ref),
            (resid_hbm, resid_ref),
            (up0_hbm, up_ref),
        ),
        load_sem,
    )
    load.start()
    mp = Mp(part, core_in, y_out, y_in, None, sems, chunks)
    mp2 = Mp(comb, core_in2, y_out2, y_in2, None, sems2, chunks)
    small = SmallSum(sizes, small_ref, total_ref, rest[:3], rest[3])
    half_rows = swapped.shape[0]
    rows = half_rows // n
    wout_peers = Peers(
        n, lambda p: wout_ref.at[cut_of(p, rows)], lambda i: wout_in.at[i], peers_sem.at[0], peers_sem.at[1]
    )
    qkv_peers = Peers(
        n, lambda p: summed.at[cut_of(p, rows)], lambda i: qkv_in.at[i], peers_sem.at[2], peers_sem.at[3]
    )
    sem = pltpu.get_barrier_semaphore()
    pl.semaphore_wait(sem, small.signal(sem))
    wout_peers.start()
    load.wait(0)

    def weight_rows(first):
        def piece(r):
            at = pl.ds(pl.multiple_of(first + r * 256, 256), 256)
            qkv_ref[at, :] = tn(h_ref[:, at], dqkv_ref[...]).astype(BF16)

        loop(half_rows // 256, piece)

    weight_rows((1 - s) * half_rows)

    def chunk_swap(k):
        p = lax.rem(c + 1 + k, n)
        return swap(qkv_ref.at[cut_of((1 - s) * n + p, rows)], swapped.at[cut_of(p, rows)], swap_sem, k)

    up_swap = swap(up_other, up_in, swap_sem, n)

    def chunk_arrived(k):
        chunk_swap(k).wait_recv()
        if k + 2 < n:
            chunk_swap(k + 2).start()
        if k + 2 == n:
            up_swap.start()
        p = lax.rem(c + 1 + k, n)
        here = cut_of(p, rows)
        summed[here, :] = (
            qkv_ref[cut_of(s * n + p, rows), :].astype(F32) + swapped[here, :].astype(F32)
        ).astype(BF16)
        if k < n - 1:
            qkv_peers.move(k + 1).start()

    for k in range(min(2, n)):
        chunk_swap(k).start()
    load.wait(1, 2, 3)
    share, width = out_ref.shape
    qw, kw = wq_ref.shape[1], wk_ref.shape[1]

    def token_rows(i):
        at = pl.ds(pl.multiple_of(i * 512, 512), 512)
        dh = nt(dqkv_ref[:, :qw], wq_ref[at, :])
        dh = dh + nt(dqkv_ref[:, qw : qw + kw], wk_ref[at, :])
        dh = dh + nt(dqkv_ref[:, qw + kw :], wv_ref[at, :])
        for p in range(part.shape[0]):
            dh_ref[p, :, at] = dh[p * share : (p + 1) * share, :]
            part[p, :, at] = dh[p * share : (p + 1) * share, :].astype(BF16)

    loop(width // 512, token_rows)
    mp.rs_core(0).start()
    mp.rs_core(1).start()
    load.wait(5)
    mp2.rs_core(0).start()
    mp2.rs_core(1).start()
    weight_rows(s * half_rows)
    mp.rs_forward()
    load.wait(4)
    total_ref[...] = small_ref[...]

    def norm_rows(p):
        normed, _ = rms_parts(tok_ref[p].astype(F32))
        total_ref[0:1, :] = total_ref[0:1, :] + jnp.sum(dh_ref[p] * normed, axis=0, keepdims=True)

    loop(part.shape[0], norm_rows)
    small.begin(1, total_ref[...])
    chunk_arrived(0)
    mp2.rs_forward()
    chunk_arrived(1)
    load.wait(6)
    for i in range(chunks):
        cut = mp.cut(i)
        dh = mp.rs_chunk(i)
        normed, inverse = rms_parts(tok_ref[mp.m, cut, :].astype(F32))
        final_ref[cut, :] = dresid_ref[cut, :] + rms_grad(dh * gain[...].reshape(1, -1), normed, inverse)
        if i + 2 < n:
            chunk_arrived(i + 2)
        if i == 0:
            small.begin(0, small.end(1))
    for k in range(chunks + 2, n):
        chunk_arrived(k)
    small.begin(2, small.end(0))
    load.wait(7)
    for i in range(chunks):
        cut = mp.cut(i)
        out_ref[cut, :] = resid_ref[cut, :] + mp2.rs_chunk(i)
    total_ref[...] = small.end(2)
    wout_peers.finish()
    wout_in[c] = wout_ref[cut_of(c, rows), :]
    total = jnp.zeros(gout_ref.shape, F32)
    for i in range(n):
        total = total + wout_in[i].astype(F32)
    gout_ref[...] = total
    mp.rs_end()
    mp2.rs_end()
    load.wait(8)
    for k in range(n):
        chunk_swap(k).wait_send()
    qkv_peers.finish()
    qkv_in[c] = summed[cut_of(c, rows), :]
    total = jnp.zeros(gqkv_ref.shape, F32)
    for i in range(n):
        total = total + qkv_in[i].astype(F32)
    gqkv_ref[...] = total
    up_swap.wait()
    up_ref[...] = up_ref[...] + up_in[...].astype(F32)


def cut_of(i, rows):
    return pl.ds(pl.multiple_of(i * rows, 16), rows)


def last(sizes, dqkv, h, wq, wk, wv, tokens, gain, dresid, small, wout, up0, up_other, comb, resid, chunks=2):
    k, share, width = comb.shape
    n = sizes[1]
    half_rows, fo = wout.shape
    fq = dqkv.shape[1]
    rows = half_rows // n
    sds = jax.ShapeDtypeStruct
    vm = lambda x: pltpu.VMEM(x.shape, x.dtype)
    return pl.pallas_call(
        functools.partial(last_kernel, chunks, sizes),
        out_shape=(
            sds((share, width), F32),
            sds((share, width), F32),
            sds(small.shape, F32),
            sds((rows, fo), F32),
            sds((rows, fq), F32),
            sds(up0.shape, F32),
        ),
        in_specs=[VMEM] + [HBM] * 5 + [VMEM, HBM, VMEM, VMEM, HBM, VMEM, HBM, HBM],
        out_specs=(VMEM,) * 6,
        scratch_shapes=mp_scratch(share, width, chunks)
        + mp_scratch(share, width, chunks)
        + [vm(h), vm(wq), vm(wk), vm(wv), vm(tokens), vm(dresid), vm(comb), vm(resid)]
        + [
            pltpu.VMEM(comb.shape, BF16),
            pltpu.VMEM(comb.shape, F32),
            pltpu.VMEM((2 * half_rows, fq), BF16),
            pltpu.VMEM((half_rows, fq), BF16),
            pltpu.VMEM((half_rows, fq), BF16),
            pltpu.VMEM((n, rows, fo), BF16),
            pltpu.VMEM((n, rows, fq), BF16),
            pltpu.VMEM(up0.shape, BF16),
            DMA((9,)),
            DMA((2, n + 1)),
            DMA((4, n)),
        ]
        + [pltpu.VMEM((d,) + small.shape, F32) for d in sizes]
        + [DMA((2, sum(sizes)))],
        compiler_params=params(4, 60),
        name="last",
        cost_estimate=cost(60),
    )(dqkv, h, wq, wk, wv, tokens, gain, dresid, small, wout, up0, up_other, comb, resid)


def finish_kernel(*refs):
    n_in = 8
    total, gout, gqkv = refs[5:n_in]
    outs = refs[n_in : n_in + 12]
    sems = refs[n_in + 12]
    output, tokens, norm1, gq, gk, gv, go, norm2, router, gate, up, down = outs
    large = Staged(tuple(zip(refs[:5], (output, tokens, gate, up, down))), sems)
    large.start()
    norm1[...] = total[0, :]
    norm2[...] = total[1, :]
    router[...] = total[8 : 8 + router.shape[0], :]
    qw, kw = gq.shape[1], gk.shape[1]
    gq[...] = gqkv[:, :qw]
    gk[...] = gqkv[:, qw : qw + kw]
    gv[...] = gqkv[:, qw + kw :]
    go[...] = gout[...].T
    large.wait(0, 1, 2, 3, 4)


def finish(experts_all, qw, output, tokens, gate, up, down, total, gout, gqkv):
    sds = jax.ShapeDtypeStruct
    width = total.shape[1]
    rows = gqkv.shape[0]
    kw = (gqkv.shape[1] - qw) // 2
    shapes = (
        output.shape,
        tokens.shape,
        (width,),
        (rows, qw),
        (rows, kw),
        (rows, kw),
        gout.shape[::-1],
        (width,),
        (experts_all, width),
        gate.shape,
        up.shape,
        down.shape,
    )
    return pl.pallas_call(
        finish_kernel,
        out_shape=tuple(sds(x, F32) for x in shapes),
        in_specs=[HBM] * 5 + [VMEM] * 3,
        out_specs=(VMEM,) * 12,
        scratch_shapes=[DMA((5,))],
        compiler_params=pltpu.CompilerParams(vmem_limit_bytes=60 * MIB),
        name="finish",
        cost_estimate=cost(6),
    )(output, tokens, gate, up, down, total, gout, gqkv)


def body(
    tokens,
    norm1_gain,
    w_query,
    key_weight_matrix,
    value_weight_matrix,
    w_out,
    norm2_gain,
    router,
    w_gate,
    w_up,
    w_down,
    routes,
    cotangent,
):
    n_seq, n_ctx, n_mp = (lax.axis_size(a) for a in ("seq", "ctx", "mp"))
    s, c, m = (lax.axis_index(a) for a in ("seq", "ctx", "mp"))
    tok, width = tokens.shape
    share = tok // n_mp
    experts_all = router.shape[1]
    exp_local = w_gate.shape[0]
    top = routes.shape[1]
    cap = share * top * 5 // (4 * experts_all)
    slots = -(-n_mp * cap // 16) * 16

    cot_all = lax.all_gather(cotangent, "mp", axis=0, tiled=True)
    by_share = tokens.reshape(n_mp, share, width)

    qt, h_one, o, heads_t, lse, kv, cot_above, routes_line = attend(
        n_ctx, tokens, norm1_gain, w_query, key_weight_matrix, value_weight_matrix, cotangent, routes.T
    )
    resid, h_two, place, place_t, place_line, cot_line = mid_forward(
        n_ctx, exp_local, slots, heads_t, w_out, norm2_gain, cotangent, cot_above, routes_line, by_share
    )
    h_two = h_two.reshape(tok, width)

    gates, gate_rows, arrived, hidden, dg, du, back, comb, arrived_line, cot_first, cot_line = moe(
        n_ctx, n_seq, experts_all, h_two, cot_all, place, place_t, routes.T, router.T, w_gate, w_up, w_down, cot_line
    )
    dresid, db, small, gate_rows_line, hidden_line, du_below, du_above, arrived_other, dg_other = mid_back(
        n_ctx,
        back.reshape(n_mp, share, -1),
        resid,
        norm2_gain,
        cotangent,
        gates.reshape(n_mp, share, -1),
        router.T,
        gate_rows,
        hidden,
        du,
        arrived,
        dg,
    )

    db = db.reshape(tok, width)
    dqkv, g_gate, g_down, up0, up_other, g_out, _, _ = attend_back(
        n_ctx,
        qt,
        db,
        w_out,
        o,
        lse,
        kv,
        arrived,
        arrived_other,
        dg,
        dg_other,
        gate_rows_line,
        du,
        du_below,
        du_above,
        hidden_line,
        hidden,
        heads_t,
        arrived_line,
        place_line,
        cot_line,
        cot_first,
    )
    output, grad_tokens, small, g_out, g_qkv, g_up = last(
        (n_seq, n_ctx, n_mp),
        dqkv,
        h_one,
        w_query,
        key_weight_matrix,
        value_weight_matrix,
        by_share,
        norm1_gain,
        dresid,
        small,
        g_out,
        up0,
        up_other,
        comb.reshape(n_mp, share, width),
        resid,
    )
    outs = finish(experts_all, w_query.shape[1], output, grad_tokens, g_gate, g_up, g_down, small, g_out, g_qkv)
    return outs[:8] + (outs[8].T,) + outs[9:]


def solution(mesh):
    placed = (
        P(("seq", "ctx"), None),
        P(),
        P(None, "mp"),
        P(None, "mp"),
        P(None, "mp"),
        P("mp", None),
        P(),
        P(),
        P("mp", None, None),
        P("mp", None, None),
        P("mp", None, None),
        P(("seq", "ctx"), None),
        P(("seq", "ctx", "mp"), None),
    )
    return jax.shard_map(
        body,
        mesh=mesh,
        in_specs=placed,
        out_specs=(
            P(("seq", "ctx", "mp"), None),
            P(("seq", "ctx", "mp"), None),
            P(),
            P(("seq", "ctx"), "mp"),
            P(("seq", "ctx"), "mp"),
            P(("seq", "ctx"), "mp"),
            P("mp", ("seq", "ctx")),
            P(),
            P(),
            P("mp", ("seq", "ctx"), None),
            P("mp", ("seq", "ctx"), None),
            P("mp", ("seq", "ctx"), None),
        ),
        check_vma=False,
    )
```

```python
import functools

import jax
import jax.numpy as jnp
from jax import lax
from jax.experimental import pallas as pl
from jax.experimental.pallas import tpu as pltpu
from jax.sharding import PartitionSpec as P

HEAD_SIZE = 64
EPS = 1e-06
MESH = pl.DeviceIdType.MESH
F32 = jnp.float32
BF16 = jnp.bfloat16
VMEM = pl.BlockSpec(memory_space=pltpu.VMEM)
HBM = pl.BlockSpec(memory_space=pl.ANY)
DMA = pltpu.SemaphoreType.DMA
MIB = 2**20


def cost(us):
    return pl.CostEstimate(flops=0, bytes_accessed=int(us * 3.6e6), transcendentals=0)


def params(collective_id, mib=56):
    return pltpu.CompilerParams(
        collective_id=collective_id, has_side_effects=True, vmem_limit_bytes=mib * MIB
    )


def nt(a, b):
    return lax.dot_general(a, b, (((1,), (1,)), ((), ())), preferred_element_type=F32)


def nn(a, b):
    return jnp.dot(a, b, preferred_element_type=F32)


class Staged:
    def __init__(self, pairs, sems):
        self.copies = [pltpu.make_async_copy(src, dst, sems.at[i]) for i, (src, dst) in enumerate(pairs)]

    def start(self):
        for copy in self.copies:
            copy.start()

    def wait(self, *which):
        for i in which:
            self.copies[i].wait()


class Spread:
    def __init__(self, n, own, below, above, all_ref, send, recv, local, short=False):
        self.n, self.own, self.below, self.above, self.all = n, own, below, above, all_ref
        self.send, self.recv, self.local = send, recv, local
        self.top = n - 2 if short else n - 1
        s, self.c, m = lax.axis_index("seq"), lax.axis_index("ctx"), lax.axis_index("mp")
        self.lower, self.upper = lax.rem(self.c + n - 1, n), lax.rem(self.c + 1, n)
        self.up, self.down = (s, self.upper, m), (s, self.lower, m)
        self.inner = jnp.logical_and(self.c > 0, self.c < n - 1)

    def move(self, b, src, device):
        return pltpu.make_async_remote_copy(
            src_ref=src,
            dst_ref=self.all.at[b],
            send_sem=self.send.at[b],
            recv_sem=self.recv.at[b],
            device_id=device,
            device_id_type=MESH,
        )

    def keep(self, i, src, b):
        return pltpu.make_async_copy(src, self.all.at[b], self.local.at[i])

    def goes_up(self, b):
        return jnp.logical_and(self.c < self.n - 1, self.c - b < self.top)

    def start(self):
        if self.below is None:

            @pl.when(self.c < self.n - 1)
            def _():
                self.move(self.c, self.own, self.up).start()
        else:

            @pl.when(jnp.logical_and(self.inner, self.goes_up(self.lower)))
            def _():
                self.move(self.lower, self.below, self.up).start()

            @pl.when(self.c > 0)
            def _():
                self.keep(1, self.below, self.lower).start()

        @pl.when(self.inner)
        def _():
            self.move(self.upper, self.above, self.down).start()

        self.keep(0, self.own, self.c).start()

        @pl.when(self.c < self.n - 1)
        def _():
            self.keep(2, self.above, self.upper).start()

    def tick(self, i):
        c, n = self.c, self.n
        off = i if self.below is None else i + 1

        @pl.when(jnp.logical_and(c - off >= 0, off <= self.top))
        def _():
            b = jnp.maximum(c - off, 0)
            self.move(b, self.all.at[b], self.up).wait_recv()

            @pl.when(self.goes_up(b))
            def _():
                self.move(b, self.all.at[b], self.up).start()

        @pl.when(c + 1 + i <= n - 1)
        def _():
            b = jnp.minimum(c + 1 + i, n - 1)
            self.move(b, self.all.at[b], self.down).wait_recv()

            @pl.when(c > 0)
            def _():
                self.move(b, self.all.at[b], self.down).start()

    def ticks(self, first):
        def later(i, carry):
            self.tick(i)
            return carry

        lax.fori_loop(first, self.n if self.below is None else self.n - 1, later, 0)

    def finish(self):
        self.keep(0, self.own, self.c).wait()

        if self.below is not None:

            @pl.when(self.c > 0)
            def _():
                self.keep(1, self.below, self.lower).wait()

        @pl.when(self.c < self.n - 1)
        def _():
            self.keep(2, self.above, self.upper).wait()

        def sent(b, carry):
            if self.below is None:
                sent_up = jnp.logical_and(b <= self.c, self.goes_up(b))
            else:
                sent_up = jnp.logical_and(b < self.c, self.goes_up(b))

            @pl.when(jnp.logical_or(sent_up, jnp.logical_and(b > self.c, self.c > 0)))
            def _():
                self.move(b, self.all.at[b], self.up).wait_send()

            return carry

        lax.fori_loop(0, self.n, sent, 0)


class Neighbours:
    def __init__(self, n, own, below, above, send, recv):
        self.n, self.own, self.below, self.above, self.send, self.recv = n, own, below, above, send, recv
        s, self.c, m = lax.axis_index("seq"), lax.axis_index("ctx"), lax.axis_index("mp")
        self.up, self.down = (s, lax.rem(self.c + 1, n), m), (s, lax.rem(self.c + n - 1, n), m)

    def move(self, way):
        return pltpu.make_async_remote_copy(
            src_ref=self.own,
            dst_ref=self.below if way == 0 else self.above,
            send_sem=self.send.at[way],
            recv_sem=self.recv.at[way],
            device_id=self.up if way == 0 else self.down,
            device_id_type=MESH,
        )

    def start_up(self):
        @pl.when(self.c < self.n - 1)
        def _():
            self.move(0).start()

    def start_down(self):
        @pl.when(self.c > 0)
        def _():
            self.move(1).start()

    def finish(self, up=True):
        @pl.when(self.c > 0)
        def _():
            if up:
                self.move(0).wait_recv()
            self.move(1).wait_send()

        @pl.when(self.c < self.n - 1)
        def _():
            self.move(1).wait_recv()
            if up:
                self.move(0).wait_send()


class LineSum:
    ahead = 2

    def __init__(self, n, parts, from_below, from_above, send, recv):
        self.n, self.parts, self.bufs, self.send, self.recv = n, parts, (from_below, from_above), send, recv
        s, self.c, m = lax.axis_index("seq"), lax.axis_index("ctx"), lax.axis_index("mp")
        self.up, self.down = (s, lax.rem(self.c + 1, n), m), (s, lax.rem(self.c + n - 1, n), m)
        self.ex, self.rows = from_below.shape[1], from_below.shape[2]
        self.units = (n - 1) * self.ex
        self.ticks = self.units + n - 3

    def own(self, k, e):
        return self.parts.at[e, pl.ds(pl.multiple_of(k * self.rows, 16), self.rows), :]

    def move(self, way, k, e, first=False):
        there = self.bufs[way].at[k, e]
        return pltpu.make_async_remote_copy(
            src_ref=self.own(k, e) if first else there,
            dst_ref=there,
            send_sem=self.send.at[way, k, e],
            recv_sem=self.recv.at[way, k, e],
            device_id=self.up if way == 0 else self.down,
            device_id_type=MESH,
        )

    def unit(self, way, u):
        k = lax.div(u, self.ex)
        return (self.n - 1 - k if way == 0 else k), lax.rem(u, self.ex)

    def first(self, u):
        for way, end in ((0, 0), (1, self.n - 1)):

            @pl.when(jnp.logical_and(self.c == end, u < self.units))
            def _():
                @pl.when(u >= self.ahead)
                def _():
                    self.move(way, *self.unit(way, jnp.maximum(u - self.ahead, 0)), True).wait_send()

                self.move(way, *self.unit(way, jnp.minimum(u, self.units - 1)), True).start()

    def tick(self, i):
        self.first(i + 1)
        for way, far in ((0, self.c), (1, self.n - 1 - self.c)):
            u = i - far

            @pl.when(jnp.logical_and(far > 0, jnp.logical_and(u >= 0, u < (self.n - 1 - far) * self.ex)))
            def _():
                k, e = self.unit(way, jnp.clip(u, 0, self.units - 1))
                self.move(way, k, e).wait_recv()
                self.bufs[way][k, e] = (
                    self.own(k, e)[...].astype(F32) + self.bufs[way][k, e].astype(F32)
                ).astype(BF16)
                self.move(way, k, e).start()

    def finish(self, out):
        c = self.c
        for e in range(self.ex):
            out[e] = self.own(c, e)[...].astype(F32)
        for way, far in ((0, c), (1, self.n - 1 - c)):

            @pl.when(far > 0)
            def _():
                for e in range(self.ex):
                    self.move(way, c, e).wait_recv()
                    out[e] = out[e] + self.bufs[way][c, e].astype(F32)

            done = jnp.where(far == 0, max(self.units - self.ahead, 0), 0)

            def sent(u, carry):
                self.move(way, *self.unit(way, u)).wait_send()
                return carry

            lax.fori_loop(done, (self.n - 1 - far) * self.ex, sent, 0)


class Peers:
    def __init__(self, n, src_of, dst_of, send, recv):
        self.n, self.src_of, self.dst_of, self.send, self.recv = n, src_of, dst_of, send, recv
        self.s, self.c, self.m = lax.axis_index("seq"), lax.axis_index("ctx"), lax.axis_index("mp")

    def move(self, d):
        peer = lax.rem(self.c + d, self.n)
        return pltpu.make_async_remote_copy(
            src_ref=self.src_of(peer),
            dst_ref=self.dst_of(self.c),
            send_sem=self.send.at[d],
            recv_sem=self.recv.at[d],
            device_id=(self.s, peer, self.m),
            device_id_type=MESH,
        )

    def signal(self, sem):
        for d in range(1, self.n):
            pl.semaphore_signal(
                sem, inc=1, device_id=(self.s, lax.rem(self.c + d, self.n), self.m), device_id_type=MESH
            )

    def start(self):
        for d in range(1, self.n):
            self.move(d).start()

    def finish(self):
        for d in range(1, self.n):
            self.move(d).wait()


class CotExchange:
    def __init__(self, n, line_ref, full, first, sems):
        self.n, self.line, self.full, self.first, self.sems = n, line_ref, full, first, sems
        self.count = full.shape[0]
        s, self.c, m = lax.axis_index("seq"), lax.axis_index("ctx"), lax.axis_index("mp")
        self.m = m
        self.share = line_ref.shape[1]
        self.sib = m + 1 - 2 * lax.rem(m, 2)
        self.opp = lax.rem(m + 2, 4)
        self.sib_id, self.opp_id = (s, self.c, self.sib), (s, self.c, self.opp)

    def signal(self, sem):
        for d in (self.sib_id, self.opp_id):
            pl.semaphore_signal(sem, inc=1, device_id=d, device_id_type=MESH)

    def place(self, i, who):
        return self.full.at[i, pl.ds(pl.multiple_of(who * self.share, 16), self.share), :]

    def mine(self, i):
        return self.line.at[lax.rem(self.c - self.first - i + 2 * self.n, self.n)]

    def move(self, kind, i):
        whose = self.opp if kind == 2 else self.m
        return pltpu.make_async_remote_copy(
            src_ref=self.place(i, self.opp) if kind == 2 else self.mine(i),
            dst_ref=self.place(i, whose),
            send_sem=self.sems.at[0, kind, i],
            recv_sem=self.sems.at[1, kind, i],
            device_id=self.opp_id if kind == 0 else self.sib_id,
            device_id_type=MESH,
        )

    def start(self):
        for i in range(self.count):
            self.move(0, i).start()
            self.move(1, i).start()

    def finish(self):
        for i in range(self.count):
            self.move(0, i).wait_recv()
            self.move(2, i).start()
        for i in range(self.count):
            self.move(1, i).wait_recv()
            self.move(2, i).wait_recv()
            for kind in range(3):
                self.move(kind, i).wait_send()


def signal_line(n, sem):
    s, c, m = lax.axis_index("seq"), lax.axis_index("ctx"), lax.axis_index("mp")

    @pl.when(c > 0)
    def _():
        pl.semaphore_signal(sem, inc=1, device_id=(s, lax.rem(c + n - 1, n), m), device_id_type=MESH)

    @pl.when(c < n - 1)
    def _():
        pl.semaphore_signal(sem, inc=1, device_id=(s, lax.rem(c + 1, n), m), device_id_type=MESH)


def line_degree(n):
    c = lax.axis_index("ctx")
    return jnp.where(c > 0, 1, 0) + jnp.where(c < n - 1, 1, 0)


def pad_heads(src, dst, heads, group):
    dst[...] = jnp.zeros_like(dst)
    for h in range(heads):
        g = h // group
        rows = slice(g * HEAD_SIZE, (g + 1) * HEAD_SIZE)
        dst[h, rows, :] = src[h * HEAD_SIZE : (h + 1) * HEAD_SIZE, :]


def causal(t):
    keys = lax.broadcasted_iota(jnp.int32, (t, t), 0)
    queries = lax.broadcasted_iota(jnp.int32, (t, t), 1)
    return keys <= queries


def attend_kernel(
    n,
    tok_ref,
    gain,
    wq_ref,
    wk_ref,
    wv_ref,
    cot_ref,
    routes_ref,
    q_ref,
    h_ref,
    o_ref,
    heads_ref,
    lse_ref,
    kv_ref,
    above_ref,
    line_ref,
    qpad,
    vt,
    top,
    tot,
    send,
    recv,
    side,
    peers_sem,
):
    s, c, m = lax.axis_index("seq"), lax.axis_index("ctx"), lax.axis_index("mp")
    t, kvw = tok_ref.shape[0], wk_ref.shape[1]
    heads = q_ref.shape[0] // HEAD_SIZE
    group = heads // (kvw // HEAD_SIZE)
    up, down = (s, lax.rem(c + 1, n), m), (s, lax.rem(c + n - 1, n), m)

    def norm_rows(i):
        rows = pl.ds(pl.multiple_of(i * 128, 128), 128)
        normed, _ = rms_parts(tok_ref[rows, :].astype(F32))
        h_ref[rows, :] = (normed * gain[...].reshape(1, -1)).astype(BF16)

    loop(t // 128, norm_rows)
    kv_ref[0, :, :kvw] = nn(h_ref[...], wk_ref[...]).astype(BF16)
    kv_ref[0, :, kvw:] = nn(h_ref[...], wv_ref[...]).astype(BF16)
    line_ref[c] = routes_ref[...]
    peers = Peers(n, lambda p: routes_ref, lambda i: line_ref.at[i], peers_sem.at[0], peers_sem.at[1])
    beside = Neighbours(n, cot_ref, None, above_ref, side.at[0], side.at[1])
    sem = pltpu.get_barrier_semaphore()
    peers.signal(sem)
    pl.semaphore_wait(sem, n - 1)

    def pass_up(slot):
        return pltpu.make_async_remote_copy(
            src_ref=kv_ref.at[slot],
            dst_ref=kv_ref.at[slot + 1],
            send_sem=send.at[slot],
            recv_sem=recv.at[slot + 1],
            device_id=up,
            device_id_type=MESH,
        )

    def got(slot):
        return pltpu.make_async_remote_copy(
            src_ref=kv_ref.at[slot],
            dst_ref=kv_ref.at[slot],
            send_sem=send.at[slot],
            recv_sem=recv.at[slot],
            device_id=up,
            device_id_type=MESH,
        )

    @pl.when(c < n - 1)
    def _():
        pass_up(0).start()

    peers.start()
    beside.start_down()
    q_ref[...] = (nn(h_ref[...], wq_ref[...]) * 0.125).astype(BF16).T
    pad_heads(q_ref, qpad, heads, group)
    top[...] = jnp.full_like(top, -1e30)
    tot[...] = jnp.zeros_like(tot)
    o_ref[...] = jnp.zeros_like(o_ref)

    def block(slot, masked):
        vt[...] = kv_ref[slot, :, kvw:].T

        def head(h, carry):
            g = lax.div(h, group)
            scores = nn(kv_ref[slot, :, :kvw], qpad[h])
            if masked:
                scores = jnp.where(causal(t), scores, -1e30)
            old = top[h]
            new = jnp.maximum(old, jnp.max(scores, axis=0, keepdims=True))
            weights = jnp.exp(scores - new)
            factor = jnp.exp(old - new)
            top[h] = new
            tot[h] = tot[h] * factor + jnp.sum(weights, axis=0, keepdims=True)
            rows = pl.ds(pl.multiple_of(h * HEAD_SIZE, HEAD_SIZE), HEAD_SIZE)
            vrows = pl.ds(pl.multiple_of(g * HEAD_SIZE, HEAD_SIZE), HEAD_SIZE)
            o_ref[rows, :] = o_ref[rows, :] * factor + nn(vt[vrows, :], weights.astype(BF16))
            return carry

        lax.fori_loop(0, heads, head, 0)

    block(0, True)

    def earlier(slot, carry):
        got(slot).wait_recv()

        @pl.when(c < n - 1)
        def _():
            pass_up(slot).start()

        block(slot, False)
        return carry

    lax.fori_loop(1, c + 1, earlier, 0)
    for h in range(heads):
        rows = slice(h * HEAD_SIZE, (h + 1) * HEAD_SIZE)
        done = o_ref[rows, :] / tot[h]
        o_ref[rows, :] = done
        heads_ref[rows, :] = done.astype(BF16)
        lse_ref[h] = top[h] + jnp.log(tot[h])

    @pl.when(c < n - 1)
    def _():
        def sent(slot, carry):
            pass_up(slot).wait_send()
            return carry

        lax.fori_loop(0, c + 1, sent, 0)

    peers.finish()
    beside.finish(up=False)


def attend(n, tokens, gain, wq, wk, wv, cot, routes):
    t, kvw = tokens.shape[0], wk.shape[1]
    qw = wq.shape[1]
    heads = qw // HEAD_SIZE
    return pl.pallas_call(
        functools.partial(attend_kernel, n),
        out_shape=(
            jax.ShapeDtypeStruct((qw, t), BF16),
            jax.ShapeDtypeStruct(tokens.shape, BF16),
            jax.ShapeDtypeStruct((qw, t), F32),
            jax.ShapeDtypeStruct((qw, t), BF16),
            jax.ShapeDtypeStruct((heads, 1, t), F32),
            jax.ShapeDtypeStruct((n, t, 2 * kvw), BF16),
            jax.ShapeDtypeStruct(cot.shape, BF16),
            jax.ShapeDtypeStruct((n,) + routes.shape, jnp.int32),
        ),
        in_specs=[VMEM] * 5 + [HBM, VMEM],
        out_specs=(VMEM,) * 6 + (HBM, VMEM),
        scratch_shapes=[
            pltpu.VMEM((heads, kvw, t), BF16),
            pltpu.VMEM((kvw, t), BF16),
            pltpu.VMEM((heads, 1, t), F32),
            pltpu.VMEM((heads, 1, t), F32),
            DMA((n,)),
            DMA((n,)),
            DMA((2, 2)),
            DMA((2, n)),
        ],
        compiler_params=params(0),
        name="attend",
        cost_estimate=cost(30),
    )(tokens, gain, wq, wk, wv, cot, routes)


def attend_back_kernel(
    n,
    q_hbm,
    db_hbm,
    wout_hbm,
    o_hbm,
    lse_ref,
    kv_hbm,
    arr_ref,
    arr_other,
    dg_ref,
    dg_other,
    rows_line,
    own_hbm,
    below_hbm,
    above_hbm,
    hid_hbm,
    hid_own,
    heads_hbm,
    arr_hbm,
    place_hbm,
    line_hbm,
    first_hbm,
    dqkv_ref,
    gate_ref,
    down_ref,
    up_ref,
    up_other,
    wsum_ref,
    all_hbm,
    rest_hbm,
    do_ref,
    qpad,
    dopad,
    delta,
    dq,
    kt,
    part,
    passing,
    sum_ref,
    from_below,
    from_above,
    place_buf,
    cot_buf,
    hid_buf,
    arr_buf,
    du_buf,
    dy,
    acc_ref,
    kv_sem,
    sum_sem,
    spread_sem,
    local,
    ysem,
    load_sem,
    swap_sem,
    wout_part,
    wout_in,
    down_out,
    down_in,
    stage_sem,
    db_ref,
    wout_ref,
    own_ref,
    below_ref,
    above_ref,
    heads_ref,
    q_ref,
    o_ref,
    kv_ref,
):
    s, c, m = lax.axis_index("seq"), lax.axis_index("ctx"), lax.axis_index("mp")
    load = Staged(
        (
            (db_hbm, db_ref),
            (wout_hbm, wout_ref),
            (own_hbm, own_ref),
            (below_hbm, below_ref),
            (above_hbm, above_ref),
            (heads_hbm, heads_ref),
            (q_hbm, q_ref),
            (o_hbm, o_ref),
            (kv_hbm, kv_ref),
        ),
        stage_sem,
    )
    load.start()
    _, t, kvw2 = kv_ref.shape
    kvw = kvw2 // 2
    heads = q_ref.shape[0] // HEAD_SIZE
    group = heads // (kvw // HEAD_SIZE)
    ex, slots, width = arr_ref.shape
    half_width = width // 2
    down = (s, lax.rem(c + n - 1, n), m)
    spread = Spread(n, own_ref, below_ref, above_ref, all_hbm, spread_sem.at[0], spread_sem.at[1], local)
    done_blocks = first_hbm.shape[0]
    cots = CotExchange(n, line_hbm, rest_hbm, done_blocks, ysem)
    line = LineSum(n, sum_ref, from_below, from_above, sum_sem.at[0], sum_sem.at[1])
    sem = pltpu.get_barrier_semaphore()
    signal_line(n, sem)
    cots.signal(sem)
    pl.semaphore_signal(sem, inc=1, device_id=swap_partner(), device_id_type=MESH)
    pl.semaphore_wait(sem, line_degree(n) + 3)
    cots.start()

    def gate_part(e, out):
        def piece(r):
            mine = pl.ds(pl.multiple_of(s * half_width + r * 256, 128), 256)
            cut = pl.ds(pl.multiple_of(r * 256, 256), 256)
            out[cut, :] = (tn(arr_ref[e, :, mine], dg_ref[e]) + tn(arr_other[e, :, cut], dg_other[e])).astype(BF16)

        loop(half_width // 256, piece)

    for e in range(ex):
        gate_part(e, sum_ref.at[e])
        if e == 0:
            line.first(0)
            load.wait(0, 1, 2, 3, 4)
            spread.start()
    do_ref[...] = nt(wout_ref[...], db_ref[...]).astype(BF16)

    load.wait(5)

    def wout_piece(r):
        at = pl.ds(pl.multiple_of(r * 512, 512), 512)
        wout_part[:, at] = nn(heads_ref[...], db_ref[:, at]).astype(BF16)

    loop(width // 512, wout_piece)
    own_half, other_half = (pl.ds(pl.multiple_of(k * half_width, 128), half_width) for k in (s, 1 - s))
    wout_swap = swap(wout_part.at[:, other_half], wout_in, swap_sem, 0)
    wout_swap.start()

    def tick(i):
        line.tick(i)
        for hop in range(1, n - 1):

            @pl.when(i == 2 * hop - 1)
            def _():
                spread.tick(hop)

    ticks = max(line.ticks, 2 * (n - 2)) + 1
    load.wait(6, 7, 8)
    pad_heads(q_ref, qpad, heads, group)
    pad_heads(do_ref, dopad, heads, group)
    for h in range(heads):
        rows = slice(h * HEAD_SIZE, (h + 1) * HEAD_SIZE)
        delta[h] = jnp.sum(do_ref[rows, :].astype(F32) * o_ref[rows, :], axis=0, keepdims=True)
    dq[...] = jnp.zeros_like(dq)

    def block(j, masked):
        slot = c - j
        acc = part.at[lax.rem(j, 2)]
        acc[...] = jnp.zeros(acc.shape, F32)
        kt[...] = kv_ref[slot, :, :kvw].T

        def head(h, carry):
            g = lax.div(h, group)
            scores = nn(kv_ref[slot, :, :kvw], qpad[h])
            probs = jnp.exp(scores - lse_ref[h])
            if masked:
                probs = jnp.where(causal(t), probs, 0.0)
            dprobs = nn(kv_ref[slot, :, kvw:], dopad[h])
            ds = (probs * (dprobs - delta[h])).astype(BF16)
            rows = pl.ds(pl.multiple_of(h * HEAD_SIZE, HEAD_SIZE), HEAD_SIZE)
            krows = pl.ds(pl.multiple_of(g * HEAD_SIZE, HEAD_SIZE), HEAD_SIZE)
            dq[rows, :] = dq[rows, :] + nn(kt[krows, :], ds)
            acc[:, :kvw] = acc[:, :kvw] + nt(ds, qpad[h])
            acc[:, kvw:] = acc[:, kvw:] + nt(probs.astype(BF16), dopad[h])
            return carry

        lax.fori_loop(0, heads, head, 0)

    def pass_down(j):
        return pltpu.make_async_remote_copy(
            src_ref=passing.at[j],
            dst_ref=passing.at[j],
            send_sem=kv_sem.at[0, j],
            recv_sem=kv_sem.at[1, j],
            device_id=down,
            device_id_type=MESH,
        )

    def gathered(j):
        acc = part.at[lax.rem(j, 2)]

        @pl.when(c < n - 1)
        def _():
            pass_down(j).wait_recv()
            acc[...] = acc[...] + passing[j].astype(F32)

        return acc

    def forward(j):
        acc = gathered(j)
        passing[j] = acc[...].astype(BF16)
        pass_down(j).start()

    def step(j, carry):
        block(j, False)

        @pl.when(jnp.logical_and(j > 0, c < n - 1))
        def _():
            forward(j - 1)

        @pl.when(c == n - 1)
        def _():
            forward(j)

        tick(j)
        return carry

    lax.fori_loop(0, c, step, 0)
    def later(i, carry):
        tick(i)
        return carry

    middle = jnp.maximum(c, min(2, ticks))
    lax.fori_loop(c, middle, later, 0)

    cots.finish()

    def load_block(i, slot, start):
        b = lax.rem(c - i + n, n)
        share = line_hbm.shape[1]
        place_copy = pltpu.make_async_copy(place_hbm.at[b], place_buf.at[slot], load_sem.at[0, slot])
        hid_copy = pltpu.make_async_copy(hid_hbm.at[b], hid_buf.at[slot], load_sem.at[1, slot])
        hid_mine = pltpu.make_async_copy(hid_own.at[b], hid_buf.at[slot], load_sem.at[1, slot])

        def rows(who):
            return pl.ds(pl.multiple_of(who * share, 16), share)

        def piece(k, who, full, at):
            return pltpu.make_async_copy(
                full.at[at, rows(who), :], cot_buf.at[slot, rows(who), :], load_sem.at[2 + k, slot]
            )

        others = (cots.sib, cots.opp, lax.rem(cots.sib + 2, 4))
        mine = pltpu.make_async_copy(line_hbm.at[b], cot_buf.at[slot, rows(m), :], load_sem.at[5, slot])
        first = [piece(k, who, first_hbm, jnp.minimum(i, done_blocks - 1)) for k, who in enumerate(others)]
        if not start:
            for copy in [place_copy, hid_copy, mine] + first:
                copy.wait()
            return
        rest = [piece(k, who, rest_hbm, jnp.maximum(i - done_blocks, 0)) for k, who in enumerate(others)]
        place_copy.start()
        mine.start()

        @pl.when(b == c)
        def _():
            hid_mine.start()

        @pl.when(b != c)
        def _():
            hid_copy.start()

        @pl.when(i < done_blocks)
        def _():
            for copy in first:
                copy.start()

        @pl.when(i >= done_blocks)
        def _():
            for copy in rest:
                copy.start()

    fa, ua = hid_hbm.shape[3], arr_hbm.shape[3]
    ff = dg_ref.shape[2]
    acc_ref[...] = jnp.zeros_like(acc_ref)
    load_block(0, 0, True)
    wide = 512

    def down_block(i):
        slot = lax.rem(i, 2)
        load_block(i, slot, False)

        @pl.when(i < n - 1)
        def _():
            load_block(i + 1, 1 - slot, True)

        cols = rows_line[lax.rem(c - i + n, n)].T
        for e in range(ex):

            def dys(k):
                cut = pl.ds(pl.multiple_of(k * wide, wide), wide)
                dy[:, cut] = (
                    cols[:slots, e : e + 1] * nn(place_buf[slot, e * slots : (e + 1) * slots, :], cot_buf[slot, :, cut])
                ).astype(BF16)

            loop(width // wide, dys)
            acc_ref[e, :fa, :] = acc_ref[e, :fa, :] + tn(hid_buf[slot, e], dy[...])

    loop(n, down_block)
    mine, other = (pl.ds(pl.multiple_of(k * (fa // 2), 16), fa // 2) for k in (s, 1 - s))
    down_ref[...] = acc_ref[:, mine, :]
    down_out[...] = acc_ref[:, other, :].astype(BF16)
    wout_swap.wait()
    down_swap = swap(down_out, down_in, swap_sem, 1)
    down_swap.start()
    wsum_ref[...] = (wout_part[:, own_half].astype(F32) + wout_in[...].astype(F32)).astype(BF16).T

    after = jnp.minimum(middle + 1, ticks)
    lax.fori_loop(middle, after, later, 0)
    block(c, True)

    @pl.when(jnp.logical_and(c > 0, c < n - 1))
    def _():
        forward(c - 1)

    qw = dq.shape[0]
    dqkv_ref[:, :qw] = (dq[...] * 0.125).astype(BF16).T
    lax.fori_loop(after, ticks, later, 0)

    spread.finish()
    acc_ref[...] = jnp.zeros_like(acc_ref)

    def load_du(b, slot):
        return (
            pltpu.make_async_copy(all_hbm.at[b], du_buf.at[slot], load_sem.at[6, slot]),
            pltpu.make_async_copy(arr_hbm.at[b], arr_buf.at[slot], load_sem.at[7, slot]),
        )

    for copy in load_du(0, 0):
        copy.start()

    def up_block(b):
        slot = lax.rem(b, 2)
        for copy in load_du(b, slot):
            copy.wait()

        @pl.when(b < n - 1)
        def _():
            for copy in load_du(b + 1, 1 - slot):
                copy.start()

        for e in range(ex):
            acc_ref[e, :ua, :ff] = acc_ref[e, :ua, :ff] + tn(arr_buf[slot, e], du_buf[slot, e])

    loop(n, up_block)
    mine, other = (pl.ds(pl.multiple_of(k * (ua // 2), 16), ua // 2) for k in (s, 1 - s))
    up_ref[...] = acc_ref[:, mine, :ff]
    up_other[...] = acc_ref[:, other, :ff].astype(BF16)

    acc = gathered(c)
    dqkv_ref[:, qw:] = acc[...].astype(BF16)
    line.finish(gate_ref)
    down_swap.wait()
    down_ref[...] = down_ref[...] + down_in[...].astype(F32)

    def sent_kv(j, carry):
        pass_down(j).wait_send()
        return carry

    lax.fori_loop(0, c, sent_kv, 0)


def attend_back(n, qt, db, w_out, o, lse, kv, arr, arr_other, dg, dg_other, rows, du, below, above, hid, hid_own, heads_t, arr_line, place, line, first):
    qw, t = qt.shape
    heads = qw // HEAD_SIZE
    kvw = kv.shape[2] // 2
    ex, slots, width = arr.shape
    ff = dg.shape[2]
    half_width = width // 2
    chunk = (ex, half_width // n, ff)
    fa, ua = hid.shape[3], arr_line.shape[3]
    blocks = first.shape[0]
    sds = jax.ShapeDtypeStruct
    return pl.pallas_call(
        functools.partial(attend_back_kernel, n),
        out_shape=(
            sds((t, qw + 2 * kvw), BF16),
            sds(chunk, F32),
            sds((ex, fa // 2, width), F32),
            sds((ex, ua // 2, ff), F32),
            sds((ex, ua // 2, ff), BF16),
            sds((half_width, qw), BF16),
            sds((n,) + du.shape, BF16),
            sds((n - blocks,) + first.shape[1:], BF16),
        ),
        in_specs=[HBM] * 4 + [VMEM, HBM] + [VMEM] * 5 + [HBM] * 10,
        out_specs=(VMEM,) * 6 + (HBM,) * 2,
        scratch_shapes=[
            pltpu.VMEM((qw, t), BF16),
            pltpu.VMEM((heads, kvw, t), BF16),
            pltpu.VMEM((heads, kvw, t), BF16),
            pltpu.VMEM((heads, 1, t), F32),
            pltpu.VMEM((qw, t), F32),
            pltpu.VMEM((kvw, t), BF16),
            pltpu.VMEM((2, t, 2 * kvw), F32),
            pltpu.VMEM((n, t, 2 * kvw), BF16),
            pltpu.VMEM((ex, half_width, ff), BF16),
            pltpu.VMEM((n,) + chunk, BF16),
            pltpu.VMEM((n,) + chunk, BF16),
            pltpu.VMEM((2,) + place.shape[1:], BF16),
            pltpu.VMEM((2,) + first.shape[1:], BF16),
            pltpu.VMEM((2, ex, slots, fa), BF16),
            pltpu.VMEM((2, ex, slots, ua), BF16),
            pltpu.VMEM((2,) + du.shape, BF16),
            pltpu.VMEM((slots, width), BF16),
            pltpu.VMEM((ex, max(fa, ua), width), F32),
            DMA((2, n)),
            DMA((2, 2, n, ex)),
            DMA((2, n)),
            DMA((3,)),
            DMA((2, 3, n - blocks)),
            DMA((8, 2)),
            DMA((2, 2)),
            pltpu.VMEM((qw, width), BF16),
            pltpu.VMEM((qw, half_width), BF16),
            pltpu.VMEM((ex, fa // 2, width), BF16),
            pltpu.VMEM((ex, fa // 2, width), BF16),
            DMA((9,)),
        ]
        + [pltpu.VMEM(x.shape, x.dtype) for x in (db, w_out, du, below, above, heads_t, qt, o, kv)],
        compiler_params=params(1, 62),
        name="attend_back",
        cost_estimate=cost(60),
    )(qt, db, w_out, o, lse, kv, arr, arr_other, dg, dg_other, rows, du, below, above, hid, hid_own, heads_t, arr_line, place, line, first)


def tn(a, b):
    return lax.dot_general(a, b, (((0,), (0,)), ((), ())), preferred_element_type=F32)


def loop(n, f):
    def step(i, carry):
        f(i)
        return carry

    lax.fori_loop(0, n, step, 0)


def moe_kernel(
    n,
    n_seq,
    experts_all,
    h_ref,
    cot_ref,
    place_ref,
    place_t_ref,
    routes_ref,
    router_ref,
    wg_hbm,
    wu_hbm,
    wd_hbm,
    line_hbm,
    gates_ref,
    rows_ref,
    arr_ref,
    hid_ref,
    dg_ref,
    du_ref,
    back_ref,
    comb_ref,
    arr_line,
    cot_first,
    line_out,
    wg,
    wu,
    wd,
    dout,
    dy,
    hid,
    back_rows,
    comb_rows,
    parts,
    cols,
    wsem,
    peers_sem,
    ysem,
    local,
    far_sem,
    router3,
    named,
):
    s, c, m = lax.axis_index("seq"), lax.axis_index("ctx"), lax.axis_index("mp")
    ex, width, ff = wg.shape
    slots = place_ref.shape[0] // ex
    first = m * ex
    lanes = gates_ref.shape[1]
    peers = Peers(n, lambda p: parts.at[p], lambda i: arr_line.at[i], peers_sem.at[0], peers_sem.at[1])
    cots = CotExchange(n, line_hbm, cot_first, 0, ysem)
    far = pltpu.make_async_remote_copy(
        src_ref=line_hbm.at[0],
        dst_ref=line_out.at[0],
        send_sem=far_sem.at[0],
        recv_sem=far_sem.at[1],
        device_id=(s, lax.rem(c + 1, n), m),
        device_id_type=MESH,
    )
    sem = pltpu.get_barrier_semaphore()
    peers.signal(sem)
    cots.signal(sem)
    weights = {}
    for e in range(ex):
        for i, (src, dst) in enumerate(((wg_hbm, wg), (wu_hbm, wu), (wd_hbm, wd))):
            weights[i, e] = pltpu.make_async_copy(src.at[e], dst.at[e], wsem.at[i, e])
            weights[i, e].start()

    pl.semaphore_wait(sem, n - 1 + 2)
    cots.start()

    @pl.when(c == n - 2)
    def _():
        far.start()

    def rows_of(e):
        return slice(e * slots, (e + 1) * slots)

    def arrive(i):
        cut = pl.ds(pl.multiple_of(i * slots, 16), slots)
        arr_ref[i] = nn(place_ref[cut, :], h_ref[...]).astype(BF16)

    loop(ex, arrive)
    size = width // (n * n_seq)
    for e in range(ex):
        for i in range(n):
            for j in range(n_seq):
                at = (j * n + i) * size
                parts[i, e, :, j * size : (j + 1) * size] = arr_ref[e, :, at : at + size]
    peers.start()
    own = pltpu.make_async_copy(parts.at[c], arr_line.at[c], local.at[0])
    own.start()

    router3[...] = jnp.zeros_like(router3)
    left = router_ref[...]
    for i in range(3):
        piece = left.astype(BF16)
        router3[i * experts_all : (i + 1) * experts_all, :] = piece
        left = left - piece.astype(F32)
    three = nt(h_ref[...], router3[...])
    logits = three + pltpu.roll(three, lanes - experts_all, 1) + pltpu.roll(three, lanes - 2 * experts_all, 1)
    which = lax.broadcasted_iota(jnp.int32, three.shape, 1)
    top = routes_ref.shape[0]
    named[...] = jnp.zeros_like(named)
    named[:top, :] = routes_ref[...].astype(F32)
    columns = named[...].T
    which = which.astype(F32)
    chosen = which == columns[:, 0:1]
    for k in range(1, top):
        chosen = jnp.logical_or(chosen, which == columns[:, k : k + 1])
    peak = jnp.max(jnp.where(chosen, logits, -1e30), axis=1, keepdims=True)
    raised = jnp.where(chosen, jnp.exp(jnp.where(chosen, logits - peak, 0.0)), 0.0)
    gates = raised / jnp.sum(raised, axis=1, keepdims=True)
    gates_ref[...] = gates
    g1 = gates.astype(BF16)
    rest = gates - g1.astype(F32)
    g2 = rest.astype(BF16)
    g3 = (rest - g2.astype(F32)).astype(BF16)
    lane = lax.broadcasted_iota(jnp.int32, (slots, lanes), 1)
    cols[...] = jnp.zeros_like(cols)
    gate_col = []
    for e in range(ex):
        pe = place_ref[rows_of(e), :]
        got = nn(pe, g1) + nn(pe, g2) + nn(pe, g3)
        col = jnp.sum(jnp.where(lane == first + e, got, 0.0), axis=1, keepdims=True)
        gate_col.append(col)
        cols[:slots, :] = cols[:slots, :] + jnp.where(lane == e, col, 0.0)

    rows_ref[...] = cols[...].T[:8, :]
    wide = 512
    for e in range(ex):
        col = gate_col[e]

        def douts(i):
            cut = pl.ds(pl.multiple_of(i * wide, wide), wide)
            d = nn(place_ref[rows_of(e), :], cot_ref[:, cut])
            dout[e, :, cut] = d.astype(BF16)
            dy[e, :, cut] = (col * d).astype(BF16)

        loop(width // wide, douts)
        for i in range(3):
            weights[i, e].wait()

        def hidden(i):
            cut = pl.ds(pl.multiple_of(i * 256, 256), 256)
            g = nn(arr_ref[e], wg[e, :, cut])
            u = nn(arr_ref[e], wu[e, :, cut])
            dh = nt(dy[e], wd[e, cut, :])
            sigma = jax.nn.sigmoid(g)
            silu = g * sigma
            hid[:, cut] = (silu * u).astype(BF16)
            dg_ref[e, :, cut] = (dh * u * sigma * (1.0 + g * (1.0 - sigma))).astype(BF16)
            du_ref[e, :, cut] = (dh * silu).astype(BF16)

        loop(ff // 256, hidden)
        size = ff // (n * n_seq)
        for i in range(n):
            for j in range(n_seq):
                at = (j * n + i) * size
                hid_ref[i, e, :, j * size : (j + 1) * size] = hid[:, at : at + size]

        def outs(i, grads):
            cut = pl.ds(pl.multiple_of(i * wide, wide), wide)
            y = nn(hid[...], wd[e, :, cut]).astype(BF16).astype(F32)
            comb_rows[rows_of(e), cut] = (col * y).astype(BF16)
            back_rows[rows_of(e), cut] = (nt(dg_ref[e], wg[e, cut, :]) + nt(du_ref[e], wu[e, cut, :])).astype(BF16)
            return grads + jnp.sum(dout[e, :, cut].astype(F32) * y, axis=1, keepdims=True)

        grads = lax.fori_loop(0, width // wide, outs, jnp.zeros((slots, 1), F32))
        high = grads.astype(BF16).astype(F32)
        here = jnp.where(lane == first + e, high, jnp.where(lane == lanes // 2 + first + e, grads - high, 0.0))
        back_rows[rows_of(e), width:] = here.astype(BF16)

    def scatter(i):
        cut = pl.ds(pl.multiple_of(i * 256, 256), 256)
        back_ref[:, cut] = nn(place_t_ref[...], back_rows[:, cut]).astype(BF16)
        comb_ref[:, cut] = nn(place_t_ref[...], comb_rows[:, cut]).astype(BF16)

    loop(width // 256, scatter)
    back_ref[:, width:] = nn(place_t_ref[...], back_rows[:, width:]).astype(BF16)
    own.wait()
    cots.finish()
    peers.finish()

    @pl.when(c == n - 2)
    def _():
        far.wait_send()

    @pl.when(c == n - 1)
    def _():
        far.wait_recv()


def moe(n, n_seq, experts_all, h, cot, place, place_t, routes, router, wg, wu, wd, line):
    ex, width, ff = wg.shape
    tok = h.shape[0]
    slots = place.shape[0] // ex
    blocks = n // 2
    sds = jax.ShapeDtypeStruct
    return pl.pallas_call(
        functools.partial(moe_kernel, n, n_seq, experts_all),
        out_shape=(
            sds((tok, 128), F32),
            sds((8, 256), F32),
            sds((ex, slots, width), BF16),
            sds((n, ex, slots, ff // n), BF16),
            sds((ex, slots, ff), BF16),
            sds((ex, slots, ff), BF16),
            sds((tok, width + 128), BF16),
            sds((tok, width), BF16),
            sds((n, ex, slots, width // n), BF16),
            sds((blocks, tok, width), BF16),
            sds(line.shape, BF16),
        ),
        in_specs=[VMEM] * 6 + [HBM] * 4,
        out_specs=(VMEM,) * 8 + (HBM,) * 3,
        scratch_shapes=[
            pltpu.VMEM(wg.shape, BF16),
            pltpu.VMEM(wu.shape, BF16),
            pltpu.VMEM(wd.shape, BF16),
            pltpu.VMEM((ex, slots, width), BF16),
            pltpu.VMEM((ex, slots, width), BF16),
            pltpu.VMEM((slots, ff), BF16),
            pltpu.VMEM((ex * slots, width + 128), BF16),
            pltpu.VMEM((ex * slots, width), BF16),
            pltpu.VMEM((n, ex, slots, width // n), BF16),
            pltpu.VMEM((256, 128), F32),
            DMA((3, ex)),
            DMA((2, n)),
            DMA((2, 3, blocks)),
            DMA((1,)),
            DMA((2,)),
            pltpu.VMEM((128, width), BF16),
            pltpu.VMEM((8, tok), F32),
        ],
        input_output_aliases={9: 10},
        compiler_params=params(6, 60),
        name="moe",
        cost_estimate=cost(30),
    )(h, cot, place, place_t, routes, router, wg, wu, wd, line)


class Mp:
    def __init__(self, part, core_in, y_out, y_in, full, sems, chunks):
        self.part, self.core_in, self.y_out, self.y_in, self.full = part, core_in, y_out, y_in, full
        self.sems, self.chunks = sems, chunks
        s, c, m = lax.axis_index("seq"), lax.axis_index("ctx"), lax.axis_index("mp")
        self.m = m
        self.sib = m + 1 - 2 * lax.rem(m, 2)
        self.opp = lax.rem(m + 2, 4)
        self.diag = lax.rem(self.sib + 2, 4)
        self.sib_id, self.opp_id = (s, c, self.sib), (s, c, self.opp)
        share = (part if part is not None else full).shape[1]
        self.rows = share // chunks

    def signal(self, sem):
        for d in (self.sib_id, self.opp_id):
            pl.semaphore_signal(sem, inc=1, device_id=d, device_id_type=MESH)

    def copy(self, src, dst, i, dev):
        return pltpu.make_async_remote_copy(
            src_ref=src,
            dst_ref=dst,
            send_sem=self.sems.at[0, i],
            recv_sem=self.sems.at[1, i],
            device_id=dev,
            device_id_type=MESH,
        )

    def cut(self, i):
        return pl.ds(i * self.rows, self.rows)

    def rs_core(self, i):
        src = self.part.at[self.diag] if i == 0 else self.part.at[self.sib]
        return self.copy(src, self.core_in.at[i], i, self.sib_id)

    def rs_y(self, i):
        return self.copy(self.y_out.at[self.cut(i)], self.y_in.at[self.cut(i)], 2 + i, self.opp_id)

    def rs_begin(self):
        self.rs_core(0).start()
        self.rs_core(1).start()
        self.rs_forward()

    def rs_forward(self):
        self.rs_core(0).wait_recv()
        for i in range(self.chunks):
            cut = self.cut(i)
            self.y_out[cut, :] = (
                self.part[self.opp, cut, :].astype(F32) + self.core_in[0, cut, :].astype(F32)
            ).astype(BF16)
            self.rs_y(i).start()
        self.rs_core(1).wait_recv()

    def rs_chunk(self, i):
        cut = self.cut(i)
        self.rs_y(i).wait_recv()
        return (
            self.part[self.m, cut, :].astype(F32) + self.core_in[1, cut, :].astype(F32)
        ) + self.y_in[cut, :].astype(F32)

    def rs_end(self):
        self.rs_core(0).wait_send()
        self.rs_core(1).wait_send()
        for i in range(self.chunks):
            self.rs_y(i).wait_send()

    def ag(self, kind, i, whose):
        block = self.full.at[whose, self.cut(i)]
        base = 2 + self.chunks
        dev = self.opp_id if kind == 0 else self.sib_id
        return self.copy(block, block, base + kind * self.chunks + i, dev)

    def ag_send(self, i):
        self.ag(0, i, self.m).start()
        self.ag(1, i, self.m).start()

    def ag_end(self):
        for i in range(self.chunks):
            self.ag(0, i, self.opp).wait_recv()
            self.ag(2, i, self.opp).start()
        for i in range(self.chunks):
            self.ag(1, i, self.sib).wait_recv()
            self.ag(2, i, self.diag).wait_recv()
            self.ag(0, i, self.m).wait_send()
            self.ag(1, i, self.m).wait_send()
            self.ag(2, i, self.opp).wait_send()


def mp_scratch(share, width, chunks):
    return [
        pltpu.VMEM((2, share, width), BF16),
        pltpu.VMEM((share, width), BF16),
        pltpu.VMEM((share, width), BF16),
        DMA((2, 2 + 4 * chunks)),
    ]


def rms_parts(rows):
    inverse = lax.rsqrt(jnp.mean(rows * rows, axis=-1, keepdims=True) + EPS)
    return rows * inverse, inverse


def rms_grad(grad_normed, normed, inverse):
    return inverse * (grad_normed - normed * jnp.mean(grad_normed * normed, axis=-1, keepdims=True))


def mid_forward_kernel(
    chunks,
    n,
    ex,
    heads_ref,
    wout_ref,
    gain,
    own,
    above,
    routes_ref,
    tok_hbm,
    resid_ref,
    h_ref,
    place_ref,
    place_t,
    place_line,
    line_ref,
    core_in,
    y_out,
    y_in,
    sems,
    send,
    recv,
    local,
    x_ref,
    x_sem,
    ranks,
    part,
):
    c = lax.axis_index("ctx")
    mp = Mp(part, core_in, y_out, y_in, h_ref, sems, chunks)
    spread = Spread(n, own, None, above, line_ref, send, recv, local, short=True)
    x_copy = pltpu.make_async_copy(tok_hbm.at[mp.m], x_ref, x_sem.at[0])
    x_copy.start()
    sem = pltpu.get_barrier_semaphore()
    mp.signal(sem)
    signal_line(n, sem)
    share, width = x_ref.shape

    def outs(i):
        at = pl.ds(pl.multiple_of(i * 512, 512), 512)
        rows = tn(heads_ref[...], wout_ref[:, at]).astype(BF16)
        for p in range(part.shape[0]):
            part[p, :, at] = rows[p * share : (p + 1) * share, :]

    loop(width // 512, outs)
    pl.semaphore_wait(sem, 2 + line_degree(n))
    mp.rs_core(0).start()
    mp.rs_core(1).start()
    spread.start()
    mp.rs_forward()
    tok = routes_ref.shape[2]
    slots = place_ref.shape[0] // ex
    before = (
        lax.broadcasted_iota(jnp.int32, (tok, tok), 0) <= lax.broadcasted_iota(jnp.int32, (tok, tok), 1)
    ).astype(BF16)

    def places(b):
        at = b * ex
        ranks[...] = jnp.zeros_like(ranks)
        for e in range(ex):
            hit = routes_ref[b] == mp.m * ex + e
            ranks[e : e + 1, :] = jnp.max(hit.astype(F32), axis=0, keepdims=True)
        sel = ranks[...]
        order = nn(sel.astype(BF16), before) - 1.0
        rows = lax.broadcasted_iota(jnp.int32, (slots, tok), 0).astype(F32)
        for e in range(ex):
            one = jnp.where(rows == order[e : e + 1, :], 1.0, 0.0) * sel[e : e + 1, :]
            place_line[b, e * slots : (e + 1) * slots, :] = one.astype(BF16)

    places(c)
    place_ref[...] = place_line[c]
    place_t[...] = place_ref[...].T
    x_copy.wait()
    for i in range(chunks):
        cut = mp.cut(i)
        resid = x_ref[cut, :].astype(F32) + mp.rs_chunk(i)
        resid_ref[cut, :] = resid
        normed, _ = rms_parts(resid)
        h_ref[mp.m, cut, :] = (normed * gain[...].reshape(1, -1)).astype(BF16)
        mp.ag_send(i)
    spread.tick(1)
    loop(n - 1, lambda i: places(lax.rem(c + 1 + i, n)))
    mp.ag_end()
    mp.rs_end()
    spread.ticks(2)
    spread.finish()


def mid_forward(n, ex, slots, heads_t, w_out, gain, own, above, routes_line, tokens, chunks=2):
    k, share, width = tokens.shape
    tok = k * share
    sds = jax.ShapeDtypeStruct
    return pl.pallas_call(
        functools.partial(mid_forward_kernel, chunks, n, ex),
        out_shape=(
            sds((share, width), F32),
            sds(tokens.shape, BF16),
            sds((ex * slots, tok), BF16),
            sds((tok, ex * slots), BF16),
            sds((n, ex * slots, tok), BF16),
            sds((n,) + own.shape, BF16),
        ),
        in_specs=[VMEM] * 6 + [HBM],
        out_specs=(VMEM,) * 5 + (HBM,),
        scratch_shapes=mp_scratch(share, width, chunks)
        + [DMA((n,)), DMA((n,)), DMA((3,)), pltpu.VMEM((share, width), BF16), DMA((1,)), pltpu.VMEM((8, tok), F32)]
        + [pltpu.VMEM(tokens.shape, BF16)],
        compiler_params=params(2, 58),
        name="mid_forward",
        cost_estimate=cost(30),
    )(heads_t, w_out, gain, own, above, routes_line, tokens)


def mid_back_kernel(
    chunks,
    n,
    part,
    resid_ref,
    gain,
    cot,
    gate_ref,
    router_ref,
    rows_ref,
    hid_ref,
    du_ref,
    arr_ref,
    dg_ref,
    dresid_ref,
    db_ref,
    small_ref,
    rows_line,
    hid_line,
    below_ref,
    above_ref,
    arr_other,
    dg_other,
    core_in,
    y_out,
    y_in,
    sems,
    side,
    peers_sem,
    swap_sem,
):
    c = lax.axis_index("ctx")
    mp = Mp(part, core_in, y_out, y_in, db_ref, sems, chunks)
    rows_peers = Peers(n, lambda p: rows_ref, lambda i: rows_line.at[i], peers_sem.at[0], peers_sem.at[1])
    hid_peers = Peers(n, lambda p: hid_ref.at[p], lambda i: hid_line.at[i], peers_sem.at[2], peers_sem.at[3])
    beside = Neighbours(n, du_ref, below_ref, above_ref, side.at[0], side.at[1])
    width = gain.shape[0]
    ex = router_ref.shape[0]
    lanes = gate_ref.shape[2]
    sem = pltpu.get_barrier_semaphore()
    mp.signal(sem)
    rows_peers.signal(sem)
    partner = swap_partner()
    pl.semaphore_signal(sem, inc=1, device_id=partner, device_id_type=MESH)
    pl.semaphore_wait(sem, 2 + n - 1 + 1)
    mp.rs_core(0).start()
    mp.rs_core(1).start()
    half_width = width // 2
    theirs = pl.ds(pl.multiple_of((1 - lax.axis_index("seq")) * half_width, 128), half_width)
    swaps = [
        swap(arr_ref.at[:, :, theirs], arr_other, swap_sem, 0),
        swap(dg_ref, dg_other, swap_sem, 1),
    ]
    for sw in swaps:
        sw.start()
    beside.start_up()
    beside.start_down()
    rows_peers.start()
    hid_peers.start()
    mp.rs_forward()
    rows_line[c] = rows_ref[...]
    small_ref[...] = jnp.zeros_like(small_ref)
    for i in range(chunks):
        cut = mp.cut(i)
        both = mp.rs_chunk(i)
        dgate = both[:, width : width + ex] + both[:, width + lanes // 2 : width + lanes // 2 + ex]
        gate = gate_ref[mp.m, cut, :ex]
        dlog = gate * (dgate - jnp.sum(gate * dgate, axis=-1, keepdims=True))
        dh = both[:, :width] + jnp.dot(
            dlog, router_ref[...], precision=lax.Precision.HIGHEST, preferred_element_type=F32
        )
        normed, inverse = rms_parts(resid_ref[cut, :])
        small_ref[1:2, :] = small_ref[1:2, :] + jnp.sum(dh * normed, axis=0, keepdims=True)
        h_two = (normed * gain[...].reshape(1, -1)).astype(BF16).astype(F32)
        small_ref[8 : 8 + ex, :] = small_ref[8 : 8 + ex, :] + lax.dot_general(
            dlog, h_two, (((0,), (0,)), ((), ())), precision=lax.Precision.HIGHEST, preferred_element_type=F32
        )
        dresid = cot[cut, :].astype(F32) + rms_grad(dh * gain[...].reshape(1, -1), normed, inverse)
        dresid_ref[cut, :] = dresid
        db_ref[mp.m, cut, :] = dresid.astype(BF16)
        mp.ag_send(i)
    mp.ag_end()
    mp.rs_end()
    rows_peers.finish()
    hid_peers.finish()
    beside.finish()
    for sw in swaps:
        sw.wait()


def swap_partner():
    return (1 - lax.axis_index("seq"), lax.axis_index("ctx"), lax.axis_index("mp"))


def swap(src, dst, sems, i):
    return pltpu.make_async_remote_copy(
        src_ref=src,
        dst_ref=dst,
        send_sem=sems.at[0, i],
        recv_sem=sems.at[1, i],
        device_id=swap_partner(),
        device_id_type=MESH,
    )


def mid_back(n, part, resid, gain, cot, gate, router_t, rows, hid, du, arr, dg, chunks=2):
    k, share, wide = part.shape
    width = gain.shape[0]
    return pl.pallas_call(
        functools.partial(mid_back_kernel, chunks, n),
        out_shape=(
            jax.ShapeDtypeStruct((share, width), F32),
            jax.ShapeDtypeStruct((k, share, width), BF16),
            jax.ShapeDtypeStruct((8 + router_t.shape[0], width), F32),
            jax.ShapeDtypeStruct((n,) + rows.shape, F32),
            jax.ShapeDtypeStruct(hid.shape, BF16),
            jax.ShapeDtypeStruct(du.shape, BF16),
            jax.ShapeDtypeStruct(du.shape, BF16),
            jax.ShapeDtypeStruct(arr.shape[:2] + (arr.shape[2] // 2,), BF16),
            jax.ShapeDtypeStruct(dg.shape, BF16),
        ),
        in_specs=[VMEM] * 7 + [HBM] * 4,
        out_specs=(VMEM,) * 4 + (HBM,) * 5,
        scratch_shapes=mp_scratch(share, wide, chunks) + [DMA((2, 2)), DMA((4, n)), DMA((2, 2))],
        compiler_params=params(3, 60),
        name="mid_back",
        cost_estimate=cost(32),
    )(part, resid, gain, cot, gate, router_t, rows, hid, du, arr, dg)


class SmallSum:
    def __init__(self, sizes, x_ref, out_ref, bufs, sems):
        self.sizes, self.x, self.out, self.bufs, self.sems = sizes, x_ref, out_ref, bufs, sems
        self.me = [lax.axis_index(a) for a in ("seq", "ctx", "mp")]

    def peer(self, axis, d):
        ids = list(self.me)
        ids[axis] = lax.rem(self.me[axis] + d, self.sizes[axis])
        return tuple(ids)

    def signal(self, sem):
        for axis in range(3):
            for d in range(1, self.sizes[axis]):
                pl.semaphore_signal(sem, inc=1, device_id=self.peer(axis, d), device_id_type=MESH)
        return sum(self.sizes) - 3

    def move(self, axis, d):
        base = sum(self.sizes[:axis])
        buf = self.bufs[axis]
        return pltpu.make_async_remote_copy(
            src_ref=buf.at[0],
            dst_ref=buf.at[d],
            send_sem=self.sems.at[0, base + d],
            recv_sem=self.sems.at[1, base + d],
            device_id=self.peer(axis, d),
            device_id_type=MESH,
        )

    def begin(self, axis, value):
        self.bufs[axis][0] = value
        for d in range(1, self.sizes[axis]):
            self.move(axis, d).start()

    def end(self, axis):
        n = self.sizes[axis]
        for d in range(1, n):
            self.move(axis, d).wait()
        total = jnp.zeros(self.out.shape, F32)
        for i in range(n):
            total = total + self.bufs[axis][lax.rem(self.me[axis] - i + n, n)]
        return total


def last_kernel(
    chunks,
    sizes,
    dqkv_ref,
    h_hbm,
    wq_hbm,
    wk_hbm,
    wv_hbm,
    tok_hbm,
    gain,
    dresid_hbm,
    small_ref,
    wout_ref,
    up0_hbm,
    up_other,
    comb_hbm,
    resid_hbm,
    out_ref,
    final_ref,
    total_ref,
    gout_ref,
    gqkv_ref,
    up_ref,
    core_in,
    y_out,
    y_in,
    sems,
    core_in2,
    y_out2,
    y_in2,
    sems2,
    h_ref,
    wq_ref,
    wk_ref,
    wv_ref,
    tok_ref,
    dresid_ref,
    comb,
    resid_ref,
    part,
    dh_ref,
    qkv_ref,
    swapped,
    summed,
    wout_in,
    qkv_in,
    up_in,
    load_sem,
    swap_sem,
    peers_sem,
    *rest,
):
    n = sizes[1]
    s, c = lax.axis_index("seq"), lax.axis_index("ctx")
    load = Staged(
        (
            (h_hbm, h_ref),
            (wq_hbm, wq_ref),
            (wk_hbm, wk_ref),
            (wv_hbm, wv_ref),
            (tok_hbm, tok_ref),
            (comb_hbm, comb),
            (dresid_hbm, dresid_ref),
            (resid_hbm, resid_ref),
            (up0_hbm, up_ref),
        ),
        load_sem,
    )
    load.start()
    mp = Mp(part, core_in, y_out, y_in, None, sems, chunks)
    mp2 = Mp(comb, core_in2, y_out2, y_in2, None, sems2, chunks)
    small = SmallSum(sizes, small_ref, total_ref, rest[:3], rest[3])
    half_rows = swapped.shape[0]
    rows = half_rows // n
    wout_peers = Peers(
        n, lambda p: wout_ref.at[cut_of(p, rows)], lambda i: wout_in.at[i], peers_sem.at[0], peers_sem.at[1]
    )
    qkv_peers = Peers(
        n, lambda p: summed.at[cut_of(p, rows)], lambda i: qkv_in.at[i], peers_sem.at[2], peers_sem.at[3]
    )
    sem = pltpu.get_barrier_semaphore()
    pl.semaphore_wait(sem, small.signal(sem))
    wout_peers.start()
    load.wait(0)

    def weight_rows(first):
        def piece(r):
            at = pl.ds(pl.multiple_of(first + r * 256, 256), 256)
            qkv_ref[at, :] = tn(h_ref[:, at], dqkv_ref[...]).astype(BF16)

        loop(half_rows // 256, piece)

    weight_rows((1 - s) * half_rows)

    def chunk_swap(k):
        p = lax.rem(c + 1 + k, n)
        return swap(qkv_ref.at[cut_of((1 - s) * n + p, rows)], swapped.at[cut_of(p, rows)], swap_sem, k)

    up_swap = swap(up_other, up_in, swap_sem, n)

    def chunk_arrived(k):
        chunk_swap(k).wait_recv()
        if k + 2 < n:
            chunk_swap(k + 2).start()
        if k + 2 == n:
            up_swap.start()
        p = lax.rem(c + 1 + k, n)
        here = cut_of(p, rows)
        summed[here, :] = (
            qkv_ref[cut_of(s * n + p, rows), :].astype(F32) + swapped[here, :].astype(F32)
        ).astype(BF16)
        if k < n - 1:
            qkv_peers.move(k + 1).start()

    for k in range(min(2, n)):
        chunk_swap(k).start()
    load.wait(1, 2, 3)
    share, width = out_ref.shape
    qw, kw = wq_ref.shape[1], wk_ref.shape[1]

    def token_rows(i):
        at = pl.ds(pl.multiple_of(i * 512, 512), 512)
        dh = nt(dqkv_ref[:, :qw], wq_ref[at, :])
        dh = dh + nt(dqkv_ref[:, qw : qw + kw], wk_ref[at, :])
        dh = dh + nt(dqkv_ref[:, qw + kw :], wv_ref[at, :])
        for p in range(part.shape[0]):
            dh_ref[p, :, at] = dh[p * share : (p + 1) * share, :]
            part[p, :, at] = dh[p * share : (p + 1) * share, :].astype(BF16)

    loop(width // 512, token_rows)
    mp.rs_core(0).start()
    mp.rs_core(1).start()
    load.wait(5)
    mp2.rs_core(0).start()
    mp2.rs_core(1).start()
    weight_rows(s * half_rows)
    mp.rs_forward()
    load.wait(4)
    total_ref[...] = small_ref[...]

    def norm_rows(p):
        normed, _ = rms_parts(tok_ref[p].astype(F32))
        total_ref[0:1, :] = total_ref[0:1, :] + jnp.sum(dh_ref[p] * normed, axis=0, keepdims=True)

    loop(part.shape[0], norm_rows)
    small.begin(1, total_ref[...])
    chunk_arrived(0)
    mp2.rs_forward()
    chunk_arrived(1)
    load.wait(6)
    for i in range(chunks):
        cut = mp.cut(i)
        dh = mp.rs_chunk(i)
        normed, inverse = rms_parts(tok_ref[mp.m, cut, :].astype(F32))
        final_ref[cut, :] = dresid_ref[cut, :] + rms_grad(dh * gain[...].reshape(1, -1), normed, inverse)
        if i + 2 < n:
            chunk_arrived(i + 2)
        if i == 0:
            small.begin(0, small.end(1))
    for k in range(chunks + 2, n):
        chunk_arrived(k)
    small.begin(2, small.end(0))
    load.wait(7)
    for i in range(chunks):
        cut = mp.cut(i)
        out_ref[cut, :] = resid_ref[cut, :] + mp2.rs_chunk(i)
    total_ref[...] = small.end(2)
    wout_peers.finish()
    wout_in[c] = wout_ref[cut_of(c, rows), :]
    total = jnp.zeros(gout_ref.shape, F32)
    for i in range(n):
        total = total + wout_in[i].astype(F32)
    gout_ref[...] = total
    mp.rs_end()
    mp2.rs_end()
    load.wait(8)
    for k in range(n):
        chunk_swap(k).wait_send()
    qkv_peers.finish()
    qkv_in[c] = summed[cut_of(c, rows), :]
    total = jnp.zeros(gqkv_ref.shape, F32)
    for i in range(n):
        total = total + qkv_in[i].astype(F32)
    gqkv_ref[...] = total
    up_swap.wait()
    up_ref[...] = up_ref[...] + up_in[...].astype(F32)


def cut_of(i, rows):
    return pl.ds(pl.multiple_of(i * rows, 16), rows)


def last(sizes, dqkv, h, wq, wk, wv, tokens, gain, dresid, small, wout, up0, up_other, comb, resid, chunks=2):
    k, share, width = comb.shape
    n = sizes[1]
    half_rows, fo = wout.shape
    fq = dqkv.shape[1]
    rows = half_rows // n
    sds = jax.ShapeDtypeStruct
    vm = lambda x: pltpu.VMEM(x.shape, x.dtype)
    return pl.pallas_call(
        functools.partial(last_kernel, chunks, sizes),
        out_shape=(
            sds((share, width), F32),
            sds((share, width), F32),
            sds(small.shape, F32),
            sds((rows, fo), F32),
            sds((rows, fq), F32),
            sds(up0.shape, F32),
        ),
        in_specs=[VMEM] + [HBM] * 5 + [VMEM, HBM, VMEM, VMEM, HBM, VMEM, HBM, HBM],
        out_specs=(VMEM,) * 6,
        scratch_shapes=mp_scratch(share, width, chunks)
        + mp_scratch(share, width, chunks)
        + [vm(h), vm(wq), vm(wk), vm(wv), vm(tokens), vm(dresid), vm(comb), vm(resid)]
        + [
            pltpu.VMEM(comb.shape, BF16),
            pltpu.VMEM(comb.shape, F32),
            pltpu.VMEM((2 * half_rows, fq), BF16),
            pltpu.VMEM((half_rows, fq), BF16),
            pltpu.VMEM((half_rows, fq), BF16),
            pltpu.VMEM((n, rows, fo), BF16),
            pltpu.VMEM((n, rows, fq), BF16),
            pltpu.VMEM(up0.shape, BF16),
            DMA((9,)),
            DMA((2, n + 1)),
            DMA((4, n)),
        ]
        + [pltpu.VMEM((d,) + small.shape, F32) for d in sizes]
        + [DMA((2, sum(sizes)))],
        compiler_params=params(4, 60),
        name="last",
        cost_estimate=cost(60),
    )(dqkv, h, wq, wk, wv, tokens, gain, dresid, small, wout, up0, up_other, comb, resid)


def finish_kernel(*refs):
    n_in = 8
    total, gout, gqkv = refs[5:n_in]
    outs = refs[n_in : n_in + 12]
    sems = refs[n_in + 12]
    output, tokens, norm1, gq, gk, gv, go, norm2, router, gate, up, down = outs
    large = Staged(tuple(zip(refs[:5], (output, tokens, gate, up, down))), sems)
    large.start()
    norm1[...] = total[0, :]
    norm2[...] = total[1, :]
    router[...] = total[8 : 8 + router.shape[0], :]
    qw, kw = gq.shape[1], gk.shape[1]
    gq[...] = gqkv[:, :qw]
    gk[...] = gqkv[:, qw : qw + kw]
    gv[...] = gqkv[:, qw + kw :]
    go[...] = gout[...].T
    large.wait(0, 1, 2, 3, 4)


def finish(experts_all, qw, output, tokens, gate, up, down, total, gout, gqkv):
    sds = jax.ShapeDtypeStruct
    width = total.shape[1]
    rows = gqkv.shape[0]
    kw = (gqkv.shape[1] - qw) // 2
    shapes = (
        output.shape,
        tokens.shape,
        (width,),
        (rows, qw),
        (rows, kw),
        (rows, kw),
        gout.shape[::-1],
        (width,),
        (experts_all, width),
        gate.shape,
        up.shape,
        down.shape,
    )
    return pl.pallas_call(
        finish_kernel,
        out_shape=tuple(sds(x, F32) for x in shapes),
        in_specs=[HBM] * 5 + [VMEM] * 3,
        out_specs=(VMEM,) * 12,
        scratch_shapes=[DMA((5,))],
        compiler_params=pltpu.CompilerParams(vmem_limit_bytes=60 * MIB),
        name="finish",
        cost_estimate=cost(6),
    )(output, tokens, gate, up, down, total, gout, gqkv)


def body(
    tokens,
    norm1_gain,
    w_query,
    key_weight_matrix,
    value_weight_matrix,
    w_out,
    norm2_gain,
    router,
    w_gate,
    w_up,
    w_down,
    routes,
    cotangent,
):
    n_seq, n_ctx, n_mp = (lax.axis_size(a) for a in ("seq", "ctx", "mp"))
    s, c, m = (lax.axis_index(a) for a in ("seq", "ctx", "mp"))
    tok, width = tokens.shape
    share = tok // n_mp
    experts_all = router.shape[1]
    exp_local = w_gate.shape[0]
    top = routes.shape[1]
    cap = share * top * 5 // (4 * experts_all)
    slots = -(-n_mp * cap // 16) * 16

    cot_all = lax.all_gather(cotangent, "mp", axis=0, tiled=True)
    by_share = tokens.reshape(n_mp, share, width)

    qt, h_one, o, heads_t, lse, kv, cot_above, routes_line = attend(
        n_ctx, tokens, norm1_gain, w_query, key_weight_matrix, value_weight_matrix, cotangent, routes.T
    )
    resid, h_two, place, place_t, place_line, cot_line = mid_forward(
        n_ctx, exp_local, slots, heads_t, w_out, norm2_gain, cotangent, cot_above, routes_line, by_share
    )
    h_two = h_two.reshape(tok, width)

    gates, gate_rows, arrived, hidden, dg, du, back, comb, arrived_line, cot_first, cot_line = moe(
        n_ctx, n_seq, experts_all, h_two, cot_all, place, place_t, routes.T, router.T, w_gate, w_up, w_down, cot_line
    )
    dresid, db, small, gate_rows_line, hidden_line, du_below, du_above, arrived_other, dg_other = mid_back(
        n_ctx,
        back.reshape(n_mp, share, -1),
        resid,
        norm2_gain,
        cotangent,
        gates.reshape(n_mp, share, -1),
        router.T,
        gate_rows,
        hidden,
        du,
        arrived,
        dg,
    )

    db = db.reshape(tok, width)
    dqkv, g_gate, g_down, up0, up_other, g_out, _, _ = attend_back(
        n_ctx,
        qt,
        db,
        w_out,
        o,
        lse,
        kv,
        arrived,
        arrived_other,
        dg,
        dg_other,
        gate_rows_line,
        du,
        du_below,
        du_above,
        hidden_line,
        hidden,
        heads_t,
        arrived_line,
        place_line,
        cot_line,
        cot_first,
    )
    output, grad_tokens, small, g_out, g_qkv, g_up = last(
        (n_seq, n_ctx, n_mp),
        dqkv,
        h_one,
        w_query,
        key_weight_matrix,
        value_weight_matrix,
        by_share,
        norm1_gain,
        dresid,
        small,
        g_out,
        up0,
        up_other,
        comb.reshape(n_mp, share, width),
        resid,
    )
    outs = finish(experts_all, w_query.shape[1], output, grad_tokens, g_gate, g_up, g_down, small, g_out, g_qkv)
    return outs[:8] + (outs[8].T,) + outs[9:]


def solution(mesh):
    placed = (
        P(("seq", "ctx"), None),
        P(),
        P(None, "mp"),
        P(None, "mp"),
        P(None, "mp"),
        P("mp", None),
        P(),
        P(),
        P("mp", None, None),
        P("mp", None, None),
        P("mp", None, None),
        P(("seq", "ctx"), None),
        P(("seq", "ctx", "mp"), None),
    )
    return jax.shard_map(
        body,
        mesh=mesh,
        in_specs=placed,
        out_specs=(
            P(("seq", "ctx", "mp"), None),
            P(("seq", "ctx", "mp"), None),
            P(),
            P(("seq", "ctx"), "mp"),
            P(("seq", "ctx"), "mp"),
            P(("seq", "ctx"), "mp"),
            P("mp", ("seq", "ctx")),
            P(),
            P(),
            P("mp", ("seq", "ctx"), None),
            P("mp", ("seq", "ctx"), None),
            P("mp", ("seq", "ctx"), None),
        ),
        check_vma=False,
    )
```

```python
import functools

import jax
import jax.numpy as jnp
from jax import lax
from jax.experimental import pallas as pl
from jax.experimental.pallas import tpu as pltpu
from jax.sharding import PartitionSpec as P

HEAD_SIZE = 64
EPS = 1e-06
MESH = pl.DeviceIdType.MESH
F32 = jnp.float32
BF16 = jnp.bfloat16
VMEM = pl.BlockSpec(memory_space=pltpu.VMEM)
HBM = pl.BlockSpec(memory_space=pl.ANY)
DMA = pltpu.SemaphoreType.DMA
MIB = 2**20


def cost(us):
    return pl.CostEstimate(flops=0, bytes_accessed=int(us * 3.6e6), transcendentals=0)


def params(collective_id, mib=56):
    return pltpu.CompilerParams(
        collective_id=collective_id, has_side_effects=True, vmem_limit_bytes=mib * MIB
    )


def nt(a, b):
    return lax.dot_general(a, b, (((1,), (1,)), ((), ())), preferred_element_type=F32)


def nn(a, b):
    return jnp.dot(a, b, preferred_element_type=F32)


class Staged:
    def __init__(self, pairs, sems):
        self.copies = [pltpu.make_async_copy(src, dst, sems.at[i]) for i, (src, dst) in enumerate(pairs)]

    def start(self):
        for copy in self.copies:
            copy.start()

    def wait(self, *which):
        for i in which:
            self.copies[i].wait()


class Spread:
    def __init__(self, n, own, below, above, all_ref, send, recv, local, short=False):
        self.n, self.own, self.below, self.above, self.all = n, own, below, above, all_ref
        self.send, self.recv, self.local = send, recv, local
        self.top = n - 2 if short else n - 1
        s, self.c, m = lax.axis_index("seq"), lax.axis_index("ctx"), lax.axis_index("mp")
        self.lower, self.upper = lax.rem(self.c + n - 1, n), lax.rem(self.c + 1, n)
        self.up, self.down = (s, self.upper, m), (s, self.lower, m)
        self.inner = jnp.logical_and(self.c > 0, self.c < n - 1)

    def move(self, b, src, device):
        return pltpu.make_async_remote_copy(
            src_ref=src,
            dst_ref=self.all.at[b],
            send_sem=self.send.at[b],
            recv_sem=self.recv.at[b],
            device_id=device,
            device_id_type=MESH,
        )

    def keep(self, i, src, b):
        return pltpu.make_async_copy(src, self.all.at[b], self.local.at[i])

    def goes_up(self, b):
        return jnp.logical_and(self.c < self.n - 1, self.c - b < self.top)

    def start(self):
        if self.below is None:

            @pl.when(self.c < self.n - 1)
            def _():
                self.move(self.c, self.own, self.up).start()
        else:

            @pl.when(jnp.logical_and(self.inner, self.goes_up(self.lower)))
            def _():
                self.move(self.lower, self.below, self.up).start()

            @pl.when(self.c > 0)
            def _():
                self.keep(1, self.below, self.lower).start()

        @pl.when(self.inner)
        def _():
            self.move(self.upper, self.above, self.down).start()

        self.keep(0, self.own, self.c).start()

        @pl.when(self.c < self.n - 1)
        def _():
            self.keep(2, self.above, self.upper).start()

    def tick(self, i):
        c, n = self.c, self.n
        off = i if self.below is None else i + 1

        @pl.when(jnp.logical_and(c - off >= 0, off <= self.top))
        def _():
            b = jnp.maximum(c - off, 0)
            self.move(b, self.all.at[b], self.up).wait_recv()

            @pl.when(self.goes_up(b))
            def _():
                self.move(b, self.all.at[b], self.up).start()

        @pl.when(c + 1 + i <= n - 1)
        def _():
            b = jnp.minimum(c + 1 + i, n - 1)
            self.move(b, self.all.at[b], self.down).wait_recv()

            @pl.when(c > 0)
            def _():
                self.move(b, self.all.at[b], self.down).start()

    def ticks(self, first):
        def later(i, carry):
            self.tick(i)
            return carry

        lax.fori_loop(first, self.n if self.below is None else self.n - 1, later, 0)

    def finish(self):
        self.keep(0, self.own, self.c).wait()

        if self.below is not None:

            @pl.when(self.c > 0)
            def _():
                self.keep(1, self.below, self.lower).wait()

        @pl.when(self.c < self.n - 1)
        def _():
            self.keep(2, self.above, self.upper).wait()

        def sent(b, carry):
            if self.below is None:
                sent_up = jnp.logical_and(b <= self.c, self.goes_up(b))
            else:
                sent_up = jnp.logical_and(b < self.c, self.goes_up(b))

            @pl.when(jnp.logical_or(sent_up, jnp.logical_and(b > self.c, self.c > 0)))
            def _():
                self.move(b, self.all.at[b], self.up).wait_send()

            return carry

        lax.fori_loop(0, self.n, sent, 0)


class Neighbours:
    def __init__(self, n, own, below, above, send, recv):
        self.n, self.own, self.below, self.above, self.send, self.recv = n, own, below, above, send, recv
        s, self.c, m = lax.axis_index("seq"), lax.axis_index("ctx"), lax.axis_index("mp")
        self.up, self.down = (s, lax.rem(self.c + 1, n), m), (s, lax.rem(self.c + n - 1, n), m)

    def move(self, way):
        return pltpu.make_async_remote_copy(
            src_ref=self.own,
            dst_ref=self.below if way == 0 else self.above,
            send_sem=self.send.at[way],
            recv_sem=self.recv.at[way],
            device_id=self.up if way == 0 else self.down,
            device_id_type=MESH,
        )

    def start_up(self):
        @pl.when(self.c < self.n - 1)
        def _():
            self.move(0).start()

    def start_down(self):
        @pl.when(self.c > 0)
        def _():
            self.move(1).start()

    def finish(self, up=True):
        @pl.when(self.c > 0)
        def _():
            if up:
                self.move(0).wait_recv()
            self.move(1).wait_send()

        @pl.when(self.c < self.n - 1)
        def _():
            self.move(1).wait_recv()
            if up:
                self.move(0).wait_send()


class LineSum:
    ahead = 2

    def __init__(self, n, parts, from_below, from_above, send, recv):
        self.n, self.parts, self.bufs, self.send, self.recv = n, parts, (from_below, from_above), send, recv
        s, self.c, m = lax.axis_index("seq"), lax.axis_index("ctx"), lax.axis_index("mp")
        self.up, self.down = (s, lax.rem(self.c + 1, n), m), (s, lax.rem(self.c + n - 1, n), m)
        self.ex, self.rows = from_below.shape[1], from_below.shape[2]
        self.units = (n - 1) * self.ex
        self.ticks = self.units + n - 3

    def own(self, k, e):
        return self.parts.at[e, pl.ds(pl.multiple_of(k * self.rows, 16), self.rows), :]

    def move(self, way, k, e, first=False):
        there = self.bufs[way].at[k, e]
        return pltpu.make_async_remote_copy(
            src_ref=self.own(k, e) if first else there,
            dst_ref=there,
            send_sem=self.send.at[way, k, e],
            recv_sem=self.recv.at[way, k, e],
            device_id=self.up if way == 0 else self.down,
            device_id_type=MESH,
        )

    def unit(self, way, u):
        k = lax.div(u, self.ex)
        return (self.n - 1 - k if way == 0 else k), lax.rem(u, self.ex)

    def first(self, u):
        for way, end in ((0, 0), (1, self.n - 1)):

            @pl.when(jnp.logical_and(self.c == end, u < self.units))
            def _():
                @pl.when(u >= self.ahead)
                def _():
                    self.move(way, *self.unit(way, jnp.maximum(u - self.ahead, 0)), True).wait_send()

                self.move(way, *self.unit(way, jnp.minimum(u, self.units - 1)), True).start()

    def tick(self, i):
        self.first(i + 1)
        for way, far in ((0, self.c), (1, self.n - 1 - self.c)):
            u = i - far

            @pl.when(jnp.logical_and(far > 0, jnp.logical_and(u >= 0, u < (self.n - 1 - far) * self.ex)))
            def _():
                k, e = self.unit(way, jnp.clip(u, 0, self.units - 1))
                self.move(way, k, e).wait_recv()
                self.bufs[way][k, e] = (
                    self.own(k, e)[...].astype(F32) + self.bufs[way][k, e].astype(F32)
                ).astype(BF16)
                self.move(way, k, e).start()

    def finish(self, out):
        c = self.c
        for e in range(self.ex):
            out[e] = self.own(c, e)[...].astype(F32)
        for way, far in ((0, c), (1, self.n - 1 - c)):

            @pl.when(far > 0)
            def _():
                for e in range(self.ex):
                    self.move(way, c, e).wait_recv()
                    out[e] = out[e] + self.bufs[way][c, e].astype(F32)

            done = jnp.where(far == 0, max(self.units - self.ahead, 0), 0)

            def sent(u, carry):
                self.move(way, *self.unit(way, u)).wait_send()
                return carry

            lax.fori_loop(done, (self.n - 1 - far) * self.ex, sent, 0)


class Peers:
    def __init__(self, n, src_of, dst_of, send, recv):
        self.n, self.src_of, self.dst_of, self.send, self.recv = n, src_of, dst_of, send, recv
        self.s, self.c, self.m = lax.axis_index("seq"), lax.axis_index("ctx"), lax.axis_index("mp")

    def move(self, d):
        peer = lax.rem(self.c + d, self.n)
        return pltpu.make_async_remote_copy(
            src_ref=self.src_of(peer),
            dst_ref=self.dst_of(self.c),
            send_sem=self.send.at[d],
            recv_sem=self.recv.at[d],
            device_id=(self.s, peer, self.m),
            device_id_type=MESH,
        )

    def signal(self, sem):
        for d in range(1, self.n):
            pl.semaphore_signal(
                sem, inc=1, device_id=(self.s, lax.rem(self.c + d, self.n), self.m), device_id_type=MESH
            )

    def start(self):
        for d in range(1, self.n):
            self.move(d).start()

    def finish(self):
        for d in range(1, self.n):
            self.move(d).wait()


class CotExchange:
    def __init__(self, n, line_ref, full, first, sems):
        self.n, self.line, self.full, self.first, self.sems = n, line_ref, full, first, sems
        self.count = full.shape[0]
        s, self.c, m = lax.axis_index("seq"), lax.axis_index("ctx"), lax.axis_index("mp")
        self.m = m
        self.share = line_ref.shape[1]
        self.sib = m + 1 - 2 * lax.rem(m, 2)
        self.opp = lax.rem(m + 2, 4)
        self.sib_id, self.opp_id = (s, self.c, self.sib), (s, self.c, self.opp)

    def signal(self, sem):
        for d in (self.sib_id, self.opp_id):
            pl.semaphore_signal(sem, inc=1, device_id=d, device_id_type=MESH)

    def place(self, i, who):
        return self.full.at[i, pl.ds(pl.multiple_of(who * self.share, 16), self.share), :]

    def mine(self, i):
        return self.line.at[lax.rem(self.c - self.first - i + 2 * self.n, self.n)]

    def move(self, kind, i):
        whose = self.opp if kind == 2 else self.m
        return pltpu.make_async_remote_copy(
            src_ref=self.place(i, self.opp) if kind == 2 else self.mine(i),
            dst_ref=self.place(i, whose),
            send_sem=self.sems.at[0, kind, i],
            recv_sem=self.sems.at[1, kind, i],
            device_id=self.opp_id if kind == 0 else self.sib_id,
            device_id_type=MESH,
        )

    def start(self):
        for i in range(self.count):
            self.move(0, i).start()
            self.move(1, i).start()

    def finish(self):
        for i in range(self.count):
            self.move(0, i).wait_recv()
            self.move(2, i).start()
        for i in range(self.count):
            self.move(1, i).wait_recv()
            self.move(2, i).wait_recv()
            for kind in range(3):
                self.move(kind, i).wait_send()


def signal_line(n, sem):
    s, c, m = lax.axis_index("seq"), lax.axis_index("ctx"), lax.axis_index("mp")

    @pl.when(c > 0)
    def _():
        pl.semaphore_signal(sem, inc=1, device_id=(s, lax.rem(c + n - 1, n), m), device_id_type=MESH)

    @pl.when(c < n - 1)
    def _():
        pl.semaphore_signal(sem, inc=1, device_id=(s, lax.rem(c + 1, n), m), device_id_type=MESH)


def line_degree(n):
    c = lax.axis_index("ctx")
    return jnp.where(c > 0, 1, 0) + jnp.where(c < n - 1, 1, 0)


def pad_heads(src, dst, heads, group):
    dst[...] = jnp.zeros_like(dst)
    for h in range(heads):
        g = h // group
        rows = slice(g * HEAD_SIZE, (g + 1) * HEAD_SIZE)
        dst[h, rows, :] = src[h * HEAD_SIZE : (h + 1) * HEAD_SIZE, :]


def causal(t):
    keys = lax.broadcasted_iota(jnp.int32, (t, t), 0)
    queries = lax.broadcasted_iota(jnp.int32, (t, t), 1)
    return keys <= queries


def attend_kernel(
    n,
    tok_ref,
    gain,
    wq_ref,
    wk_ref,
    wv_ref,
    cot_ref,
    routes_ref,
    q_ref,
    h_ref,
    o_ref,
    heads_ref,
    lse_ref,
    kv_ref,
    above_ref,
    line_ref,
    qpad,
    vt,
    top,
    tot,
    send,
    recv,
    side,
    peers_sem,
):
    s, c, m = lax.axis_index("seq"), lax.axis_index("ctx"), lax.axis_index("mp")
    t, kvw = tok_ref.shape[0], wk_ref.shape[1]
    heads = q_ref.shape[0] // HEAD_SIZE
    group = heads // (kvw // HEAD_SIZE)
    up, down = (s, lax.rem(c + 1, n), m), (s, lax.rem(c + n - 1, n), m)

    def norm_rows(i):
        rows = pl.ds(pl.multiple_of(i * 128, 128), 128)
        normed, _ = rms_parts(tok_ref[rows, :].astype(F32))
        h_ref[rows, :] = (normed * gain[...].reshape(1, -1)).astype(BF16)

    loop(t // 128, norm_rows)
    kv_ref[0, :, :kvw] = nn(h_ref[...], wk_ref[...]).astype(BF16)
    kv_ref[0, :, kvw:] = nn(h_ref[...], wv_ref[...]).astype(BF16)
    line_ref[c] = routes_ref[...]
    peers = Peers(n, lambda p: routes_ref, lambda i: line_ref.at[i], peers_sem.at[0], peers_sem.at[1])
    beside = Neighbours(n, cot_ref, None, above_ref, side.at[0], side.at[1])
    sem = pltpu.get_barrier_semaphore()
    peers.signal(sem)
    pl.semaphore_wait(sem, n - 1)

    def pass_up(slot):
        return pltpu.make_async_remote_copy(
            src_ref=kv_ref.at[slot],
            dst_ref=kv_ref.at[slot + 1],
            send_sem=send.at[slot],
            recv_sem=recv.at[slot + 1],
            device_id=up,
            device_id_type=MESH,
        )

    def got(slot):
        return pltpu.make_async_remote_copy(
            src_ref=kv_ref.at[slot],
            dst_ref=kv_ref.at[slot],
            send_sem=send.at[slot],
            recv_sem=recv.at[slot],
            device_id=up,
            device_id_type=MESH,
        )

    @pl.when(c < n - 1)
    def _():
        pass_up(0).start()

    peers.start()
    beside.start_down()
    q_ref[...] = (nn(h_ref[...], wq_ref[...]) * 0.125).astype(BF16).T
    pad_heads(q_ref, qpad, heads, group)
    top[...] = jnp.full_like(top, -1e30)
    tot[...] = jnp.zeros_like(tot)
    o_ref[...] = jnp.zeros_like(o_ref)

    def block(slot, masked):
        vt[...] = kv_ref[slot, :, kvw:].T

        def head(h, carry):
            g = lax.div(h, group)
            scores = nn(kv_ref[slot, :, :kvw], qpad[h])
            if masked:
                scores = jnp.where(causal(t), scores, -1e30)
            old = top[h]
            new = jnp.maximum(old, jnp.max(scores, axis=0, keepdims=True))
            weights = jnp.exp(scores - new)
            factor = jnp.exp(old - new)
            top[h] = new
            tot[h] = tot[h] * factor + jnp.sum(weights, axis=0, keepdims=True)
            rows = pl.ds(pl.multiple_of(h * HEAD_SIZE, HEAD_SIZE), HEAD_SIZE)
            vrows = pl.ds(pl.multiple_of(g * HEAD_SIZE, HEAD_SIZE), HEAD_SIZE)
            o_ref[rows, :] = o_ref[rows, :] * factor + nn(vt[vrows, :], weights.astype(BF16))
            return carry

        lax.fori_loop(0, heads, head, 0)

    block(0, True)

    def earlier(slot, carry):
        got(slot).wait_recv()

        @pl.when(c < n - 1)
        def _():
            pass_up(slot).start()

        block(slot, False)
        return carry

    lax.fori_loop(1, c + 1, earlier, 0)
    for h in range(heads):
        rows = slice(h * HEAD_SIZE, (h + 1) * HEAD_SIZE)
        done = o_ref[rows, :] / tot[h]
        o_ref[rows, :] = done
        heads_ref[rows, :] = done.astype(BF16)
        lse_ref[h] = top[h] + jnp.log(tot[h])

    @pl.when(c < n - 1)
    def _():
        def sent(slot, carry):
            pass_up(slot).wait_send()
            return carry

        lax.fori_loop(0, c + 1, sent, 0)

    peers.finish()
    beside.finish(up=False)


def attend(n, tokens, gain, wq, wk, wv, cot, routes):
    t, kvw = tokens.shape[0], wk.shape[1]
    qw = wq.shape[1]
    heads = qw // HEAD_SIZE
    return pl.pallas_call(
        functools.partial(attend_kernel, n),
        out_shape=(
            jax.ShapeDtypeStruct((qw, t), BF16),
            jax.ShapeDtypeStruct(tokens.shape, BF16),
            jax.ShapeDtypeStruct((qw, t), F32),
            jax.ShapeDtypeStruct((qw, t), BF16),
            jax.ShapeDtypeStruct((heads, 1, t), F32),
            jax.ShapeDtypeStruct((n, t, 2 * kvw), BF16),
            jax.ShapeDtypeStruct(cot.shape, BF16),
            jax.ShapeDtypeStruct((n,) + routes.shape, jnp.int32),
        ),
        in_specs=[VMEM] * 5 + [HBM, VMEM],
        out_specs=(VMEM,) * 6 + (HBM, VMEM),
        scratch_shapes=[
            pltpu.VMEM((heads, kvw, t), BF16),
            pltpu.VMEM((kvw, t), BF16),
            pltpu.VMEM((heads, 1, t), F32),
            pltpu.VMEM((heads, 1, t), F32),
            DMA((n,)),
            DMA((n,)),
            DMA((2, 2)),
            DMA((2, n)),
        ],
        compiler_params=params(0),
        name="attend",
        cost_estimate=cost(30),
    )(tokens, gain, wq, wk, wv, cot, routes)


def attend_back_kernel(
    n,
    q_hbm,
    db_hbm,
    wout_hbm,
    o_hbm,
    lse_ref,
    kv_hbm,
    arr_ref,
    arr_other,
    dg_ref,
    dg_other,
    rows_line,
    own_hbm,
    below_hbm,
    above_hbm,
    hid_hbm,
    hid_own,
    heads_hbm,
    arr_hbm,
    place_hbm,
    line_hbm,
    first_hbm,
    dqkv_ref,
    gate_ref,
    down_ref,
    up_ref,
    up_other,
    wsum_ref,
    all_hbm,
    rest_hbm,
    do_ref,
    qpad,
    dopad,
    delta,
    dq,
    kt,
    part,
    passing,
    sum_ref,
    from_below,
    from_above,
    place_buf,
    cot_buf,
    hid_buf,
    arr_buf,
    du_buf,
    dy,
    acc_ref,
    kv_sem,
    sum_sem,
    spread_sem,
    local,
    ysem,
    load_sem,
    swap_sem,
    wout_part,
    wout_in,
    down_out,
    down_in,
    stage_sem,
    db_ref,
    wout_ref,
    own_ref,
    below_ref,
    above_ref,
    heads_ref,
    q_ref,
    o_ref,
    kv_ref,
):
    s, c, m = lax.axis_index("seq"), lax.axis_index("ctx"), lax.axis_index("mp")
    load = Staged(
        (
            (db_hbm, db_ref),
            (wout_hbm, wout_ref),
            (own_hbm, own_ref),
            (below_hbm, below_ref),
            (above_hbm, above_ref),
            (heads_hbm, heads_ref),
            (q_hbm, q_ref),
            (o_hbm, o_ref),
            (kv_hbm, kv_ref),
        ),
        stage_sem,
    )
    load.start()
    _, t, kvw2 = kv_ref.shape
    kvw = kvw2 // 2
    heads = q_ref.shape[0] // HEAD_SIZE
    group = heads // (kvw // HEAD_SIZE)
    ex, slots, width = arr_ref.shape
    half_width = width // 2
    down = (s, lax.rem(c + n - 1, n), m)
    spread = Spread(n, own_ref, below_ref, above_ref, all_hbm, spread_sem.at[0], spread_sem.at[1], local)
    done_blocks = first_hbm.shape[0]
    cots = CotExchange(n, line_hbm, rest_hbm, done_blocks, ysem)
    line = LineSum(n, sum_ref, from_below, from_above, sum_sem.at[0], sum_sem.at[1])
    sem = pltpu.get_barrier_semaphore()
    signal_line(n, sem)
    cots.signal(sem)
    pl.semaphore_signal(sem, inc=1, device_id=swap_partner(), device_id_type=MESH)
    pl.semaphore_wait(sem, line_degree(n) + 3)
    cots.start()

    def gate_part(e, out):
        def piece(r):
            mine = pl.ds(pl.multiple_of(s * half_width + r * 256, 128), 256)
            cut = pl.ds(pl.multiple_of(r * 256, 256), 256)
            out[cut, :] = (tn(arr_ref[e, :, mine], dg_ref[e]) + tn(arr_other[e, :, cut], dg_other[e])).astype(BF16)

        loop(half_width // 256, piece)

    for e in range(ex):
        gate_part(e, sum_ref.at[e])
        if e == 0:
            line.first(0)
            load.wait(0, 1, 2, 3, 4)
            spread.start()
    do_ref[...] = nt(wout_ref[...], db_ref[...]).astype(BF16)

    load.wait(5)

    def wout_piece(r):
        at = pl.ds(pl.multiple_of(r * 512, 512), 512)
        wout_part[:, at] = nn(heads_ref[...], db_ref[:, at]).astype(BF16)

    loop(width // 512, wout_piece)
    own_half, other_half = (pl.ds(pl.multiple_of(k * half_width, 128), half_width) for k in (s, 1 - s))
    wout_swap = swap(wout_part.at[:, other_half], wout_in, swap_sem, 0)
    wout_swap.start()

    def tick(i):
        line.tick(i)
        for hop in range(1, n - 1):

            @pl.when(i == 2 * hop - 1)
            def _():
                spread.tick(hop)

    ticks = max(line.ticks, 2 * (n - 2)) + 1
    load.wait(6, 7, 8)
    pad_heads(q_ref, qpad, heads, group)
    pad_heads(do_ref, dopad, heads, group)
    for h in range(heads):
        rows = slice(h * HEAD_SIZE, (h + 1) * HEAD_SIZE)
        delta[h] = jnp.sum(do_ref[rows, :].astype(F32) * o_ref[rows, :], axis=0, keepdims=True)
    dq[...] = jnp.zeros_like(dq)

    def block(j, masked):
        slot = c - j
        acc = part.at[lax.rem(j, 2)]
        acc[...] = jnp.zeros(acc.shape, F32)
        kt[...] = kv_ref[slot, :, :kvw].T

        def head(h, carry):
            g = lax.div(h, group)
            scores = nn(kv_ref[slot, :, :kvw], qpad[h])
            probs = jnp.exp(scores - lse_ref[h])
            if masked:
                probs = jnp.where(causal(t), probs, 0.0)
            dprobs = nn(kv_ref[slot, :, kvw:], dopad[h])
            ds = (probs * (dprobs - delta[h])).astype(BF16)
            rows = pl.ds(pl.multiple_of(h * HEAD_SIZE, HEAD_SIZE), HEAD_SIZE)
            krows = pl.ds(pl.multiple_of(g * HEAD_SIZE, HEAD_SIZE), HEAD_SIZE)
            dq[rows, :] = dq[rows, :] + nn(kt[krows, :], ds)
            acc[:, :kvw] = acc[:, :kvw] + nt(ds, qpad[h])
            acc[:, kvw:] = acc[:, kvw:] + nt(probs.astype(BF16), dopad[h])
            return carry

        lax.fori_loop(0, heads, head, 0)

    def pass_down(j):
        return pltpu.make_async_remote_copy(
            src_ref=passing.at[j],
            dst_ref=passing.at[j],
            send_sem=kv_sem.at[0, j],
            recv_sem=kv_sem.at[1, j],
            device_id=down,
            device_id_type=MESH,
        )

    def gathered(j):
        acc = part.at[lax.rem(j, 2)]

        @pl.when(c < n - 1)
        def _():
            pass_down(j).wait_recv()
            acc[...] = acc[...] + passing[j].astype(F32)

        return acc

    def forward(j):
        acc = gathered(j)
        passing[j] = acc[...].astype(BF16)
        pass_down(j).start()

    def step(j, carry):
        block(j, False)

        @pl.when(jnp.logical_and(j > 0, c < n - 1))
        def _():
            forward(j - 1)

        @pl.when(c == n - 1)
        def _():
            forward(j)

        tick(j)
        return carry

    lax.fori_loop(0, c, step, 0)
    def later(i, carry):
        tick(i)
        return carry

    middle = jnp.maximum(c, min(2, ticks))
    lax.fori_loop(c, middle, later, 0)

    cots.finish()

    def load_block(i, slot, start):
        b = lax.rem(c - i + n, n)
        share = line_hbm.shape[1]
        place_copy = pltpu.make_async_copy(place_hbm.at[b], place_buf.at[slot], load_sem.at[0, slot])
        hid_copy = pltpu.make_async_copy(hid_hbm.at[b], hid_buf.at[slot], load_sem.at[1, slot])
        hid_mine = pltpu.make_async_copy(hid_own.at[b], hid_buf.at[slot], load_sem.at[1, slot])

        def rows(who):
            return pl.ds(pl.multiple_of(who * share, 16), share)

        def piece(k, who, full, at):
            return pltpu.make_async_copy(
                full.at[at, rows(who), :], cot_buf.at[slot, rows(who), :], load_sem.at[2 + k, slot]
            )

        others = (cots.sib, cots.opp, lax.rem(cots.sib + 2, 4))
        mine = pltpu.make_async_copy(line_hbm.at[b], cot_buf.at[slot, rows(m), :], load_sem.at[5, slot])
        first = [piece(k, who, first_hbm, jnp.minimum(i, done_blocks - 1)) for k, who in enumerate(others)]
        if not start:
            for copy in [place_copy, hid_copy, mine] + first:
                copy.wait()
            return
        rest = [piece(k, who, rest_hbm, jnp.maximum(i - done_blocks, 0)) for k, who in enumerate(others)]
        place_copy.start()
        mine.start()

        @pl.when(b == c)
        def _():
            hid_mine.start()

        @pl.when(b != c)
        def _():
            hid_copy.start()

        @pl.when(i < done_blocks)
        def _():
            for copy in first:
                copy.start()

        @pl.when(i >= done_blocks)
        def _():
            for copy in rest:
                copy.start()

    fa, ua = hid_hbm.shape[3], arr_hbm.shape[3]
    ff = dg_ref.shape[2]
    acc_ref[...] = jnp.zeros_like(acc_ref)
    load_block(0, 0, True)
    wide = 512

    def down_block(i):
        slot = lax.rem(i, 2)
        load_block(i, slot, False)

        @pl.when(i < n - 1)
        def _():
            load_block(i + 1, 1 - slot, True)

        cols = rows_line[lax.rem(c - i + n, n)].T
        for e in range(ex):

            def dys(k):
                cut = pl.ds(pl.multiple_of(k * wide, wide), wide)
                dy[:, cut] = (
                    cols[:slots, e : e + 1] * nn(place_buf[slot, e * slots : (e + 1) * slots, :], cot_buf[slot, :, cut])
                ).astype(BF16)

            loop(width // wide, dys)
            acc_ref[e, :fa, :] = acc_ref[e, :fa, :] + tn(hid_buf[slot, e], dy[...])

    loop(n, down_block)
    mine, other = (pl.ds(pl.multiple_of(k * (fa // 2), 16), fa // 2) for k in (s, 1 - s))
    down_ref[...] = acc_ref[:, mine, :]
    down_out[...] = acc_ref[:, other, :].astype(BF16)
    wout_swap.wait()
    down_swap = swap(down_out, down_in, swap_sem, 1)
    down_swap.start()
    wsum_ref[...] = (wout_part[:, own_half].astype(F32) + wout_in[...].astype(F32)).astype(BF16).T

    after = jnp.minimum(middle + 1, ticks)
    lax.fori_loop(middle, after, later, 0)
    block(c, True)

    @pl.when(jnp.logical_and(c > 0, c < n - 1))
    def _():
        forward(c - 1)

    qw = dq.shape[0]
    dqkv_ref[:, :qw] = (dq[...] * 0.125).astype(BF16).T
    lax.fori_loop(after, ticks, later, 0)

    spread.finish()
    acc_ref[...] = jnp.zeros_like(acc_ref)

    def load_du(b, slot):
        return (
            pltpu.make_async_copy(all_hbm.at[b], du_buf.at[slot], load_sem.at[6, slot]),
            pltpu.make_async_copy(arr_hbm.at[b], arr_buf.at[slot], load_sem.at[7, slot]),
        )

    for copy in load_du(0, 0):
        copy.start()

    def up_block(b):
        slot = lax.rem(b, 2)
        for copy in load_du(b, slot):
            copy.wait()

        @pl.when(b < n - 1)
        def _():
            for copy in load_du(b + 1, 1 - slot):
                copy.start()

        for e in range(ex):
            acc_ref[e, :ua, :ff] = acc_ref[e, :ua, :ff] + tn(arr_buf[slot, e], du_buf[slot, e])

    loop(n, up_block)
    mine, other = (pl.ds(pl.multiple_of(k * (ua // 2), 16), ua // 2) for k in (s, 1 - s))
    up_ref[...] = acc_ref[:, mine, :ff]
    up_other[...] = acc_ref[:, other, :ff].astype(BF16)

    acc = gathered(c)
    dqkv_ref[:, qw:] = acc[...].astype(BF16)
    line.finish(gate_ref)
    down_swap.wait()
    down_ref[...] = down_ref[...] + down_in[...].astype(F32)

    def sent_kv(j, carry):
        pass_down(j).wait_send()
        return carry

    lax.fori_loop(0, c, sent_kv, 0)


def attend_back(n, qt, db, w_out, o, lse, kv, arr, arr_other, dg, dg_other, rows, du, below, above, hid, hid_own, heads_t, arr_line, place, line, first):
    qw, t = qt.shape
    heads = qw // HEAD_SIZE
    kvw = kv.shape[2] // 2
    ex, slots, width = arr.shape
    ff = dg.shape[2]
    half_width = width // 2
    chunk = (ex, half_width // n, ff)
    fa, ua = hid.shape[3], arr_line.shape[3]
    blocks = first.shape[0]
    sds = jax.ShapeDtypeStruct
    return pl.pallas_call(
        functools.partial(attend_back_kernel, n),
        out_shape=(
            sds((t, qw + 2 * kvw), BF16),
            sds(chunk, F32),
            sds((ex, fa // 2, width), F32),
            sds((ex, ua // 2, ff), F32),
            sds((ex, ua // 2, ff), BF16),
            sds((half_width, qw), BF16),
            sds((n,) + du.shape, BF16),
            sds((n - blocks,) + first.shape[1:], BF16),
        ),
        in_specs=[HBM] * 4 + [VMEM, HBM] + [VMEM] * 5 + [HBM] * 10,
        out_specs=(VMEM,) * 6 + (HBM,) * 2,
        scratch_shapes=[
            pltpu.VMEM((qw, t), BF16),
            pltpu.VMEM((heads, kvw, t), BF16),
            pltpu.VMEM((heads, kvw, t), BF16),
            pltpu.VMEM((heads, 1, t), F32),
            pltpu.VMEM((qw, t), F32),
            pltpu.VMEM((kvw, t), BF16),
            pltpu.VMEM((2, t, 2 * kvw), F32),
            pltpu.VMEM((n, t, 2 * kvw), BF16),
            pltpu.VMEM((ex, half_width, ff), BF16),
            pltpu.VMEM((n,) + chunk, BF16),
            pltpu.VMEM((n,) + chunk, BF16),
            pltpu.VMEM((2,) + place.shape[1:], BF16),
            pltpu.VMEM((2,) + first.shape[1:], BF16),
            pltpu.VMEM((2, ex, slots, fa), BF16),
            pltpu.VMEM((2, ex, slots, ua), BF16),
            pltpu.VMEM((2,) + du.shape, BF16),
            pltpu.VMEM((slots, width), BF16),
            pltpu.VMEM((ex, max(fa, ua), width), F32),
            DMA((2, n)),
            DMA((2, 2, n, ex)),
            DMA((2, n)),
            DMA((3,)),
            DMA((2, 3, n - blocks)),
            DMA((8, 2)),
            DMA((2, 2)),
            pltpu.VMEM((qw, width), BF16),
            pltpu.VMEM((qw, half_width), BF16),
            pltpu.VMEM((ex, fa // 2, width), BF16),
            pltpu.VMEM((ex, fa // 2, width), BF16),
            DMA((9,)),
        ]
        + [pltpu.VMEM(x.shape, x.dtype) for x in (db, w_out, du, below, above, heads_t, qt, o, kv)],
        compiler_params=params(1, 62),
        name="attend_back",
        cost_estimate=cost(60),
    )(qt, db, w_out, o, lse, kv, arr, arr_other, dg, dg_other, rows, du, below, above, hid, hid_own, heads_t, arr_line, place, line, first)


def tn(a, b):
    return lax.dot_general(a, b, (((0,), (0,)), ((), ())), preferred_element_type=F32)


def loop(n, f):
    def step(i, carry):
        f(i)
        return carry

    lax.fori_loop(0, n, step, 0)


def moe_kernel(
    n,
    n_seq,
    experts_all,
    h_ref,
    cot_hbm,
    place_ref,
    place_t_hbm,
    routes_ref,
    router_ref,
    wg_hbm,
    wu_hbm,
    wd_hbm,
    line_hbm,
    gates_ref,
    rows_ref,
    arr_ref,
    hid_ref,
    dg_ref,
    du_ref,
    back_ref,
    comb_ref,
    arr_line,
    cot_first,
    line_out,
    wg,
    wu,
    wd,
    dout,
    dy,
    hid,
    back_rows,
    comb_rows,
    parts,
    cols,
    wsem,
    peers_sem,
    ysem,
    local,
    far_sem,
    router3,
    named,
    stage_sem,
    cot_ref,
    place_t_ref,
):
    s, c, m = lax.axis_index("seq"), lax.axis_index("ctx"), lax.axis_index("mp")
    load = Staged(((cot_hbm, cot_ref), (place_t_hbm, place_t_ref)), stage_sem)
    load.start()
    ex, width, ff = wg.shape
    slots = place_ref.shape[0] // ex
    first = m * ex
    lanes = gates_ref.shape[1]
    peers = Peers(n, lambda p: parts.at[p], lambda i: arr_line.at[i], peers_sem.at[0], peers_sem.at[1])
    cots = CotExchange(n, line_hbm, cot_first, 0, ysem)
    far = pltpu.make_async_remote_copy(
        src_ref=line_hbm.at[0],
        dst_ref=line_out.at[0],
        send_sem=far_sem.at[0],
        recv_sem=far_sem.at[1],
        device_id=(s, lax.rem(c + 1, n), m),
        device_id_type=MESH,
    )
    sem = pltpu.get_barrier_semaphore()
    peers.signal(sem)
    cots.signal(sem)
    weights = {}
    for e in range(ex):
        for i, (src, dst) in enumerate(((wg_hbm, wg), (wu_hbm, wu), (wd_hbm, wd))):
            weights[i, e] = pltpu.make_async_copy(src.at[e], dst.at[e], wsem.at[i, e])
            weights[i, e].start()

    pl.semaphore_wait(sem, n - 1 + 2)
    cots.start()

    @pl.when(c == n - 2)
    def _():
        far.start()

    def rows_of(e):
        return slice(e * slots, (e + 1) * slots)

    def arrive(i):
        cut = pl.ds(pl.multiple_of(i * slots, 16), slots)
        arr_ref[i] = nn(place_ref[cut, :], h_ref[...]).astype(BF16)

    loop(ex, arrive)
    size = width // (n * n_seq)
    for e in range(ex):
        for i in range(n):
            for j in range(n_seq):
                at = (j * n + i) * size
                parts[i, e, :, j * size : (j + 1) * size] = arr_ref[e, :, at : at + size]
    peers.start()
    own = pltpu.make_async_copy(parts.at[c], arr_line.at[c], local.at[0])
    own.start()

    router3[...] = jnp.zeros_like(router3)
    left = router_ref[...]
    for i in range(3):
        piece = left.astype(BF16)
        router3[i * experts_all : (i + 1) * experts_all, :] = piece
        left = left - piece.astype(F32)
    three = nt(h_ref[...], router3[...])
    logits = three + pltpu.roll(three, lanes - experts_all, 1) + pltpu.roll(three, lanes - 2 * experts_all, 1)
    which = lax.broadcasted_iota(jnp.int32, three.shape, 1)
    top = routes_ref.shape[0]
    named[...] = jnp.zeros_like(named)
    named[:top, :] = routes_ref[...].astype(F32)
    columns = named[...].T
    which = which.astype(F32)
    chosen = which == columns[:, 0:1]
    for k in range(1, top):
        chosen = jnp.logical_or(chosen, which == columns[:, k : k + 1])
    peak = jnp.max(jnp.where(chosen, logits, -1e30), axis=1, keepdims=True)
    raised = jnp.where(chosen, jnp.exp(jnp.where(chosen, logits - peak, 0.0)), 0.0)
    gates = raised / jnp.sum(raised, axis=1, keepdims=True)
    gates_ref[...] = gates
    g1 = gates.astype(BF16)
    rest = gates - g1.astype(F32)
    g2 = rest.astype(BF16)
    g3 = (rest - g2.astype(F32)).astype(BF16)
    lane = lax.broadcasted_iota(jnp.int32, (slots, lanes), 1)
    cols[...] = jnp.zeros_like(cols)
    gate_col = []
    for e in range(ex):
        pe = place_ref[rows_of(e), :]
        got = nn(pe, g1) + nn(pe, g2) + nn(pe, g3)
        col = jnp.sum(jnp.where(lane == first + e, got, 0.0), axis=1, keepdims=True)
        gate_col.append(col)
        cols[:slots, :] = cols[:slots, :] + jnp.where(lane == e, col, 0.0)

    rows_ref[...] = cols[...].T[:8, :]
    wide = 512
    load.wait(0)
    for e in range(ex):
        col = gate_col[e]

        def douts(i):
            cut = pl.ds(pl.multiple_of(i * wide, wide), wide)
            d = nn(place_ref[rows_of(e), :], cot_ref[:, cut])
            dout[e, :, cut] = d.astype(BF16)
            dy[e, :, cut] = (col * d).astype(BF16)

        loop(width // wide, douts)
        for i in range(3):
            weights[i, e].wait()

        def hidden(i):
            cut = pl.ds(pl.multiple_of(i * 256, 256), 256)
            g = nn(arr_ref[e], wg[e, :, cut])
            u = nn(arr_ref[e], wu[e, :, cut])
            dh = nt(dy[e], wd[e, cut, :])
            sigma = jax.nn.sigmoid(g)
            silu = g * sigma
            hid[:, cut] = (silu * u).astype(BF16)
            dg_ref[e, :, cut] = (dh * u * sigma * (1.0 + g * (1.0 - sigma))).astype(BF16)
            du_ref[e, :, cut] = (dh * silu).astype(BF16)

        loop(ff // 256, hidden)
        size = ff // (n * n_seq)
        for i in range(n):
            for j in range(n_seq):
                at = (j * n + i) * size
                hid_ref[i, e, :, j * size : (j + 1) * size] = hid[:, at : at + size]

        def outs(i, grads):
            cut = pl.ds(pl.multiple_of(i * wide, wide), wide)
            y = nn(hid[...], wd[e, :, cut]).astype(BF16).astype(F32)
            comb_rows[rows_of(e), cut] = (col * y).astype(BF16)
            back_rows[rows_of(e), cut] = (nt(dg_ref[e], wg[e, cut, :]) + nt(du_ref[e], wu[e, cut, :])).astype(BF16)
            return grads + jnp.sum(dout[e, :, cut].astype(F32) * y, axis=1, keepdims=True)

        grads = lax.fori_loop(0, width // wide, outs, jnp.zeros((slots, 1), F32))
        high = grads.astype(BF16).astype(F32)
        here = jnp.where(lane == first + e, high, jnp.where(lane == lanes // 2 + first + e, grads - high, 0.0))
        back_rows[rows_of(e), width:] = here.astype(BF16)

    load.wait(1)

    def scatter(i):
        cut = pl.ds(pl.multiple_of(i * 256, 256), 256)
        back_ref[:, cut] = nn(place_t_ref[...], back_rows[:, cut]).astype(BF16)
        comb_ref[:, cut] = nn(place_t_ref[...], comb_rows[:, cut]).astype(BF16)

    loop(width // 256, scatter)
    back_ref[:, width:] = nn(place_t_ref[...], back_rows[:, width:]).astype(BF16)
    own.wait()
    cots.finish()
    peers.finish()

    @pl.when(c == n - 2)
    def _():
        far.wait_send()

    @pl.when(c == n - 1)
    def _():
        far.wait_recv()


def moe(n, n_seq, experts_all, h, cot, place, place_t, routes, router, wg, wu, wd, line):
    ex, width, ff = wg.shape
    tok = h.shape[0]
    slots = place.shape[0] // ex
    blocks = n // 2
    sds = jax.ShapeDtypeStruct
    return pl.pallas_call(
        functools.partial(moe_kernel, n, n_seq, experts_all),
        out_shape=(
            sds((tok, 128), F32),
            sds((8, 256), F32),
            sds((ex, slots, width), BF16),
            sds((n, ex, slots, ff // n), BF16),
            sds((ex, slots, ff), BF16),
            sds((ex, slots, ff), BF16),
            sds((tok, width + 128), BF16),
            sds((tok, width), BF16),
            sds((n, ex, slots, width // n), BF16),
            sds((blocks, tok, width), BF16),
            sds(line.shape, BF16),
        ),
        in_specs=[VMEM, HBM, VMEM, HBM, VMEM, VMEM] + [HBM] * 4,
        out_specs=(VMEM,) * 8 + (HBM,) * 3,
        scratch_shapes=[
            pltpu.VMEM(wg.shape, BF16),
            pltpu.VMEM(wu.shape, BF16),
            pltpu.VMEM(wd.shape, BF16),
            pltpu.VMEM((ex, slots, width), BF16),
            pltpu.VMEM((ex, slots, width), BF16),
            pltpu.VMEM((slots, ff), BF16),
            pltpu.VMEM((ex * slots, width + 128), BF16),
            pltpu.VMEM((ex * slots, width), BF16),
            pltpu.VMEM((n, ex, slots, width // n), BF16),
            pltpu.VMEM((256, 128), F32),
            DMA((3, ex)),
            DMA((2, n)),
            DMA((2, 3, blocks)),
            DMA((1,)),
            DMA((2,)),
            pltpu.VMEM((128, width), BF16),
            pltpu.VMEM((8, tok), F32),
            DMA((2,)),
            pltpu.VMEM(cot.shape, BF16),
            pltpu.VMEM(place_t.shape, BF16),
        ],
        input_output_aliases={9: 10},
        compiler_params=params(6, 60),
        name="moe",
        cost_estimate=cost(30),
    )(h, cot, place, place_t, routes, router, wg, wu, wd, line)


class Mp:
    def __init__(self, part, core_in, y_out, y_in, full, sems, chunks):
        self.part, self.core_in, self.y_out, self.y_in, self.full = part, core_in, y_out, y_in, full
        self.sems, self.chunks = sems, chunks
        s, c, m = lax.axis_index("seq"), lax.axis_index("ctx"), lax.axis_index("mp")
        self.m = m
        self.sib = m + 1 - 2 * lax.rem(m, 2)
        self.opp = lax.rem(m + 2, 4)
        self.diag = lax.rem(self.sib + 2, 4)
        self.sib_id, self.opp_id = (s, c, self.sib), (s, c, self.opp)
        share = (part if part is not None else full).shape[1]
        self.rows = share // chunks

    def signal(self, sem):
        for d in (self.sib_id, self.opp_id):
            pl.semaphore_signal(sem, inc=1, device_id=d, device_id_type=MESH)

    def copy(self, src, dst, i, dev):
        return pltpu.make_async_remote_copy(
            src_ref=src,
            dst_ref=dst,
            send_sem=self.sems.at[0, i],
            recv_sem=self.sems.at[1, i],
            device_id=dev,
            device_id_type=MESH,
        )

    def cut(self, i):
        return pl.ds(i * self.rows, self.rows)

    def rs_core(self, i):
        src = self.part.at[self.diag] if i == 0 else self.part.at[self.sib]
        return self.copy(src, self.core_in.at[i], i, self.sib_id)

    def rs_y(self, i):
        return self.copy(self.y_out.at[self.cut(i)], self.y_in.at[self.cut(i)], 2 + i, self.opp_id)

    def rs_begin(self):
        self.rs_core(0).start()
        self.rs_core(1).start()
        self.rs_forward()

    def rs_forward(self):
        self.rs_core(0).wait_recv()
        for i in range(self.chunks):
            cut = self.cut(i)
            self.y_out[cut, :] = (
                self.part[self.opp, cut, :].astype(F32) + self.core_in[0, cut, :].astype(F32)
            ).astype(BF16)
            self.rs_y(i).start()
        self.rs_core(1).wait_recv()

    def rs_chunk(self, i):
        cut = self.cut(i)
        self.rs_y(i).wait_recv()
        return (
            self.part[self.m, cut, :].astype(F32) + self.core_in[1, cut, :].astype(F32)
        ) + self.y_in[cut, :].astype(F32)

    def rs_end(self):
        self.rs_core(0).wait_send()
        self.rs_core(1).wait_send()
        for i in range(self.chunks):
            self.rs_y(i).wait_send()

    def ag(self, kind, i, whose):
        block = self.full.at[whose, self.cut(i)]
        base = 2 + self.chunks
        dev = self.opp_id if kind == 0 else self.sib_id
        return self.copy(block, block, base + kind * self.chunks + i, dev)

    def ag_send(self, i):
        self.ag(0, i, self.m).start()
        self.ag(1, i, self.m).start()

    def ag_end(self):
        for i in range(self.chunks):
            self.ag(0, i, self.opp).wait_recv()
            self.ag(2, i, self.opp).start()
        for i in range(self.chunks):
            self.ag(1, i, self.sib).wait_recv()
            self.ag(2, i, self.diag).wait_recv()
            self.ag(0, i, self.m).wait_send()
            self.ag(1, i, self.m).wait_send()
            self.ag(2, i, self.opp).wait_send()


def mp_scratch(share, width, chunks):
    return [
        pltpu.VMEM((2, share, width), BF16),
        pltpu.VMEM((share, width), BF16),
        pltpu.VMEM((share, width), BF16),
        DMA((2, 2 + 4 * chunks)),
    ]


def rms_parts(rows):
    inverse = lax.rsqrt(jnp.mean(rows * rows, axis=-1, keepdims=True) + EPS)
    return rows * inverse, inverse


def rms_grad(grad_normed, normed, inverse):
    return inverse * (grad_normed - normed * jnp.mean(grad_normed * normed, axis=-1, keepdims=True))


def mid_forward_kernel(
    chunks,
    n,
    ex,
    heads_ref,
    wout_ref,
    gain,
    own,
    above,
    routes_ref,
    tok_hbm,
    resid_ref,
    h_ref,
    place_ref,
    place_t,
    place_line,
    line_ref,
    core_in,
    y_out,
    y_in,
    sems,
    send,
    recv,
    local,
    x_ref,
    x_sem,
    ranks,
    part,
):
    c = lax.axis_index("ctx")
    mp = Mp(part, core_in, y_out, y_in, h_ref, sems, chunks)
    spread = Spread(n, own, None, above, line_ref, send, recv, local, short=True)
    x_copy = pltpu.make_async_copy(tok_hbm.at[mp.m], x_ref, x_sem.at[0])
    x_copy.start()
    sem = pltpu.get_barrier_semaphore()
    mp.signal(sem)
    signal_line(n, sem)
    share, width = x_ref.shape

    def outs(i):
        at = pl.ds(pl.multiple_of(i * 512, 512), 512)
        rows = tn(heads_ref[...], wout_ref[:, at]).astype(BF16)
        for p in range(part.shape[0]):
            part[p, :, at] = rows[p * share : (p + 1) * share, :]

    loop(width // 512, outs)
    pl.semaphore_wait(sem, 2 + line_degree(n))
    mp.rs_core(0).start()
    mp.rs_core(1).start()
    spread.start()
    mp.rs_forward()
    tok = routes_ref.shape[2]
    slots = place_ref.shape[0] // ex
    before = (
        lax.broadcasted_iota(jnp.int32, (tok, tok), 0) <= lax.broadcasted_iota(jnp.int32, (tok, tok), 1)
    ).astype(BF16)

    def places(b):
        at = b * ex
        ranks[...] = jnp.zeros_like(ranks)
        for e in range(ex):
            hit = routes_ref[b] == mp.m * ex + e
            ranks[e : e + 1, :] = jnp.max(hit.astype(F32), axis=0, keepdims=True)
        sel = ranks[...]
        order = nn(sel.astype(BF16), before) - 1.0
        rows = lax.broadcasted_iota(jnp.int32, (slots, tok), 0).astype(F32)
        for e in range(ex):
            one = jnp.where(rows == order[e : e + 1, :], 1.0, 0.0) * sel[e : e + 1, :]
            place_line[b, e * slots : (e + 1) * slots, :] = one.astype(BF16)

    places(c)
    place_ref[...] = place_line[c]
    place_t[...] = place_ref[...].T
    x_copy.wait()
    for i in range(chunks):
        cut = mp.cut(i)
        resid = x_ref[cut, :].astype(F32) + mp.rs_chunk(i)
        resid_ref[cut, :] = resid
        normed, _ = rms_parts(resid)
        h_ref[mp.m, cut, :] = (normed * gain[...].reshape(1, -1)).astype(BF16)
        mp.ag_send(i)
    spread.tick(1)
    loop(n - 1, lambda i: places(lax.rem(c + 1 + i, n)))
    mp.ag_end()
    mp.rs_end()
    spread.ticks(2)
    spread.finish()


def mid_forward(n, ex, slots, heads_t, w_out, gain, own, above, routes_line, tokens, chunks=2):
    k, share, width = tokens.shape
    tok = k * share
    sds = jax.ShapeDtypeStruct
    return pl.pallas_call(
        functools.partial(mid_forward_kernel, chunks, n, ex),
        out_shape=(
            sds((share, width), F32),
            sds(tokens.shape, BF16),
            sds((ex * slots, tok), BF16),
            sds((tok, ex * slots), BF16),
            sds((n, ex * slots, tok), BF16),
            sds((n,) + own.shape, BF16),
        ),
        in_specs=[VMEM] * 6 + [HBM],
        out_specs=(VMEM,) * 5 + (HBM,),
        scratch_shapes=mp_scratch(share, width, chunks)
        + [DMA((n,)), DMA((n,)), DMA((3,)), pltpu.VMEM((share, width), BF16), DMA((1,)), pltpu.VMEM((8, tok), F32)]
        + [pltpu.VMEM(tokens.shape, BF16)],
        compiler_params=params(2, 58),
        name="mid_forward",
        cost_estimate=cost(30),
    )(heads_t, w_out, gain, own, above, routes_line, tokens)


def mid_back_kernel(
    chunks,
    n,
    part,
    resid_hbm,
    gain,
    cot_hbm,
    gate_hbm,
    router_ref,
    rows_ref,
    hid_ref,
    du_ref,
    arr_ref,
    dg_ref,
    dresid_ref,
    db_ref,
    small_ref,
    rows_line,
    hid_line,
    below_ref,
    above_ref,
    arr_other,
    dg_other,
    core_in,
    y_out,
    y_in,
    sems,
    side,
    peers_sem,
    swap_sem,
    stage_sem,
    resid_ref,
    cot,
    gate_ref,
):
    c = lax.axis_index("ctx")
    load = Staged(((resid_hbm, resid_ref), (cot_hbm, cot), (gate_hbm, gate_ref)), stage_sem)
    load.start()
    mp = Mp(part, core_in, y_out, y_in, db_ref, sems, chunks)
    rows_peers = Peers(n, lambda p: rows_ref, lambda i: rows_line.at[i], peers_sem.at[0], peers_sem.at[1])
    hid_peers = Peers(n, lambda p: hid_ref.at[p], lambda i: hid_line.at[i], peers_sem.at[2], peers_sem.at[3])
    beside = Neighbours(n, du_ref, below_ref, above_ref, side.at[0], side.at[1])
    width = gain.shape[0]
    ex = router_ref.shape[0]
    lanes = gate_ref.shape[2]
    sem = pltpu.get_barrier_semaphore()
    mp.signal(sem)
    rows_peers.signal(sem)
    partner = swap_partner()
    pl.semaphore_signal(sem, inc=1, device_id=partner, device_id_type=MESH)
    pl.semaphore_wait(sem, 2 + n - 1 + 1)
    mp.rs_core(0).start()
    mp.rs_core(1).start()
    half_width = width // 2
    theirs = pl.ds(pl.multiple_of((1 - lax.axis_index("seq")) * half_width, 128), half_width)
    swaps = [
        swap(arr_ref.at[:, :, theirs], arr_other, swap_sem, 0),
        swap(dg_ref, dg_other, swap_sem, 1),
    ]
    for sw in swaps:
        sw.start()
    beside.start_up()
    beside.start_down()
    rows_peers.start()
    hid_peers.start()
    mp.rs_forward()
    rows_line[c] = rows_ref[...]
    small_ref[...] = jnp.zeros_like(small_ref)
    load.wait(0, 1, 2)
    for i in range(chunks):
        cut = mp.cut(i)
        both = mp.rs_chunk(i)
        dgate = both[:, width : width + ex] + both[:, width + lanes // 2 : width + lanes // 2 + ex]
        gate = gate_ref[mp.m, cut, :ex]
        dlog = gate * (dgate - jnp.sum(gate * dgate, axis=-1, keepdims=True))
        dh = both[:, :width] + jnp.dot(
            dlog, router_ref[...], precision=lax.Precision.HIGHEST, preferred_element_type=F32
        )
        normed, inverse = rms_parts(resid_ref[cut, :])
        small_ref[1:2, :] = small_ref[1:2, :] + jnp.sum(dh * normed, axis=0, keepdims=True)
        h_two = (normed * gain[...].reshape(1, -1)).astype(BF16).astype(F32)
        small_ref[8 : 8 + ex, :] = small_ref[8 : 8 + ex, :] + lax.dot_general(
            dlog, h_two, (((0,), (0,)), ((), ())), precision=lax.Precision.HIGHEST, preferred_element_type=F32
        )
        dresid = cot[cut, :].astype(F32) + rms_grad(dh * gain[...].reshape(1, -1), normed, inverse)
        dresid_ref[cut, :] = dresid
        db_ref[mp.m, cut, :] = dresid.astype(BF16)
        mp.ag_send(i)
    mp.ag_end()
    mp.rs_end()
    rows_peers.finish()
    hid_peers.finish()
    beside.finish()
    for sw in swaps:
        sw.wait()


def swap_partner():
    return (1 - lax.axis_index("seq"), lax.axis_index("ctx"), lax.axis_index("mp"))


def swap(src, dst, sems, i):
    return pltpu.make_async_remote_copy(
        src_ref=src,
        dst_ref=dst,
        send_sem=sems.at[0, i],
        recv_sem=sems.at[1, i],
        device_id=swap_partner(),
        device_id_type=MESH,
    )


def mid_back(n, part, resid, gain, cot, gate, router_t, rows, hid, du, arr, dg, chunks=2):
    k, share, wide = part.shape
    width = gain.shape[0]
    return pl.pallas_call(
        functools.partial(mid_back_kernel, chunks, n),
        out_shape=(
            jax.ShapeDtypeStruct((share, width), F32),
            jax.ShapeDtypeStruct((k, share, width), BF16),
            jax.ShapeDtypeStruct((8 + router_t.shape[0], width), F32),
            jax.ShapeDtypeStruct((n,) + rows.shape, F32),
            jax.ShapeDtypeStruct(hid.shape, BF16),
            jax.ShapeDtypeStruct(du.shape, BF16),
            jax.ShapeDtypeStruct(du.shape, BF16),
            jax.ShapeDtypeStruct(arr.shape[:2] + (arr.shape[2] // 2,), BF16),
            jax.ShapeDtypeStruct(dg.shape, BF16),
        ),
        in_specs=[VMEM, HBM, VMEM, HBM, HBM, VMEM, VMEM] + [HBM] * 4,
        out_specs=(VMEM,) * 4 + (HBM,) * 5,
        scratch_shapes=mp_scratch(share, wide, chunks) + [DMA((2, 2)), DMA((4, n)), DMA((2, 2)), DMA((3,))]
        + [pltpu.VMEM(x.shape, x.dtype) for x in (resid, cot, gate)],
        compiler_params=params(3, 60),
        name="mid_back",
        cost_estimate=cost(32),
    )(part, resid, gain, cot, gate, router_t, rows, hid, du, arr, dg)


class SmallSum:
    def __init__(self, sizes, x_ref, out_ref, bufs, sems):
        self.sizes, self.x, self.out, self.bufs, self.sems = sizes, x_ref, out_ref, bufs, sems
        self.me = [lax.axis_index(a) for a in ("seq", "ctx", "mp")]

    def peer(self, axis, d):
        ids = list(self.me)
        ids[axis] = lax.rem(self.me[axis] + d, self.sizes[axis])
        return tuple(ids)

    def signal(self, sem):
        for axis in range(3):
            for d in range(1, self.sizes[axis]):
                pl.semaphore_signal(sem, inc=1, device_id=self.peer(axis, d), device_id_type=MESH)
        return sum(self.sizes) - 3

    def move(self, axis, d):
        base = sum(self.sizes[:axis])
        buf = self.bufs[axis]
        return pltpu.make_async_remote_copy(
            src_ref=buf.at[0],
            dst_ref=buf.at[d],
            send_sem=self.sems.at[0, base + d],
            recv_sem=self.sems.at[1, base + d],
            device_id=self.peer(axis, d),
            device_id_type=MESH,
        )

    def begin(self, axis, value):
        self.bufs[axis][0] = value
        for d in range(1, self.sizes[axis]):
            self.move(axis, d).start()

    def end(self, axis):
        n = self.sizes[axis]
        for d in range(1, n):
            self.move(axis, d).wait()
        total = jnp.zeros(self.out.shape, F32)
        for i in range(n):
            total = total + self.bufs[axis][lax.rem(self.me[axis] - i + n, n)]
        return total


def last_kernel(
    chunks,
    sizes,
    dqkv_ref,
    h_hbm,
    wq_hbm,
    wk_hbm,
    wv_hbm,
    tok_hbm,
    gain,
    dresid_hbm,
    small_ref,
    wout_ref,
    up0_hbm,
    up_other,
    comb_hbm,
    resid_hbm,
    out_ref,
    final_ref,
    total_ref,
    gout_ref,
    gqkv_ref,
    up_ref,
    core_in,
    y_out,
    y_in,
    sems,
    core_in2,
    y_out2,
    y_in2,
    sems2,
    h_ref,
    wq_ref,
    wk_ref,
    wv_ref,
    tok_ref,
    dresid_ref,
    comb,
    resid_ref,
    part,
    dh_ref,
    qkv_ref,
    swapped,
    summed,
    wout_in,
    qkv_in,
    up_in,
    load_sem,
    swap_sem,
    peers_sem,
    *rest,
):
    n = sizes[1]
    s, c = lax.axis_index("seq"), lax.axis_index("ctx")
    load = Staged(
        (
            (h_hbm, h_ref),
            (wq_hbm, wq_ref),
            (wk_hbm, wk_ref),
            (wv_hbm, wv_ref),
            (tok_hbm, tok_ref),
            (comb_hbm, comb),
            (dresid_hbm, dresid_ref),
            (resid_hbm, resid_ref),
            (up0_hbm, up_ref),
        ),
        load_sem,
    )
    load.start()
    mp = Mp(part, core_in, y_out, y_in, None, sems, chunks)
    mp2 = Mp(comb, core_in2, y_out2, y_in2, None, sems2, chunks)
    small = SmallSum(sizes, small_ref, total_ref, rest[:3], rest[3])
    half_rows = swapped.shape[0]
    rows = half_rows // n
    wout_peers = Peers(
        n, lambda p: wout_ref.at[cut_of(p, rows)], lambda i: wout_in.at[i], peers_sem.at[0], peers_sem.at[1]
    )
    qkv_peers = Peers(
        n, lambda p: summed.at[cut_of(p, rows)], lambda i: qkv_in.at[i], peers_sem.at[2], peers_sem.at[3]
    )
    sem = pltpu.get_barrier_semaphore()
    pl.semaphore_wait(sem, small.signal(sem))
    wout_peers.start()
    load.wait(0)

    def weight_rows(first):
        def piece(r):
            at = pl.ds(pl.multiple_of(first + r * 256, 256), 256)
            qkv_ref[at, :] = tn(h_ref[:, at], dqkv_ref[...]).astype(BF16)

        loop(half_rows // 256, piece)

    weight_rows((1 - s) * half_rows)

    def chunk_swap(k):
        p = lax.rem(c + 1 + k, n)
        return swap(qkv_ref.at[cut_of((1 - s) * n + p, rows)], swapped.at[cut_of(p, rows)], swap_sem, k)

    up_swap = swap(up_other, up_in, swap_sem, n)

    def chunk_arrived(k):
        chunk_swap(k).wait_recv()
        if k + 2 < n:
            chunk_swap(k + 2).start()
        if k + 2 == n:
            up_swap.start()
        p = lax.rem(c + 1 + k, n)
        here = cut_of(p, rows)
        summed[here, :] = (
            qkv_ref[cut_of(s * n + p, rows), :].astype(F32) + swapped[here, :].astype(F32)
        ).astype(BF16)
        if k < n - 1:
            qkv_peers.move(k + 1).start()

    for k in range(min(2, n)):
        chunk_swap(k).start()
    load.wait(1, 2, 3)
    share, width = out_ref.shape
    qw, kw = wq_ref.shape[1], wk_ref.shape[1]

    def token_rows(i):
        at = pl.ds(pl.multiple_of(i * 512, 512), 512)
        dh = nt(dqkv_ref[:, :qw], wq_ref[at, :])
        dh = dh + nt(dqkv_ref[:, qw : qw + kw], wk_ref[at, :])
        dh = dh + nt(dqkv_ref[:, qw + kw :], wv_ref[at, :])
        for p in range(part.shape[0]):
            dh_ref[p, :, at] = dh[p * share : (p + 1) * share, :]
            part[p, :, at] = dh[p * share : (p + 1) * share, :].astype(BF16)

    loop(width // 512, token_rows)
    mp.rs_core(0).start()
    mp.rs_core(1).start()
    load.wait(5)
    mp2.rs_core(0).start()
    mp2.rs_core(1).start()
    weight_rows(s * half_rows)
    mp.rs_forward()
    load.wait(4)
    total_ref[...] = small_ref[...]

    def norm_rows(p):
        normed, _ = rms_parts(tok_ref[p].astype(F32))
        total_ref[0:1, :] = total_ref[0:1, :] + jnp.sum(dh_ref[p] * normed, axis=0, keepdims=True)

    loop(part.shape[0], norm_rows)
    small.begin(1, total_ref[...])
    chunk_arrived(0)
    mp2.rs_forward()
    chunk_arrived(1)
    load.wait(6)
    for i in range(chunks):
        cut = mp.cut(i)
        dh = mp.rs_chunk(i)
        normed, inverse = rms_parts(tok_ref[mp.m, cut, :].astype(F32))
        final_ref[cut, :] = dresid_ref[cut, :] + rms_grad(dh * gain[...].reshape(1, -1), normed, inverse)
        if i + 2 < n:
            chunk_arrived(i + 2)
        if i == 0:
            small.begin(0, small.end(1))
    for k in range(chunks + 2, n):
        chunk_arrived(k)
    small.begin(2, small.end(0))
    load.wait(7)
    for i in range(chunks):
        cut = mp.cut(i)
        out_ref[cut, :] = resid_ref[cut, :] + mp2.rs_chunk(i)
    total_ref[...] = small.end(2)
    wout_peers.finish()
    wout_in[c] = wout_ref[cut_of(c, rows), :]
    total = jnp.zeros(gout_ref.shape, F32)
    for i in range(n):
        total = total + wout_in[i].astype(F32)
    gout_ref[...] = total
    mp.rs_end()
    mp2.rs_end()
    load.wait(8)
    for k in range(n):
        chunk_swap(k).wait_send()
    qkv_peers.finish()
    qkv_in[c] = summed[cut_of(c, rows), :]
    total = jnp.zeros(gqkv_ref.shape, F32)
    for i in range(n):
        total = total + qkv_in[i].astype(F32)
    gqkv_ref[...] = total
    up_swap.wait()
    up_ref[...] = up_ref[...] + up_in[...].astype(F32)


def cut_of(i, rows):
    return pl.ds(pl.multiple_of(i * rows, 16), rows)


def last(sizes, dqkv, h, wq, wk, wv, tokens, gain, dresid, small, wout, up0, up_other, comb, resid, chunks=2):
    k, share, width = comb.shape
    n = sizes[1]
    half_rows, fo = wout.shape
    fq = dqkv.shape[1]
    rows = half_rows // n
    sds = jax.ShapeDtypeStruct
    vm = lambda x: pltpu.VMEM(x.shape, x.dtype)
    return pl.pallas_call(
        functools.partial(last_kernel, chunks, sizes),
        out_shape=(
            sds((share, width), F32),
            sds((share, width), F32),
            sds(small.shape, F32),
            sds((rows, fo), F32),
            sds((rows, fq), F32),
            sds(up0.shape, F32),
        ),
        in_specs=[VMEM] + [HBM] * 5 + [VMEM, HBM, VMEM, VMEM, HBM, VMEM, HBM, HBM],
        out_specs=(VMEM,) * 6,
        scratch_shapes=mp_scratch(share, width, chunks)
        + mp_scratch(share, width, chunks)
        + [vm(h), vm(wq), vm(wk), vm(wv), vm(tokens), vm(dresid), vm(comb), vm(resid)]
        + [
            pltpu.VMEM(comb.shape, BF16),
            pltpu.VMEM(comb.shape, F32),
            pltpu.VMEM((2 * half_rows, fq), BF16),
            pltpu.VMEM((half_rows, fq), BF16),
            pltpu.VMEM((half_rows, fq), BF16),
            pltpu.VMEM((n, rows, fo), BF16),
            pltpu.VMEM((n, rows, fq), BF16),
            pltpu.VMEM(up0.shape, BF16),
            DMA((9,)),
            DMA((2, n + 1)),
            DMA((4, n)),
        ]
        + [pltpu.VMEM((d,) + small.shape, F32) for d in sizes]
        + [DMA((2, sum(sizes)))],
        compiler_params=params(4, 60),
        name="last",
        cost_estimate=cost(60),
    )(dqkv, h, wq, wk, wv, tokens, gain, dresid, small, wout, up0, up_other, comb, resid)


def finish_kernel(*refs):
    n_in = 8
    total, gout, gqkv = refs[5:n_in]
    outs = refs[n_in : n_in + 12]
    sems = refs[n_in + 12]
    output, tokens, norm1, gq, gk, gv, go, norm2, router, gate, up, down = outs
    large = Staged(tuple(zip(refs[:5], (output, tokens, gate, up, down))), sems)
    large.start()
    norm1[...] = total[0, :]
    norm2[...] = total[1, :]
    router[...] = total[8 : 8 + router.shape[0], :]
    qw, kw = gq.shape[1], gk.shape[1]
    gq[...] = gqkv[:, :qw]
    gk[...] = gqkv[:, qw : qw + kw]
    gv[...] = gqkv[:, qw + kw :]
    go[...] = gout[...].T
    large.wait(0, 1, 2, 3, 4)


def finish(experts_all, qw, output, tokens, gate, up, down, total, gout, gqkv):
    sds = jax.ShapeDtypeStruct
    width = total.shape[1]
    rows = gqkv.shape[0]
    kw = (gqkv.shape[1] - qw) // 2
    shapes = (
        output.shape,
        tokens.shape,
        (width,),
        (rows, qw),
        (rows, kw),
        (rows, kw),
        gout.shape[::-1],
        (width,),
        (experts_all, width),
        gate.shape,
        up.shape,
        down.shape,
    )
    return pl.pallas_call(
        finish_kernel,
        out_shape=tuple(sds(x, F32) for x in shapes),
        in_specs=[HBM] * 5 + [VMEM] * 3,
        out_specs=(VMEM,) * 12,
        scratch_shapes=[DMA((5,))],
        compiler_params=pltpu.CompilerParams(vmem_limit_bytes=60 * MIB),
        name="finish",
        cost_estimate=cost(6),
    )(output, tokens, gate, up, down, total, gout, gqkv)


def body(
    tokens,
    norm1_gain,
    w_query,
    key_weight_matrix,
    value_weight_matrix,
    w_out,
    norm2_gain,
    router,
    w_gate,
    w_up,
    w_down,
    routes,
    cotangent,
):
    n_seq, n_ctx, n_mp = (lax.axis_size(a) for a in ("seq", "ctx", "mp"))
    s, c, m = (lax.axis_index(a) for a in ("seq", "ctx", "mp"))
    tok, width = tokens.shape
    share = tok // n_mp
    experts_all = router.shape[1]
    exp_local = w_gate.shape[0]
    top = routes.shape[1]
    cap = share * top * 5 // (4 * experts_all)
    slots = -(-n_mp * cap // 16) * 16

    cot_all = lax.all_gather(cotangent, "mp", axis=0, tiled=True)
    by_share = tokens.reshape(n_mp, share, width)

    qt, h_one, o, heads_t, lse, kv, cot_above, routes_line = attend(
        n_ctx, tokens, norm1_gain, w_query, key_weight_matrix, value_weight_matrix, cotangent, routes.T
    )
    resid, h_two, place, place_t, place_line, cot_line = mid_forward(
        n_ctx, exp_local, slots, heads_t, w_out, norm2_gain, cotangent, cot_above, routes_line, by_share
    )
    h_two = h_two.reshape(tok, width)

    gates, gate_rows, arrived, hidden, dg, du, back, comb, arrived_line, cot_first, cot_line = moe(
        n_ctx, n_seq, experts_all, h_two, cot_all, place, place_t, routes.T, router.T, w_gate, w_up, w_down, cot_line
    )
    dresid, db, small, gate_rows_line, hidden_line, du_below, du_above, arrived_other, dg_other = mid_back(
        n_ctx,
        back.reshape(n_mp, share, -1),
        resid,
        norm2_gain,
        cotangent,
        gates.reshape(n_mp, share, -1),
        router.T,
        gate_rows,
        hidden,
        du,
        arrived,
        dg,
    )

    db = db.reshape(tok, width)
    dqkv, g_gate, g_down, up0, up_other, g_out, _, _ = attend_back(
        n_ctx,
        qt,
        db,
        w_out,
        o,
        lse,
        kv,
        arrived,
        arrived_other,
        dg,
        dg_other,
        gate_rows_line,
        du,
        du_below,
        du_above,
        hidden_line,
        hidden,
        heads_t,
        arrived_line,
        place_line,
        cot_line,
        cot_first,
    )
    output, grad_tokens, small, g_out, g_qkv, g_up = last(
        (n_seq, n_ctx, n_mp),
        dqkv,
        h_one,
        w_query,
        key_weight_matrix,
        value_weight_matrix,
        by_share,
        norm1_gain,
        dresid,
        small,
        g_out,
        up0,
        up_other,
        comb.reshape(n_mp, share, width),
        resid,
    )
    outs = finish(experts_all, w_query.shape[1], output, grad_tokens, g_gate, g_up, g_down, small, g_out, g_qkv)
    return outs[:8] + (outs[8].T,) + outs[9:]


def solution(mesh):
    placed = (
        P(("seq", "ctx"), None),
        P(),
        P(None, "mp"),
        P(None, "mp"),
        P(None, "mp"),
        P("mp", None),
        P(),
        P(),
        P("mp", None, None),
        P("mp", None, None),
        P("mp", None, None),
        P(("seq", "ctx"), None),
        P(("seq", "ctx", "mp"), None),
    )
    return jax.shard_map(
        body,
        mesh=mesh,
        in_specs=placed,
        out_specs=(
            P(("seq", "ctx", "mp"), None),
            P(("seq", "ctx", "mp"), None),
            P(),
            P(("seq", "ctx"), "mp"),
            P(("seq", "ctx"), "mp"),
            P(("seq", "ctx"), "mp"),
            P("mp", ("seq", "ctx")),
            P(),
            P(),
            P("mp", ("seq", "ctx"), None),
            P("mp", ("seq", "ctx"), None),
            P("mp", ("seq", "ctx"), None),
        ),
        check_vma=False,
    )
```
